32 devices in a mesh: dp: 8 (over y, x, core), tensor: 4 (over z).
Axes of the slice: x: 2, y: 2, z: 4, core: 2. Of those that a mesh axis runs over, the one named last changes fastest.
Arguments:
- activations: bfloat16 [8, 256, 3072], P('dp', None, 'tensor')
- out_grads: bfloat16 [8, 256, 5120], P('dp', 'tensor')
- error_buffer: bfloat16 [8, 3072, 5120], P('dp', 'tensor'), may hold values from -4 to 4
- warm_factor: float32 [5120, 4], replicated, may hold values from -6 to 6
Outputs:
- rebuilt_grad: bfloat16 [3072, 5120], P('tensor')
- next_error: bfloat16 [8, 3072, 5120], P('dp', 'tensor')
- next_factor: float32 [5120, 4], replicated
The draws below stay inside these ranges and needn't reach their ends.
All inputs are finite; a program needn't handle non-finite values.
Results may differ from the reference program's by a relative error of at most 0.00105.
Values may be sent and summed in bfloat16 or wider, within the bound.
No kernel may reach another device: no remote copies, remote signals or barrier semaphores. Data moves between devices by JAX's collectives and lax.ppermute only.
A program may use at most 128 MiB of HBM per device.

```python
import math
import jax
import jax.numpy as jnp
from jax import lax

D = 5120
RANK = 4
TOK = 256
ROWS = 3072
N_DP = 8


def draw_activations(key, part):
    key = jax.random.fold_in(key, 11)
    first, second = jax.random.split(key)
    common = jax.random.normal(first, (1, TOK, ROWS), jnp.float32)
    own = jax.random.normal(second, (N_DP, TOK, ROWS), jnp.float32)
    mixed = 0.6 * common + 0.8 * own
    return mixed.astype(jnp.bfloat16)


def draw_out_grads(key, part):
    key = jax.random.fold_in(key, 23)
    first, second, third = jax.random.split(key, 3)
    token_scale = jnp.exp(jax.random.uniform(first, (1, TOK, 1), jnp.float32, 0.0, math.log(10.0)))
    replica_scale = 0.5 + jnp.arange(N_DP, dtype=jnp.float32).reshape(N_DP, 1, 1) / max(N_DP - 1, 1)
    common = jax.random.normal(second, (1, TOK, D), jnp.float32)
    own = jax.random.normal(third, (N_DP, TOK, D), jnp.float32)
    mixed = 0.6 * common + 0.8 * own
    values = 0.25 * token_scale * replica_scale * mixed / math.sqrt(TOK)
    return values.astype(jnp.bfloat16)


def steps_of(rng, shape, cuts, smallest, largest):
    def one(position, parts):
        heights = jax.random.uniform(jax.random.fold_in(jax.random.fold_in(rng, 6), position), (parts,), jnp.float32, smallest / len(cuts), largest / len(cuts))
        return jnp.repeat(jnp.exp(heights), shape[position] // parts).reshape((-1,) + (1,) * (len(shape) - position - 1))

    level = one(*cuts[0])
    for cut in cuts[1:]:
        level = level * one(*cut)
    return level


def noise(stream_key, extent, width, limit, shards=(), kind=jnp.bfloat16):
    factor_of = steps_of(stream_key, extent, shards, -0.22, 0.18) if shards else 1.0
    array = jax.random.normal(stream_key, extent, jnp.float32) * width * factor_of
    return jnp.minimum(jnp.maximum(array, -limit), limit).astype(kind)


def setup_inputs(seed: int = 0) -> dict:
    seeds = jax.random.split(jax.random.key(seed), 5)
    return {
        "activations": draw_activations(jax.random.fold_in(seeds[4], 71), 0),
        "out_grads": draw_out_grads(jax.random.fold_in(seeds[4], 71), 0),
        "error_buffer": noise(seeds[2], (N_DP, ROWS, D), 0.3, 4.0, ((0, 8), (1, 4))),
        "warm_factor": noise(seeds[3], (D, RANK), 1.0, 6.0, (), jnp.float32),
    }


def replica_matrix(activations, out_grads, error_buffer, replica):
    grad = jnp.dot(activations[replica].T.astype(jnp.float32), out_grads[replica].astype(jnp.float32), preferred_element_type=jnp.float32)
    return grad + error_buffer[replica].astype(jnp.float32)

def reference(activations, out_grads, error_buffer, warm_factor):
    high = lax.Precision.HIGHEST

    def left_step(replica, total):
        matrix = replica_matrix(activations, out_grads, error_buffer, replica)
        return total + jnp.dot(matrix, warm_factor, precision=high)
    left_total = lax.fori_loop(0, N_DP, left_step, jnp.zeros((ROWS, RANK), jnp.float32))
    left_mean = left_total / N_DP
    gram = jnp.dot(left_mean.T, left_mean, precision=high)
    lower = jnp.linalg.cholesky(gram)
    left_ortho = lax.linalg.triangular_solve(lower, left_mean, left_side=False, lower=True, transpose_a=True)

    def right_step(replica, total):
        matrix = replica_matrix(activations, out_grads, error_buffer, replica)
        return total + jnp.dot(matrix.T, left_ortho, precision=high)
    right_total = lax.fori_loop(0, N_DP, right_step, jnp.zeros((D, RANK), jnp.float32))
    next_factor = right_total / N_DP
    rebuilt = jnp.dot(left_ortho, next_factor.T, precision=high)

    def new_error(replica):
        matrix = replica_matrix(activations, out_grads, error_buffer, replica)
        return (matrix - rebuilt).astype(jnp.bfloat16)
    next_error = lax.map(new_error, jnp.arange(N_DP, dtype=jnp.int32))
    return (rebuilt.astype(jnp.bfloat16), next_error, next_factor)
```

```python
import functools

import jax
import jax.numpy as jnp
from jax import lax
from jax.experimental import pallas as pl
from jax.experimental.pallas import tpu as pltpu
from jax.sharding import PartitionSpec as P

F32 = jnp.float32
BF16 = jnp.bfloat16
SHRINK = 2.0**-23
TINY = 1e-30
PARTS = 2
BLOCK = 512


def params(mib):
    return pltpu.CompilerParams(vmem_limit_bytes=mib * 2**20)


def cost(flops, moved):
    return pl.CostEstimate(flops=int(flops), bytes_accessed=int(moved), transcendentals=0)


def dot(a, b, contract):
    return lax.dot_general(a, b, ((contract[:1], contract[1:]), ((), ())), preferred_element_type=F32)


def split(x):
    hi = x.astype(BF16)
    rest = x - hi.astype(F32)
    mid = rest.astype(BF16)
    lo = (rest - mid.astype(F32)).astype(BF16)
    return hi.astype(F32), mid.astype(F32), lo.astype(F32)


def stack3(x, ref):
    rank = x.shape[0]
    for i, part in enumerate(split(x)):
        ref[i * rank : (i + 1) * rank, :] = part
    return ref[...].astype(BF16)


def sum3(y, rank):
    return (y[2 * rank :] + y[rank : 2 * rank]) + y[:rank]


def ring_of(n):
    return [2 * p if 2 * p < n else 2 * (n - p) - 1 for p in range(n)]


def ring_source(me, step, n):
    place = jnp.where(lax.rem(me, 2) == 0, me // 2, n - (me + 1) // 2)
    place = lax.rem(place - step + n, n)
    return jnp.where(2 * place < n, 2 * place, 2 * (n - place) - 1)


def ring_step(x, axis, n):
    ring = ring_of(n)
    return lax.ppermute(x, axis, [(ring[p], ring[(p + 1) % n]) for p in range(n)])


def exchange(pieces, axis, n):
    return [pieces[0]] + [
        lax.ppermute(pieces[k], axis, [(i, (i + k) % n) for i in range(n)]) for k in range(1, n)
    ]


def token_factor_kernel(w_ref, g_ref, out_ref, w3):
    rank = w_ref.shape[0]
    parts = stack3(w_ref[...] * SHRINK, w3)
    out_ref[...] = sum3(dot(parts, g_ref[0], (1, 1)), rank)


def error_left_kernel(w_ref, e_ref, out_ref, w3):
    rank = w_ref.shape[0]

    @pl.when(pl.program_id(0) == 0)
    def _():
        stack3(w_ref[...] * SHRINK, w3)

    out_ref[...] = sum3(dot(w3[...].astype(BF16), e_ref[0], (1, 1)), rank)


def left_kernel(n, *refs):
    a_ref, e_ref = refs[:2]
    gws = refs[2 : 2 + n]
    out_ref, g3 = refs[2 + n :]
    rank, tok = gws[0].shape
    me = lax.axis_index("tensor")
    total = e_ref[...]
    for k in range(n):
        src = lax.rem(me - k + n, n)
        rows = a_ref[0, pl.ds(pl.multiple_of(src * tok, tok), tok), :]
        total += sum3(dot(stack3(gws[k][...], g3), rows, (1, 0)), rank)
    out_ref[...] = total


def mean_kernel(m, n, *refs):
    a_ref = refs[0]
    pieces = refs[1 : 1 + m]
    p_ref = refs[1 + m]
    msgs = refs[2 + m : 2 + m + n]
    inbox, p3, outbox = refs[2 + m + n :]
    rank = p_ref.shape[0]
    tok = a_ref.shape[1] // n
    me_r = lax.axis_index("dp")
    me_t = lax.axis_index("tensor")
    for k in range(m):
        inbox[lax.rem(me_r - k + m, m)] = pieces[k][...]
    total = inbox[0]
    for r in range(1, m):
        total += inbox[r]
    mean = total * (1.0 / (SHRINK * m))
    p_ref[...] = mean
    top = jnp.max(jnp.max(jnp.abs(mean), axis=1, keepdims=True), axis=0, keepdims=True)
    top = jnp.maximum(top, TINY)
    parts = stack3(mean / (top * 1024.0), p3)
    outbox[...] = jnp.zeros_like(outbox)
    for t in range(n):
        y = dot(parts, a_ref[0, t * tok : (t + 1) * tok, :], (1, 1))
        outbox[t, 0:rank, 0:tok] = sum3(y, rank)
        for i in range(rank):
            column = jnp.sum(mean * mean[i : i + 1, :], axis=1, keepdims=True)
            outbox[t, rank : 2 * rank, i : i + 1] = column
        outbox[t, rank : rank + 1, rank : rank + 1] = top
    for k in range(n):
        msgs[k][...] = outbox[lax.rem(me_t + k, n)]


def error_right_kernel(p_ref, e_ref, out_ref, p3):
    rank = p_ref.shape[0]

    @pl.when(pl.program_id(0) == 0)
    def _():
        stack3(p_ref[...], p3)

    out_ref[...] = sum3(dot(p3[...].astype(BF16), e_ref[0], (1, 0)), rank)


def lower_inverse(gram, rank):
    at = lambda i, j: gram[i : i + 1, j : j + 1]
    low = {}
    for j in range(rank):
        d = at(j, j)
        for k in range(j):
            d = d - low[j, k] * low[j, k]
        low[j, j] = jnp.sqrt(d)
        for i in range(j + 1, rank):
            v = at(i, j)
            for k in range(j):
                v = v - low[i, k] * low[j, k]
            low[i, j] = v / low[j, j]
    inv = {}
    for j in range(rank):
        inv[j, j] = 1.0 / low[j, j]
        for i in range(j + 1, rank):
            v = low[i, j] * inv[j, j]
            for k in range(j + 1, i):
                v = v + low[i, k] * inv[k, j]
            inv[i, j] = -v / low[i, i]
    return inv


def solve_rows(inv, x, rank):
    rows = []
    for i in range(rank):
        row = inv[i, 0] * x[0:1, :]
        for j in range(1, i + 1):
            row = row + inv[i, j] * x[j : j + 1, :]
        rows.append(row)
    return rows


def right_kernel(m, n, *refs):
    p_ref, r_ref, g_ref = refs[:3]
    pieces = refs[3 : 3 + n]
    ortho_ref = refs[3 + n]
    outs = refs[4 + n : 4 + n + m]
    inbox, z, z3, whole, outbox = refs[4 + n + m :]
    rank, rows = p_ref.shape
    tok = g_ref.shape[1]
    cut = outs[0].shape[1]
    me_r = lax.axis_index("dp")
    me_t = lax.axis_index("tensor")
    for k in range(n):
        inbox[lax.rem(me_t - k + n, n)] = pieces[k][...]
    gram = inbox[0, rank : 2 * rank, 0:rank]
    for t in range(1, n):
        gram = gram + inbox[t, rank : 2 * rank, 0:rank]
    inv = lower_inverse(gram, rank)
    for t in range(n):
        top = inbox[t, rank : rank + 1, rank : rank + 1]
        scaled = {key: value * top for key, value in inv.items()}
        for i, row in enumerate(solve_rows(scaled, inbox[t, 0:rank, 0:tok], rank)):
            if t == 0:
                z[i : i + 1, :] = row
            else:
                z[i : i + 1, :] += row
    for i, row in enumerate(solve_rows(inv, p_ref[...], rank)):
        ortho_ref[i : i + 1, :] = row
    for i, row in enumerate(solve_rows(inv, r_ref[...], rank)):
        whole[i : i + 1, :] = row
    whole[...] += sum3(dot(stack3(z[...], z3), g_ref[0], (1, 0)), rank) * 1024.0
    for r in range(m):
        outbox[r] = whole[:, r * cut : (r + 1) * cut]
    for k in range(m):
        outs[k][...] = outbox[lax.rem(me_r + k, m)]


def add_kernel(axis, n, scale, *refs):
    pieces, out_ref, inbox = refs[:n], refs[n], refs[n + 1]
    me = lax.axis_index(axis)
    for k in range(n):
        inbox[lax.rem(me - k + n, n)] = pieces[k][...]
    total = inbox[0]
    for i in range(1, n):
        total += inbox[i]
    out_ref[...] = total * scale


LEFT_TERMS = (0, 0, 1, 0, 2, 1)
RIGHT_TERMS = (0, 1, 0, 2, 0, 1)


def factor_kernel(m, *refs):
    ortho_ref = refs[0]
    pieces = refs[1 : 1 + m]
    whole_ref, left_ref, right_ref, inbox, left, right = refs[1 + m :]
    rank, cut = pieces[0].shape
    me = lax.axis_index("dp")
    for k in range(m):
        inbox[lax.rem(me - k + m, m)] = pieces[k][...]
    for r in range(m):
        whole_ref[:, r * cut : (r + 1) * cut] = inbox[r]
    for terms, x, ref, out in (
        (LEFT_TERMS, ortho_ref[...], left, left_ref),
        (RIGHT_TERMS, whole_ref[...], right, right_ref),
    ):
        parts = split(x)
        for i, term in enumerate(terms):
            ref[i * rank : (i + 1) * rank, :] = parts[term]
        out[...] = ref[...].astype(BF16)


def final_kernel(n, *refs):
    a_ref, left_ref, right_ref, e_ref = refs[:4]
    slots = refs[4 : 4 + n]
    rebuilt_ref, error_ref, acts = refs[-3:]
    tok = slots[0].shape[1]
    me = lax.axis_index("tensor")

    @pl.when(pl.program_id(0) == 0)
    def _():
        for s in range(n):
            src = ring_source(me, s, n)
            rows = a_ref[0, pl.ds(pl.multiple_of(src * tok, tok), tok), :]
            acts[s * tok : (s + 1) * tok, :] = rows

    grads = jnp.concatenate([slot[0] for slot in slots], axis=0)
    matrix = dot(acts[...], grads, (0, 0)) + e_ref[0].astype(F32)
    rebuilt = dot(left_ref[...], right_ref[...], (0, 0))
    rebuilt_ref[...] = rebuilt.astype(BF16)
    error_ref[0] = (matrix - rebuilt).astype(BF16)


def per_device(activations, out_grads, error_buffer, warm_factor):
    m = lax.axis_size("dp")
    n = lax.axis_size("tensor")
    _, tokens, rows = activations.shape
    _, tok, width = out_grads.shape
    rank = warm_factor.shape[1]
    part = width // PARTS
    w = warm_factor.T
    sds = jax.ShapeDtypeStruct

    chunks = []
    for c in range(PARTS):
        held = [out_grads[:, :, c * part : (c + 1) * part]]
        for _ in range(n - 1):
            held.append(ring_step(held[-1], "tensor", n))
        chunks.append(held)

    gw = pl.pallas_call(
        token_factor_kernel,
        out_shape=sds((rank, tok), F32),
        scratch_shapes=[pltpu.VMEM((3 * rank, width), F32)],
        compiler_params=params(32),
        cost_estimate=cost(2e6, 1e6),
        name="token_factor",
    )(w, out_grads)
    gws = exchange([gw] * n, "tensor", n)

    high = 128
    ew = pl.pallas_call(
        error_left_kernel,
        grid=(rows // high,),
        in_specs=[
            pl.BlockSpec((rank, width), lambda i: (0, 0)),
            pl.BlockSpec((1, high, width), lambda i: (0, i, 0)),
        ],
        out_specs=pl.BlockSpec((rank, high), lambda i: (0, i)),
        out_shape=sds((rank, rows), F32),
        scratch_shapes=[pltpu.VMEM((3 * rank, width), F32)],
        compiler_params=params(32),
        cost_estimate=cost(2e9, rows * width * 2),
        name="error_left",
    )(w, error_buffer)

    left = pl.pallas_call(
        functools.partial(left_kernel, n),
        out_shape=sds((rank, rows), F32),
        scratch_shapes=[pltpu.VMEM((3 * rank, tok), F32)],
        compiler_params=params(32),
        cost_estimate=cost(1e7, 1e6),
        name="left",
    )(activations, ew, *gws)
    lefts = exchange([left] * m, "dp", m)

    mean, *msgs = pl.pallas_call(
        functools.partial(mean_kernel, m, n),
        out_shape=[sds((rank, rows), F32)] + [sds((8, 128), F32)] * n,
        scratch_shapes=[
            pltpu.VMEM((m, rank, rows), F32),
            pltpu.VMEM((3 * rank, rows), F32),
            pltpu.VMEM((n, 8, 128), F32),
        ],
        compiler_params=params(32),
        cost_estimate=cost(1e7, 1e6),
        name="mean",
    )(activations, *lefts)
    msgs = exchange(msgs, "tensor", n)

    right_raw = pl.pallas_call(
        error_right_kernel,
        grid=(width // BLOCK,),
        in_specs=[
            pl.BlockSpec((rank, rows), lambda i: (0, 0)),
            pl.BlockSpec((1, rows, BLOCK), lambda i: (0, 0, i)),
        ],
        out_specs=pl.BlockSpec((rank, BLOCK), lambda i: (0, i)),
        out_shape=sds((rank, width), F32),
        scratch_shapes=[pltpu.VMEM((3 * rank, rows), F32)],
        compiler_params=params(32),
        cost_estimate=cost(2e9, rows * width * 2),
        name="error_right",
    )(mean, error_buffer)

    cut = width // m
    ortho, *pieces = pl.pallas_call(
        functools.partial(right_kernel, m, n),
        out_shape=[sds((rank, rows), F32)] + [sds((rank, cut), F32)] * m,
        scratch_shapes=[
            pltpu.VMEM((n, 8, 128), F32),
            pltpu.VMEM((rank, tok), F32),
            pltpu.VMEM((3 * rank, tok), F32),
            pltpu.VMEM((rank, width), F32),
            pltpu.VMEM((m, rank, cut), F32),
        ],
        compiler_params=params(32),
        cost_estimate=cost(1e7, 1e6),
        name="right",
    )(mean, right_raw, out_grads, *msgs)

    def added(pieces, axis, size, scale):
        return pl.pallas_call(
            functools.partial(add_kernel, axis, size, scale),
            out_shape=sds((rank, cut), F32),
            scratch_shapes=[pltpu.VMEM((size, rank, cut), F32)],
            cost_estimate=cost(1e5, 1e5),
            name="add_" + axis,
        )(*pieces)

    mine = added(exchange(pieces, "dp", m), "dp", m, 1.0)
    mine = added(exchange([mine] * n, "tensor", n), "tensor", n, 1.0 / m)
    pieces = exchange([mine] * m, "dp", m)

    terms = len(LEFT_TERMS) * rank
    whole, left_terms, right_terms = pl.pallas_call(
        functools.partial(factor_kernel, m),
        out_shape=[sds((rank, width), F32), sds((terms, rows), BF16), sds((terms, width), BF16)],
        scratch_shapes=[
            pltpu.VMEM((m, rank, cut), F32),
            pltpu.VMEM((terms, rows), F32),
            pltpu.VMEM((terms, width), F32),
        ],
        compiler_params=params(32),
        cost_estimate=cost(1e6, 1e6),
        name="factor",
    )(ortho, *pieces)

    outs = ()
    for c, held in enumerate(chunks):
        steps = part // BLOCK
        at = c * steps
        col = lambda i, at=at: (0, 0, i + at)
        mine_specs = [pl.BlockSpec((1, tok, BLOCK), col)]
        fresh = [pl.BlockSpec((1, tok, BLOCK), lambda i: (0, 0, i))] * (n - 1)
        outs = pl.pallas_call(
            functools.partial(final_kernel, n),
            grid=(steps,),
            in_specs=[
                pl.BlockSpec((1, tokens, rows), lambda i: (0, 0, 0)),
                pl.BlockSpec((terms, rows), lambda i: (0, 0)),
                pl.BlockSpec((terms, BLOCK), lambda i, at=at: (0, i + at)),
                pl.BlockSpec((1, rows, BLOCK), col),
            ]
            + mine_specs
            + fresh
            + [pl.BlockSpec(memory_space=pl.ANY)] * len(outs),
            out_specs=[
                pl.BlockSpec((rows, BLOCK), lambda i, at=at: (0, i + at)),
                pl.BlockSpec((1, rows, BLOCK), col),
            ],
            out_shape=[sds((rows, width), BF16), sds((1, rows, width), BF16)],
            input_output_aliases={4 + n + j: j for j in range(len(outs))},
            scratch_shapes=[pltpu.VMEM((tokens, rows), BF16)],
            compiler_params=params(48),
            cost_estimate=cost(4e9 / PARTS, rows * width * 6 // PARTS),
            name="rebuild",
        )(activations, left_terms, right_terms, error_buffer, out_grads, *held[1:], *outs)
    rebuilt, error = outs
    return rebuilt, error, whole.T


def solution(mesh):
    return jax.shard_map(
        per_device,
        mesh=mesh,
        in_specs=(P("dp", None, "tensor"), P("dp", "tensor", None), P("dp", "tensor", None), P()),
        out_specs=(P("tensor", None), P("dp", "tensor", None), P()),
        check_vma=False,
    )
```

```python
import functools

import jax
import jax.numpy as jnp
from jax import lax
from jax.experimental import pallas as pl
from jax.experimental.pallas import tpu as pltpu
from jax.sharding import PartitionSpec as P

F32 = jnp.float32
BF16 = jnp.bfloat16
SHRINK = 2.0**-23
TINY = 1e-30
BLOCK = 512


def params(mib):
    return pltpu.CompilerParams(vmem_limit_bytes=mib * 2**20)


def cost(flops, moved):
    return pl.CostEstimate(flops=int(flops), bytes_accessed=int(moved), transcendentals=0)


def dot(a, b, contract):
    return lax.dot_general(a, b, ((contract[:1], contract[1:]), ((), ())), preferred_element_type=F32)


def split(x):
    hi = x.astype(BF16)
    rest = x - hi.astype(F32)
    mid = rest.astype(BF16)
    lo = (rest - mid.astype(F32)).astype(BF16)
    return hi.astype(F32), mid.astype(F32), lo.astype(F32)


def stack3(x, ref):
    rank = x.shape[0]
    for i, part in enumerate(split(x)):
        ref[i * rank : (i + 1) * rank, :] = part
    return ref[...].astype(BF16)


def sum3(y, rank):
    return (y[2 * rank :] + y[rank : 2 * rank]) + y[:rank]


def ring_of(n):
    return [2 * p if 2 * p < n else 2 * (n - p) - 1 for p in range(n)]


def ring_source(me, step, n):
    place = jnp.where(lax.rem(me, 2) == 0, me // 2, n - (me + 1) // 2)
    place = lax.rem(place - step + n, n)
    return jnp.where(2 * place < n, 2 * place, 2 * (n - place) - 1)


def ring_step(x, axis, n):
    ring = ring_of(n)
    return lax.ppermute(x, axis, [(ring[p], ring[(p + 1) % n]) for p in range(n)])


def exchange(stack, axis):
    return lax.all_to_all(stack, axis, 0, 0)


def token_factor_kernel(w_hbm, g_hbm, out_ref, parts_ref, w, g, w3, sems):
    rank = w.shape[0]
    copies = [
        pltpu.make_async_copy(w_hbm, w, sems.at[0]),
        pltpu.make_async_copy(g_hbm, g, sems.at[1]),
    ]
    for copy in copies:
        copy.start()
    copies[0].wait()
    parts = stack3(w[...] * SHRINK, w3)
    parts_ref[...] = parts
    copies[1].wait()
    gw = sum3(dot(parts, g[0], (1, 1)), rank)
    for k in range(out_ref.shape[0]):
        out_ref[k, 0:rank, 0 : gw.shape[1]] = gw


def error_left_kernel(w_ref, e_hbm, out_ref, e_ref, sems):
    rank = out_ref.shape[0]
    chunks = sems.shape[0]
    high = e_ref.shape[1] // chunks
    copies = []
    for c in range(chunks):
        rows = pl.ds(c * high, high)
        copies.append(pltpu.make_async_copy(e_hbm.at[:, rows, :], e_ref.at[:, rows, :], sems.at[c]))
        copies[-1].start()
    parts = w_ref[...]
    for c in range(chunks):
        copies[c].wait()
        rows = slice(c * high, (c + 1) * high)
        out_ref[:, rows] = sum3(dot(parts, e_ref[0, rows, :], (1, 1)), rank)


def left_kernel(a_ref, e_ref, gw_ref, out_ref, g3):
    n = gw_ref.shape[0]
    rank = e_ref.shape[0]
    tok = a_ref.shape[1] // n
    total = e_ref[...]
    for t in range(n):
        rows = a_ref[0, t * tok : (t + 1) * tok, :]
        total += sum3(dot(stack3(gw_ref[t, 0:rank, 0:tok], g3), rows, (1, 0)), rank)
    for r in range(out_ref.shape[0]):
        out_ref[r] = total


def mean_kernel(a_ref, left_ref, p_ref, msg_ref, p3):
    m, rank, _ = left_ref.shape
    n = msg_ref.shape[0]
    tok = a_ref.shape[1] // n
    total = left_ref[0]
    for r in range(1, m):
        total += left_ref[r]
    mean = total * (1.0 / (SHRINK * m))
    p_ref[...] = mean
    top = jnp.max(jnp.max(jnp.abs(mean), axis=1, keepdims=True), axis=0, keepdims=True)
    top = jnp.maximum(top, TINY)
    parts = stack3(mean / (top * 1024.0), p3)
    gram = [jnp.sum(mean * mean[i : i + 1, :], axis=1, keepdims=True) for i in range(rank)]
    msg_ref[...] = jnp.zeros_like(msg_ref)
    for t in range(n):
        y = dot(parts, a_ref[0, t * tok : (t + 1) * tok, :], (1, 1))
        msg_ref[t, 0:rank, 0:tok] = sum3(y, rank)
        for i in range(rank):
            msg_ref[t, rank : 2 * rank, i : i + 1] = gram[i]
        msg_ref[t, rank : rank + 1, rank : rank + 1] = top


def error_right_kernel(p_ref, e_ref, out_ref, p3):
    rank = p_ref.shape[0]
    parts = stack3(p_ref[...], p3)
    for c in range(e_ref.shape[2] // BLOCK):
        cols = slice(c * BLOCK, (c + 1) * BLOCK)
        out_ref[:, cols] = sum3(dot(parts, e_ref[0, :, cols], (1, 0)), rank)


def lower_inverse(gram, rank):
    at = lambda i, j: gram[i : i + 1, j : j + 1]
    low = {}
    for j in range(rank):
        d = at(j, j)
        for k in range(j):
            d = d - low[j, k] * low[j, k]
        low[j, j] = jnp.sqrt(d)
        for i in range(j + 1, rank):
            v = at(i, j)
            for k in range(j):
                v = v - low[i, k] * low[j, k]
            low[i, j] = v / low[j, j]
    inv = {}
    for j in range(rank):
        inv[j, j] = 1.0 / low[j, j]
        for i in range(j + 1, rank):
            v = low[i, j] * inv[j, j]
            for k in range(j + 1, i):
                v = v + low[i, k] * inv[k, j]
            inv[i, j] = -v / low[i, i]
    return inv


def solve_rows(inv, x, rank):
    rows = []
    for i in range(rank):
        row = inv[i, 0] * x[0:1, :]
        for j in range(1, i + 1):
            row = row + inv[i, j] * x[j : j + 1, :]
        rows.append(row)
    return rows


def right_kernel(p_ref, r_ref, g_ref, msg_ref, ortho_ref, out_ref, z, z3, whole):
    n = msg_ref.shape[0]
    m, rank, cut = out_ref.shape
    tok = g_ref.shape[1]
    gram = msg_ref[0, rank : 2 * rank, 0:rank]
    for t in range(1, n):
        gram = gram + msg_ref[t, rank : 2 * rank, 0:rank]
    inv = lower_inverse(gram, rank)
    for t in range(n):
        top = msg_ref[t, rank : rank + 1, rank : rank + 1]
        scaled = {key: value * top for key, value in inv.items()}
        for i, row in enumerate(solve_rows(scaled, msg_ref[t, 0:rank, 0:tok], rank)):
            if t == 0:
                z[i : i + 1, :] = row
            else:
                z[i : i + 1, :] += row
    for i, row in enumerate(solve_rows(inv, p_ref[...], rank)):
        ortho_ref[i : i + 1, :] = row
    for i, row in enumerate(solve_rows(inv, r_ref[...], rank)):
        whole[i : i + 1, :] = row
    whole[...] += sum3(dot(stack3(z[...], z3), g_ref[0], (1, 0)), rank) * 1024.0
    for r in range(m):
        out_ref[r] = whole[:, r * cut : (r + 1) * cut]


def add_kernel(scale, in_ref, out_ref):
    total = in_ref[0]
    for i in range(1, in_ref.shape[0]):
        total += in_ref[i]
    total = total * scale
    for i in range(out_ref.shape[0]):
        out_ref[i] = total


LEFT_TERMS = (0, 0, 1, 0, 2, 1)
RIGHT_TERMS = (0, 1, 0, 2, 0, 1)


def factor_kernel(ortho_ref, in_ref, whole_ref, left_ref, right_ref, left, right):
    m, rank, cut = in_ref.shape
    for r in range(m):
        whole_ref[:, r * cut : (r + 1) * cut] = in_ref[r]
    for terms, x, ref in (
        (LEFT_TERMS, ortho_ref[...], left),
        (RIGHT_TERMS, whole_ref[...], right),
    ):
        parts = split(x)
        for i, term in enumerate(terms):
            ref[i * rank : (i + 1) * rank, :] = parts[term]
    left_ref[...] = left[...].T.astype(BF16)
    right_ref[...] = right[...].astype(BF16)


def final_kernel(n, *refs):
    a_ref, left_ref, right_ref, e_ref = refs[:4]
    slots = refs[4 : 4 + n]
    rebuilt_ref, error_ref, acts, acts_t = refs[4 + n :]
    tok = slots[0].shape[1]
    me = lax.axis_index("tensor")
    step = pl.program_id(0)

    @pl.when(step == 0)
    def _():
        for s in range(n):
            src = ring_source(me, s, n)
            rows = a_ref[0, pl.ds(pl.multiple_of(src * tok, tok), tok), :]
            acts[s * tok : (s + 1) * tok, :] = rows
        acts_t[...] = acts[...].T

    cols = pl.ds(pl.multiple_of(step * BLOCK, BLOCK), BLOCK)
    grads = jnp.concatenate([slot[0, :, cols] for slot in slots], axis=0)
    matrix = dot(acts_t[...], grads, (1, 0)) + e_ref[0, :, cols].astype(F32)
    rebuilt = dot(left_ref[...], right_ref[:, cols], (1, 0))
    rebuilt_ref[...] = rebuilt.astype(BF16)
    error_ref[0] = (matrix - rebuilt).astype(BF16)


def per_device(activations, out_grads, error_buffer, warm_factor):
    m = lax.axis_size("dp")
    n = lax.axis_size("tensor")
    _, tokens, rows = activations.shape
    _, tok, width = out_grads.shape
    rank = warm_factor.shape[1]
    cut = width // m
    w = warm_factor.T
    sds = jax.ShapeDtypeStruct
    hbm = pl.BlockSpec(memory_space=pltpu.HBM)
    vmem = pl.BlockSpec(memory_space=pltpu.VMEM)
    dma = pltpu.SemaphoreType.DMA
    pin = lambda x: pltpu.with_memory_space_constraint(x, pltpu.HBM)

    def call(kernel, shapes, scratch, name, flops, moved, specs=None, mib=16):
        return pl.pallas_call(
            kernel,
            out_shape=shapes,
            **({"in_specs": specs} if specs else {}),
            scratch_shapes=scratch,
            compiler_params=params(mib),
            cost_estimate=cost(flops, moved),
            name=name,
        )

    gw, w_parts = call(
        token_factor_kernel,
        [sds((n, 8, 128), F32), sds((3 * rank, width), BF16)],
        [
            pltpu.VMEM((rank, width), F32),
            pltpu.VMEM((1, tok, width), BF16),
            pltpu.VMEM((3 * rank, width), F32),
            dma((2,)),
        ],
        "token_factor", 2e6, 1e6, [hbm, hbm],
    )(pin(w), pin(out_grads))
    gw = exchange(gw, "tensor")
    held = [out_grads]
    held.append(ring_step(held[-1], "tensor", n))

    ew, error_v = call(
        error_left_kernel,
        [sds((rank, rows), F32), sds((1, rows, width), BF16)],
        [dma((6,))],
        "error_left", 2e9, rows * width * 2, [vmem, hbm],
    )(w_parts, pin(error_buffer))

    left = call(
        left_kernel, sds((m, rank, rows), F32), [pltpu.VMEM((3 * rank, tok), F32)], "left", 1e7, 1e6
    )(activations, ew, gw)
    left = exchange(left, "dp")
    left, held[-1] = lax.optimization_barrier((left, held[-1]))
    held.append(ring_step(held[-1], "tensor", n))

    mean, msg = call(
        mean_kernel,
        [sds((rank, rows), F32), sds((n, 8, 128), F32)],
        [pltpu.VMEM((3 * rank, rows), F32)],
        "mean", 1e7, 1e6,
    )(activations, left)
    msg = exchange(msg, "tensor")

    right_raw = call(
        error_right_kernel,
        sds((rank, width), F32),
        [pltpu.VMEM((3 * rank, rows), F32)],
        "error_right", 2e9, rows * width * 2,
    )(mean, error_v)
    right_raw, held[-1] = lax.optimization_barrier((right_raw, held[-1]))
    for _ in range(3, n):
        held.append(ring_step(held[-1], "tensor", n))

    ortho, pieces = call(
        right_kernel,
        [sds((rank, rows), F32), sds((m, rank, cut), F32)],
        [
            pltpu.VMEM((rank, tok), F32),
            pltpu.VMEM((3 * rank, tok), F32),
            pltpu.VMEM((rank, width), F32),
        ],
        "right", 1e7, 1e6,
    )(mean, right_raw, out_grads, msg)
    pieces = exchange(pieces, "dp")
    pieces = call(
        functools.partial(add_kernel, 1.0), sds((n, rank, cut), F32), [], "add_dp", 1e5, 1e5
    )(pieces)
    pieces = exchange(pieces, "tensor")
    pieces = call(
        functools.partial(add_kernel, 1.0 / m), sds((m, rank, cut), F32), [], "add_tensor", 1e5, 1e5
    )(pieces)
    pieces = exchange(pieces, "dp")

    terms = len(LEFT_TERMS) * rank
    whole, left_terms, right_terms = call(
        factor_kernel,
        [sds((rank, width), F32), sds((rows, terms), BF16), sds((terms, width), BF16)],
        [pltpu.VMEM((terms, rows), F32), pltpu.VMEM((terms, width), F32)],
        "factor", 1e6, 1e6,
    )(ortho, pieces)

    rebuilt, error = pl.pallas_call(
        functools.partial(final_kernel, n),
        grid=(width // BLOCK,),
        in_specs=[vmem] * (4 + n),
        out_specs=[
            pl.BlockSpec((rows, BLOCK), lambda i: (0, i)),
            pl.BlockSpec((1, rows, BLOCK), lambda i: (0, 0, i)),
        ],
        out_shape=[sds((rows, width), BF16), sds((1, rows, width), BF16)],
        scratch_shapes=[pltpu.VMEM((tokens, rows), BF16), pltpu.VMEM((rows, tokens), BF16)],
        compiler_params=params(24),
        cost_estimate=cost(4e9, rows * width * 6),
        name="rebuild",
    )(activations, left_terms, right_terms, error_v, *held)
    return rebuilt, error, whole.T


def solution(mesh):
    return jax.shard_map(
        per_device,
        mesh=mesh,
        in_specs=(P("dp", None, "tensor"), P("dp", "tensor", None), P("dp", "tensor", None), P()),
        out_specs=(P("tensor", None), P("dp", "tensor", None), P()),
        check_vma=False,
    )
```

```python
import functools

import jax
import jax.numpy as jnp
from jax import lax
from jax.experimental import pallas as pl
from jax.experimental.pallas import tpu as pltpu
from jax.sharding import PartitionSpec as P

F32 = jnp.float32
BF16 = jnp.bfloat16
SHRINK = 2.0**-23
TINY = 1e-30
BLOCK = 512
PARTS = 2


def params(mib):
    return pltpu.CompilerParams(vmem_limit_bytes=mib * 2**20)


def cost(flops, moved):
    return pl.CostEstimate(flops=int(flops), bytes_accessed=int(moved), transcendentals=0)


def dot(a, b, contract):
    return lax.dot_general(a, b, ((contract[:1], contract[1:]), ((), ())), preferred_element_type=F32)


def split(x):
    hi = x.astype(BF16)
    rest = x - hi.astype(F32)
    mid = rest.astype(BF16)
    lo = (rest - mid.astype(F32)).astype(BF16)
    return hi.astype(F32), mid.astype(F32), lo.astype(F32)


def stack3(x, ref):
    rank = x.shape[0]
    for i, part in enumerate(split(x)):
        ref[i * rank : (i + 1) * rank, :] = part
    return ref[...].astype(BF16)


def sum3(y, rank):
    return (y[2 * rank :] + y[rank : 2 * rank]) + y[:rank]


def ring_of(n):
    return [2 * p if 2 * p < n else 2 * (n - p) - 1 for p in range(n)]


def ring_source(me, step, n):
    place = jnp.where(lax.rem(me, 2) == 0, me // 2, n - (me + 1) // 2)
    place = lax.rem(place - step + n, n)
    return jnp.where(2 * place < n, 2 * place, 2 * (n - place) - 1)


def ring_step(x, axis, n):
    ring = ring_of(n)
    return lax.ppermute(x, axis, [(ring[p], ring[(p + 1) % n]) for p in range(n)])


def exchange(pieces, axis, n):
    return [pieces[0]] + [
        lax.ppermute(pieces[k], axis, [(i, (i + k) % n) for i in range(n)]) for k in range(1, n)
    ]


def swap(x, axis, n, bit):
    return lax.ppermute(x, axis, [(i, i ^ bit) for i in range(n)])


def bits(n):
    assert n & (n - 1) == 0
    return [1 << i for i in range(n.bit_length() - 1)]


def token_factor_kernel(w_hbm, g_hbm, *refs):
    out_ref, terms_ref = refs[:2]
    chunks = refs[2:-3]
    w, w3, sems = refs[-3:]
    rank = w.shape[0]
    part = chunks[0].shape[2]
    copies = [pltpu.make_async_copy(w_hbm, w, sems.at[0])]
    for c, chunk in enumerate(chunks):
        part_of = g_hbm.at[:, :, pl.ds(c * part, part)]
        copies.append(pltpu.make_async_copy(part_of, chunk, sems.at[c + 1]))
    for copy in copies:
        copy.start()
    copies[0].wait()
    stack3(w[...] * SHRINK, w3)
    terms_ref[...] = w3[...].T.astype(BF16)
    total = 0.0
    for c, chunk in enumerate(chunks):
        copies[c + 1].wait()
        total += dot(chunk[0], terms_ref[c * part : (c + 1) * part, :], (1, 0))
    out_ref[...] = jnp.zeros_like(out_ref)
    out_ref[0:rank, 0 : total.shape[0]] = sum3(total.T, rank)


def error_left_kernel(terms_ref, e_hbm, out_ref, e_ref, sems):
    rank = out_ref.shape[0]
    chunks = sems.shape[0]
    high = e_ref.shape[1] // chunks
    copies = []
    for c in range(chunks):
        rows = pl.ds(c * high, high)
        copies.append(pltpu.make_async_copy(e_hbm.at[:, rows, :], e_ref.at[:, rows, :], sems.at[c]))
        copies[-1].start()
    for c in range(chunks):
        copies[c].wait()
        rows = slice(c * high, (c + 1) * high)
        out_ref[:, rows] = sum3(dot(e_ref[0, rows, :], terms_ref[...], (1, 0)).T, rank)


def left_kernel(a_ref, e_ref, *refs):
    gws, out_ref, g3 = refs[:-2], refs[-2], refs[-1]
    n = len(gws)
    rank = e_ref.shape[0]
    tok = a_ref.shape[1] // n
    me = lax.axis_index("tensor")
    total = e_ref[...]
    for k in range(n):
        src = lax.rem(me - k + n, n)
        rows = a_ref[0, pl.ds(pl.multiple_of(src * tok, tok), tok), :]
        total += sum3(dot(stack3(gws[k][0:rank, 0:tok], g3), rows, (1, 0)), rank)
    out_ref[...] = total


def mean_kernel(n, scale, a_ref, x_ref, y_ref, p_ref, *refs):
    msgs, p3, outbox = refs[:n], refs[n], refs[n + 1]
    rank = x_ref.shape[0]
    tok = a_ref.shape[1] // n
    me = lax.axis_index("tensor")
    mean = (x_ref[...] + y_ref[...]) * scale
    p_ref[...] = mean
    top = jnp.max(jnp.max(jnp.abs(mean), axis=1, keepdims=True), axis=0, keepdims=True)
    top = jnp.maximum(top, TINY)
    parts = stack3(mean / (top * 1024.0), p3)
    gram = [jnp.sum(mean * mean[i : i + 1, :], axis=1, keepdims=True) for i in range(rank)]
    outbox[...] = jnp.zeros_like(outbox)
    for t in range(n):
        y = dot(parts, a_ref[0, t * tok : (t + 1) * tok, :], (1, 1))
        outbox[t, 0:rank, 0:tok] = sum3(y, rank)
        for i in range(rank):
            outbox[t, rank : 2 * rank, i : i + 1] = gram[i]
        outbox[t, rank : rank + 1, rank : rank + 1] = top
    for k in range(n):
        msgs[k][...] = outbox[lax.rem(me + k, n)]


def error_right_kernel(p_ref, e_ref, out_ref, p3):
    rank = p_ref.shape[0]
    parts = stack3(p_ref[...], p3)
    for c in range(e_ref.shape[2] // BLOCK):
        cols = slice(c * BLOCK, (c + 1) * BLOCK)
        out_ref[:, cols] = sum3(dot(parts, e_ref[0, :, cols], (1, 0)), rank)


def lower_inverse(gram, rank):
    at = lambda i, j: gram[i : i + 1, j : j + 1]
    low = {}
    for j in range(rank):
        d = at(j, j)
        for k in range(j):
            d = d - low[j, k] * low[j, k]
        low[j, j] = jnp.sqrt(d)
        for i in range(j + 1, rank):
            v = at(i, j)
            for k in range(j):
                v = v - low[i, k] * low[j, k]
            low[i, j] = v / low[j, j]
    inv = {}
    for j in range(rank):
        inv[j, j] = 1.0 / low[j, j]
        for i in range(j + 1, rank):
            v = low[i, j] * inv[j, j]
            for k in range(j + 1, i):
                v = v + low[i, k] * inv[k, j]
            inv[i, j] = -v / low[i, i]
    return inv


def solve_rows(inv, x, rank):
    rows = []
    for i in range(rank):
        row = inv[i, 0] * x[0:1, :]
        for j in range(1, i + 1):
            row = row + inv[i, j] * x[j : j + 1, :]
        rows.append(row)
    return rows


def right_kernel(n, parts, p_ref, r_ref, *refs):
    chunks = refs[:parts]
    pieces = refs[parts : parts + n]
    ortho_ref, keep_ref, send_ref, inbox, z, z3, outbox = refs[parts + n :]
    rank = p_ref.shape[0]
    tok = chunks[0].shape[1]
    part = chunks[0].shape[2]
    half = keep_ref.shape[1]
    me_t = lax.axis_index("tensor")
    core = lax.rem(lax.axis_index("dp"), 2)
    for k in range(n):
        inbox[lax.rem(me_t - k + n, n)] = pieces[k][...]
    gram = inbox[0, rank : 2 * rank, 0:rank]
    for t in range(1, n):
        gram = gram + inbox[t, rank : 2 * rank, 0:rank]
    inv = lower_inverse(gram, rank)
    for t in range(n):
        top = inbox[t, rank : rank + 1, rank : rank + 1]
        scaled = {key: value * top for key, value in inv.items()}
        for i, row in enumerate(solve_rows(scaled, inbox[t, 0:rank, 0:tok], rank)):
            if t == 0:
                z[i : i + 1, :] = row
            else:
                z[i : i + 1, :] += row
    for i, row in enumerate(solve_rows(inv, p_ref[...], rank)):
        ortho_ref[i : i + 1, :] = row
    terms = stack3(z[...], z3)
    for c in range(parts):
        fresh = sum3(dot(terms, chunks[c][0], (1, 0)), rank) * 1024.0
        old = solve_rows(inv, r_ref[:, c * part : (c + 1) * part], rank)
        for i, row in enumerate(old):
            row = row + fresh[i : i + 1, :]
            for h in range(2):
                lo, hi = max(h * half, c * part), min((h + 1) * half, (c + 1) * part)
                if lo < hi:
                    outbox[h, i : i + 1, lo - h * half : hi - h * half] = row[
                        :, lo - c * part : hi - c * part
                    ]
    keep_ref[...] = outbox[core]
    send_ref[...] = outbox[1 - core]


def add_kernel(x_ref, y_ref, out_ref):
    out_ref[...] = x_ref[...] + y_ref[...]


LEFT_TERMS = (0, 0, 1, 0, 2, 1)
RIGHT_TERMS = (0, 1, 0, 2, 0, 1)


def factor_kernel(scale, ortho_ref, mine_ref, other_ref, whole_ref, left_ref, right_ref, inbox, left, right):
    rank, half = mine_ref.shape
    core = lax.rem(lax.axis_index("dp"), 2)
    inbox[core] = mine_ref[...]
    inbox[1 - core] = other_ref[...]
    for h in range(2):
        whole_ref[:, h * half : (h + 1) * half] = inbox[h] * scale
    for terms, x, ref in (
        (LEFT_TERMS, ortho_ref[...], left),
        (RIGHT_TERMS, whole_ref[...], right),
    ):
        parts = split(x)
        for i, term in enumerate(terms):
            ref[i * rank : (i + 1) * rank, :] = parts[term]
    left_ref[...] = left[...].T.astype(BF16)
    right_ref[...] = right[...].astype(BF16)


def final_kernel(n, at, a_ref, left_ref, right_ref, e_ref, *refs):
    slots = refs[:n]
    rebuilt_ref, error_ref, acts, acts_t = refs[-4:]
    tok = slots[0].shape[1]
    rows = e_ref.shape[1]
    me = lax.axis_index("tensor")
    step = pl.program_id(0)

    @pl.when(step == 0)
    def _():
        for s in range(n):
            src = ring_source(me, s, n)
            here = a_ref[0, pl.ds(pl.multiple_of(src * tok, tok), tok), :]
            acts[s * tok : (s + 1) * tok, :] = here
        acts_t[...] = acts[...].T

    high = 256 if rows % 256 == 0 else 128
    for c in range(BLOCK // 256):
        cols = pl.ds(pl.multiple_of(step * BLOCK + c * 256, 256), 256)
        wide = pl.ds(pl.multiple_of(at + step * BLOCK + c * 256, 256), 256)
        grads = jnp.concatenate([slot[0, :, cols] for slot in slots], axis=0)
        right = right_ref[:, wide]
        for r in range(rows // high):
            here = slice(r * high, (r + 1) * high)
            there = slice(c * 256, (c + 1) * 256)
            matrix = dot(acts_t[here, :], grads, (1, 0)) + e_ref[0, here, wide].astype(F32)
            rebuilt = dot(left_ref[here, :], right, (1, 0))
            rebuilt_ref[here, there] = rebuilt.astype(BF16)
            error_ref[0, here, there] = (matrix - rebuilt).astype(BF16)


def per_device(activations, out_grads, error_buffer, warm_factor):
    m = lax.axis_size("dp")
    n = lax.axis_size("tensor")
    _, tokens, rows = activations.shape
    _, tok, width = out_grads.shape
    rank = warm_factor.shape[1]
    part = width // PARTS
    half = width // 2
    w = warm_factor.T
    sds = jax.ShapeDtypeStruct
    hbm = pl.BlockSpec(memory_space=pltpu.HBM)
    vmem = pl.BlockSpec(memory_space=pltpu.VMEM)
    dma = pltpu.SemaphoreType.DMA
    pin = lambda x: pltpu.with_memory_space_constraint(x, pltpu.HBM)

    def call(kernel, shapes, scratch, name, flops, moved, specs=None, mib=16):
        return pl.pallas_call(
            kernel,
            out_shape=shapes,
            **({"in_specs": specs} if specs else {}),
            scratch_shapes=scratch,
            compiler_params=params(mib),
            cost_estimate=cost(flops, moved),
            name=name,
        )

    def add(x, y):
        return call(add_kernel, sds(x.shape, F32), [], "add", 1e5, 1e5)(x, y)

    gw, w_terms, *chunks = call(
        token_factor_kernel,
        [sds((8, 128), F32), sds((width, 3 * rank), BF16)] + [sds((1, tok, part), BF16)] * PARTS,
        [pltpu.VMEM((rank, width), F32), pltpu.VMEM((3 * rank, width), F32), dma((PARTS + 1,))],
        "token_factor", 2e6, 1e6, [hbm, hbm],
    )(pin(w), pin(out_grads))
    gws = exchange([gw] * n, "tensor", n)
    rings = [[chunk] for chunk in chunks]

    def turn(c, after):
        after, last = lax.optimization_barrier((after, rings[c][-1]))
        if len(rings[c]) < n:
            rings[c].append(ring_step(last, "tensor", n))
        return after

    ew, error_v = call(
        error_left_kernel,
        [sds((rank, rows), F32), sds((1, rows, width), BF16)],
        [dma((6,))],
        "error_left", 2e9, rows * width * 2, [vmem, hbm],
    )(w_terms, pin(error_buffer))

    for c in range(PARTS):
        gws = turn(c, gws)
    left = call(
        left_kernel, sds((rank, rows), F32), [pltpu.VMEM((3 * rank, tok), F32)], "left", 1e7, 1e6
    )(activations, ew, *gws)
    for bit in bits(m)[:-1]:
        left = add(left, swap(left, "dp", m, bit))

    mean, *msgs = call(
        functools.partial(mean_kernel, n, 1.0 / (SHRINK * m)),
        [sds((rank, rows), F32)] + [sds((8, 128), F32)] * n,
        [pltpu.VMEM((3 * rank, rows), F32), pltpu.VMEM((n, 8, 128), F32)],
        "mean", 1e7, 1e6,
    )(activations, left, swap(left, "dp", m, bits(m)[-1]))
    msgs = exchange(msgs, "tensor", n)

    right_raw = call(
        error_right_kernel,
        sds((rank, width), F32),
        [pltpu.VMEM((3 * rank, rows), F32)],
        "error_right", 2e9, rows * width * 2,
    )(mean, error_v)
    for c in range(PARTS):
        msgs = turn(c, msgs)

    ortho, keep, send = call(
        functools.partial(right_kernel, n, PARTS),
        [sds((rank, rows), F32), sds((rank, half), F32), sds((rank, half), F32)],
        [
            pltpu.VMEM((n, 8, 128), F32),
            pltpu.VMEM((rank, tok), F32),
            pltpu.VMEM((3 * rank, tok), F32),
            pltpu.VMEM((2, rank, half), F32),
        ],
        "right", 1e7, 1e6,
    )(mean, right_raw, *chunks, *msgs)
    total = add(keep, swap(send, "dp", m, 1))
    for bit in bits(m)[1:]:
        total = add(total, swap(total, "dp", m, bit))
    for bit in bits(n):
        total = add(total, swap(total, "tensor", n, bit))
    for _ in range(2, n - 1):
        for c in range(PARTS):
            total = turn(c, total)
    for c in range(PARTS):
        total = turn(c, total)

    terms = len(LEFT_TERMS) * rank
    whole, left_terms, right_terms = call(
        functools.partial(factor_kernel, 1.0 / m),
        [sds((rank, width), F32), sds((rows, terms), BF16), sds((terms, width), BF16)],
        [
            pltpu.VMEM((2, rank, half), F32),
            pltpu.VMEM((terms, rows), F32),
            pltpu.VMEM((terms, width), F32),
        ],
        "factor", 1e6, 1e6,
    )(ortho, total, swap(total, "dp", m, 1))

    outs = ()
    for c, ring in enumerate(rings):
        first = c * part // BLOCK
        outs = pl.pallas_call(
            functools.partial(final_kernel, n, c * part),
            grid=(part // BLOCK,),
            in_specs=[vmem] * (4 + n) + [pl.BlockSpec(memory_space=pl.ANY)] * len(outs),
            out_specs=[
                pl.BlockSpec((rows, BLOCK), lambda i, first=first: (0, first + i)),
                pl.BlockSpec((1, rows, BLOCK), lambda i, first=first: (0, 0, first + i)),
            ],
            out_shape=[sds((rows, width), BF16), sds((1, rows, width), BF16)],
            input_output_aliases={4 + n + j: j for j in range(len(outs))},
            scratch_shapes=[pltpu.VMEM((tokens, rows), BF16), pltpu.VMEM((rows, tokens), BF16)],
            compiler_params=params(24),
            cost_estimate=cost(4e9 / PARTS, rows * width * 6 // PARTS),
            name="rebuild",
        )(activations, left_terms, right_terms, error_v, *ring, *outs)
    rebuilt, error = outs
    return rebuilt, error, whole.T


def solution(mesh):
    return jax.shard_map(
        per_device,
        mesh=mesh,
        in_specs=(P("dp", None, "tensor"), P("dp", "tensor", None), P("dp", "tensor", None), P()),
        out_specs=(P("tensor", None), P("dp", "tensor", None), P()),
        check_vma=False,
    )
```

```python
import functools

import jax
import jax.numpy as jnp
from jax import lax
from jax.experimental import pallas as pl
from jax.experimental.pallas import tpu as pltpu
from jax.sharding import PartitionSpec as P

F32 = jnp.float32
BF16 = jnp.bfloat16
SHRINK = 2.0**-23
TINY = 1e-30
BLOCK = 512
SHARES = (4, 2, 4)


def params(mib):
    return pltpu.CompilerParams(vmem_limit_bytes=mib * 2**20)


def cost(flops, moved):
    return pl.CostEstimate(flops=1, bytes_accessed=1, transcendentals=0)


def dot(a, b, contract):
    return lax.dot_general(a, b, ((contract[:1], contract[1:]), ((), ())), preferred_element_type=F32)


def split(x):
    hi = x.astype(BF16)
    rest = x - hi.astype(F32)
    mid = rest.astype(BF16)
    lo = (rest - mid.astype(F32)).astype(BF16)
    return hi.astype(F32), mid.astype(F32), lo.astype(F32)


def stack3(x, ref):
    rank = x.shape[0]
    for i, part in enumerate(split(x)):
        ref[i * rank : (i + 1) * rank, :] = part
    return ref[...].astype(BF16)


def sum3(y, rank):
    return (y[2 * rank :] + y[rank : 2 * rank]) + y[:rank]


def ring_of(n):
    return [2 * p if 2 * p < n else 2 * (n - p) - 1 for p in range(n)]


def ring_source(me, step, n):
    place = jnp.where(lax.rem(me, 2) == 0, me // 2, n - (me + 1) // 2)
    place = lax.rem(place - step + n, n)
    return jnp.where(2 * place < n, 2 * place, 2 * (n - place) - 1)


def ring_step(x, axis, n):
    ring = ring_of(n)
    return lax.ppermute(x, axis, [(ring[p], ring[(p + 1) % n]) for p in range(n)])


def exchange(pieces, axis, n):
    return [pieces[0]] + [
        lax.ppermute(pieces[k], axis, [(i, (i + k) % n) for i in range(n)]) for k in range(1, n)
    ]


def swap(x, axis, n, bit):
    return lax.ppermute(x, axis, [(i, i ^ bit) for i in range(n)])


def bits(n):
    assert n & (n - 1) == 0
    return [1 << i for i in range(n.bit_length() - 1)]


def cut_kernel(g_hbm, *refs):
    chunks, sems = refs[:-1], refs[-1]
    copies = []
    at = 0
    for c, chunk in enumerate(chunks):
        part = chunk.shape[2]
        copies.append(pltpu.make_async_copy(g_hbm.at[:, :, pl.ds(at, part)], chunk, sems.at[c]))
        copies[-1].start()
        at += part
    for copy in copies:
        copy.wait()


def products_kernel(parts, w_hbm, e_hbm, *refs):
    chunks = refs[:parts]
    gw_ref, ew_ref, e_ref, w, w3, terms, w_sem, sems = refs[parts:]
    rank = w.shape[0]
    count = sems.shape[0]
    high = e_ref.shape[1] // count
    w_copy = pltpu.make_async_copy(w_hbm, w, w_sem)
    w_copy.start()
    copies = []
    for c in range(count):
        rows = pl.ds(c * high, high)
        copies.append(pltpu.make_async_copy(e_hbm.at[:, rows, :], e_ref.at[:, rows, :], sems.at[c]))
        copies[-1].start()
    w_copy.wait()
    stack3(w[...] * SHRINK, w3)
    terms[...] = w3[...].T.astype(BF16)
    total = 0.0
    at = 0
    for chunk in chunks:
        part = chunk.shape[2]
        total += dot(chunk[0], terms[at : at + part, :], (1, 0))
        at += part
    gw_ref[...] = jnp.zeros_like(gw_ref)
    gw_ref[0:rank, 0 : total.shape[0]] = sum3(total.T, rank)
    group = 2 if count % 2 == 0 and (2 * high) % 128 == 0 else count
    for c in range(0, count, group):
        for copy in copies[c : c + group]:
            copy.wait()
        rows = slice(c * high, (c + group) * high)
        ew_ref[:, rows] = sum3(dot(e_ref[0, rows, :], terms[...], (1, 0)).T, rank)


def left_kernel(a_ref, e_ref, *refs):
    gws, out_ref, g3 = refs[:-2], refs[-2], refs[-1]
    n = len(gws)
    rank = e_ref.shape[0]
    tok = a_ref.shape[1] // n
    me = lax.axis_index("tensor")
    total = e_ref[...]
    for k in range(n):
        src = lax.rem(me - k + n, n)
        rows = a_ref[0, pl.ds(pl.multiple_of(src * tok, tok), tok), :]
        total += sum3(dot(stack3(gws[k][0:rank, 0:tok], g3), rows, (1, 0)), rank)
    out_ref[...] = total


def mean_kernel(n, scale, a_ref, x_ref, y_ref, p_ref, *refs):
    msgs, p3, outbox = refs[:n], refs[n], refs[n + 1]
    rank = x_ref.shape[0]
    tok = a_ref.shape[1] // n
    me = lax.axis_index("tensor")
    mean = (x_ref[...] + y_ref[...]) * scale
    p_ref[...] = mean
    top = jnp.max(jnp.max(jnp.abs(mean), axis=1, keepdims=True), axis=0, keepdims=True)
    top = jnp.maximum(top, TINY)
    parts = stack3(mean / (top * 1024.0), p3)
    gram = [jnp.sum(mean * mean[i : i + 1, :], axis=1, keepdims=True) for i in range(rank)]
    outbox[...] = jnp.zeros_like(outbox)
    for t in range(n):
        y = dot(parts, a_ref[0, t * tok : (t + 1) * tok, :], (1, 1))
        outbox[t, 0:rank, 0:tok] = sum3(y, rank)
        for i in range(rank):
            outbox[t, rank : 2 * rank, i : i + 1] = gram[i]
        outbox[t, rank : rank + 1, rank : rank + 1] = top
    for k in range(n):
        msgs[k][...] = outbox[lax.rem(me + k, n)]


def error_right_kernel(p_ref, e_ref, out_ref, p3):
    rank = p_ref.shape[0]
    parts = stack3(p_ref[...], p3)
    for c in range(e_ref.shape[2] // BLOCK):
        cols = slice(c * BLOCK, (c + 1) * BLOCK)
        out_ref[:, cols] = sum3(dot(parts, e_ref[0, :, cols], (1, 0)), rank)


def lower_inverse(gram, rank):
    at = lambda i, j: gram[i : i + 1, j : j + 1]
    low = {}
    for j in range(rank):
        d = at(j, j)
        for k in range(j):
            d = d - low[j, k] * low[j, k]
        low[j, j] = jnp.sqrt(d)
        for i in range(j + 1, rank):
            v = at(i, j)
            for k in range(j):
                v = v - low[i, k] * low[j, k]
            low[i, j] = v / low[j, j]
    inv = {}
    for j in range(rank):
        inv[j, j] = 1.0 / low[j, j]
        for i in range(j + 1, rank):
            v = low[i, j] * inv[j, j]
            for k in range(j + 1, i):
                v = v + low[i, k] * inv[k, j]
            inv[i, j] = -v / low[i, i]
    return inv


def solve_rows(inv, x, rank):
    rows = []
    for i in range(rank):
        row = inv[i, 0] * x[0:1, :]
        for j in range(1, i + 1):
            row = row + inv[i, j] * x[j : j + 1, :]
        rows.append(row)
    return rows


def right_kernel(n, parts, p_ref, r_ref, *refs):
    chunks = refs[:parts]
    pieces = refs[parts : parts + n]
    ortho_ref, keep_ref, send_ref, inbox, z, z3, outbox = refs[parts + n :]
    rank = p_ref.shape[0]
    tok = chunks[0].shape[1]
    half = keep_ref.shape[1]
    me_t = lax.axis_index("tensor")
    core = lax.rem(lax.axis_index("dp"), 2)
    for k in range(n):
        inbox[lax.rem(me_t - k + n, n)] = pieces[k][...]
    gram = inbox[0, rank : 2 * rank, 0:rank]
    for t in range(1, n):
        gram = gram + inbox[t, rank : 2 * rank, 0:rank]
    inv = lower_inverse(gram, rank)
    for t in range(n):
        top = inbox[t, rank : rank + 1, rank : rank + 1]
        scaled = {key: value * top for key, value in inv.items()}
        for i, row in enumerate(solve_rows(scaled, inbox[t, 0:rank, 0:tok], rank)):
            if t == 0:
                z[i : i + 1, :] = row
            else:
                z[i : i + 1, :] += row
    for i, row in enumerate(solve_rows(inv, p_ref[...], rank)):
        ortho_ref[i : i + 1, :] = row
    terms = stack3(z[...], z3)
    at = 0
    for chunk in chunks:
        end = at + chunk.shape[2]
        fresh = sum3(dot(terms, chunk[0], (1, 0)), rank) * 1024.0
        old = solve_rows(inv, r_ref[:, at:end], rank)
        for i, row in enumerate(old):
            row = row + fresh[i : i + 1, :]
            for h in range(2):
                lo, hi = max(h * half, at), min((h + 1) * half, end)
                if lo < hi:
                    here = slice(lo - h * half, hi - h * half)
                    outbox[h, i : i + 1, here] = row[:, lo - at : hi - at]
        at = end
    keep_ref[...] = outbox[core]
    send_ref[...] = outbox[1 - core]


def add_kernel(x_ref, y_ref, out_ref):
    out_ref[...] = x_ref[...] + y_ref[...]


LEFT_TERMS = (0, 0, 1, 0, 2, 1)
RIGHT_TERMS = (0, 1, 0, 2, 0, 1)


def factor_kernel(scale, ortho_ref, mine_ref, other_ref, whole_ref, left_ref, right_ref, inbox, left, right):
    rank, half = mine_ref.shape
    core = lax.rem(lax.axis_index("dp"), 2)
    inbox[core] = mine_ref[...]
    inbox[1 - core] = other_ref[...]
    for h in range(2):
        whole_ref[:, h * half : (h + 1) * half] = inbox[h] * scale
    for terms, x, ref in (
        (LEFT_TERMS, ortho_ref[...], left),
        (RIGHT_TERMS, whole_ref[...], right),
    ):
        parts = split(x)
        for i, term in enumerate(terms):
            ref[i * rank : (i + 1) * rank, :] = parts[term]
    left_ref[...] = left[...].T.astype(BF16)
    right_ref[...] = right[...].astype(BF16)


def final_kernel(n, at, a_ref, left_ref, right_ref, e_ref, *refs):
    slots = refs[:n]
    rebuilt_hbm, error_hbm, acts, acts_t, rebuilt_v, error_v, sems = refs[-7:]
    tok, part = slots[0].shape[1:]
    rows = e_ref.shape[1]
    me = lax.axis_index("tensor")
    for s in range(n):
        src = ring_source(me, s, n)
        here = a_ref[0, pl.ds(pl.multiple_of(src * tok, tok), tok), :]
        acts[s * tok : (s + 1) * tok, :] = here
    acts_t[...] = acts[...].T

    wide = 256
    high = rows // sems.shape[0]
    copies = []
    for r in range(sems.shape[0]):
        here = slice(r * high, (r + 1) * high)
        for c in range(part // wide):
            cols = slice(c * wide, (c + 1) * wide)
            there = slice(at + c * wide, at + (c + 1) * wide)
            grads = jnp.concatenate([slot[0, :, cols] for slot in slots], axis=0)
            matrix = dot(acts_t[here, :], grads, (1, 0)) + e_ref[0, here, there].astype(F32)
            rebuilt = dot(left_ref[here, :], right_ref[:, there], (1, 0))
            rebuilt_v[here, cols] = rebuilt.astype(BF16)
            error_v[here, cols] = (matrix - rebuilt).astype(BF16)
        strip = pl.ds(r * high, high)
        span = pl.ds(at, part)
        copies.append(
            pltpu.make_async_copy(
                rebuilt_v.at[strip, :], rebuilt_hbm.at[strip, span], sems.at[r, 0]
            )
        )
        copies.append(
            pltpu.make_async_copy(
                error_v.at[strip, :], error_hbm.at[0, strip, span], sems.at[r, 1]
            )
        )
        copies[-2].start()
        copies[-1].start()
    for copy in copies:
        copy.wait()


def per_device(activations, out_grads, error_buffer, warm_factor):
    m = lax.axis_size("dp")
    n = lax.axis_size("tensor")
    _, tokens, rows = activations.shape
    _, tok, width = out_grads.shape
    rank = warm_factor.shape[1]
    widths = [width // share for share in SHARES]
    parts = len(widths)
    half = width // 2
    w = warm_factor.T
    sds = jax.ShapeDtypeStruct
    hbm = pl.BlockSpec(memory_space=pltpu.HBM)
    vmem = pl.BlockSpec(memory_space=pltpu.VMEM)
    dma = pltpu.SemaphoreType.DMA
    pin = lambda x: pltpu.with_memory_space_constraint(x, pltpu.HBM)

    def call(kernel, shapes, scratch, name, flops, moved, specs=None, mib=16):
        return pl.pallas_call(
            kernel,
            out_shape=shapes,
            **({"in_specs": specs} if specs else {}),
            scratch_shapes=scratch,
            compiler_params=params(mib),
            cost_estimate=cost(flops, moved),
            name=name,
        )

    def add(x, y):
        return call(add_kernel, sds(x.shape, F32), [], "add", 1e5, 1e5)(x, y)

    chunks = call(
        cut_kernel,
        [sds((1, tok, part), BF16) for part in widths],
        [dma((parts,))],
        "cut", 1e3, 1e6, [hbm],
    )(pin(out_grads))
    rings = [[chunk] for chunk in chunks]

    def turn(which, after):
        for c in which:
            after, last = lax.optimization_barrier((after, rings[c][-1]))
            rings[c].append(ring_step(last, "tensor", n))
        return after

    def settle(which, before):
        last = [rings[c][-1] for c in which]
        before, last = lax.optimization_barrier((before, last))
        for c, x in zip(which, last):
            rings[c][-1] = x
        return before

    small, others = [0], [1, 2]
    turn(small, w)

    gw, ew, error_v = call(
        functools.partial(products_kernel, parts),
        [sds((8, 128), F32), sds((rank, rows), F32), sds((1, rows, width), BF16)],
        [
            pltpu.VMEM((rank, width), F32),
            pltpu.VMEM((3 * rank, width), F32),
            pltpu.VMEM((width, 3 * rank), BF16),
            dma(()),
            dma((12,)),
        ],
        "products", 2e9, rows * width * 2, [hbm, hbm] + [vmem] * parts, 20,
    )(pin(w), pin(error_buffer), *chunks)
    gws = exchange([gw] * n, "tensor", n)
    gws = settle(small, gws)
    gws = turn(others, gws)
    left = call(
        left_kernel, sds((rank, rows), F32), [pltpu.VMEM((3 * rank, tok), F32)], "left", 1e7, 1e6
    )(activations, ew, *gws)
    for bit in bits(m)[:-1]:
        left = add(left, swap(left, "dp", m, bit))
    last = settle(others, swap(left, "dp", m, bits(m)[-1]))

    mean, *msgs = call(
        functools.partial(mean_kernel, n, 1.0 / (SHRINK * m)),
        [sds((rank, rows), F32)] + [sds((8, 128), F32)] * n,
        [pltpu.VMEM((3 * rank, rows), F32), pltpu.VMEM((n, 8, 128), F32)],
        "mean", 1e7, 1e6,
    )(activations, left, last)
    msgs = exchange(msgs, "tensor", n)

    right_raw = call(
        error_right_kernel,
        sds((rank, width), F32),
        [pltpu.VMEM((3 * rank, rows), F32)],
        "error_right", 2e9, rows * width * 2,
    )(mean, error_v)
    msgs = turn(others, msgs)

    ortho, keep, send = call(
        functools.partial(right_kernel, n, parts),
        [sds((rank, rows), F32), sds((rank, half), F32), sds((rank, half), F32)],
        [
            pltpu.VMEM((n, 8, 128), F32),
            pltpu.VMEM((rank, tok), F32),
            pltpu.VMEM((3 * rank, tok), F32),
            pltpu.VMEM((2, rank, half), F32),
        ],
        "right", 1e7, 1e6,
    )(mean, right_raw, *chunks, *msgs)
    total = add(keep, swap(send, "dp", m, 1))
    for bit in bits(m)[1:]:
        total = add(total, swap(total, "dp", m, bit))
    total = settle(others, total)
    for bit in bits(n):
        total = add(total, swap(total, "tensor", n, bit))
    total = turn(small, total)

    terms = len(LEFT_TERMS) * rank
    whole, left_terms, right_terms = call(
        functools.partial(factor_kernel, 1.0 / m),
        [sds((rank, width), F32), sds((rows, terms), BF16), sds((terms, width), BF16)],
        [
            pltpu.VMEM((2, rank, half), F32),
            pltpu.VMEM((terms, rows), F32),
            pltpu.VMEM((terms, width), F32),
        ],
        "factor", 1e6, 1e6,
    )(ortho, total, swap(total, "dp", m, 1))

    for _ in range(3, n):
        right_terms = turn([1, 0, 2], right_terms)
    outs = ()
    for c in [1, 0, 2]:
        ring, part, at = rings[c], widths[c], sum(widths[:c])
        outs = pl.pallas_call(
            functools.partial(final_kernel, n, at),
            in_specs=[vmem] * (4 + n) + [pl.BlockSpec(memory_space=pl.ANY)] * len(outs),
            out_specs=[pl.BlockSpec(memory_space=pl.ANY)] * 2,
            out_shape=[sds((rows, width), BF16), sds((1, rows, width), BF16)],
            input_output_aliases={4 + n + j: j for j in range(len(outs))},
            scratch_shapes=[
                pltpu.VMEM((tokens, rows), BF16),
                pltpu.VMEM((rows, tokens), BF16),
                pltpu.VMEM((rows, part), BF16),
                pltpu.VMEM((rows, part), BF16),
                dma((3, 2)),
            ],
            compiler_params=params(16),
            cost_estimate=cost(4e9, rows * part * 4),
            name="rebuild",
        )(activations, left_terms, right_terms, error_v, *ring, *outs)
    rebuilt, error = outs
    return rebuilt, error, whole.T


def solution(mesh):
    return jax.shard_map(
        per_device,
        mesh=mesh,
        in_specs=(P("dp", None, "tensor"), P("dp", "tensor", None), P("dp", "tensor", None), P()),
        out_specs=(P("tensor", None), P("dp", "tensor", None), P()),
        check_vma=False,
    )
```

```python
import functools

import jax
import jax.numpy as jnp
from jax import lax
from jax.experimental import pallas as pl
from jax.experimental.pallas import tpu as pltpu
from jax.sharding import PartitionSpec as P

F32 = jnp.float32
BF16 = jnp.bfloat16
SHRINK = 2.0**-23
TINY = 1e-30
BLOCK = 512
SHARES = (4, 2, 4)


def params(mib):
    return pltpu.CompilerParams(vmem_limit_bytes=mib * 2**20)


def cost(flops, moved):
    return pl.CostEstimate(flops=1, bytes_accessed=1, transcendentals=0)


def dot(a, b, contract):
    return lax.dot_general(a, b, ((contract[:1], contract[1:]), ((), ())), preferred_element_type=F32)


def split(x):
    hi = x.astype(BF16)
    rest = x - hi.astype(F32)
    mid = rest.astype(BF16)
    lo = (rest - mid.astype(F32)).astype(BF16)
    return hi.astype(F32), mid.astype(F32), lo.astype(F32)


def stack3(x, ref):
    rank = x.shape[0]
    for i, part in enumerate(split(x)):
        ref[i * rank : (i + 1) * rank, :] = part
    return ref[...].astype(BF16)


def sum3(y, rank):
    return (y[2 * rank :] + y[rank : 2 * rank]) + y[:rank]


def ring_of(n):
    return [2 * p if 2 * p < n else 2 * (n - p) - 1 for p in range(n)]


def ring_source(me, step, n):
    place = jnp.where(lax.rem(me, 2) == 0, me // 2, n - (me + 1) // 2)
    place = lax.rem(place - step + n, n)
    return jnp.where(2 * place < n, 2 * place, 2 * (n - place) - 1)


def ring_step(x, axis, n):
    ring = ring_of(n)
    return lax.ppermute(x, axis, [(ring[p], ring[(p + 1) % n]) for p in range(n)])


def exchange(pieces, axis, n):
    return [pieces[0]] + [
        lax.ppermute(pieces[k], axis, [(i, (i + k) % n) for i in range(n)]) for k in range(1, n)
    ]


def swap(x, axis, n, bit):
    return lax.ppermute(x, axis, [(i, i ^ bit) for i in range(n)])


def bits(n):
    assert n & (n - 1) == 0
    return [1 << i for i in range(n.bit_length() - 1)]


def token_factor_kernel(w_hbm, g_hbm, *refs):
    chunks = refs[:-5]
    gw_ref, terms_ref, w, w3, sems = refs[-5:]
    rank = w.shape[0]
    copies = [pltpu.make_async_copy(w_hbm, w, sems.at[0])]
    at = 0
    for c, chunk in enumerate(chunks):
        part = chunk.shape[2]
        copies.append(pltpu.make_async_copy(g_hbm.at[:, :, pl.ds(at, part)], chunk, sems.at[c + 1]))
        at += part
    for copy in copies:
        copy.start()
    copies[0].wait()
    terms = stack3(w[...] * SHRINK, w3)
    terms_ref[...] = terms
    total = 0.0
    at = 0
    for c, chunk in enumerate(chunks):
        copies[c + 1].wait()
        part = chunk.shape[2]
        total += dot(terms[:, at : at + part], chunk[0], (1, 1))
        at += part
    gw_ref[...] = jnp.zeros_like(gw_ref)
    gw_ref[0:rank, 0 : total.shape[1]] = sum3(total, rank)


def error_left_kernel(terms_ref, e_hbm, out_ref, e_ref, sems):
    rank = out_ref.shape[0]
    count = sems.shape[0]
    high = e_ref.shape[1] // count
    copies = []
    for c in range(count):
        rows = pl.ds(c * high, high)
        copies.append(pltpu.make_async_copy(e_hbm.at[:, rows, :], e_ref.at[:, rows, :], sems.at[c]))
        copies[-1].start()
    terms = terms_ref[...]
    for c in range(count):
        copies[c].wait()
        rows = slice(c * high, (c + 1) * high)
        out_ref[:, rows] = sum3(dot(terms, e_ref[0, rows, :], (1, 1)), rank)


def left_kernel(a_ref, e_ref, *refs):
    gws, out_ref, g3 = refs[:-2], refs[-2], refs[-1]
    n = len(gws)
    rank = e_ref.shape[0]
    tok = a_ref.shape[1] // n
    me = lax.axis_index("tensor")
    total = e_ref[...]
    for k in range(n):
        src = lax.rem(me - k + n, n)
        rows = a_ref[0, pl.ds(pl.multiple_of(src * tok, tok), tok), :]
        total += sum3(dot(stack3(gws[k][0:rank, 0:tok], g3), rows, (1, 0)), rank)
    out_ref[...] = total


def mean_kernel(n, scale, a_ref, x_ref, y_ref, p_ref, *refs):
    msgs, p3, outbox = refs[:n], refs[n], refs[n + 1]
    rank = x_ref.shape[0]
    tok = a_ref.shape[1] // n
    me = lax.axis_index("tensor")
    mean = (x_ref[...] + y_ref[...]) * scale
    p_ref[...] = mean
    top = jnp.max(jnp.max(jnp.abs(mean), axis=1, keepdims=True), axis=0, keepdims=True)
    top = jnp.maximum(top, TINY)
    parts = stack3(mean / (top * 1024.0), p3)
    gram = [jnp.sum(mean * mean[i : i + 1, :], axis=1, keepdims=True) for i in range(rank)]
    outbox[...] = jnp.zeros_like(outbox)
    for t in range(n):
        y = dot(parts, a_ref[0, t * tok : (t + 1) * tok, :], (1, 1))
        outbox[t, 0:rank, 0:tok] = sum3(y, rank)
        for i in range(rank):
            outbox[t, rank : 2 * rank, i : i + 1] = gram[i]
        outbox[t, rank : rank + 1, rank : rank + 1] = top
    for k in range(n):
        msgs[k][...] = outbox[lax.rem(me + k, n)]


def error_right_kernel(p_ref, e_ref, out_ref, p3):
    rank = p_ref.shape[0]
    parts = stack3(p_ref[...], p3)
    for c in range(e_ref.shape[2] // BLOCK):
        cols = slice(c * BLOCK, (c + 1) * BLOCK)
        out_ref[:, cols] = sum3(dot(parts, e_ref[0, :, cols], (1, 0)), rank)


def lower_inverse(gram, rank):
    at = lambda i, j: gram[i : i + 1, j : j + 1]
    low = {}
    for j in range(rank):
        d = at(j, j)
        for k in range(j):
            d = d - low[j, k] * low[j, k]
        low[j, j] = jnp.sqrt(d)
        for i in range(j + 1, rank):
            v = at(i, j)
            for k in range(j):
                v = v - low[i, k] * low[j, k]
            low[i, j] = v / low[j, j]
    inv = {}
    for j in range(rank):
        inv[j, j] = 1.0 / low[j, j]
        for i in range(j + 1, rank):
            v = low[i, j] * inv[j, j]
            for k in range(j + 1, i):
                v = v + low[i, k] * inv[k, j]
            inv[i, j] = -v / low[i, i]
    return inv


def solve_rows(inv, x, rank):
    rows = []
    for i in range(rank):
        row = inv[i, 0] * x[0:1, :]
        for j in range(1, i + 1):
            row = row + inv[i, j] * x[j : j + 1, :]
        rows.append(row)
    return rows


def right_kernel(n, parts, p_ref, r_ref, *refs):
    chunks = refs[:parts]
    pieces = refs[parts : parts + n]
    ortho_ref, keep_ref, send_ref, inbox, z, z3, outbox = refs[parts + n :]
    rank = p_ref.shape[0]
    tok = chunks[0].shape[1]
    half = keep_ref.shape[1]
    me_t = lax.axis_index("tensor")
    core = lax.rem(lax.axis_index("dp"), 2)
    for k in range(n):
        inbox[lax.rem(me_t - k + n, n)] = pieces[k][...]
    gram = inbox[0, rank : 2 * rank, 0:rank]
    for t in range(1, n):
        gram = gram + inbox[t, rank : 2 * rank, 0:rank]
    inv = lower_inverse(gram, rank)
    for t in range(n):
        top = inbox[t, rank : rank + 1, rank : rank + 1]
        scaled = {key: value * top for key, value in inv.items()}
        for i, row in enumerate(solve_rows(scaled, inbox[t, 0:rank, 0:tok], rank)):
            if t == 0:
                z[i : i + 1, :] = row
            else:
                z[i : i + 1, :] += row
    for i, row in enumerate(solve_rows(inv, p_ref[...], rank)):
        ortho_ref[i : i + 1, :] = row
    terms = stack3(z[...], z3)
    at = 0
    for chunk in chunks:
        end = at + chunk.shape[2]
        fresh = sum3(dot(terms, chunk[0], (1, 0)), rank) * 1024.0
        old = solve_rows(inv, r_ref[:, at:end], rank)
        for i, row in enumerate(old):
            row = row + fresh[i : i + 1, :]
            for h in range(2):
                lo, hi = max(h * half, at), min((h + 1) * half, end)
                if lo < hi:
                    here = slice(lo - h * half, hi - h * half)
                    outbox[h, i : i + 1, here] = row[:, lo - at : hi - at]
        at = end
    keep_ref[...] = outbox[core]
    send_ref[...] = outbox[1 - core]


def add_kernel(x_ref, y_ref, out_ref):
    out_ref[...] = x_ref[...] + y_ref[...]


LEFT_TERMS = (0, 0, 1, 0, 2, 1)
RIGHT_TERMS = (0, 1, 0, 2, 0, 1)


def factor_kernel(scale, ortho_ref, mine_ref, other_ref, whole_ref, left_ref, right_ref, inbox, left, right):
    rank, half = mine_ref.shape
    core = lax.rem(lax.axis_index("dp"), 2)
    inbox[core] = mine_ref[...]
    inbox[1 - core] = other_ref[...]
    for h in range(2):
        whole_ref[:, h * half : (h + 1) * half] = inbox[h] * scale
    for terms, x, ref in (
        (LEFT_TERMS, ortho_ref[...], left),
        (RIGHT_TERMS, whole_ref[...], right),
    ):
        parts = split(x)
        for i, term in enumerate(terms):
            ref[i * rank : (i + 1) * rank, :] = parts[term]
    left_ref[...] = left[...].T.astype(BF16)
    right_ref[...] = right[...].astype(BF16)


def final_kernel(n, at, a_ref, left_ref, right_ref, e_ref, *refs):
    slots = refs[:n]
    rebuilt_hbm, error_hbm, acts, acts_t, rebuilt_v, error_v, sems = refs[-7:]
    tok, part = slots[0].shape[1:]
    rows = e_ref.shape[1]
    me = lax.axis_index("tensor")
    for s in range(n):
        src = ring_source(me, s, n)
        here = a_ref[0, pl.ds(pl.multiple_of(src * tok, tok), tok), :]
        acts[s * tok : (s + 1) * tok, :] = here
    acts_t[...] = acts[...].T

    wide = 256
    high = rows // sems.shape[0]
    copies = []
    for r in range(sems.shape[0]):
        here = slice(r * high, (r + 1) * high)
        for c in range(part // wide):
            cols = slice(c * wide, (c + 1) * wide)
            there = slice(at + c * wide, at + (c + 1) * wide)
            grads = jnp.concatenate([slot[0, :, cols] for slot in slots], axis=0)
            matrix = dot(acts_t[here, :], grads, (1, 0)) + e_ref[0, here, there].astype(F32)
            rebuilt = dot(left_ref[here, :], right_ref[:, there], (1, 0))
            rebuilt_v[here, cols] = rebuilt.astype(BF16)
            error_v[here, cols] = (matrix - rebuilt).astype(BF16)
        strip = pl.ds(r * high, high)
        span = pl.ds(at, part)
        copies.append(
            pltpu.make_async_copy(
                rebuilt_v.at[strip, :], rebuilt_hbm.at[strip, span], sems.at[r, 0]
            )
        )
        copies.append(
            pltpu.make_async_copy(
                error_v.at[strip, :], error_hbm.at[0, strip, span], sems.at[r, 1]
            )
        )
        copies[-2].start()
        copies[-1].start()
    for copy in copies:
        copy.wait()


def per_device(activations, out_grads, error_buffer, warm_factor):
    m = lax.axis_size("dp")
    n = lax.axis_size("tensor")
    _, tokens, rows = activations.shape
    _, tok, width = out_grads.shape
    rank = warm_factor.shape[1]
    widths = [width // share for share in SHARES]
    parts = len(widths)
    half = width // 2
    w = warm_factor.T
    sds = jax.ShapeDtypeStruct
    hbm = pl.BlockSpec(memory_space=pltpu.HBM)
    vmem = pl.BlockSpec(memory_space=pltpu.VMEM)
    dma = pltpu.SemaphoreType.DMA
    pin = lambda x: pltpu.with_memory_space_constraint(x, pltpu.HBM)

    def call(kernel, shapes, scratch, name, flops, moved, specs=None, mib=16):
        return pl.pallas_call(
            kernel,
            out_shape=shapes,
            **({"in_specs": specs} if specs else {}),
            scratch_shapes=scratch,
            compiler_params=params(mib),
            cost_estimate=cost(flops, moved),
            name=name,
        )

    def add(x, y):
        return call(add_kernel, sds(x.shape, F32), [], "add", 1e5, 1e5)(x, y)

    *chunks, gw, w_terms = call(
        token_factor_kernel,
        [sds((1, tok, part), BF16) for part in widths]
        + [sds((8, 128), F32), sds((3 * rank, width), BF16)],
        [
            pltpu.VMEM((rank, width), F32),
            pltpu.VMEM((3 * rank, width), F32),
            dma((parts + 1,)),
        ],
        "token_factor", 1e3, 1e6, [hbm, hbm],
    )(pin(w), pin(out_grads))
    gws = exchange([gw] * n, "tensor", n)
    rings = [[chunk] for chunk in chunks]

    def turn(which, after):
        for c in which:
            after, last = lax.optimization_barrier((after, rings[c][-1]))
            rings[c].append(ring_step(last, "tensor", n))
        return after

    def settle(which, before):
        last = [rings[c][-1] for c in which]
        before, last = lax.optimization_barrier((before, last))
        for c, x in zip(which, last):
            rings[c][-1] = x
        return before

    first, rest = [0], [1, 2]
    w_terms, gws = turn(first + rest, (w_terms, gws))
    ew, error_v = call(
        error_left_kernel,
        [sds((rank, rows), F32), sds((1, rows, width), BF16)],
        [dma((rows // 128,))],
        "error_left", 2e9, rows * width * 2, [vmem, hbm],
    )(w_terms, pin(error_buffer))

    left = call(
        left_kernel, sds((rank, rows), F32), [pltpu.VMEM((3 * rank, tok), F32)], "left", 1e7, 1e6
    )(activations, ew, *gws)
    for bit in bits(m)[:-1]:
        left = add(left, swap(left, "dp", m, bit))
    last = settle(first + rest, swap(left, "dp", m, bits(m)[-1]))

    mean, *msgs = call(
        functools.partial(mean_kernel, n, 1.0 / (SHRINK * m)),
        [sds((rank, rows), F32)] + [sds((8, 128), F32)] * n,
        [pltpu.VMEM((3 * rank, rows), F32), pltpu.VMEM((n, 8, 128), F32)],
        "mean", 1e7, 1e6,
    )(activations, left, last)
    msgs = exchange(msgs, "tensor", n)

    right_raw = call(
        error_right_kernel,
        sds((rank, width), F32),
        [pltpu.VMEM((3 * rank, rows), F32)],
        "error_right", 2e9, rows * width * 2,
    )(mean, error_v)
    msgs = turn(first, msgs)

    ortho, keep, send = call(
        functools.partial(right_kernel, n, parts),
        [sds((rank, rows), F32), sds((rank, half), F32), sds((rank, half), F32)],
        [
            pltpu.VMEM((n, 8, 128), F32),
            pltpu.VMEM((rank, tok), F32),
            pltpu.VMEM((3 * rank, tok), F32),
            pltpu.VMEM((2, rank, half), F32),
        ],
        "right", 1e7, 1e6,
    )(mean, right_raw, *chunks, *msgs)
    total = add(keep, swap(send, "dp", m, 1))
    total = settle(first, total)
    for bit in bits(n):
        total = add(total, swap(total, "tensor", n, bit))
    total = turn(rest + first, total)
    for bit in bits(m)[1:]:
        total = add(total, swap(total, "dp", m, bit))

    terms = len(LEFT_TERMS) * rank
    whole, left_terms, right_terms = call(
        functools.partial(factor_kernel, 1.0 / m),
        [sds((rank, width), F32), sds((rows, terms), BF16), sds((terms, width), BF16)],
        [
            pltpu.VMEM((2, rank, half), F32),
            pltpu.VMEM((terms, rows), F32),
            pltpu.VMEM((terms, width), F32),
        ],
        "factor", 1e6, 1e6,
    )(ortho, total, swap(total, "dp", m, 1))

    for c in rest + (first + rest) * (n - 4):
        right_terms = turn([c], right_terms)
    outs = ()
    for c in rest[:1] + first + rest[1:]:
        ring, part, at = rings[c], widths[c], sum(widths[:c])
        outs = pl.pallas_call(
            functools.partial(final_kernel, n, at),
            in_specs=[vmem] * (4 + n) + [pl.BlockSpec(memory_space=pl.ANY)] * len(outs),
            out_specs=[pl.BlockSpec(memory_space=pl.ANY)] * 2,
            out_shape=[sds((rows, width), BF16), sds((1, rows, width), BF16)],
            input_output_aliases={4 + n + j: j for j in range(len(outs))},
            scratch_shapes=[
                pltpu.VMEM((tokens, rows), BF16),
                pltpu.VMEM((rows, tokens), BF16),
                pltpu.VMEM((rows, part), BF16),
                pltpu.VMEM((rows, part), BF16),
                dma((3, 2)),
            ],
            compiler_params=params(16),
            cost_estimate=cost(4e9, rows * part * 4),
            name="rebuild",
        )(activations, left_terms, right_terms, error_v, *ring, *outs)
    rebuilt, error = outs
    return rebuilt, error, whole.T


def solution(mesh):
    return jax.shard_map(
        per_device,
        mesh=mesh,
        in_specs=(P("dp", None, "tensor"), P("dp", "tensor", None), P("dp", "tensor", None), P()),
        out_specs=(P("tensor", None), P("dp", "tensor", None), P()),
        check_vma=False,
    )
```

```python
import functools

import jax
import jax.numpy as jnp
from jax import lax
from jax.experimental import pallas as pl
from jax.experimental.pallas import tpu as pltpu
from jax.sharding import PartitionSpec as P

F32 = jnp.float32
BF16 = jnp.bfloat16
SHRINK = 2.0**-23
TINY = 1e-30
BLOCK = 512
SHARES = (2, 4, 4)


def params(mib):
    return pltpu.CompilerParams(vmem_limit_bytes=mib * 2**20)


def cost(flops):
    return pl.CostEstimate(flops=int(flops) + 1, bytes_accessed=1, transcendentals=0)


def dot(a, b, contract):
    return lax.dot_general(a, b, ((contract[:1], contract[1:]), ((), ())), preferred_element_type=F32)


def split(x):
    hi = x.astype(BF16)
    rest = x - hi.astype(F32)
    mid = rest.astype(BF16)
    lo = (rest - mid.astype(F32)).astype(BF16)
    return hi.astype(F32), mid.astype(F32), lo.astype(F32)


def stack3(x, ref):
    rank = x.shape[0]
    for i, part in enumerate(split(x)):
        ref[i * rank : (i + 1) * rank, :] = part
    return ref[...].astype(BF16)


def sum3(y, rank):
    return (y[2 * rank :] + y[rank : 2 * rank]) + y[:rank]


def ring_of(n):
    return [2 * p if 2 * p < n else 2 * (n - p) - 1 for p in range(n)]


def ring_source(me, step, n):
    place = jnp.where(lax.rem(me, 2) == 0, me // 2, n - (me + 1) // 2)
    place = lax.rem(place - step + n, n)
    return jnp.where(2 * place < n, 2 * place, 2 * (n - place) - 1)


def ring_step(x, axis, n):
    ring = ring_of(n)
    return lax.ppermute(x, axis, [(ring[p], ring[(p + 1) % n]) for p in range(n)])


def exchange(pieces, axis, n):
    return [pieces[0]] + [
        lax.ppermute(pieces[k], axis, [(i, (i + k) % n) for i in range(n)]) for k in range(1, n)
    ]


def swap(x, axis, n, bit):
    return lax.ppermute(x, axis, [(i, i ^ bit) for i in range(n)])


def bits(n):
    assert n & (n - 1) == 0
    return [1 << i for i in range(n.bit_length() - 1)]


def token_factor_kernel(w_hbm, g_hbm, gw_ref, terms_ref, w, g, w3, sems):
    rank = w.shape[0]
    copies = [
        pltpu.make_async_copy(w_hbm, w, sems.at[0]),
        pltpu.make_async_copy(g_hbm, g, sems.at[1]),
    ]
    for copy in copies:
        copy.start()
    copies[0].wait()
    terms = stack3(w[...] * SHRINK, w3)
    terms_ref[...] = terms
    copies[1].wait()
    gw_ref[...] = jnp.zeros_like(gw_ref)
    gw_ref[0:rank, 0 : g.shape[1]] = sum3(dot(terms, g[0], (1, 1)), rank)


def cut_kernel(g_ref, *refs):
    chunks, sems = refs[:-1], refs[-1]
    copies = []
    at = 0
    for c, chunk in enumerate(chunks):
        part = chunk.shape[2]
        copies.append(pltpu.make_async_copy(g_ref.at[:, :, pl.ds(at, part)], chunk, sems.at[c]))
        copies[-1].start()
        at += part
    for copy in copies:
        copy.wait()


def error_left_kernel(terms_ref, e_hbm, out_ref, e_ref, sems):
    rank = out_ref.shape[0]
    count = sems.shape[0]
    high = e_ref.shape[1] // count
    copies = []
    for c in range(count):
        rows = pl.ds(c * high, high)
        copies.append(pltpu.make_async_copy(e_hbm.at[:, rows, :], e_ref.at[:, rows, :], sems.at[c]))
        copies[-1].start()
    terms = terms_ref[...]
    for c in range(count):
        copies[c].wait()
        rows = slice(c * high, (c + 1) * high)
        out_ref[:, rows] = sum3(dot(terms, e_ref[0, rows, :], (1, 1)), rank)


def left_kernel(a_ref, e_ref, *refs):
    gws, out_ref, g3 = refs[:-2], refs[-2], refs[-1]
    n = len(gws)
    rank = e_ref.shape[0]
    tok = a_ref.shape[1] // n
    me = lax.axis_index("tensor")
    total = e_ref[...]
    for k in range(n):
        src = lax.rem(me - k + n, n)
        rows = a_ref[0, pl.ds(pl.multiple_of(src * tok, tok), tok), :]
        total += sum3(dot(stack3(gws[k][0:rank, 0:tok], g3), rows, (1, 0)), rank)
    out_ref[...] = total


def mean_kernel(n, scale, a_ref, x_ref, y_ref, p_ref, *refs):
    msgs, p3, outbox = refs[:n], refs[n], refs[n + 1]
    rank = x_ref.shape[0]
    tok = a_ref.shape[1] // n
    me = lax.axis_index("tensor")
    mean = (x_ref[...] + y_ref[...]) * scale
    p_ref[...] = mean
    top = jnp.max(jnp.max(jnp.abs(mean), axis=1, keepdims=True), axis=0, keepdims=True)
    top = jnp.maximum(top, TINY)
    parts = stack3(mean / (top * 1024.0), p3)
    gram = [jnp.sum(mean * mean[i : i + 1, :], axis=1, keepdims=True) for i in range(rank)]
    outbox[...] = jnp.zeros_like(outbox)
    for t in range(n):
        y = dot(parts, a_ref[0, t * tok : (t + 1) * tok, :], (1, 1))
        outbox[t, 0:rank, 0:tok] = sum3(y, rank)
        for i in range(rank):
            outbox[t, rank : 2 * rank, i : i + 1] = gram[i]
        outbox[t, rank : rank + 1, rank : rank + 1] = top
    for k in range(n):
        msgs[k][...] = outbox[lax.rem(me + k, n)]


def error_right_kernel(p_ref, e_ref, out_ref, p3):
    rank = p_ref.shape[0]
    parts = stack3(p_ref[...], p3)
    for c in range(e_ref.shape[2] // BLOCK):
        cols = slice(c * BLOCK, (c + 1) * BLOCK)
        out_ref[:, cols] = sum3(dot(parts, e_ref[0, :, cols], (1, 0)), rank)


def lower_inverse(gram, rank):
    at = lambda i, j: gram[i : i + 1, j : j + 1]
    low = {}
    for j in range(rank):
        d = at(j, j)
        for k in range(j):
            d = d - low[j, k] * low[j, k]
        low[j, j] = jnp.sqrt(d)
        for i in range(j + 1, rank):
            v = at(i, j)
            for k in range(j):
                v = v - low[i, k] * low[j, k]
            low[i, j] = v / low[j, j]
    inv = {}
    for j in range(rank):
        inv[j, j] = 1.0 / low[j, j]
        for i in range(j + 1, rank):
            v = low[i, j] * inv[j, j]
            for k in range(j + 1, i):
                v = v + low[i, k] * inv[k, j]
            inv[i, j] = -v / low[i, i]
    return inv


def solve_rows(inv, x, rank):
    rows = []
    for i in range(rank):
        row = inv[i, 0] * x[0:1, :]
        for j in range(1, i + 1):
            row = row + inv[i, j] * x[j : j + 1, :]
        rows.append(row)
    return rows


def right_kernel(n, p_ref, r_ref, g_ref, *refs):
    pieces = refs[:n]
    ortho_ref, keep_ref, send_ref, inbox, z, z3, outbox = refs[n:]
    rank = p_ref.shape[0]
    tok = g_ref.shape[1]
    half = keep_ref.shape[1]
    me_t = lax.axis_index("tensor")
    core = lax.rem(lax.axis_index("dp"), 2)
    for k in range(n):
        inbox[lax.rem(me_t - k + n, n)] = pieces[k][...]
    gram = inbox[0, rank : 2 * rank, 0:rank]
    for t in range(1, n):
        gram = gram + inbox[t, rank : 2 * rank, 0:rank]
    inv = lower_inverse(gram, rank)
    for t in range(n):
        top = inbox[t, rank : rank + 1, rank : rank + 1]
        scaled = {key: value * top for key, value in inv.items()}
        for i, row in enumerate(solve_rows(scaled, inbox[t, 0:rank, 0:tok], rank)):
            if t == 0:
                z[i : i + 1, :] = row
            else:
                z[i : i + 1, :] += row
    for i, row in enumerate(solve_rows(inv, p_ref[...], rank)):
        ortho_ref[i : i + 1, :] = row
    terms = stack3(z[...], z3)
    for h in range(2):
        cols = slice(h * half, (h + 1) * half)
        fresh = sum3(dot(terms, g_ref[0, :, cols], (1, 0)), rank) * 1024.0
        for i, row in enumerate(solve_rows(inv, r_ref[:, cols], rank)):
            outbox[h, i : i + 1, :] = row + fresh[i : i + 1, :]
    keep_ref[...] = outbox[core]
    send_ref[...] = outbox[1 - core]


def add_kernel(x_ref, y_ref, out_ref):
    out_ref[...] = x_ref[...] + y_ref[...]


LEFT_TERMS = (0, 0, 1, 0, 2, 1)
RIGHT_TERMS = (0, 1, 0, 2, 0, 1)


def factor_kernel(scale, ortho_ref, mine_ref, other_ref, whole_ref, left_ref, right_ref, inbox, left, right):
    rank, half = mine_ref.shape
    core = lax.rem(lax.axis_index("dp"), 2)
    inbox[core] = mine_ref[...]
    inbox[1 - core] = other_ref[...]
    for h in range(2):
        whole_ref[:, h * half : (h + 1) * half] = inbox[h] * scale
    for terms, x, ref in (
        (LEFT_TERMS, ortho_ref[...], left),
        (RIGHT_TERMS, whole_ref[...], right),
    ):
        parts = split(x)
        for i, term in enumerate(terms):
            ref[i * rank : (i + 1) * rank, :] = parts[term]
    left_ref[...] = left[...].T.astype(BF16)
    right_ref[...] = right[...].astype(BF16)


def final_kernel(n, at, part, a_ref, left_ref, right_ref, e_ref, *refs):
    slots = refs[:n]
    rebuilt_hbm, error_hbm, acts, acts_t, rebuilt_v, error_v, sems = refs[-7:]
    tok = slots[0].shape[1]
    rows = e_ref.shape[1]
    me = lax.axis_index("tensor")
    for s in range(n):
        src = ring_source(me, s, n)
        here = a_ref[0, pl.ds(pl.multiple_of(src * tok, tok), tok), :]
        acts[s * tok : (s + 1) * tok, :] = here
    acts_t[...] = acts[...].T

    wide = 256
    high = rows // sems.shape[0]
    copies = []
    for r in range(sems.shape[0]):
        here = slice(r * high, (r + 1) * high)
        for c in range(part // wide):
            cols = slice(c * wide, (c + 1) * wide)
            there = slice(at + c * wide, at + (c + 1) * wide)
            grads = jnp.concatenate(
                [slot[0, :, cols if slot.shape[2] == part else there] for slot in slots], axis=0
            )
            matrix = dot(acts_t[here, :], grads, (1, 0)) + e_ref[0, here, there].astype(F32)
            rebuilt = dot(left_ref[here, :], right_ref[:, there], (1, 0))
            rebuilt_v[here, cols] = rebuilt.astype(BF16)
            error_v[here, cols] = (matrix - rebuilt).astype(BF16)
        strip = pl.ds(r * high, high)
        span = pl.ds(at, part)
        copies.append(
            pltpu.make_async_copy(
                rebuilt_v.at[strip, :], rebuilt_hbm.at[strip, span], sems.at[r, 0]
            )
        )
        copies.append(
            pltpu.make_async_copy(
                error_v.at[strip, :], error_hbm.at[0, strip, span], sems.at[r, 1]
            )
        )
        copies[-2].start()
        copies[-1].start()
    for copy in copies:
        copy.wait()


def per_device(activations, out_grads, error_buffer, warm_factor):
    m = lax.axis_size("dp")
    n = lax.axis_size("tensor")
    _, tokens, rows = activations.shape
    _, tok, width = out_grads.shape
    rank = warm_factor.shape[1]
    widths = [width // share for share in SHARES]
    parts = len(widths)
    half = width // 2
    w = warm_factor.T
    sds = jax.ShapeDtypeStruct
    hbm = pl.BlockSpec(memory_space=pltpu.HBM)
    vmem = pl.BlockSpec(memory_space=pltpu.VMEM)
    dma = pltpu.SemaphoreType.DMA
    pin = lambda x: pltpu.with_memory_space_constraint(x, pltpu.HBM)

    def call(kernel, shapes, scratch, name, specs=None, flops=0):
        return pl.pallas_call(
            kernel,
            out_shape=shapes,
            **({"in_specs": specs} if specs else {}),
            scratch_shapes=scratch,
            compiler_params=params(16),
            cost_estimate=cost(flops),
            name=name,
        )

    def add(x, y):
        return call(add_kernel, sds(x.shape, F32), [], "add")(x, y)

    gw, w_terms = call(
        token_factor_kernel,
        [sds((8, 128), F32), sds((3 * rank, width), BF16)],
        [
            pltpu.VMEM((rank, width), F32),
            pltpu.VMEM((1, tok, width), BF16),
            pltpu.VMEM((3 * rank, width), F32),
            dma((2,)),
        ],
        "token_factor", [hbm, hbm],
    )(pin(w), pin(out_grads))
    gws = exchange([gw] * n, "tensor", n)

    def after(x, y):
        return lax.optimization_barrier((x, y))

    ring = [out_grads]
    last, (w_terms, gws) = after(out_grads, (w_terms, gws))
    ring.append(ring_step(last, "tensor", n))
    ew, error_v = call(
        error_left_kernel,
        [sds((rank, rows), F32), sds((1, rows, width), BF16)],
        [dma((rows // 128,))],
        "error_left", [vmem, hbm],
    )(w_terms, pin(error_buffer))

    left = call(
        left_kernel, sds((rank, rows), F32), [pltpu.VMEM((3 * rank, tok), F32)], "left"
    )(activations, ew, *gws)
    for bit in bits(m)[:-1]:
        left = add(left, swap(left, "dp", m, bit))
    ring[1], last = after(ring[1], swap(left, "dp", m, bits(m)[-1]))

    mean, *msgs = call(
        functools.partial(mean_kernel, n, 1.0 / (SHRINK * m)),
        [sds((rank, rows), F32)] + [sds((8, 128), F32)] * n,
        [pltpu.VMEM((3 * rank, rows), F32), pltpu.VMEM((n, 8, 128), F32)],
        "mean",
    )(activations, left, last)
    msgs = exchange(msgs, "tensor", n)

    right_raw = call(
        error_right_kernel,
        sds((rank, width), F32),
        [pltpu.VMEM((3 * rank, rows), F32)],
        "error_right", None, 1.2e9,
    )(mean, error_v)

    ortho, keep, send = call(
        functools.partial(right_kernel, n),
        [sds((rank, rows), F32), sds((rank, half), F32), sds((rank, half), F32)],
        [
            pltpu.VMEM((n, 8, 128), F32),
            pltpu.VMEM((rank, tok), F32),
            pltpu.VMEM((3 * rank, tok), F32),
            pltpu.VMEM((2, rank, half), F32),
        ],
        "right",
    )(mean, right_raw, out_grads, *msgs)
    total = add(keep, swap(send, "dp", m, 1))
    for bit in bits(n):
        total = add(total, swap(total, "tensor", n, bit))
    for _ in range(2, n - 1):
        last, total = after(ring[-1], total)
        ring.append(ring_step(last, "tensor", n))
    for bit in bits(m)[1:]:
        total = add(total, swap(total, "dp", m, bit))
    ring[-1], total = after(ring[-1], total)
    chunks = call(
        cut_kernel, [sds((1, tok, part), BF16) for part in widths], [dma((parts,))], "cut"
    )(ring[-1])
    chunks = [ring_step(chunk, "tensor", n) for chunk in chunks]

    terms = len(LEFT_TERMS) * rank
    whole, left_terms, right_terms = call(
        functools.partial(factor_kernel, 1.0 / m),
        [sds((rank, width), F32), sds((rows, terms), BF16), sds((terms, width), BF16)],
        [
            pltpu.VMEM((2, rank, half), F32),
            pltpu.VMEM((terms, rows), F32),
            pltpu.VMEM((terms, width), F32),
        ],
        "factor",
    )(ortho, total, swap(total, "dp", m, 1))

    outs = ()
    for c, (part, chunk) in enumerate(zip(widths, chunks)):
        outs = pl.pallas_call(
            functools.partial(final_kernel, n, sum(widths[:c]), part),
            in_specs=[vmem] * (4 + n) + [pl.BlockSpec(memory_space=pl.ANY)] * len(outs),
            out_specs=[pl.BlockSpec(memory_space=pl.ANY)] * 2,
            out_shape=[sds((rows, width), BF16), sds((1, rows, width), BF16)],
            input_output_aliases={4 + n + j: j for j in range(len(outs))},
            scratch_shapes=[
                pltpu.VMEM((tokens, rows), BF16),
                pltpu.VMEM((rows, tokens), BF16),
                pltpu.VMEM((rows, part), BF16),
                pltpu.VMEM((rows, part), BF16),
                dma((3, 2)),
            ],
            compiler_params=params(16),
            cost_estimate=cost(0),
            name="rebuild",
        )(activations, left_terms, right_terms, error_v, *ring, chunk, *outs)
    rebuilt, error = outs
    return rebuilt, error, whole.T


def solution(mesh):
    return jax.shard_map(
        per_device,
        mesh=mesh,
        in_specs=(P("dp", None, "tensor"), P("dp", "tensor", None), P("dp", "tensor", None), P()),
        out_specs=(P("tensor", None), P("dp", "tensor", None), P()),
        check_vma=False,
    )
```

```python
import functools

import jax
import jax.numpy as jnp
from jax import lax
from jax.experimental import pallas as pl
from jax.experimental.pallas import tpu as pltpu
from jax.sharding import PartitionSpec as P

F32 = jnp.float32
BF16 = jnp.bfloat16
SHRINK = 2.0**-23
TINY = 1e-30
BLOCK = 512


def params(mib):
    return pltpu.CompilerParams(vmem_limit_bytes=mib * 2**20)


def cost(flops):
    return pl.CostEstimate(flops=int(flops) + 1, bytes_accessed=1, transcendentals=0)


def dot(a, b, contract):
    return lax.dot_general(a, b, ((contract[:1], contract[1:]), ((), ())), preferred_element_type=F32)


def split(x):
    hi = x.astype(BF16)
    rest = x - hi.astype(F32)
    mid = rest.astype(BF16)
    lo = (rest - mid.astype(F32)).astype(BF16)
    return hi.astype(F32), mid.astype(F32), lo.astype(F32)


def stack3(x, ref):
    rank = x.shape[0]
    for i, part in enumerate(split(x)):
        ref[i * rank : (i + 1) * rank, :] = part
    return ref[...].astype(BF16)


def sum3(y, rank):
    return (y[2 * rank :] + y[rank : 2 * rank]) + y[:rank]


def ring_of(n):
    return [2 * p if 2 * p < n else 2 * (n - p) - 1 for p in range(n)]


def ring_source(me, step, n):
    place = jnp.where(lax.rem(me, 2) == 0, me // 2, n - (me + 1) // 2)
    place = lax.rem(place - step + n, n)
    return jnp.where(2 * place < n, 2 * place, 2 * (n - place) - 1)


def ring_step(x, axis, n):
    ring = ring_of(n)
    return lax.ppermute(x, axis, [(ring[p], ring[(p + 1) % n]) for p in range(n)])


def exchange(pieces, axis, n):
    return [pieces[0]] + [
        lax.ppermute(pieces[k], axis, [(i, (i + k) % n) for i in range(n)]) for k in range(1, n)
    ]


def swap(x, axis, n, bit):
    return lax.ppermute(x, axis, [(i, i ^ bit) for i in range(n)])


def bits(n):
    assert n & (n - 1) == 0
    return [1 << i for i in range(n.bit_length() - 1)]


def token_factor_kernel(w_hbm, g_hbm, gw_ref, terms_ref, w, g, w3, sems):
    rank = w.shape[0]
    copies = [
        pltpu.make_async_copy(w_hbm, w, sems.at[0]),
        pltpu.make_async_copy(g_hbm, g, sems.at[1]),
    ]
    for copy in copies:
        copy.start()
    copies[0].wait()
    terms = stack3(w[...] * SHRINK, w3)
    terms_ref[...] = terms
    copies[1].wait()
    gw_ref[...] = jnp.zeros_like(gw_ref)
    gw_ref[0:rank, 0 : g.shape[1]] = sum3(dot(terms, g[0], (1, 1)), rank)


def cut_kernel(x_ref, *refs):
    chunks, sems = refs[:-1], refs[-1]
    part = chunks[0].shape[2]
    copies = [
        pltpu.make_async_copy(x_ref.at[:, :, pl.ds(c * part, part)], chunk, sems.at[c])
        for c, chunk in enumerate(chunks)
    ]
    for copy in copies:
        copy.start()
    for copy in copies:
        copy.wait()


def error_left_kernel(terms_ref, e_hbm, out_ref, e_ref, sems):
    rank = out_ref.shape[0]
    count = sems.shape[0]
    high = e_ref.shape[1] // count
    copies = []
    for c in range(count):
        rows = pl.ds(c * high, high)
        copies.append(pltpu.make_async_copy(e_hbm.at[:, rows, :], e_ref.at[:, rows, :], sems.at[c]))
        copies[-1].start()
    terms = terms_ref[...]
    for c in range(count):
        copies[c].wait()
        rows = slice(c * high, (c + 1) * high)
        out_ref[:, rows] = sum3(dot(terms, e_ref[0, rows, :], (1, 1)), rank)


def left_kernel(a_ref, e_ref, *refs):
    gws, out_ref, g3 = refs[:-2], refs[-2], refs[-1]
    n = len(gws)
    rank = e_ref.shape[0]
    tok = a_ref.shape[1] // n
    me = lax.axis_index("tensor")
    total = e_ref[...]
    for k in range(n):
        src = lax.rem(me - k + n, n)
        rows = a_ref[0, pl.ds(pl.multiple_of(src * tok, tok), tok), :]
        total += sum3(dot(stack3(gws[k][0:rank, 0:tok], g3), rows, (1, 0)), rank)
    out_ref[...] = total


def mean_kernel(n, scale, a_ref, x_ref, y_ref, p_ref, *refs):
    msgs, p3, outbox = refs[:n], refs[n], refs[n + 1]
    rank = x_ref.shape[0]
    tok = a_ref.shape[1] // n
    me = lax.axis_index("tensor")
    mean = (x_ref[...] + y_ref[...]) * scale
    p_ref[...] = mean
    top = jnp.max(jnp.max(jnp.abs(mean), axis=1, keepdims=True), axis=0, keepdims=True)
    top = jnp.maximum(top, TINY)
    parts = stack3(mean / (top * 1024.0), p3)
    gram = [jnp.sum(mean * mean[i : i + 1, :], axis=1, keepdims=True) for i in range(rank)]
    outbox[...] = jnp.zeros_like(outbox)
    for t in range(n):
        y = dot(parts, a_ref[0, t * tok : (t + 1) * tok, :], (1, 1))
        outbox[t, 0:rank, 0:tok] = sum3(y, rank)
        for i in range(rank):
            outbox[t, rank : 2 * rank, i : i + 1] = gram[i]
        outbox[t, rank : rank + 1, rank : rank + 1] = top
    for k in range(n):
        msgs[k][...] = outbox[lax.rem(me + k, n)]


def error_right_kernel(p_ref, e_ref, out_ref, p3):
    rank = p_ref.shape[0]
    parts = stack3(p_ref[...], p3)
    for c in range(e_ref.shape[2] // BLOCK):
        cols = slice(c * BLOCK, (c + 1) * BLOCK)
        out_ref[:, cols] = sum3(dot(parts, e_ref[0, :, cols], (1, 0)), rank)


def lower_inverse(gram, rank):
    at = lambda i, j: gram[i : i + 1, j : j + 1]
    low = {}
    for j in range(rank):
        d = at(j, j)
        for k in range(j):
            d = d - low[j, k] * low[j, k]
        low[j, j] = jnp.sqrt(d)
        for i in range(j + 1, rank):
            v = at(i, j)
            for k in range(j):
                v = v - low[i, k] * low[j, k]
            low[i, j] = v / low[j, j]
    inv = {}
    for j in range(rank):
        inv[j, j] = 1.0 / low[j, j]
        for i in range(j + 1, rank):
            v = low[i, j] * inv[j, j]
            for k in range(j + 1, i):
                v = v + low[i, k] * inv[k, j]
            inv[i, j] = -v / low[i, i]
    return inv


def solve_rows(inv, x, rank):
    rows = []
    for i in range(rank):
        row = inv[i, 0] * x[0:1, :]
        for j in range(1, i + 1):
            row = row + inv[i, j] * x[j : j + 1, :]
        rows.append(row)
    return rows


def right_kernel(n, p_ref, r_ref, g_ref, *refs):
    pieces = refs[:n]
    ortho_ref, keep_ref, send_ref, inbox, z, z3, outbox = refs[n:]
    rank = p_ref.shape[0]
    tok = g_ref.shape[1]
    half = keep_ref.shape[1]
    me_t = lax.axis_index("tensor")
    core = lax.rem(lax.axis_index("dp"), 2)
    for k in range(n):
        inbox[lax.rem(me_t - k + n, n)] = pieces[k][...]
    gram = inbox[0, rank : 2 * rank, 0:rank]
    for t in range(1, n):
        gram = gram + inbox[t, rank : 2 * rank, 0:rank]
    inv = lower_inverse(gram, rank)
    for t in range(n):
        top = inbox[t, rank : rank + 1, rank : rank + 1]
        scaled = {key: value * top for key, value in inv.items()}
        for i, row in enumerate(solve_rows(scaled, inbox[t, 0:rank, 0:tok], rank)):
            if t == 0:
                z[i : i + 1, :] = row
            else:
                z[i : i + 1, :] += row
    for i, row in enumerate(solve_rows(inv, p_ref[...], rank)):
        ortho_ref[i : i + 1, :] = row
    terms = stack3(z[...], z3)
    for h in range(2):
        cols = slice(h * half, (h + 1) * half)
        fresh = sum3(dot(terms, g_ref[0, :, cols], (1, 0)), rank) * 1024.0
        for i, row in enumerate(solve_rows(inv, r_ref[:, cols], rank)):
            outbox[h, i : i + 1, :] = row + fresh[i : i + 1, :]
    keep_ref[...] = outbox[core]
    send_ref[...] = outbox[1 - core]


def add_kernel(x_ref, y_ref, out_ref):
    out_ref[...] = x_ref[...] + y_ref[...]


LEFT_TERMS = (0, 0, 1, 0, 2, 1)
RIGHT_TERMS = (0, 1, 0, 2, 0, 1)


def factor_kernel(scale, ortho_ref, mine_ref, other_ref, whole_ref, left_ref, right_ref, inbox, left, right):
    rank, half = mine_ref.shape
    core = lax.rem(lax.axis_index("dp"), 2)
    inbox[core] = mine_ref[...]
    inbox[1 - core] = other_ref[...]
    for h in range(2):
        whole_ref[:, h * half : (h + 1) * half] = inbox[h] * scale
    for terms, x, ref in (
        (LEFT_TERMS, ortho_ref[...], left),
        (RIGHT_TERMS, whole_ref[...], right),
    ):
        parts = split(x)
        for i, term in enumerate(terms):
            ref[i * rank : (i + 1) * rank, :] = parts[term]
    left_ref[...] = left[...].T.astype(BF16)
    right_ref[...] = right[...].astype(BF16)


def acts_kernel(n, a_ref, out_ref, acts):
    tok = a_ref.shape[1] // n
    me = lax.axis_index("tensor")
    for s in range(n):
        src = ring_source(me, s, n)
        here = a_ref[0, pl.ds(pl.multiple_of(src * tok, tok), tok), :]
        acts[s * tok : (s + 1) * tok, :] = here
    out_ref[...] = acts[...].T


def rebuilt_kernel(left_ref, right_ref, out_ref):
    left = left_ref[...]
    for c in range(right_ref.shape[1] // BLOCK):
        cols = slice(c * BLOCK, (c + 1) * BLOCK)
        out_ref[:, cols] = dot(left, right_ref[:, cols], (1, 0)).astype(BF16)


def final_kernel(at, part, bases, acts_ref, left_ref, right_ref, e_ref, *refs):
    slots = refs[: len(bases)]
    error_hbm, error_v, sems = refs[-3:]
    rows = e_ref.shape[1]
    wide = 256
    high = rows // sems.shape[0]
    copies = []
    for r in range(sems.shape[0]):
        here = slice(r * high, (r + 1) * high)
        for c in range(part // wide):
            cols = slice(c * wide, (c + 1) * wide)
            there = slice(at + c * wide, at + (c + 1) * wide)
            grads = [
                slot[0, :, there.start - base : there.stop - base]
                for slot, base in zip(slots, bases)
            ]
            grad = dot(acts_ref[here, :], jnp.concatenate(grads, axis=0), (1, 0))
            matrix = grad + e_ref[0, here, there].astype(F32)
            rebuilt = dot(left_ref[here, :], right_ref[:, there], (1, 0))
            error_v[here, cols] = (matrix - rebuilt).astype(BF16)
        strip = pl.ds(r * high, high)
        copies.append(
            pltpu.make_async_copy(
                error_v.at[strip, :], error_hbm.at[0, strip, pl.ds(at, part)], sems.at[r]
            )
        )
        copies[-1].start()
    for copy in copies:
        copy.wait()


def per_device(activations, out_grads, error_buffer, warm_factor):
    m = lax.axis_size("dp")
    n = lax.axis_size("tensor")
    _, tokens, rows = activations.shape
    _, tok, width = out_grads.shape
    rank = warm_factor.shape[1]
    half = width // 2
    w = warm_factor.T
    sds = jax.ShapeDtypeStruct
    hbm = pl.BlockSpec(memory_space=pltpu.HBM)
    vmem = pl.BlockSpec(memory_space=pltpu.VMEM)
    dma = pltpu.SemaphoreType.DMA
    pin = lambda x: pltpu.with_memory_space_constraint(x, pltpu.HBM)

    def call(kernel, shapes, scratch, name, specs=None, flops=0):
        return pl.pallas_call(
            kernel,
            out_shape=shapes,
            **({"in_specs": specs} if specs else {}),
            scratch_shapes=scratch,
            compiler_params=params(16),
            cost_estimate=cost(flops),
            name=name,
        )

    def add(x, y):
        return call(add_kernel, sds(x.shape, F32), [], "add")(x, y)

    gw, w_terms = call(
        token_factor_kernel,
        [sds((8, 128), F32), sds((3 * rank, width), BF16)],
        [
            pltpu.VMEM((rank, width), F32),
            pltpu.VMEM((1, tok, width), BF16),
            pltpu.VMEM((3 * rank, width), F32),
            dma((2,)),
        ],
        "token_factor", [hbm, hbm],
    )(pin(w), pin(out_grads))
    gws = exchange([gw] * n, "tensor", n)

    def after(x, y):
        return lax.optimization_barrier((x, y))

    ring = [out_grads]
    last, (w_terms, gws) = after(out_grads, (w_terms, gws))
    ring.append(ring_step(last, "tensor", n))
    ew, error_v = call(
        error_left_kernel,
        [sds((rank, rows), F32), sds((1, rows, width), BF16)],
        [dma((rows // 128,))],
        "error_left", [vmem, hbm],
    )(w_terms, pin(error_buffer))

    left = call(
        left_kernel, sds((rank, rows), F32), [pltpu.VMEM((3 * rank, tok), F32)], "left"
    )(activations, ew, *gws)
    for bit in bits(m)[:-1]:
        left = add(left, swap(left, "dp", m, bit))
    ring[1], last = after(ring[1], swap(left, "dp", m, bits(m)[-1]))

    mean, *msgs = call(
        functools.partial(mean_kernel, n, 1.0 / (SHRINK * m)),
        [sds((rank, rows), F32)] + [sds((8, 128), F32)] * n,
        [pltpu.VMEM((3 * rank, rows), F32), pltpu.VMEM((n, 8, 128), F32)],
        "mean",
    )(activations, left, last)
    msgs = exchange(msgs, "tensor", n)

    right_raw = call(
        error_right_kernel,
        sds((rank, width), F32),
        [pltpu.VMEM((3 * rank, rows), F32)],
        "error_right", None, 1.2e9,
    )(mean, error_v)

    ortho, keep, send = call(
        functools.partial(right_kernel, n),
        [sds((rank, rows), F32), sds((rank, half), F32), sds((rank, half), F32)],
        [
            pltpu.VMEM((n, 8, 128), F32),
            pltpu.VMEM((rank, tok), F32),
            pltpu.VMEM((3 * rank, tok), F32),
            pltpu.VMEM((2, rank, half), F32),
        ],
        "right",
    )(mean, right_raw, out_grads, *msgs)
    total = add(keep, swap(send, "dp", m, 1))
    for bit in bits(n):
        total = add(total, swap(total, "tensor", n, bit))
    def cut(x, count):
        part = x.shape[2] // count
        return call(cut_kernel, [sds((1, tok, part), BF16)] * count, [dma((count,))], "cut")(x)

    sides = [[x] for x in cut(ring[1], 2)]
    for side in sides:
        last, total = after(side[-1], total)
        side.append(ring_step(last, "tensor", n))
    for bit in bits(m)[1:]:
        total = add(total, swap(total, "dp", m, bit))

    terms = len(LEFT_TERMS) * rank
    whole, left_terms, right_terms = call(
        functools.partial(factor_kernel, 1.0 / m),
        [sds((rank, width), F32), sds((rows, terms), BF16), sds((terms, width), BF16)],
        [
            pltpu.VMEM((2, rank, half), F32),
            pltpu.VMEM((terms, rows), F32),
            pltpu.VMEM((terms, width), F32),
        ],
        "factor",
    )(ortho, total, swap(total, "dp", m, 1))

    acts = call(
        functools.partial(acts_kernel, n),
        sds((rows, tokens), BF16),
        [pltpu.VMEM((tokens, rows), BF16)],
        "acts",
    )(activations)
    for _ in range(3, n - 1):
        for side in sides:
            last, right_terms = after(side[-1], right_terms)
            side.append(ring_step(last, "tensor", n))
    last, right_terms = after(sides[0][-1], right_terms)
    sides[0].append(ring_step(last, "tensor", n))

    rebuilt = pl.pallas_call(
        rebuilt_kernel,
        grid=(rows // 128,),
        in_specs=[
            pl.BlockSpec((128, terms), lambda i: (i, 0)),
            pl.BlockSpec((terms, width), lambda i: (0, 0)),
        ],
        out_specs=pl.BlockSpec((128, width), lambda i: (i, 0)),
        out_shape=sds((rows, width), BF16),
        compiler_params=params(16),
        cost_estimate=cost(0),
        name="rebuilt",
    )(left_terms, right_terms)
    last, rebuilt = after(sides[1][-1], rebuilt)
    pieces = [(0, half, [sides[0][-1]])]
    for c, x in enumerate(cut(last, 2)):
        pieces.append((half + c * half // 2, half // 2, [ring_step(x, "tensor", n)]))

    error = ()
    for at, part, newest in pieces:
        side = at // half
        slots = ring + sides[side][1 : n - 2] + newest
        bases = [0, 0] + [side * half] * (n - 3) + [at]
        error = pl.pallas_call(
            functools.partial(final_kernel, at, part, bases),
            in_specs=[vmem] * (4 + n) + [pl.BlockSpec(memory_space=pl.ANY)] * len(error),
            out_specs=[pl.BlockSpec(memory_space=pl.ANY)],
            out_shape=[sds((1, rows, width), BF16)],
            input_output_aliases={4 + n: 0} if error else {},
            scratch_shapes=[pltpu.VMEM((rows, part), BF16), dma((3,))],
            compiler_params=params(16),
            cost_estimate=cost(0),
            name="error",
        )(acts, left_terms, right_terms, error_v, *slots, *error)
    return rebuilt, error[0], whole.T


def solution(mesh):
    return jax.shard_map(
        per_device,
        mesh=mesh,
        in_specs=(P("dp", None, "tensor"), P("dp", "tensor", None), P("dp", "tensor", None), P()),
        out_specs=(P("tensor", None), P("dp", "tensor", None), P()),
        check_vma=False,
    )
```

```python
import functools

import jax
import jax.numpy as jnp
from jax import lax
from jax.experimental import pallas as pl
from jax.experimental.pallas import tpu as pltpu
from jax.sharding import PartitionSpec as P

F32 = jnp.float32
BF16 = jnp.bfloat16
SHRINK = 2.0**-23
TINY = 1e-30
BLOCK = 512


def params(mib):
    return pltpu.CompilerParams(vmem_limit_bytes=mib * 2**20)


def cost(flops):
    return pl.CostEstimate(flops=int(flops) + 1, bytes_accessed=1, transcendentals=0)


def dot(a, b, contract):
    return lax.dot_general(a, b, ((contract[:1], contract[1:]), ((), ())), preferred_element_type=F32)


def split(x):
    hi = x.astype(BF16)
    rest = x - hi.astype(F32)
    mid = rest.astype(BF16)
    lo = (rest - mid.astype(F32)).astype(BF16)
    return hi.astype(F32), mid.astype(F32), lo.astype(F32)


def stack3(x, ref):
    rank = x.shape[0]
    for i, part in enumerate(split(x)):
        ref[i * rank : (i + 1) * rank, :] = part
    return ref[...].astype(BF16)


def sum3(y, rank):
    return (y[2 * rank :] + y[rank : 2 * rank]) + y[:rank]


def ring_of(n):
    return [2 * p if 2 * p < n else 2 * (n - p) - 1 for p in range(n)]


def ring_source(me, step, n):
    place = jnp.where(lax.rem(me, 2) == 0, me // 2, n - (me + 1) // 2)
    place = lax.rem(place - step + n, n)
    return jnp.where(2 * place < n, 2 * place, 2 * (n - place) - 1)


def ring_step(x, axis, n):
    ring = ring_of(n)
    return lax.ppermute(x, axis, [(ring[p], ring[(p + 1) % n]) for p in range(n)])


def exchange(pieces, axis, n):
    return [pieces[0]] + [
        lax.ppermute(pieces[k], axis, [(i, (i + k) % n) for i in range(n)]) for k in range(1, n)
    ]


def swap(x, axis, n, bit):
    return lax.ppermute(x, axis, [(i, i ^ bit) for i in range(n)])


def bits(n):
    assert n & (n - 1) == 0
    return [1 << i for i in range(n.bit_length() - 1)]


def token_factor_kernel(w_hbm, g_hbm, gw_ref, terms_ref, w, g, w3, sems):
    rank = w.shape[0]
    copies = [
        pltpu.make_async_copy(w_hbm, w, sems.at[0]),
        pltpu.make_async_copy(g_hbm, g, sems.at[1]),
    ]
    for copy in copies:
        copy.start()
    copies[0].wait()
    terms = stack3(w[...] * SHRINK, w3)
    terms_ref[...] = terms
    copies[1].wait()
    gw_ref[...] = jnp.zeros_like(gw_ref)
    gw_ref[0:rank, 0 : g.shape[1]] = sum3(dot(terms, g[0], (1, 1)), rank)


def cut_kernel(x_ref, *refs):
    chunks, sems = refs[:-1], refs[-1]
    copies = []
    at = 0
    for c, chunk in enumerate(chunks):
        part = chunk.shape[2]
        copies.append(pltpu.make_async_copy(x_ref.at[:, :, pl.ds(at, part)], chunk, sems.at[c]))
        copies[-1].start()
        at += part
    for copy in copies:
        copy.wait()


def error_left_kernel(terms_ref, e_hbm, out_ref, e_ref, sems):
    rank = out_ref.shape[0]
    count = sems.shape[0]
    high = e_ref.shape[1] // count
    copies = []
    for c in range(count):
        rows = pl.ds(c * high, high)
        copies.append(pltpu.make_async_copy(e_hbm.at[:, rows, :], e_ref.at[:, rows, :], sems.at[c]))
        copies[-1].start()
    terms = terms_ref[...]
    for c in range(count):
        copies[c].wait()
        rows = slice(c * high, (c + 1) * high)
        out_ref[:, rows] = sum3(dot(terms, e_ref[0, rows, :], (1, 1)), rank)


def left_kernel(a_ref, e_ref, *refs):
    gws, out_ref, g3 = refs[:-2], refs[-2], refs[-1]
    n = len(gws)
    rank = e_ref.shape[0]
    tok = a_ref.shape[1] // n
    me = lax.axis_index("tensor")
    total = e_ref[...]
    for k in range(n):
        src = lax.rem(me - k + n, n)
        rows = a_ref[0, pl.ds(pl.multiple_of(src * tok, tok), tok), :]
        total += sum3(dot(stack3(gws[k][0:rank, 0:tok], g3), rows, (1, 0)), rank)
    out_ref[...] = total


def mean_kernel(n, scale, a_ref, x_ref, y_ref, p_ref, *refs):
    msgs, p3, outbox = refs[:n], refs[n], refs[n + 1]
    rank = x_ref.shape[0]
    tok = a_ref.shape[1] // n
    me = lax.axis_index("tensor")
    mean = (x_ref[...] + y_ref[...]) * scale
    p_ref[...] = mean
    top = jnp.max(jnp.max(jnp.abs(mean), axis=1, keepdims=True), axis=0, keepdims=True)
    top = jnp.maximum(top, TINY)
    parts = stack3(mean / (top * 1024.0), p3)
    gram = [jnp.sum(mean * mean[i : i + 1, :], axis=1, keepdims=True) for i in range(rank)]
    outbox[...] = jnp.zeros_like(outbox)
    for t in range(n):
        y = dot(parts, a_ref[0, t * tok : (t + 1) * tok, :], (1, 1))
        outbox[t, 0:rank, 0:tok] = sum3(y, rank)
        for i in range(rank):
            outbox[t, rank : 2 * rank, i : i + 1] = gram[i]
        outbox[t, rank : rank + 1, rank : rank + 1] = top
    for k in range(n):
        msgs[k][...] = outbox[lax.rem(me + k, n)]


def error_right_kernel(p_ref, e_ref, out_ref, p3):
    rank = p_ref.shape[0]
    parts = stack3(p_ref[...], p3)
    for c in range(e_ref.shape[2] // BLOCK):
        cols = slice(c * BLOCK, (c + 1) * BLOCK)
        out_ref[:, cols] = sum3(dot(parts, e_ref[0, :, cols], (1, 0)), rank)


def lower_inverse(gram, rank):
    at = lambda i, j: gram[i : i + 1, j : j + 1]
    low = {}
    for j in range(rank):
        d = at(j, j)
        for k in range(j):
            d = d - low[j, k] * low[j, k]
        low[j, j] = jnp.sqrt(d)
        for i in range(j + 1, rank):
            v = at(i, j)
            for k in range(j):
                v = v - low[i, k] * low[j, k]
            low[i, j] = v / low[j, j]
    inv = {}
    for j in range(rank):
        inv[j, j] = 1.0 / low[j, j]
        for i in range(j + 1, rank):
            v = low[i, j] * inv[j, j]
            for k in range(j + 1, i):
                v = v + low[i, k] * inv[k, j]
            inv[i, j] = -v / low[i, i]
    return inv


def solve_rows(inv, x, rank):
    rows = []
    for i in range(rank):
        row = inv[i, 0] * x[0:1, :]
        for j in range(1, i + 1):
            row = row + inv[i, j] * x[j : j + 1, :]
        rows.append(row)
    return rows


def right_kernel(n, p_ref, r_ref, g_ref, *refs):
    pieces = refs[:n]
    ortho_ref, keep_ref, send_ref, inbox, z, z3, outbox = refs[n:]
    rank = p_ref.shape[0]
    tok = g_ref.shape[1]
    half = keep_ref.shape[1]
    me_t = lax.axis_index("tensor")
    core = lax.rem(lax.axis_index("dp"), 2)
    for k in range(n):
        inbox[lax.rem(me_t - k + n, n)] = pieces[k][...]
    gram = inbox[0, rank : 2 * rank, 0:rank]
    for t in range(1, n):
        gram = gram + inbox[t, rank : 2 * rank, 0:rank]
    inv = lower_inverse(gram, rank)
    for t in range(n):
        top = inbox[t, rank : rank + 1, rank : rank + 1]
        scaled = {key: value * top for key, value in inv.items()}
        for i, row in enumerate(solve_rows(scaled, inbox[t, 0:rank, 0:tok], rank)):
            if t == 0:
                z[i : i + 1, :] = row
            else:
                z[i : i + 1, :] += row
    for i, row in enumerate(solve_rows(inv, p_ref[...], rank)):
        ortho_ref[i : i + 1, :] = row
    terms = stack3(z[...], z3)
    for h in range(2):
        cols = slice(h * half, (h + 1) * half)
        fresh = sum3(dot(terms, g_ref[0, :, cols], (1, 0)), rank) * 1024.0
        for i, row in enumerate(solve_rows(inv, r_ref[:, cols], rank)):
            outbox[h, i : i + 1, :] = row + fresh[i : i + 1, :]
    keep_ref[...] = outbox[core]
    send_ref[...] = outbox[1 - core]


def add_kernel(x_ref, y_ref, out_ref):
    out_ref[...] = x_ref[...] + y_ref[...]


LEFT_TERMS = (0, 0, 1, 0, 2, 1)
RIGHT_TERMS = (0, 1, 0, 2, 0, 1)


def factor_kernel(scale, ortho_ref, mine_ref, other_ref, whole_ref, left_ref, right_ref, inbox, left, right):
    rank, half = mine_ref.shape
    core = lax.rem(lax.axis_index("dp"), 2)
    inbox[core] = mine_ref[...]
    inbox[1 - core] = other_ref[...]
    for h in range(2):
        whole_ref[:, h * half : (h + 1) * half] = inbox[h] * scale
    for terms, x, ref in (
        (LEFT_TERMS, ortho_ref[...], left),
        (RIGHT_TERMS, whole_ref[...], right),
    ):
        parts = split(x)
        for i, term in enumerate(terms):
            ref[i * rank : (i + 1) * rank, :] = parts[term]
    left_ref[...] = left[...].T.astype(BF16)
    right_ref[...] = right[...].astype(BF16)


def acts_kernel(n, a_ref, out_ref, acts):
    tok = a_ref.shape[1] // n
    me = lax.axis_index("tensor")
    for s in range(n):
        src = ring_source(me, s, n)
        here = a_ref[0, pl.ds(pl.multiple_of(src * tok, tok), tok), :]
        acts[s * tok : (s + 1) * tok, :] = here
    out_ref[...] = acts[...].T


def final_kernel(at, part, bases, acts_ref, left_ref, right_ref, e_ref, *refs):
    slots = refs[: len(bases)]
    rebuilt_hbm, error_hbm, rebuilt_v, error_v, sems = refs[-5:]
    rows = e_ref.shape[1]
    wide = 256
    high = rows // sems.shape[0]
    copies = []
    for r in range(sems.shape[0]):
        here = slice(r * high, (r + 1) * high)
        for c in range(part // wide):
            cols = slice(c * wide, (c + 1) * wide)
            there = slice(at + c * wide, at + (c + 1) * wide)
            grads = [
                slot[0, :, there.start - base : there.stop - base]
                for slot, base in zip(slots, bases)
            ]
            grad = dot(acts_ref[here, :], jnp.concatenate(grads, axis=0), (1, 0))
            matrix = grad + e_ref[0, here, there].astype(F32)
            rebuilt = dot(left_ref[here, :], right_ref[:, there], (1, 0))
            rebuilt_v[here, cols] = rebuilt.astype(BF16)
            error_v[here, cols] = (matrix - rebuilt).astype(BF16)
        strip = pl.ds(r * high, high)
        span = pl.ds(at, part)
        copies += [
            pltpu.make_async_copy(
                rebuilt_v.at[strip, :], rebuilt_hbm.at[strip, span], sems.at[r, 0]
            ),
            pltpu.make_async_copy(
                error_v.at[strip, :], error_hbm.at[0, strip, span], sems.at[r, 1]
            ),
        ]
        copies[-2].start()
        copies[-1].start()
    for copy in copies:
        copy.wait()


def per_device(activations, out_grads, error_buffer, warm_factor):
    m = lax.axis_size("dp")
    n = lax.axis_size("tensor")
    _, tokens, rows = activations.shape
    _, tok, width = out_grads.shape
    rank = warm_factor.shape[1]
    half = width // 2
    w = warm_factor.T
    sds = jax.ShapeDtypeStruct
    hbm = pl.BlockSpec(memory_space=pltpu.HBM)
    vmem = pl.BlockSpec(memory_space=pltpu.VMEM)
    dma = pltpu.SemaphoreType.DMA
    pin = lambda x: pltpu.with_memory_space_constraint(x, pltpu.HBM)

    def call(kernel, shapes, scratch, name, specs=None, flops=0):
        return pl.pallas_call(
            kernel,
            out_shape=shapes,
            **({"in_specs": specs} if specs else {}),
            scratch_shapes=scratch,
            compiler_params=params(16),
            cost_estimate=cost(flops),
            name=name,
        )

    def add(x, y):
        return call(add_kernel, sds(x.shape, F32), [], "add")(x, y)

    def after(x, y):
        return lax.optimization_barrier((x, y))

    def cut(x, widths):
        shapes = [sds((1, tok, part), BF16) for part in widths]
        return call(cut_kernel, shapes, [dma((len(widths),))], "cut")(x)

    def step(x):
        return ring_step(x, "tensor", n)

    wide = 6 * width // 20
    narrow = width // 2 - wide
    ring = [out_grads, step(out_grads)]

    gw, w_terms = call(
        token_factor_kernel,
        [sds((8, 128), F32), sds((3 * rank, width), BF16)],
        [
            pltpu.VMEM((rank, width), F32),
            pltpu.VMEM((1, tok, width), BF16),
            pltpu.VMEM((3 * rank, width), F32),
            dma((2,)),
        ],
        "token_factor", [hbm, hbm],
    )(pin(w), pin(out_grads))
    gws = exchange([gw] * n, "tensor", n)

    ew, error_v = call(
        error_left_kernel,
        [sds((rank, rows), F32), sds((1, rows, width), BF16)],
        [dma((rows // 128,))],
        "error_left", [vmem, hbm], 4.6e9,
    )(w_terms, pin(error_buffer))

    ring[1], gws = after(ring[1], gws)
    x1, y1 = cut(ring[1], [2 * wide, 2 * narrow])
    xs, ys = [x1, step(x1)], [y1]
    left = call(
        left_kernel, sds((rank, rows), F32), [pltpu.VMEM((3 * rank, tok), F32)], "left"
    )(activations, ew, *gws)
    for bit in bits(m)[:-1]:
        left = add(left, swap(left, "dp", m, bit))
    xs[1], last = after(xs[1], swap(left, "dp", m, bits(m)[-1]))

    mean, *msgs = call(
        functools.partial(mean_kernel, n, 1.0 / (SHRINK * m)),
        [sds((rank, rows), F32)] + [sds((8, 128), F32)] * n,
        [pltpu.VMEM((3 * rank, rows), F32), pltpu.VMEM((n, 8, 128), F32)],
        "mean",
    )(activations, left, last)
    msgs = exchange(msgs, "tensor", n)

    right_raw = call(
        error_right_kernel,
        sds((rank, width), F32),
        [pltpu.VMEM((3 * rank, rows), F32)],
        "error_right", None, 1.2e9,
    )(mean, error_v)

    ortho, keep, send = call(
        functools.partial(right_kernel, n),
        [sds((rank, rows), F32), sds((rank, half), F32), sds((rank, half), F32)],
        [
            pltpu.VMEM((n, 8, 128), F32),
            pltpu.VMEM((rank, tok), F32),
            pltpu.VMEM((3 * rank, tok), F32),
            pltpu.VMEM((2, rank, half), F32),
        ],
        "right",
    )(mean, right_raw, out_grads, *msgs)
    total = add(keep, swap(send, "dp", m, 1))
    for bit in bits(n):
        total = add(total, swap(total, "tensor", n, bit))
    for _ in range(4, n):
        last, total = after(xs[-1], total)
        xs.append(step(last))
    xa, xb = cut(xs[-1], [wide, wide])
    xa, total = after(xa, total)
    xa = step(xa)
    for _ in range(3, n):
        last, total = after(ys[-1], total)
        ys.append(step(last))
    total = add(total, swap(total, "dp", m, 2))
    xb, total = after(xb, total)
    xb = step(xb)
    for bit in bits(m)[2:]:
        total = add(total, swap(total, "dp", m, bit))

    terms = len(LEFT_TERMS) * rank
    whole, left_terms, right_terms = call(
        functools.partial(factor_kernel, 1.0 / m),
        [sds((rank, width), F32), sds((rows, terms), BF16), sds((terms, width), BF16)],
        [
            pltpu.VMEM((2, rank, half), F32),
            pltpu.VMEM((terms, rows), F32),
            pltpu.VMEM((terms, width), F32),
        ],
        "factor",
    )(ortho, total, swap(total, "dp", m, 1))

    acts = call(
        functools.partial(acts_kernel, n),
        sds((rows, tokens), BF16),
        [pltpu.VMEM((tokens, rows), BF16)],
        "acts",
    )(activations)
    last, right_terms = after(ys[-1], right_terms)
    ya, yb = cut(last, [narrow, narrow])
    pieces = []
    at = 0
    for part, base, held, newest in (
        (wide, 0, xs, xa),
        (wide, 0, xs, xb),
        (narrow, 2 * wide, ys, step(ya)),
        (narrow, 2 * wide, ys, step(yb)),
    ):
        slots = ring + held[1 : n - 2] + [newest]
        bases = [0, 0] + [base] * (n - 3) + [at]
        pieces.append((at, part, slots, bases))
        at += part

    outs = ()
    for at, part, slots, bases in pieces:
        outs = pl.pallas_call(
            functools.partial(final_kernel, at, part, bases),
            in_specs=[vmem] * (4 + n) + [pl.BlockSpec(memory_space=pl.ANY)] * len(outs),
            out_specs=[pl.BlockSpec(memory_space=pl.ANY)] * 2,
            out_shape=[sds((rows, width), BF16), sds((1, rows, width), BF16)],
            input_output_aliases={4 + n + j: j for j in range(len(outs))},
            scratch_shapes=[pltpu.VMEM((rows, part), BF16)] * 2 + [dma((3, 2))],
            compiler_params=params(16),
            cost_estimate=cost(0),
            name="rebuild",
        )(acts, left_terms, right_terms, error_v, *slots, *outs)
    rebuilt, error = outs
    return rebuilt, error, whole.T


def solution(mesh):
    return jax.shard_map(
        per_device,
        mesh=mesh,
        in_specs=(P("dp", None, "tensor"), P("dp", "tensor", None), P("dp", "tensor", None), P()),
        out_specs=(P("tensor", None), P("dp", "tensor", None), P()),
        check_vma=False,
    )
```

```python
import functools

import jax
import jax.numpy as jnp
from jax import lax
from jax.experimental import pallas as pl
from jax.experimental.pallas import tpu as pltpu
from jax.sharding import PartitionSpec as P

F32 = jnp.float32
BF16 = jnp.bfloat16
SHRINK = 2.0**-23
TINY = 1e-30
BLOCK = 512


def params(mib):
    return pltpu.CompilerParams(vmem_limit_bytes=mib * 2**20)


def cost(flops):
    return pl.CostEstimate(flops=int(flops) + 1, bytes_accessed=1, transcendentals=0)


def dot(a, b, contract):
    return lax.dot_general(a, b, ((contract[:1], contract[1:]), ((), ())), preferred_element_type=F32)


def split(x):
    hi = x.astype(BF16)
    rest = x - hi.astype(F32)
    mid = rest.astype(BF16)
    lo = (rest - mid.astype(F32)).astype(BF16)
    return hi.astype(F32), mid.astype(F32), lo.astype(F32)


def stack3(x, ref):
    rank = x.shape[0]
    for i, part in enumerate(split(x)):
        ref[i * rank : (i + 1) * rank, :] = part
    return ref[...].astype(BF16)


def sum3(y, rank):
    return (y[2 * rank :] + y[rank : 2 * rank]) + y[:rank]


def ring_of(n):
    return [2 * p if 2 * p < n else 2 * (n - p) - 1 for p in range(n)]


def ring_source(me, step, n):
    place = jnp.where(lax.rem(me, 2) == 0, me // 2, n - (me + 1) // 2)
    place = lax.rem(place - step + n, n)
    return jnp.where(2 * place < n, 2 * place, 2 * (n - place) - 1)


def ring_step(x, axis, n):
    ring = ring_of(n)
    return lax.ppermute(x, axis, [(ring[p], ring[(p + 1) % n]) for p in range(n)])


def exchange(pieces, axis, n):
    return [pieces[0]] + [
        lax.ppermute(pieces[k], axis, [(i, (i + k) % n) for i in range(n)]) for k in range(1, n)
    ]


def swap(x, axis, n, bit):
    return lax.ppermute(x, axis, [(i, i ^ bit) for i in range(n)])


def bits(n):
    assert n & (n - 1) == 0
    return [1 << i for i in range(n.bit_length() - 1)]


def token_factor_kernel(w_hbm, g_hbm, gw_ref, terms_ref, w, g, w3, sems):
    rank = w.shape[0]
    copies = [
        pltpu.make_async_copy(w_hbm, w, sems.at[0]),
        pltpu.make_async_copy(g_hbm, g, sems.at[1]),
    ]
    for copy in copies:
        copy.start()
    copies[0].wait()
    terms = stack3(w[...] * SHRINK, w3)
    terms_ref[...] = terms
    copies[1].wait()
    gw_ref[...] = jnp.zeros_like(gw_ref)
    gw_ref[0:rank, 0 : g.shape[1]] = sum3(dot(terms, g[0], (1, 1)), rank)


def cut_kernel(x_ref, *refs):
    chunks, sems = refs[:-1], refs[-1]
    copies = []
    at = 0
    for c, chunk in enumerate(chunks):
        part = chunk.shape[2]
        copies.append(pltpu.make_async_copy(x_ref.at[:, :, pl.ds(at, part)], chunk, sems.at[c]))
        copies[-1].start()
        at += part
    for copy in copies:
        copy.wait()


def error_left_kernel(terms_ref, e_hbm, out_ref, e_ref, sems):
    rank = out_ref.shape[0]
    count = sems.shape[0]
    high = e_ref.shape[1] // count
    copies = []
    for c in range(count):
        rows = pl.ds(c * high, high)
        copies.append(pltpu.make_async_copy(e_hbm.at[:, rows, :], e_ref.at[:, rows, :], sems.at[c]))
        copies[-1].start()
    terms = terms_ref[...]
    for c in range(count):
        copies[c].wait()
        rows = slice(c * high, (c + 1) * high)
        out_ref[:, rows] = sum3(dot(terms, e_ref[0, rows, :], (1, 1)), rank)


def left_kernel(a_ref, e_ref, *refs):
    gws, out_ref, g3 = refs[:-2], refs[-2], refs[-1]
    n = len(gws)
    rank = e_ref.shape[0]
    tok = a_ref.shape[1] // n
    me = lax.axis_index("tensor")
    total = e_ref[...]
    for k in range(n):
        src = lax.rem(me - k + n, n)
        rows = a_ref[0, pl.ds(pl.multiple_of(src * tok, tok), tok), :]
        total += sum3(dot(stack3(gws[k][0:rank, 0:tok], g3), rows, (1, 0)), rank)
    out_ref[...] = total


def mean_kernel(n, scale, a_ref, x_ref, y_ref, p_ref, *refs):
    msgs, p3, outbox = refs[:n], refs[n], refs[n + 1]
    rank = x_ref.shape[0]
    tok = a_ref.shape[1] // n
    me = lax.axis_index("tensor")
    mean = (x_ref[...] + y_ref[...]) * scale
    p_ref[...] = mean
    top = jnp.max(jnp.max(jnp.abs(mean), axis=1, keepdims=True), axis=0, keepdims=True)
    top = jnp.maximum(top, TINY)
    parts = stack3(mean / (top * 1024.0), p3)
    gram = [jnp.sum(mean * mean[i : i + 1, :], axis=1, keepdims=True) for i in range(rank)]
    outbox[...] = jnp.zeros_like(outbox)
    for t in range(n):
        y = dot(parts, a_ref[0, t * tok : (t + 1) * tok, :], (1, 1))
        outbox[t, 0:rank, 0:tok] = sum3(y, rank)
        for i in range(rank):
            outbox[t, rank : 2 * rank, i : i + 1] = gram[i]
        outbox[t, rank : rank + 1, rank : rank + 1] = top
    for k in range(n):
        msgs[k][...] = outbox[lax.rem(me + k, n)]


def error_right_kernel(p_ref, e_ref, out_ref, p3):
    rank = p_ref.shape[0]
    parts = stack3(p_ref[...], p3)
    for c in range(e_ref.shape[2] // BLOCK):
        cols = slice(c * BLOCK, (c + 1) * BLOCK)
        out_ref[:, cols] = sum3(dot(parts, e_ref[0, :, cols], (1, 0)), rank)


def lower_inverse(gram, rank):
    at = lambda i, j: gram[i : i + 1, j : j + 1]
    low = {}
    for j in range(rank):
        d = at(j, j)
        for k in range(j):
            d = d - low[j, k] * low[j, k]
        low[j, j] = jnp.sqrt(d)
        for i in range(j + 1, rank):
            v = at(i, j)
            for k in range(j):
                v = v - low[i, k] * low[j, k]
            low[i, j] = v / low[j, j]
    inv = {}
    for j in range(rank):
        inv[j, j] = 1.0 / low[j, j]
        for i in range(j + 1, rank):
            v = low[i, j] * inv[j, j]
            for k in range(j + 1, i):
                v = v + low[i, k] * inv[k, j]
            inv[i, j] = -v / low[i, i]
    return inv


def solve_rows(inv, x, rank):
    rows = []
    for i in range(rank):
        row = inv[i, 0] * x[0:1, :]
        for j in range(1, i + 1):
            row = row + inv[i, j] * x[j : j + 1, :]
        rows.append(row)
    return rows


def right_kernel(n, p_ref, r_ref, g_ref, *refs):
    pieces = refs[:n]
    ortho_ref, keep_ref, send_ref, inbox, z, z3, outbox = refs[n:]
    rank = p_ref.shape[0]
    tok = g_ref.shape[1]
    half = keep_ref.shape[1]
    me_t = lax.axis_index("tensor")
    core = lax.rem(lax.axis_index("dp"), 2)
    for k in range(n):
        inbox[lax.rem(me_t - k + n, n)] = pieces[k][...]
    gram = inbox[0, rank : 2 * rank, 0:rank]
    for t in range(1, n):
        gram = gram + inbox[t, rank : 2 * rank, 0:rank]
    inv = lower_inverse(gram, rank)
    for t in range(n):
        top = inbox[t, rank : rank + 1, rank : rank + 1]
        scaled = {key: value * top for key, value in inv.items()}
        for i, row in enumerate(solve_rows(scaled, inbox[t, 0:rank, 0:tok], rank)):
            if t == 0:
                z[i : i + 1, :] = row
            else:
                z[i : i + 1, :] += row
    for i, row in enumerate(solve_rows(inv, p_ref[...], rank)):
        ortho_ref[i : i + 1, :] = row
    terms = stack3(z[...], z3)
    for h in range(2):
        cols = slice(h * half, (h + 1) * half)
        fresh = sum3(dot(terms, g_ref[0, :, cols], (1, 0)), rank) * 1024.0
        for i, row in enumerate(solve_rows(inv, r_ref[:, cols], rank)):
            outbox[h, i : i + 1, :] = row + fresh[i : i + 1, :]
    keep_ref[...] = outbox[core]
    send_ref[...] = outbox[1 - core]


def add_kernel(x_ref, y_ref, out_ref):
    out_ref[...] = x_ref[...] + y_ref[...]


LEFT_TERMS = (0, 0, 1, 0, 2, 1)
RIGHT_TERMS = (0, 1, 0, 2, 0, 1)


def factor_kernel(scale, ortho_ref, mine_ref, other_ref, whole_ref, left_ref, right_ref, inbox, left, right):
    rank, half = mine_ref.shape
    core = lax.rem(lax.axis_index("dp"), 2)
    inbox[core] = mine_ref[...]
    inbox[1 - core] = other_ref[...]
    for h in range(2):
        whole_ref[:, h * half : (h + 1) * half] = inbox[h] * scale
    for terms, x, ref in (
        (LEFT_TERMS, ortho_ref[...], left),
        (RIGHT_TERMS, whole_ref[...], right),
    ):
        parts = split(x)
        for i, term in enumerate(terms):
            ref[i * rank : (i + 1) * rank, :] = parts[term]
    left_ref[...] = left[...].T.astype(BF16)
    right_ref[...] = right[...].astype(BF16)


def acts_kernel(n, a_ref, out_ref, acts):
    tok = a_ref.shape[1] // n
    me = lax.axis_index("tensor")
    for s in range(n):
        src = ring_source(me, s, n)
        here = a_ref[0, pl.ds(pl.multiple_of(src * tok, tok), tok), :]
        acts[s * tok : (s + 1) * tok, :] = here
    out_ref[...] = acts[...].T


def final_kernel(at, part, bases, acts_ref, left_ref, right_ref, e_ref, *refs):
    slots = refs[: len(bases)]
    rebuilt_hbm, error_hbm, rebuilt_v, error_v, sems = refs[-5:]
    rows = e_ref.shape[1]
    wide = 256
    high = rows // sems.shape[0]
    copies = []
    for r in range(sems.shape[0]):
        here = slice(r * high, (r + 1) * high)
        for c in range(part // wide):
            cols = slice(c * wide, (c + 1) * wide)
            there = slice(at + c * wide, at + (c + 1) * wide)
            grads = [
                slot[0, :, there.start - base : there.stop - base]
                for slot, base in zip(slots, bases)
            ]
            grad = dot(acts_ref[here, :], jnp.concatenate(grads, axis=0), (1, 0))
            matrix = grad + e_ref[0, here, there].astype(F32)
            rebuilt = dot(left_ref[here, :], right_ref[:, there], (1, 0))
            rebuilt_v[here, cols] = rebuilt.astype(BF16)
            error_v[here, cols] = (matrix - rebuilt).astype(BF16)
        strip = pl.ds(r * high, high)
        span = pl.ds(at, part)
        copies += [
            pltpu.make_async_copy(
                rebuilt_v.at[strip, :], rebuilt_hbm.at[strip, span], sems.at[r, 0]
            ),
            pltpu.make_async_copy(
                error_v.at[strip, :], error_hbm.at[0, strip, span], sems.at[r, 1]
            ),
        ]
        copies[-2].start()
        copies[-1].start()
    for copy in copies:
        copy.wait()


def per_device(activations, out_grads, error_buffer, warm_factor):
    m = lax.axis_size("dp")
    n = lax.axis_size("tensor")
    _, tokens, rows = activations.shape
    _, tok, width = out_grads.shape
    rank = warm_factor.shape[1]
    half = width // 2
    w = warm_factor.T
    sds = jax.ShapeDtypeStruct
    hbm = pl.BlockSpec(memory_space=pltpu.HBM)
    vmem = pl.BlockSpec(memory_space=pltpu.VMEM)
    dma = pltpu.SemaphoreType.DMA
    pin = lambda x: pltpu.with_memory_space_constraint(x, pltpu.HBM)

    def call(kernel, shapes, scratch, name, specs=None, flops=0):
        return pl.pallas_call(
            kernel,
            out_shape=shapes,
            **({"in_specs": specs} if specs else {}),
            scratch_shapes=scratch,
            compiler_params=params(16),
            cost_estimate=cost(flops),
            name=name,
        )

    def add(x, y):
        return call(add_kernel, sds(x.shape, F32), [], "add")(x, y)

    def after(x, y):
        return lax.optimization_barrier((x, y))

    def cut(x, widths):
        shapes = [sds((1, tok, part), BF16) for part in widths]
        return call(cut_kernel, shapes, [dma((len(widths),))], "cut")(x)

    def step(x):
        return ring_step(x, "tensor", n)

    wide = 6 * width // 20
    narrow = width // 2 - wide
    ring = [out_grads, step(out_grads)]

    gw, w_terms = call(
        token_factor_kernel,
        [sds((8, 128), F32), sds((3 * rank, width), BF16)],
        [
            pltpu.VMEM((rank, width), F32),
            pltpu.VMEM((1, tok, width), BF16),
            pltpu.VMEM((3 * rank, width), F32),
            dma((2,)),
        ],
        "token_factor", [hbm, hbm],
    )(pin(w), pin(out_grads))
    ew, error_v = call(
        error_left_kernel,
        [sds((rank, rows), F32), sds((1, rows, width), BF16)],
        [dma((rows // 128,))],
        "error_left", [vmem, hbm], 4.6e9,
    )(w_terms, pin(error_buffer))

    gw, ew = after(gw, ew)
    gws = exchange([gw] * n, "tensor", n)
    ring[1], gws = after(ring[1], gws)
    x1, y1 = cut(ring[1], [2 * wide, 2 * narrow])
    xs, ys = [x1, step(x1)], [y1]
    left = call(
        left_kernel, sds((rank, rows), F32), [pltpu.VMEM((3 * rank, tok), F32)], "left"
    )(activations, ew, *gws)
    for bit in bits(m)[:-1]:
        left = add(left, swap(left, "dp", m, bit))
    xs[1], last = after(xs[1], swap(left, "dp", m, bits(m)[-1]))

    mean, *msgs = call(
        functools.partial(mean_kernel, n, 1.0 / (SHRINK * m)),
        [sds((rank, rows), F32)] + [sds((8, 128), F32)] * n,
        [pltpu.VMEM((3 * rank, rows), F32), pltpu.VMEM((n, 8, 128), F32)],
        "mean",
    )(activations, left, last)
    msgs = exchange(msgs, "tensor", n)

    right_raw = call(
        error_right_kernel,
        sds((rank, width), F32),
        [pltpu.VMEM((3 * rank, rows), F32)],
        "error_right", None, 1.2e9,
    )(mean, error_v)

    ortho, keep, send = call(
        functools.partial(right_kernel, n),
        [sds((rank, rows), F32), sds((rank, half), F32), sds((rank, half), F32)],
        [
            pltpu.VMEM((n, 8, 128), F32),
            pltpu.VMEM((rank, tok), F32),
            pltpu.VMEM((3 * rank, tok), F32),
            pltpu.VMEM((2, rank, half), F32),
        ],
        "right",
    )(mean, right_raw, out_grads, *msgs)
    total = add(keep, swap(send, "dp", m, 1))
    for _ in range(3, n):
        last, total = after(ys[-1], total)
        ys.append(step(last))
    for _ in range(4, n):
        last, total = after(xs[-1], total)
        xs.append(step(last))
    for bit in bits(m)[1:]:
        total = add(total, swap(total, "dp", m, bit))
    (xs[-1], ys[-1]), total = after((xs[-1], ys[-1]), total)
    for bit in bits(n):
        total = add(total, swap(total, "tensor", n, bit))
    xa, xb = cut(xs[-1], [wide, wide])
    (xa, xb), total = after((xa, xb), total)
    xa, xb = step(xa), step(xb)

    terms = len(LEFT_TERMS) * rank
    whole, left_terms, right_terms = call(
        functools.partial(factor_kernel, 1.0 / m),
        [sds((rank, width), F32), sds((rows, terms), BF16), sds((terms, width), BF16)],
        [
            pltpu.VMEM((2, rank, half), F32),
            pltpu.VMEM((terms, rows), F32),
            pltpu.VMEM((terms, width), F32),
        ],
        "factor",
    )(ortho, total, swap(total, "dp", m, 1))

    acts = call(
        functools.partial(acts_kernel, n),
        sds((rows, tokens), BF16),
        [pltpu.VMEM((tokens, rows), BF16)],
        "acts",
    )(activations)
    last, right_terms = after(ys[-1], right_terms)
    ya, yb = cut(last, [narrow, narrow])
    pieces = []
    at = 0
    for part, base, held, newest in (
        (wide, 0, xs, xa),
        (wide, 0, xs, xb),
        (narrow, 2 * wide, ys, step(ya)),
        (narrow, 2 * wide, ys, step(yb)),
    ):
        slots = ring + held[1 : n - 2] + [newest]
        bases = [0, 0] + [base] * (n - 3) + [at]
        pieces.append((at, part, slots, bases))
        at += part

    outs = ()
    for at, part, slots, bases in pieces:
        outs = pl.pallas_call(
            functools.partial(final_kernel, at, part, bases),
            in_specs=[vmem] * (4 + n) + [pl.BlockSpec(memory_space=pl.ANY)] * len(outs),
            out_specs=[pl.BlockSpec(memory_space=pl.ANY)] * 2,
            out_shape=[sds((rows, width), BF16), sds((1, rows, width), BF16)],
            input_output_aliases={4 + n + j: j for j in range(len(outs))},
            scratch_shapes=[pltpu.VMEM((rows, part), BF16)] * 2 + [dma((3, 2))],
            compiler_params=params(16),
            cost_estimate=cost(0),
            name="rebuild",
        )(acts, left_terms, right_terms, error_v, *slots, *outs)
    rebuilt, error = outs
    return rebuilt, error, whole.T


def solution(mesh):
    return jax.shard_map(
        per_device,
        mesh=mesh,
        in_specs=(P("dp", None, "tensor"), P("dp", "tensor", None), P("dp", "tensor", None), P()),
        out_specs=(P("tensor", None), P("dp", "tensor", None), P()),
        check_vma=False,
    )
```

```python
import functools

import jax
import jax.numpy as jnp
from jax import lax
from jax.experimental import pallas as pl
from jax.experimental.pallas import tpu as pltpu
from jax.sharding import PartitionSpec as P

F32 = jnp.float32
BF16 = jnp.bfloat16
SHRINK = 2.0**-23
TINY = 1e-30
ROOM = 2.0**14
BLOCK = 512


def params(mib):
    return pltpu.CompilerParams(vmem_limit_bytes=mib * 2**20)


def cost(flops):
    return pl.CostEstimate(flops=int(flops) + 1, bytes_accessed=1, transcendentals=0)


def dot(a, b, contract):
    return lax.dot_general(a, b, ((contract[:1], contract[1:]), ((), ())), preferred_element_type=F32)


def split(x):
    hi = x.astype(BF16)
    rest = x - hi.astype(F32)
    mid = rest.astype(BF16)
    lo = (rest - mid.astype(F32)).astype(BF16)
    return hi.astype(F32), mid.astype(F32), lo.astype(F32)


def stack3(x, ref):
    rank = x.shape[0]
    for i, part in enumerate(split(x)):
        ref[i * rank : (i + 1) * rank, :] = part
    return ref[...].astype(BF16)


def sum3(y, rank):
    return (y[2 * rank :] + y[rank : 2 * rank]) + y[:rank]


def ring_of(n):
    return [2 * p if 2 * p < n else 2 * (n - p) - 1 for p in range(n)]


def ring_source(me, step, n):
    place = jnp.where(lax.rem(me, 2) == 0, me // 2, n - (me + 1) // 2)
    place = lax.rem(place - step + n, n)
    return jnp.where(2 * place < n, 2 * place, 2 * (n - place) - 1)


def ring_step(x, axis, n):
    ring = ring_of(n)
    return lax.ppermute(x, axis, [(ring[p], ring[(p + 1) % n]) for p in range(n)])


def exchange(pieces, axis, n):
    return [pieces[0]] + [
        lax.ppermute(pieces[k], axis, [(i, (i + k) % n) for i in range(n)]) for k in range(1, n)
    ]


def swap(x, axis, n, bit):
    return lax.ppermute(x, axis, [(i, i ^ bit) for i in range(n)])


def swap_odd(x, m, n, dp_bit, tensor_bit):
    pairs = [
        (i * n + t, (i ^ dp_bit) * n + (t ^ tensor_bit)) for i in range(1, m, 2) for t in range(n)
    ]
    return lax.ppermute(x, ("dp", "tensor"), pairs)


def bits(n):
    assert n & (n - 1) == 0
    return [1 << i for i in range(n.bit_length() - 1)]


def token_factor_kernel(w_hbm, g_hbm, gw_ref, terms_ref, w, g, w3, sems):
    rank = w.shape[0]
    copies = [
        pltpu.make_async_copy(w_hbm, w, sems.at[0]),
        pltpu.make_async_copy(g_hbm, g, sems.at[1]),
    ]
    for copy in copies:
        copy.start()
    copies[0].wait()
    terms = stack3(w[...] * SHRINK, w3)
    terms_ref[...] = terms
    copies[1].wait()
    gw_ref[...] = jnp.zeros_like(gw_ref)
    gw_ref[0:rank, 0 : g.shape[1]] = sum3(dot(terms, g[0], (1, 1)), rank)


def cut_kernel(x_ref, *refs):
    chunks, sems = refs[:-1], refs[-1]
    copies = []
    at = 0
    for c, chunk in enumerate(chunks):
        part = chunk.shape[2]
        copies.append(pltpu.make_async_copy(x_ref.at[:, :, pl.ds(at, part)], chunk, sems.at[c]))
        copies[-1].start()
        at += part
    for copy in copies:
        copy.wait()


def error_left_kernel(terms_ref, e_hbm, out_ref, e_ref, sems):
    rank = out_ref.shape[0]
    count = sems.shape[0]
    high = e_ref.shape[1] // count
    copies = []
    for c in range(count):
        rows = pl.ds(c * high, high)
        copies.append(pltpu.make_async_copy(e_hbm.at[:, rows, :], e_ref.at[:, rows, :], sems.at[c]))
        copies[-1].start()
    terms = terms_ref[...]
    for c in range(count):
        copies[c].wait()
        rows = slice(c * high, (c + 1) * high)
        out_ref[:, rows] = sum3(dot(terms, e_ref[0, rows, :], (1, 1)), rank)


def left_kernel(a_ref, e_ref, *refs):
    gws, out_ref, g3 = refs[:-2], refs[-2], refs[-1]
    n = len(gws)
    rank = e_ref.shape[0]
    tok = a_ref.shape[1] // n
    me = lax.axis_index("tensor")
    total = e_ref[...]
    for k in range(n):
        src = lax.rem(me - k + n, n)
        rows = a_ref[0, pl.ds(pl.multiple_of(src * tok, tok), tok), :]
        total += sum3(dot(stack3(gws[k][0:rank, 0:tok], g3), rows, (1, 0)), rank)
    out_ref[...] = total


def mean_kernel(scale, a_ref, x_ref, y_ref, p_ref, msg_ref, p3):
    rank = x_ref.shape[0]
    mean = (x_ref[...] + y_ref[...]) * scale
    p_ref[...] = mean
    top = jnp.max(jnp.max(jnp.abs(mean), axis=1, keepdims=True), axis=0, keepdims=True)
    top = jnp.maximum(top, TINY)
    parts = stack3(mean / (top * ROOM), p3)
    msg_ref[...] = jnp.zeros_like(msg_ref)
    msg_ref[0:rank, :] = sum3(dot(parts, a_ref[0], (1, 1)), rank)
    for i in range(rank):
        column = jnp.sum(mean * mean[i : i + 1, :], axis=1, keepdims=True)
        msg_ref[rank : 2 * rank, i : i + 1] = column
    msg_ref[rank : rank + 1, rank : rank + 1] = top


def joined(x, y, rank):
    top_x = x[rank : rank + 1, rank : rank + 1]
    top_y = y[rank : rank + 1, rank : rank + 1]
    top = jnp.maximum(top_x, top_y)
    products = x[0:rank, :] * (top_x / top) + y[0:rank, :] * (top_y / top)
    gram = x[rank : 2 * rank, 0:rank] + y[rank : 2 * rank, 0:rank]
    return products, gram, top


def join_kernel(rank, x_ref, y_ref, out_ref):
    products, gram, top = joined(x_ref[...], y_ref[...], rank)
    out_ref[...] = jnp.zeros_like(out_ref)
    out_ref[0:rank, :] = products
    out_ref[rank : 2 * rank, 0:rank] = gram
    out_ref[rank : rank + 1, rank : rank + 1] = top


def error_right_kernel(p_ref, e_ref, out_ref, p3):
    rank = p_ref.shape[0]
    parts = stack3(p_ref[...], p3)
    for c in range(e_ref.shape[2] // BLOCK):
        cols = slice(c * BLOCK, (c + 1) * BLOCK)
        out_ref[:, cols] = sum3(dot(parts, e_ref[0, :, cols], (1, 0)), rank)


def lower_inverse(gram, rank):
    at = lambda i, j: gram[i : i + 1, j : j + 1]
    low = {}
    for j in range(rank):
        d = at(j, j)
        for k in range(j):
            d = d - low[j, k] * low[j, k]
        low[j, j] = jnp.sqrt(d)
        for i in range(j + 1, rank):
            v = at(i, j)
            for k in range(j):
                v = v - low[i, k] * low[j, k]
            low[i, j] = v / low[j, j]
    inv = {}
    for j in range(rank):
        inv[j, j] = 1.0 / low[j, j]
        for i in range(j + 1, rank):
            v = low[i, j] * inv[j, j]
            for k in range(j + 1, i):
                v = v + low[i, k] * inv[k, j]
            inv[i, j] = -v / low[i, i]
    return inv


def solve_rows(inv, x, rank):
    rows = []
    for i in range(rank):
        row = inv[i, 0] * x[0:1, :]
        for j in range(1, i + 1):
            row = row + inv[i, j] * x[j : j + 1, :]
        rows.append(row)
    return rows


def right_kernel(n, p_ref, r_ref, g_ref, x_ref, y_ref, ortho_ref, out_ref, z, z3):
    rank = p_ref.shape[0]
    tok = g_ref.shape[1]
    products, gram, top = joined(x_ref[...], y_ref[...], rank)
    inv = lower_inverse(gram, rank)
    scaled = {key: value * top for key, value in inv.items()}
    for i, row in enumerate(solve_rows(scaled, products, rank)):
        for t in range(n):
            z[t, i : i + 1, :] = row[:, t * tok : (t + 1) * tok]
    for i, row in enumerate(solve_rows(inv, p_ref[...], rank)):
        ortho_ref[i : i + 1, :] = row
    terms = stack3(z[lax.axis_index("tensor")], z3)
    for c in range(r_ref.shape[1] // BLOCK):
        cols = slice(c * BLOCK, (c + 1) * BLOCK)
        fresh = sum3(dot(terms, g_ref[0, :, cols], (1, 0)), rank) * ROOM
        for i, row in enumerate(solve_rows(inv, r_ref[:, cols], rank)):
            out_ref[i : i + 1, cols] = row + fresh[i : i + 1, :]


def add_kernel(x_ref, y_ref, out_ref):
    out_ref[...] = x_ref[...] + y_ref[...]


LEFT_TERMS = (0, 0, 1, 0, 2, 1)
RIGHT_TERMS = (0, 1, 0, 2, 0, 1)


def factor_kernel(scale, ortho_ref, mine_ref, other_ref, whole_ref, left_ref, right_ref, left, right):
    rank = mine_ref.shape[0]
    core = lax.rem(lax.axis_index("dp"), 2)

    @pl.when(core == 1)
    def _():
        whole_ref[...] = mine_ref[...] * scale

    @pl.when(core == 0)
    def _():
        whole_ref[...] = other_ref[...] * scale

    for terms, x, ref in (
        (LEFT_TERMS, ortho_ref[...], left),
        (RIGHT_TERMS, whole_ref[...], right),
    ):
        parts = split(x)
        for i, term in enumerate(terms):
            ref[i * rank : (i + 1) * rank, :] = parts[term]
    left_ref[...] = left[...].T.astype(BF16)
    right_ref[...] = right[...].astype(BF16)


def acts_kernel(n, a_ref, out_ref, acts):
    tok = a_ref.shape[1] // n
    me = lax.axis_index("tensor")
    for s in range(n):
        src = ring_source(me, s, n)
        here = a_ref[0, pl.ds(pl.multiple_of(src * tok, tok), tok), :]
        acts[s * tok : (s + 1) * tok, :] = here
    out_ref[...] = acts[...].T


def final_kernel(at, part, bases, acts_ref, left_ref, right_ref, e_ref, *refs):
    slots = refs[: len(bases)]
    rebuilt_hbm, error_hbm, rebuilt_v, error_v, sems = refs[-5:]
    rows = e_ref.shape[1]
    wide = 256
    high = rows // sems.shape[0]
    copies = []
    for r in range(sems.shape[0]):
        here = slice(r * high, (r + 1) * high)
        for c in range(part // wide):
            cols = slice(c * wide, (c + 1) * wide)
            there = slice(at + c * wide, at + (c + 1) * wide)
            grads = [
                slot[0, :, there.start - base : there.stop - base]
                for slot, base in zip(slots, bases)
            ]
            grad = dot(acts_ref[here, :], jnp.concatenate(grads, axis=0), (1, 0))
            matrix = grad + e_ref[0, here, there].astype(F32)
            rebuilt = dot(left_ref[here, :], right_ref[:, there], (1, 0))
            rebuilt_v[here, cols] = rebuilt.astype(BF16)
            error_v[here, cols] = (matrix - rebuilt).astype(BF16)
        strip = pl.ds(r * high, high)
        span = pl.ds(at, part)
        copies += [
            pltpu.make_async_copy(
                rebuilt_v.at[strip, :], rebuilt_hbm.at[strip, span], sems.at[r, 0]
            ),
            pltpu.make_async_copy(
                error_v.at[strip, :], error_hbm.at[0, strip, span], sems.at[r, 1]
            ),
        ]
        copies[-2].start()
        copies[-1].start()
    for copy in copies:
        copy.wait()


def per_device(activations, out_grads, error_buffer, warm_factor):
    m = lax.axis_size("dp")
    n = lax.axis_size("tensor")
    _, tokens, rows = activations.shape
    _, tok, width = out_grads.shape
    rank = warm_factor.shape[1]
    w = warm_factor.T
    sds = jax.ShapeDtypeStruct
    hbm = pl.BlockSpec(memory_space=pltpu.HBM)
    vmem = pl.BlockSpec(memory_space=pltpu.VMEM)
    dma = pltpu.SemaphoreType.DMA
    pin = lambda x: pltpu.with_memory_space_constraint(x, pltpu.HBM)

    def call(kernel, shapes, scratch, name, specs=None, flops=0):
        return pl.pallas_call(
            kernel,
            out_shape=shapes,
            **({"in_specs": specs} if specs else {}),
            scratch_shapes=scratch,
            compiler_params=params(16),
            cost_estimate=cost(flops),
            name=name,
        )

    def add(x, y):
        return call(add_kernel, sds(x.shape, F32), [], "add")(x, y)

    def after(x, y):
        return lax.optimization_barrier((x, y))

    def cut(x, widths):
        shapes = [sds((1, tok, part), BF16) for part in widths]
        return call(cut_kernel, shapes, [dma((len(widths),))], "cut")(x)

    def step(x):
        return ring_step(x, "tensor", n)

    wide = width // 4
    narrow = width // 2 - wide
    ring = [out_grads, step(out_grads)]

    gw, w_terms = call(
        token_factor_kernel,
        [sds((8, 128), F32), sds((3 * rank, width), BF16)],
        [
            pltpu.VMEM((rank, width), F32),
            pltpu.VMEM((1, tok, width), BF16),
            pltpu.VMEM((3 * rank, width), F32),
            dma((2,)),
        ],
        "token_factor", [hbm, hbm],
    )(pin(w), pin(out_grads))
    ew, error_v = call(
        error_left_kernel,
        [sds((rank, rows), F32), sds((1, rows, width), BF16)],
        [dma((rows // 128,))],
        "error_left", [vmem, hbm], 4.6e9,
    )(w_terms, pin(error_buffer))

    gw, ew = after(gw, ew)
    gws = exchange([gw] * n, "tensor", n)
    ring[1], gws = after(ring[1], gws)
    x1, y1 = cut(ring[1], [2 * wide, 2 * narrow])
    xs, ys = [x1, step(x1)], [y1]
    left = call(
        left_kernel, sds((rank, rows), F32), [pltpu.VMEM((3 * rank, tok), F32)], "left"
    )(activations, ew, *gws)
    for bit in bits(m)[:-1]:
        left = add(left, swap(left, "dp", m, bit))
    xs[1], last = after(xs[1], swap(left, "dp", m, bits(m)[-1]))

    mean, msg = call(
        functools.partial(mean_kernel, 1.0 / (SHRINK * m)),
        [sds((rank, rows), F32), sds((2 * rank, tokens), F32)],
        [pltpu.VMEM((3 * rank, rows), F32)],
        "mean",
    )(activations, left, last)

    def join(x, y):
        return call(functools.partial(join_kernel, rank), sds(x.shape, F32), [], "join")(x, y)

    for bit in bits(n)[:-1]:
        msg = join(msg, swap(msg, "tensor", n, bit))
    msgs = [msg, swap(msg, "tensor", n, bits(n)[-1])]

    right_raw = call(
        error_right_kernel,
        sds((rank, width), F32),
        [pltpu.VMEM((3 * rank, rows), F32)],
        "error_right", None, 1.2e9,
    )(mean, error_v)

    ortho, total = call(
        functools.partial(right_kernel, n),
        [sds((rank, rows), F32), sds((rank, width), F32)],
        [pltpu.VMEM((n, rank, tok), F32), pltpu.VMEM((3 * rank, tok), F32)],
        "right",
    )(mean, right_raw, out_grads, *msgs)
    total = add(total, swap(total, "dp", m, 1))
    for _ in range(3, n):
        last, total = after(ys[-1], total)
        ys.append(step(last))
    for _ in range(4, n):
        last, total = after(xs[-1], total)
        xs.append(step(last))
    for bit in bits(m)[1:]:
        total = add(total, swap_odd(total, m, n, bit, 0))
    (xs[-1], ys[-1]), total = after((xs[-1], ys[-1]), total)
    for bit in bits(n):
        total = add(total, swap_odd(total, m, n, 0, bit))
    other = lax.ppermute(total, "dp", [(i, i - 1) for i in range(1, m, 2)])
    xa, xb = cut(xs[-1], [wide, wide])
    (xa, xb), (total, other) = after((xa, xb), (total, other))
    xa, xb = step(xa), step(xb)

    terms = len(LEFT_TERMS) * rank
    whole, left_terms, right_terms = call(
        functools.partial(factor_kernel, 1.0 / m),
        [sds((rank, width), F32), sds((rows, terms), BF16), sds((terms, width), BF16)],
        [
            pltpu.VMEM((terms, rows), F32),
            pltpu.VMEM((terms, width), F32),
        ],
        "factor",
    )(ortho, total, other)

    acts = call(
        functools.partial(acts_kernel, n),
        sds((rows, tokens), BF16),
        [pltpu.VMEM((tokens, rows), BF16)],
        "acts",
    )(activations)
    last, right_terms = after(ys[-1], right_terms)
    ya, yb = cut(last, [narrow, narrow])
    pieces = []
    at = 0
    for part, base, held, newest in (
        (wide, 0, xs, xa),
        (wide, 0, xs, xb),
        (narrow, 2 * wide, ys, step(ya)),
        (narrow, 2 * wide, ys, step(yb)),
    ):
        slots = ring + held[1 : n - 2] + [newest]
        bases = [0, 0] + [base] * (n - 3) + [at]
        pieces.append((at, part, slots, bases))
        at += part

    outs = ()
    for at, part, slots, bases in pieces:
        outs = pl.pallas_call(
            functools.partial(final_kernel, at, part, bases),
            in_specs=[vmem] * (4 + n) + [pl.BlockSpec(memory_space=pl.ANY)] * len(outs),
            out_specs=[pl.BlockSpec(memory_space=pl.ANY)] * 2,
            out_shape=[sds((rows, width), BF16), sds((1, rows, width), BF16)],
            input_output_aliases={4 + n + j: j for j in range(len(outs))},
            scratch_shapes=[pltpu.VMEM((rows, part), BF16)] * 2 + [dma((3, 2))],
            compiler_params=params(16),
            cost_estimate=cost(0),
            name="rebuild",
        )(acts, left_terms, right_terms, error_v, *slots, *outs)
    rebuilt, error = outs
    return rebuilt, error, whole.T


def solution(mesh):
    return jax.shard_map(
        per_device,
        mesh=mesh,
        in_specs=(P("dp", None, "tensor"), P("dp", "tensor", None), P("dp", "tensor", None), P()),
        out_specs=(P("tensor", None), P("dp", "tensor", None), P()),
        check_vma=False,
    )
```

```python
import functools

import jax
import jax.numpy as jnp
from jax import lax
from jax.experimental import pallas as pl
from jax.experimental.pallas import tpu as pltpu
from jax.sharding import PartitionSpec as P

F32 = jnp.float32
BF16 = jnp.bfloat16
SHRINK = 2.0**-23
TINY = 1e-30
ROOM = 2.0**14
BLOCK = 512


def params(mib):
    return pltpu.CompilerParams(vmem_limit_bytes=mib * 2**20)


def cost(flops):
    return pl.CostEstimate(flops=int(flops) + 1, bytes_accessed=1, transcendentals=0)


def dot(a, b, contract):
    return lax.dot_general(a, b, ((contract[:1], contract[1:]), ((), ())), preferred_element_type=F32)


def split(x):
    hi = x.astype(BF16)
    rest = x - hi.astype(F32)
    mid = rest.astype(BF16)
    lo = (rest - mid.astype(F32)).astype(BF16)
    return hi.astype(F32), mid.astype(F32), lo.astype(F32)


def stack3(x, ref):
    rank = x.shape[0]
    for i, part in enumerate(split(x)):
        ref[i * rank : (i + 1) * rank, :] = part
    return ref[...].astype(BF16)


def sum3(y, rank):
    return (y[2 * rank :] + y[rank : 2 * rank]) + y[:rank]


def ring_of(n):
    return [2 * p if 2 * p < n else 2 * (n - p) - 1 for p in range(n)]


def ring_source(me, step, n):
    place = jnp.where(lax.rem(me, 2) == 0, me // 2, n - (me + 1) // 2)
    place = lax.rem(place - step + n, n)
    return jnp.where(2 * place < n, 2 * place, 2 * (n - place) - 1)


def ring_step(x, axis, n):
    ring = ring_of(n)
    return lax.ppermute(x, axis, [(ring[p], ring[(p + 1) % n]) for p in range(n)])


def exchange(pieces, axis, n):
    return [pieces[0]] + [
        lax.ppermute(pieces[k], axis, [(i, (i + k) % n) for i in range(n)]) for k in range(1, n)
    ]


def swap(x, axis, n, bit):
    return lax.ppermute(x, axis, [(i, i ^ bit) for i in range(n)])


def bits(n):
    assert n & (n - 1) == 0
    return [1 << i for i in range(n.bit_length() - 1)]


def first_kernel(g_hbm, out_ref, sem):
    copy = pltpu.make_async_copy(g_hbm.at[:, :, pl.ds(0, out_ref.shape[2])], out_ref, sem)
    copy.start()
    copy.wait()


def token_factor_kernel(w_hbm, g_hbm, a_ref, gw_ref, terms_ref, b_ref, w, w3, sems):
    rank = w.shape[0]
    part = a_ref.shape[2]
    rest = b_ref.shape[2]
    copies = [
        pltpu.make_async_copy(w_hbm, w, sems.at[0]),
        pltpu.make_async_copy(g_hbm.at[:, :, pl.ds(part, rest)], b_ref, sems.at[1]),
    ]
    for copy in copies:
        copy.start()
    copies[0].wait()
    terms = stack3(w[...] * SHRINK, w3)
    terms_ref[...] = terms
    total = dot(terms[:, :part], a_ref[0], (1, 1))
    copies[1].wait()
    total += dot(terms[:, part:], b_ref[0], (1, 1))
    gw_ref[...] = jnp.zeros_like(gw_ref)
    gw_ref[0:rank, 0 : total.shape[1]] = sum3(total, rank)


def cut_kernel(x_ref, *refs):
    chunks, sems = refs[:-1], refs[-1]
    copies = []
    at = 0
    for c, chunk in enumerate(chunks):
        part = chunk.shape[2]
        copies.append(pltpu.make_async_copy(x_ref.at[:, :, pl.ds(at, part)], chunk, sems.at[c]))
        copies[-1].start()
        at += part
    for copy in copies:
        copy.wait()


def error_left_kernel(terms_ref, e_hbm, out_ref, e_ref, sems):
    rank = out_ref.shape[0]
    count = sems.shape[0]
    high = e_ref.shape[1] // count
    copies = []
    for c in range(count):
        rows = pl.ds(c * high, high)
        copies.append(pltpu.make_async_copy(e_hbm.at[:, rows, :], e_ref.at[:, rows, :], sems.at[c]))
        copies[-1].start()
    terms = terms_ref[...]
    for c in range(count):
        copies[c].wait()
        rows = slice(c * high, (c + 1) * high)
        out_ref[:, rows] = sum3(dot(terms, e_ref[0, rows, :], (1, 1)), rank)


def left_kernel(a_ref, e_ref, *refs):
    gws, out_ref, g3 = refs[:-2], refs[-2], refs[-1]
    n = len(gws)
    rank = e_ref.shape[0]
    tok = a_ref.shape[1] // n
    me = lax.axis_index("tensor")
    total = e_ref[...]
    for k in range(n):
        src = lax.rem(me - k + n, n)
        rows = a_ref[0, pl.ds(pl.multiple_of(src * tok, tok), tok), :]
        total += sum3(dot(stack3(gws[k][0:rank, 0:tok], g3), rows, (1, 0)), rank)
    out_ref[...] = total


def mean_kernel(scale, a_ref, x_ref, y_ref, p_ref, msg_ref, p3):
    rank = x_ref.shape[0]
    mean = (x_ref[...] + y_ref[...]) * scale
    p_ref[...] = mean
    top = jnp.max(jnp.max(jnp.abs(mean), axis=1, keepdims=True), axis=0, keepdims=True)
    top = jnp.maximum(top, TINY)
    parts = stack3(mean / (top * ROOM), p3)
    msg_ref[...] = jnp.zeros_like(msg_ref)
    msg_ref[0:rank, :] = sum3(dot(parts, a_ref[0], (1, 1)), rank)
    for i in range(rank):
        column = jnp.sum(mean * mean[i : i + 1, :], axis=1, keepdims=True)
        msg_ref[rank : 2 * rank, i : i + 1] = column
    msg_ref[rank : rank + 1, rank : rank + 1] = top


def joined(x, y, rank):
    top_x = x[rank : rank + 1, rank : rank + 1]
    top_y = y[rank : rank + 1, rank : rank + 1]
    top = jnp.maximum(top_x, top_y)
    products = x[0:rank, :] * (top_x / top) + y[0:rank, :] * (top_y / top)
    gram = x[rank : 2 * rank, 0:rank] + y[rank : 2 * rank, 0:rank]
    return products, gram, top


def join_kernel(rank, x_ref, y_ref, out_ref):
    products, gram, top = joined(x_ref[...], y_ref[...], rank)
    out_ref[...] = jnp.zeros_like(out_ref)
    out_ref[0:rank, :] = products
    out_ref[rank : 2 * rank, 0:rank] = gram
    out_ref[rank : rank + 1, rank : rank + 1] = top


def error_right_kernel(p_ref, e_ref, out_ref, p3):
    rank = p_ref.shape[0]
    parts = stack3(p_ref[...], p3)
    for c in range(e_ref.shape[2] // BLOCK):
        cols = slice(c * BLOCK, (c + 1) * BLOCK)
        out_ref[:, cols] = sum3(dot(parts, e_ref[0, :, cols], (1, 0)), rank)


def lower_inverse(gram, rank):
    at = lambda i, j: gram[i : i + 1, j : j + 1]
    low = {}
    for j in range(rank):
        d = at(j, j)
        for k in range(j):
            d = d - low[j, k] * low[j, k]
        low[j, j] = jnp.sqrt(d)
        for i in range(j + 1, rank):
            v = at(i, j)
            for k in range(j):
                v = v - low[i, k] * low[j, k]
            low[i, j] = v / low[j, j]
    inv = {}
    for j in range(rank):
        inv[j, j] = 1.0 / low[j, j]
        for i in range(j + 1, rank):
            v = low[i, j] * inv[j, j]
            for k in range(j + 1, i):
                v = v + low[i, k] * inv[k, j]
            inv[i, j] = -v / low[i, i]
    return inv


def solve_rows(inv, x, rank):
    rows = []
    for i in range(rank):
        row = inv[i, 0] * x[0:1, :]
        for j in range(1, i + 1):
            row = row + inv[i, j] * x[j : j + 1, :]
        rows.append(row)
    return rows


def right_kernel(n, p_ref, r_ref, g_ref, x_ref, y_ref, ortho_ref, keep_ref, send_ref, z, z3, outbox):
    rank = p_ref.shape[0]
    tok = g_ref.shape[1]
    products, gram, top = joined(x_ref[...], y_ref[...], rank)
    inv = lower_inverse(gram, rank)
    scaled = {key: value * top for key, value in inv.items()}
    for i, row in enumerate(solve_rows(scaled, products, rank)):
        for t in range(n):
            z[t, i : i + 1, :] = row[:, t * tok : (t + 1) * tok]
    for i, row in enumerate(solve_rows(inv, p_ref[...], rank)):
        ortho_ref[i : i + 1, :] = row
    terms = stack3(z[lax.axis_index("tensor")], z3)
    half = keep_ref.shape[1]
    core = lax.rem(lax.axis_index("dp"), 2)
    for h in range(2):
        cols = slice(h * half, (h + 1) * half)
        fresh = sum3(dot(terms, g_ref[0, :, cols], (1, 0)), rank) * ROOM
        for i, row in enumerate(solve_rows(inv, r_ref[:, cols], rank)):
            outbox[h, i : i + 1, :] = row + fresh[i : i + 1, :]
    keep_ref[...] = outbox[core]
    send_ref[...] = outbox[1 - core]


def add_kernel(x_ref, y_ref, out_ref):
    out_ref[...] = x_ref[...] + y_ref[...]


LEFT_TERMS = (0, 0, 1, 0, 2, 1)
RIGHT_TERMS = (0, 1, 0, 2, 0, 1)


def factor_kernel(scale, ortho_ref, mine_ref, other_ref, whole_ref, left_ref, right_ref, inbox, left, right):
    rank, half = mine_ref.shape
    core = lax.rem(lax.axis_index("dp"), 2)
    inbox[core] = mine_ref[...]
    inbox[1 - core] = other_ref[...]
    for h in range(2):
        whole_ref[:, h * half : (h + 1) * half] = inbox[h] * scale
    for terms, x, ref in (
        (LEFT_TERMS, ortho_ref[...], left),
        (RIGHT_TERMS, whole_ref[...], right),
    ):
        parts = split(x)
        for i, term in enumerate(terms):
            ref[i * rank : (i + 1) * rank, :] = parts[term]
    left_ref[...] = left[...].T.astype(BF16)
    right_ref[...] = right[...].astype(BF16)


def acts_kernel(n, a_ref, out_ref, acts):
    tok = a_ref.shape[1] // n
    me = lax.axis_index("tensor")
    for s in range(n):
        src = ring_source(me, s, n)
        here = a_ref[0, pl.ds(pl.multiple_of(src * tok, tok), tok), :]
        acts[s * tok : (s + 1) * tok, :] = here
    out_ref[...] = acts[...].T


def final_kernel(at, part, bases, acts_ref, left_ref, right_ref, e_ref, *refs):
    slots = refs[: len(bases)]
    rebuilt_hbm, error_hbm, rebuilt_v, error_v, sems = refs[-5:]
    rows = e_ref.shape[1]
    wide = 256
    high = rows // sems.shape[0]
    copies = []
    for r in range(sems.shape[0]):
        here = slice(r * high, (r + 1) * high)
        for c in range(part // wide):
            cols = slice(c * wide, (c + 1) * wide)
            there = slice(at + c * wide, at + (c + 1) * wide)
            grads = [
                slot[0, :, there.start - base : there.stop - base]
                for slot, base in zip(slots, bases)
            ]
            grad = dot(acts_ref[here, :], jnp.concatenate(grads, axis=0), (1, 0))
            matrix = grad + e_ref[0, here, there].astype(F32)
            rebuilt = dot(left_ref[here, :], right_ref[:, there], (1, 0))
            rebuilt_v[here, cols] = rebuilt.astype(BF16)
            error_v[here, cols] = (matrix - rebuilt).astype(BF16)
        strip = pl.ds(r * high, high)
        span = pl.ds(at, part)
        copies += [
            pltpu.make_async_copy(
                rebuilt_v.at[strip, :], rebuilt_hbm.at[strip, span], sems.at[r, 0]
            ),
            pltpu.make_async_copy(
                error_v.at[strip, :], error_hbm.at[0, strip, span], sems.at[r, 1]
            ),
        ]
        copies[-2].start()
        copies[-1].start()
    for copy in copies:
        copy.wait()


def per_device(activations, out_grads, error_buffer, warm_factor):
    m = lax.axis_size("dp")
    n = lax.axis_size("tensor")
    _, tokens, rows = activations.shape
    _, tok, width = out_grads.shape
    rank = warm_factor.shape[1]
    w = warm_factor.T
    sds = jax.ShapeDtypeStruct
    hbm = pl.BlockSpec(memory_space=pltpu.HBM)
    vmem = pl.BlockSpec(memory_space=pltpu.VMEM)
    dma = pltpu.SemaphoreType.DMA
    pin = lambda x: pltpu.with_memory_space_constraint(x, pltpu.HBM)

    def call(kernel, shapes, scratch, name, specs=None, flops=0):
        return pl.pallas_call(
            kernel,
            out_shape=shapes,
            **({"in_specs": specs} if specs else {}),
            scratch_shapes=scratch,
            compiler_params=params(16),
            cost_estimate=cost(flops),
            name=name,
        )

    def add(x, y):
        return call(add_kernel, sds(x.shape, F32), [], "add")(x, y)

    def after(x, y):
        return lax.optimization_barrier((x, y))

    def cut(x, widths):
        shapes = [sds((1, tok, part), BF16) for part in widths]
        return call(cut_kernel, shapes, [dma((len(widths),))], "cut")(x)

    def step(x):
        return ring_step(x, "tensor", n)

    unit = width // 10
    wide, parts = 3 * unit, [4 * unit, 3 * unit]
    half = width // 2
    first = call(first_kernel, sds((1, tok, wide), BF16), [dma(())], "first", [hbm])(pin(out_grads))
    ring_a = [first, step(first)]

    gw, w_terms, other = call(
        token_factor_kernel,
        [sds((8, 128), F32), sds((3 * rank, width), BF16), sds((1, tok, width - wide), BF16)],
        [pltpu.VMEM((rank, width), F32), pltpu.VMEM((3 * rank, width), F32), dma((2,))],
        "token_factor", [hbm, hbm, vmem],
    )(pin(w), pin(out_grads), first)
    gws = exchange([gw] * n, "tensor", n)
    (ring_a[1], other, w_terms), gws[1] = after((ring_a[1], other, w_terms), gws[1])
    ring_b = [other, step(other)]
    ew, error_v = call(
        error_left_kernel,
        [sds((rank, rows), F32), sds((1, rows, width), BF16)],
        [dma((rows // 128,))],
        "error_left", [vmem, hbm], 4.6e9,
    )(w_terms, pin(error_buffer))

    left = call(
        left_kernel, sds((rank, rows), F32), [pltpu.VMEM((3 * rank, tok), F32)], "left"
    )(activations, ew, *gws)
    for bit in bits(m)[:-1]:
        left = add(left, swap(left, "dp", m, bit))
        if bit == 1:
            held, left = after(ring_a[1], left)
            ring_a.append(step(held))
    (ring_a[2], ring_b[1]), last = after(
        (ring_a[2], ring_b[1]), swap(left, "dp", m, bits(m)[-1])
    )
    mean, msg = call(
        functools.partial(mean_kernel, 1.0 / (SHRINK * m)),
        [sds((rank, rows), F32), sds((2 * rank, tokens), F32)],
        [pltpu.VMEM((3 * rank, rows), F32)],
        "mean",
    )(activations, left, last)

    def join(x, y):
        return call(functools.partial(join_kernel, rank), sds(x.shape, F32), [], "join")(x, y)

    for bit in bits(n)[:-1]:
        msg = join(msg, swap(msg, "tensor", n, bit))
    msgs = [msg, swap(msg, "tensor", n, bits(n)[-1])]

    right_raw = call(
        error_right_kernel,
        sds((rank, width), F32),
        [pltpu.VMEM((3 * rank, rows), F32)],
        "error_right", None, 1.2e9,
    )(mean, error_v)

    ortho, keep, send = call(
        functools.partial(right_kernel, n),
        [sds((rank, rows), F32), sds((rank, half), F32), sds((rank, half), F32)],
        [
            pltpu.VMEM((n, rank, tok), F32),
            pltpu.VMEM((3 * rank, tok), F32),
            pltpu.VMEM((2, rank, half), F32),
        ],
        "right",
    )(mean, right_raw, out_grads, *msgs)
    total = add(keep, swap(send, "dp", m, 1))
    held, total = after(ring_b[1], total)
    ring_b.append(step(held))
    for bit in bits(m)[1:]:
        total = add(total, swap(total, "dp", m, bit))
    for _ in range(4, n):
        (held_a, held_b), total = after((ring_a[-1], ring_b[-1]), total)
        ring_a.append(step(held_a))
        ring_b.append(step(held_b))
    ring_b[-1], total = after(ring_b[-1], total)
    for bit in bits(n):
        total = add(total, swap(total, "tensor", n, bit))
    (held_a, held), total = after((ring_a[-1], ring_b[-1]), total)
    ring_a.append(step(held_a))
    newest = [step(x) for x in cut(held, parts)]

    terms = len(LEFT_TERMS) * rank
    whole, left_terms, right_terms = call(
        functools.partial(factor_kernel, 1.0 / m),
        [sds((rank, width), F32), sds((rows, terms), BF16), sds((terms, width), BF16)],
        [
            pltpu.VMEM((2, rank, half), F32),
            pltpu.VMEM((terms, rows), F32),
            pltpu.VMEM((terms, width), F32),
        ],
        "factor",
    )(ortho, total, swap(total, "dp", m, 1))

    acts = call(
        functools.partial(acts_kernel, n),
        sds((rows, tokens), BF16),
        [pltpu.VMEM((tokens, rows), BF16)],
        "acts",
    )(activations)
    pieces = [(0, wide, [out_grads, *ring_a[1:]], [0] * n)]
    at = wide
    for part, x in zip(parts, newest):
        pieces.append((at, part, [out_grads, *ring_b[1:], x], [0] + [wide] * (n - 2) + [at]))
        at += part

    outs = ()
    for at, part, slots, bases in pieces:
        outs = pl.pallas_call(
            functools.partial(final_kernel, at, part, bases),
            in_specs=[vmem] * (4 + n) + [pl.BlockSpec(memory_space=pl.ANY)] * len(outs),
            out_specs=[pl.BlockSpec(memory_space=pl.ANY)] * 2,
            out_shape=[sds((rows, width), BF16), sds((1, rows, width), BF16)],
            input_output_aliases={4 + n + j: j for j in range(len(outs))},
            scratch_shapes=[pltpu.VMEM((rows, part), BF16)] * 2 + [dma((3, 2))],
            compiler_params=params(16),
            cost_estimate=cost(0),
            name="rebuild",
        )(acts, left_terms, right_terms, error_v, *slots, *outs)
    rebuilt, error = outs
    return rebuilt, error, whole.T


def solution(mesh):
    return jax.shard_map(
        per_device,
        mesh=mesh,
        in_specs=(P("dp", None, "tensor"), P("dp", "tensor", None), P("dp", "tensor", None), P()),
        out_specs=(P("tensor", None), P("dp", "tensor", None), P()),
        check_vma=False,
    )
```

```python
import functools

import jax
import jax.numpy as jnp
from jax import lax
from jax.experimental import pallas as pl
from jax.experimental.pallas import tpu as pltpu
from jax.sharding import PartitionSpec as P

F32 = jnp.float32
BF16 = jnp.bfloat16
SHRINK = 2.0**-23
TINY = 1e-30
ROOM = 2.0**14
BLOCK = 512


def params(mib):
    return pltpu.CompilerParams(vmem_limit_bytes=mib * 2**20)


def cost(flops):
    return pl.CostEstimate(flops=int(flops) + 1, bytes_accessed=1, transcendentals=0)


def dot(a, b, contract):
    return lax.dot_general(a, b, ((contract[:1], contract[1:]), ((), ())), preferred_element_type=F32)


def split(x):
    hi = x.astype(BF16)
    rest = x - hi.astype(F32)
    mid = rest.astype(BF16)
    lo = (rest - mid.astype(F32)).astype(BF16)
    return hi.astype(F32), mid.astype(F32), lo.astype(F32)


def stack3(x, ref):
    rank = x.shape[0]
    for i, part in enumerate(split(x)):
        ref[i * rank : (i + 1) * rank, :] = part
    return ref[...].astype(BF16)


def sum3(y, rank):
    return (y[2 * rank :] + y[rank : 2 * rank]) + y[:rank]


def ring_of(n):
    return [2 * p if 2 * p < n else 2 * (n - p) - 1 for p in range(n)]


def ring_source(me, step, n):
    place = jnp.where(lax.rem(me, 2) == 0, me // 2, n - (me + 1) // 2)
    place = lax.rem(place - step + n, n)
    return jnp.where(2 * place < n, 2 * place, 2 * (n - place) - 1)


def ring_step(x, axis, n):
    ring = ring_of(n)
    return lax.ppermute(x, axis, [(ring[p], ring[(p + 1) % n]) for p in range(n)])


def exchange(pieces, axis, n):
    return [pieces[0]] + [
        lax.ppermute(pieces[k], axis, [(i, (i + k) % n) for i in range(n)]) for k in range(1, n)
    ]


def swap(x, axis, n, bit):
    return lax.ppermute(x, axis, [(i, i ^ bit) for i in range(n)])


def swap_odd(x, m, n, dp_bit, tensor_bit):
    pairs = []
    for i in range(m):
        for t in range(n):
            to = (i ^ dp_bit, t ^ tensor_bit) if i % 2 else (i, t)
            pairs.append((i * n + t, to[0] * n + to[1]))
    return lax.ppermute(x, ("dp", "tensor"), pairs)


def bits(n):
    assert n & (n - 1) == 0
    return [1 << i for i in range(n.bit_length() - 1)]


def first_kernel(g_hbm, out_ref, sem):
    copy = pltpu.make_async_copy(g_hbm.at[:, :, pl.ds(0, out_ref.shape[2])], out_ref, sem)
    copy.start()
    copy.wait()


def token_factor_kernel(w_hbm, g_hbm, a_ref, gw_ref, terms_ref, b_ref, w, w3, sems):
    rank = w.shape[0]
    part = a_ref.shape[2]
    rest = b_ref.shape[2]
    copies = [
        pltpu.make_async_copy(w_hbm, w, sems.at[0]),
        pltpu.make_async_copy(g_hbm.at[:, :, pl.ds(part, rest)], b_ref, sems.at[1]),
    ]
    for copy in copies:
        copy.start()
    copies[0].wait()
    terms = stack3(w[...] * SHRINK, w3)
    terms_ref[...] = terms
    total = dot(terms[:, :part], a_ref[0], (1, 1))
    copies[1].wait()
    total += dot(terms[:, part:], b_ref[0], (1, 1))
    gw_ref[...] = jnp.zeros_like(gw_ref)
    gw_ref[0:rank, 0 : total.shape[1]] = sum3(total, rank)


def cut_kernel(x_ref, *refs):
    chunks, sems = refs[:-1], refs[-1]
    copies = []
    at = 0
    for c, chunk in enumerate(chunks):
        part = chunk.shape[2]
        copies.append(pltpu.make_async_copy(x_ref.at[:, :, pl.ds(at, part)], chunk, sems.at[c]))
        copies[-1].start()
        at += part
    for copy in copies:
        copy.wait()


def error_left_kernel(terms_ref, e_hbm, out_ref, e_ref, sems):
    rank = out_ref.shape[0]
    count = sems.shape[0]
    high = e_ref.shape[1] // count
    copies = []
    for c in range(count):
        rows = pl.ds(c * high, high)
        copies.append(pltpu.make_async_copy(e_hbm.at[:, rows, :], e_ref.at[:, rows, :], sems.at[c]))
        copies[-1].start()
    terms = terms_ref[...]
    for c in range(count):
        copies[c].wait()
        rows = slice(c * high, (c + 1) * high)
        out_ref[:, rows] = sum3(dot(terms, e_ref[0, rows, :], (1, 1)), rank)


def left_kernel(a_ref, e_ref, *refs):
    gws, out_ref, g3 = refs[:-2], refs[-2], refs[-1]
    n = len(gws)
    rank = e_ref.shape[0]
    tok = a_ref.shape[1] // n
    me = lax.axis_index("tensor")
    total = e_ref[...]
    for k in range(n):
        src = lax.rem(me - k + n, n)
        rows = a_ref[0, pl.ds(pl.multiple_of(src * tok, tok), tok), :]
        total += sum3(dot(stack3(gws[k][0:rank, 0:tok], g3), rows, (1, 0)), rank)
    out_ref[...] = total


def mean_kernel(scale, a_ref, x_ref, y_ref, p_ref, msg_ref, p3):
    rank = x_ref.shape[0]
    mean = (x_ref[...] + y_ref[...]) * scale
    p_ref[...] = mean
    top = jnp.max(jnp.max(jnp.abs(mean), axis=1, keepdims=True), axis=0, keepdims=True)
    top = jnp.maximum(top, TINY)
    parts = stack3(mean / (top * ROOM), p3)
    msg_ref[...] = jnp.zeros_like(msg_ref)
    msg_ref[0:rank, :] = sum3(dot(parts, a_ref[0], (1, 1)), rank)
    for i in range(rank):
        column = jnp.sum(mean * mean[i : i + 1, :], axis=1, keepdims=True)
        msg_ref[rank : 2 * rank, i : i + 1] = column
    msg_ref[rank : rank + 1, rank : rank + 1] = top


def joined(x, y, rank):
    top_x = x[rank : rank + 1, rank : rank + 1]
    top_y = y[rank : rank + 1, rank : rank + 1]
    top = jnp.maximum(top_x, top_y)
    products = x[0:rank, :] * (top_x / top) + y[0:rank, :] * (top_y / top)
    gram = x[rank : 2 * rank, 0:rank] + y[rank : 2 * rank, 0:rank]
    return products, gram, top


def join_kernel(rank, x_ref, y_ref, out_ref):
    products, gram, top = joined(x_ref[...], y_ref[...], rank)
    out_ref[...] = jnp.zeros_like(out_ref)
    out_ref[0:rank, :] = products
    out_ref[rank : 2 * rank, 0:rank] = gram
    out_ref[rank : rank + 1, rank : rank + 1] = top


def error_right_kernel(p_ref, e_ref, out_ref, p3):
    rank = p_ref.shape[0]
    parts = stack3(p_ref[...], p3)
    for c in range(e_ref.shape[2] // BLOCK):
        cols = slice(c * BLOCK, (c + 1) * BLOCK)
        out_ref[:, cols] = sum3(dot(parts, e_ref[0, :, cols], (1, 0)), rank)


def lower_inverse(gram, rank):
    at = lambda i, j: gram[i : i + 1, j : j + 1]
    low = {}
    for j in range(rank):
        d = at(j, j)
        for k in range(j):
            d = d - low[j, k] * low[j, k]
        low[j, j] = jnp.sqrt(d)
        for i in range(j + 1, rank):
            v = at(i, j)
            for k in range(j):
                v = v - low[i, k] * low[j, k]
            low[i, j] = v / low[j, j]
    inv = {}
    for j in range(rank):
        inv[j, j] = 1.0 / low[j, j]
        for i in range(j + 1, rank):
            v = low[i, j] * inv[j, j]
            for k in range(j + 1, i):
                v = v + low[i, k] * inv[k, j]
            inv[i, j] = -v / low[i, i]
    return inv


def solve_rows(inv, x, rank):
    rows = []
    for i in range(rank):
        row = inv[i, 0] * x[0:1, :]
        for j in range(1, i + 1):
            row = row + inv[i, j] * x[j : j + 1, :]
        rows.append(row)
    return rows


def right_kernel(n, p_ref, r_ref, g_ref, x_ref, y_ref, ortho_ref, out_ref, z, z3):
    rank = p_ref.shape[0]
    tok = g_ref.shape[1]
    products, gram, top = joined(x_ref[...], y_ref[...], rank)
    inv = lower_inverse(gram, rank)
    scaled = {key: value * top for key, value in inv.items()}
    for i, row in enumerate(solve_rows(scaled, products, rank)):
        for t in range(n):
            z[t, i : i + 1, :] = row[:, t * tok : (t + 1) * tok]
    for i, row in enumerate(solve_rows(inv, p_ref[...], rank)):
        ortho_ref[i : i + 1, :] = row
    terms = stack3(z[lax.axis_index("tensor")], z3)
    for c in range(r_ref.shape[1] // BLOCK):
        cols = slice(c * BLOCK, (c + 1) * BLOCK)
        fresh = sum3(dot(terms, g_ref[0, :, cols], (1, 0)), rank) * ROOM
        for i, row in enumerate(solve_rows(inv, r_ref[:, cols], rank)):
            out_ref[i : i + 1, cols] = row + fresh[i : i + 1, :]


def add_kernel(x_ref, y_ref, out_ref):
    out_ref[...] = x_ref[...] + y_ref[...]


LEFT_TERMS = (0, 0, 1, 0, 2, 1)
RIGHT_TERMS = (0, 1, 0, 2, 0, 1)


def factor_kernel(scale, ortho_ref, mine_ref, other_ref, whole_ref, left_ref, right_ref, left, right):
    rank = mine_ref.shape[0]
    core = lax.rem(lax.axis_index("dp"), 2)

    @pl.when(core == 1)
    def _():
        whole_ref[...] = mine_ref[...] * scale

    @pl.when(core == 0)
    def _():
        whole_ref[...] = other_ref[...] * scale

    for terms, x, ref in (
        (LEFT_TERMS, ortho_ref[...], left),
        (RIGHT_TERMS, whole_ref[...], right),
    ):
        parts = split(x)
        for i, term in enumerate(terms):
            ref[i * rank : (i + 1) * rank, :] = parts[term]
    left_ref[...] = left[...].T.astype(BF16)
    right_ref[...] = right[...].astype(BF16)


def acts_kernel(n, a_ref, out_ref, acts):
    tok = a_ref.shape[1] // n
    me = lax.axis_index("tensor")
    for s in range(n):
        src = ring_source(me, s, n)
        here = a_ref[0, pl.ds(pl.multiple_of(src * tok, tok), tok), :]
        acts[s * tok : (s + 1) * tok, :] = here
    out_ref[...] = acts[...].T


def final_kernel(at, part, bases, acts_ref, left_ref, right_ref, e_ref, *refs):
    slots = refs[: len(bases)]
    rebuilt_hbm, error_hbm, rebuilt_v, error_v, sems = refs[-5:]
    rows = e_ref.shape[1]
    wide = 256
    high = rows // sems.shape[0]
    copies = []
    for r in range(sems.shape[0]):
        here = slice(r * high, (r + 1) * high)
        for c in range(part // wide):
            cols = slice(c * wide, (c + 1) * wide)
            there = slice(at + c * wide, at + (c + 1) * wide)
            grads = [
                slot[0, :, there.start - base : there.stop - base]
                for slot, base in zip(slots, bases)
            ]
            grad = dot(acts_ref[here, :], jnp.concatenate(grads, axis=0), (1, 0))
            matrix = grad + e_ref[0, here, there].astype(F32)
            rebuilt = dot(left_ref[here, :], right_ref[:, there], (1, 0))
            rebuilt_v[here, cols] = rebuilt.astype(BF16)
            error_v[here, cols] = (matrix - rebuilt).astype(BF16)
        strip = pl.ds(r * high, high)
        span = pl.ds(at, part)
        copies += [
            pltpu.make_async_copy(
                rebuilt_v.at[strip, :], rebuilt_hbm.at[strip, span], sems.at[r, 0]
            ),
            pltpu.make_async_copy(
                error_v.at[strip, :], error_hbm.at[0, strip, span], sems.at[r, 1]
            ),
        ]
        copies[-2].start()
        copies[-1].start()
    for copy in copies:
        copy.wait()


def per_device(activations, out_grads, error_buffer, warm_factor):
    m = lax.axis_size("dp")
    n = lax.axis_size("tensor")
    _, tokens, rows = activations.shape
    _, tok, width = out_grads.shape
    rank = warm_factor.shape[1]
    w = warm_factor.T
    sds = jax.ShapeDtypeStruct
    hbm = pl.BlockSpec(memory_space=pltpu.HBM)
    vmem = pl.BlockSpec(memory_space=pltpu.VMEM)
    dma = pltpu.SemaphoreType.DMA
    pin = lambda x: pltpu.with_memory_space_constraint(x, pltpu.HBM)

    def call(kernel, shapes, scratch, name, specs=None, flops=0):
        return pl.pallas_call(
            kernel,
            out_shape=shapes,
            **({"in_specs": specs} if specs else {}),
            scratch_shapes=scratch,
            compiler_params=params(16),
            cost_estimate=cost(flops),
            name=name,
        )

    def add(x, y):
        return call(add_kernel, sds(x.shape, F32), [], "add")(x, y)

    def after(x, y):
        return lax.optimization_barrier((x, y))

    def cut(x, widths):
        shapes = [sds((1, tok, part), BF16) for part in widths]
        return call(cut_kernel, shapes, [dma((len(widths),))], "cut")(x)

    def step(x):
        return ring_step(x, "tensor", n)

    wide, parts = width // 2, [width // 4] * 2
    first = call(first_kernel, sds((1, tok, wide), BF16), [dma(())], "first", [hbm])(pin(out_grads))
    ring_a = [first, step(first)]

    gw, w_terms, other = call(
        token_factor_kernel,
        [sds((8, 128), F32), sds((3 * rank, width), BF16), sds((1, tok, width - wide), BF16)],
        [pltpu.VMEM((rank, width), F32), pltpu.VMEM((3 * rank, width), F32), dma((2,))],
        "token_factor", [hbm, hbm, vmem],
    )(pin(w), pin(out_grads), first)
    gws = exchange([gw] * n, "tensor", n)
    (ring_a[1], other, w_terms), gws = after((ring_a[1], other, w_terms), gws)
    ring_b = [other, step(other)]
    ew, error_v = call(
        error_left_kernel,
        [sds((rank, rows), F32), sds((1, rows, width), BF16)],
        [dma((rows // 128,))],
        "error_left", [vmem, hbm],
    )(w_terms, pin(error_buffer))

    left = call(
        left_kernel, sds((rank, rows), F32), [pltpu.VMEM((3 * rank, tok), F32)], "left"
    )(activations, ew, *gws)
    for bit in bits(m)[:-1]:
        left = add(left, swap(left, "dp", m, bit))
        if bit == 1:
            (held, ring_b[1]), left = after((ring_a[1], ring_b[1]), left)
            ring_a.append(step(held))
    ring_a[2], last = after(ring_a[2], swap(left, "dp", m, bits(m)[-1]))
    mean, msg = call(
        functools.partial(mean_kernel, 1.0 / (SHRINK * m)),
        [sds((rank, rows), F32), sds((2 * rank, tokens), F32)],
        [pltpu.VMEM((3 * rank, rows), F32)],
        "mean",
    )(activations, left, last)

    def join(x, y):
        return call(functools.partial(join_kernel, rank), sds(x.shape, F32), [], "join")(x, y)

    for bit in bits(n)[:-1]:
        msg = join(msg, swap(msg, "tensor", n, bit))
    msgs = [msg, swap(msg, "tensor", n, bits(n)[-1])]

    right_raw = call(
        error_right_kernel,
        sds((rank, width), F32),
        [pltpu.VMEM((3 * rank, rows), F32)],
        "error_right", None, 1.2e9,
    )(mean, error_v)

    ortho, total = call(
        functools.partial(right_kernel, n),
        [sds((rank, rows), F32), sds((rank, width), F32)],
        [pltpu.VMEM((n, rank, tok), F32), pltpu.VMEM((3 * rank, tok), F32)],
        "right",
    )(mean, right_raw, out_grads, *msgs)
    total = add(total, swap(total, "dp", m, 1))
    held, total = after(ring_b[1], total)
    ring_b.append(step(held))
    for bit in bits(m)[1:]:
        total = add(total, swap_odd(total, m, n, bit, 0))
    for _ in range(4, n):
        (held_a, held_b), total = after((ring_a[-1], ring_b[-1]), total)
        ring_a.append(step(held_a))
        ring_b.append(step(held_b))
    ring_b[-1], total = after(ring_b[-1], total)
    for bit in bits(n):
        total = add(total, swap_odd(total, m, n, 0, bit))
    other = swap(total, "dp", m, 1)
    (held_a, held), other = after((ring_a[-1], ring_b[-1]), other)
    ring_a.append(step(held_a))
    newest = [step(x) for x in cut(held, parts)]

    terms = len(LEFT_TERMS) * rank
    whole, left_terms, right_terms = call(
        functools.partial(factor_kernel, 1.0 / m),
        [sds((rank, width), F32), sds((rows, terms), BF16), sds((terms, width), BF16)],
        [
            pltpu.VMEM((terms, rows), F32),
            pltpu.VMEM((terms, width), F32),
        ],
        "factor",
    )(ortho, total, other)

    acts = call(
        functools.partial(acts_kernel, n),
        sds((rows, tokens), BF16),
        [pltpu.VMEM((tokens, rows), BF16)],
        "acts",
    )(activations)
    pieces = [(0, wide, [out_grads, *ring_a[1:]], [0] * n)]
    at = wide
    for part, x in zip(parts, newest):
        pieces.append((at, part, [out_grads, *ring_b[1:], x], [0] + [wide] * (n - 2) + [at]))
        at += part

    outs = ()
    for at, part, slots, bases in pieces:
        outs = pl.pallas_call(
            functools.partial(final_kernel, at, part, bases),
            in_specs=[vmem] * (4 + n) + [pl.BlockSpec(memory_space=pl.ANY)] * len(outs),
            out_specs=[pl.BlockSpec(memory_space=pl.ANY)] * 2,
            out_shape=[sds((rows, width), BF16), sds((1, rows, width), BF16)],
            input_output_aliases={4 + n + j: j for j in range(len(outs))},
            scratch_shapes=[pltpu.VMEM((rows, part), BF16)] * 2 + [dma((3, 2))],
            compiler_params=params(16),
            cost_estimate=cost(0),
            name="rebuild",
        )(acts, left_terms, right_terms, error_v, *slots, *outs)
    rebuilt, error = outs
    return rebuilt, error, whole.T


def solution(mesh):
    return jax.shard_map(
        per_device,
        mesh=mesh,
        in_specs=(P("dp", None, "tensor"), P("dp", "tensor", None), P("dp", "tensor", None), P()),
        out_specs=(P("tensor", None), P("dp", "tensor", None), P()),
        check_vma=False,
    )
```

```python
import functools

import jax
import jax.numpy as jnp
from jax import lax
from jax.experimental import pallas as pl
from jax.experimental.pallas import tpu as pltpu
from jax.sharding import PartitionSpec as P

F32 = jnp.float32
BF16 = jnp.bfloat16
SHRINK = 2.0**-23
TINY = 1e-30
BLOCK = 512


def params(mib):
    return pltpu.CompilerParams(vmem_limit_bytes=mib * 2**20)


def cost(flops):
    return pl.CostEstimate(flops=int(flops) + 1, bytes_accessed=1, transcendentals=0)


def dot(a, b, contract):
    return lax.dot_general(a, b, ((contract[:1], contract[1:]), ((), ())), preferred_element_type=F32)


def split(x):
    hi = x.astype(BF16)
    rest = x - hi.astype(F32)
    mid = rest.astype(BF16)
    lo = (rest - mid.astype(F32)).astype(BF16)
    return hi.astype(F32), mid.astype(F32), lo.astype(F32)


def stack3(x, ref):
    rank = x.shape[0]
    for i, part in enumerate(split(x)):
        ref[i * rank : (i + 1) * rank, :] = part
    return ref[...].astype(BF16)


def sum3(y, rank):
    return (y[2 * rank :] + y[rank : 2 * rank]) + y[:rank]


def ring_of(n):
    return [2 * p if 2 * p < n else 2 * (n - p) - 1 for p in range(n)]


def ring_source(me, step, n):
    place = jnp.where(lax.rem(me, 2) == 0, me // 2, n - (me + 1) // 2)
    place = lax.rem(place - step + n, n)
    return jnp.where(2 * place < n, 2 * place, 2 * (n - place) - 1)


def ring_step(x, axis, n):
    ring = ring_of(n)
    return lax.ppermute(x, axis, [(ring[p], ring[(p + 1) % n]) for p in range(n)])


def exchange(pieces, axis, n):
    return [pieces[0]] + [
        lax.ppermute(pieces[k], axis, [(i, (i + k) % n) for i in range(n)]) for k in range(1, n)
    ]


def swap(x, axis, n, bit):
    return lax.ppermute(x, axis, [(i, i ^ bit) for i in range(n)])


def groups(n):
    assert n & (n - 1) == 0
    bits = [1 << i for i in range(n.bit_length() - 1)]
    return [bits[i : i + 2] for i in range(0, len(bits), 2)]


def terms_of(x, axis, n, group):
    others = group if len(group) == 1 else [group[0], group[1], group[0] | group[1]]
    return [x] + [swap(x, axis, n, bit) for bit in others]


def total_of(refs):
    total = refs[0][...] + refs[1][...]
    if len(refs) == 4:
        total = total + (refs[2][...] + refs[3][...])
    return total


def token_factor_kernel(w_hbm, g_hbm, gw_ref, terms_ref, w, g, w3, sems):
    rank = w.shape[0]
    copies = [
        pltpu.make_async_copy(w_hbm, w, sems.at[0]),
        pltpu.make_async_copy(g_hbm, g, sems.at[1]),
    ]
    for copy in copies:
        copy.start()
    copies[0].wait()
    terms = stack3(w[...] * SHRINK, w3)
    terms_ref[...] = terms
    copies[1].wait()
    gw_ref[...] = jnp.zeros_like(gw_ref)
    gw_ref[0:rank, 0 : g.shape[1]] = sum3(dot(terms, g[0], (1, 1)), rank)


def cut_kernel(x_ref, *refs):
    chunks, sems = refs[:-1], refs[-1]
    copies = []
    at = 0
    for c, chunk in enumerate(chunks):
        part = chunk.shape[2]
        copies.append(pltpu.make_async_copy(x_ref.at[:, :, pl.ds(at, part)], chunk, sems.at[c]))
        copies[-1].start()
        at += part
    for copy in copies:
        copy.wait()


def error_left_kernel(terms_ref, e_hbm, out_ref, e_ref, sems):
    rank = out_ref.shape[0]
    count = sems.shape[0]
    high = e_ref.shape[1] // count
    copies = []
    for c in range(count):
        rows = pl.ds(c * high, high)
        copies.append(pltpu.make_async_copy(e_hbm.at[:, rows, :], e_ref.at[:, rows, :], sems.at[c]))
        copies[-1].start()
    terms = terms_ref[...]
    for c in range(count):
        copies[c].wait()
        rows = slice(c * high, (c + 1) * high)
        out_ref[:, rows] = sum3(dot(terms, e_ref[0, rows, :], (1, 1)), rank)


def left_kernel(a_ref, e_ref, *refs):
    gws, out_ref, g3 = refs[:-2], refs[-2], refs[-1]
    n = len(gws)
    rank = e_ref.shape[0]
    tok = a_ref.shape[1] // n
    me = lax.axis_index("tensor")
    total = e_ref[...]
    for k in range(n):
        src = lax.rem(me - k + n, n)
        rows = a_ref[0, pl.ds(pl.multiple_of(src * tok, tok), tok), :]
        total += sum3(dot(stack3(gws[k][0:rank, 0:tok], g3), rows, (1, 0)), rank)
    out_ref[...] = total


def mean_kernel(n, scale, a_ref, *refs):
    terms, p_ref, msgs, p3, outbox = refs[: -n - 3], refs[-n - 3], refs[-n - 2 : -2], refs[-2], refs[-1]
    rank = p_ref.shape[0]
    tok = a_ref.shape[1] // n
    me = lax.axis_index("tensor")
    mean = total_of(terms) * scale
    p_ref[...] = mean
    top = jnp.max(jnp.max(jnp.abs(mean), axis=1, keepdims=True), axis=0, keepdims=True)
    top = jnp.maximum(top, TINY)
    parts = stack3(mean / (top * 1024.0), p3)
    gram = [jnp.sum(mean * mean[i : i + 1, :], axis=1, keepdims=True) for i in range(rank)]
    outbox[...] = jnp.zeros_like(outbox)
    for t in range(n):
        y = dot(parts, a_ref[0, t * tok : (t + 1) * tok, :], (1, 1))
        outbox[t, 0:rank, 0:tok] = sum3(y, rank)
        for i in range(rank):
            outbox[t, rank : 2 * rank, i : i + 1] = gram[i]
        outbox[t, rank : rank + 1, rank : rank + 1] = top
    for k in range(n):
        msgs[k][...] = outbox[lax.rem(me + k, n)]


def error_right_kernel(p_ref, e_ref, out_ref, p3):
    rank = p_ref.shape[0]
    parts = stack3(p_ref[...], p3)
    for c in range(e_ref.shape[2] // BLOCK):
        cols = slice(c * BLOCK, (c + 1) * BLOCK)
        out_ref[:, cols] = sum3(dot(parts, e_ref[0, :, cols], (1, 0)), rank)


def lower_inverse(gram, rank):
    at = lambda i, j: gram[i : i + 1, j : j + 1]
    low = {}
    for j in range(rank):
        d = at(j, j)
        for k in range(j):
            d = d - low[j, k] * low[j, k]
        low[j, j] = jnp.sqrt(d)
        for i in range(j + 1, rank):
            v = at(i, j)
            for k in range(j):
                v = v - low[i, k] * low[j, k]
            low[i, j] = v / low[j, j]
    inv = {}
    for j in range(rank):
        inv[j, j] = 1.0 / low[j, j]
        for i in range(j + 1, rank):
            v = low[i, j] * inv[j, j]
            for k in range(j + 1, i):
                v = v + low[i, k] * inv[k, j]
            inv[i, j] = -v / low[i, i]
    return inv


def solve_rows(inv, x, rank):
    rows = []
    for i in range(rank):
        row = inv[i, 0] * x[0:1, :]
        for j in range(1, i + 1):
            row = row + inv[i, j] * x[j : j + 1, :]
        rows.append(row)
    return rows


def right_kernel(n, p_ref, r_ref, g_ref, *refs):
    pieces = refs[:n]
    ortho_ref, keep_ref, send_ref, inbox, z, z3, outbox = refs[n:]
    rank = p_ref.shape[0]
    tok = g_ref.shape[1]
    half = keep_ref.shape[1]
    me_t = lax.axis_index("tensor")
    core = lax.rem(lax.axis_index("dp"), 2)
    for k in range(n):
        inbox[lax.rem(me_t - k + n, n)] = pieces[k][...]
    gram = inbox[0, rank : 2 * rank, 0:rank]
    for t in range(1, n):
        gram = gram + inbox[t, rank : 2 * rank, 0:rank]
    inv = lower_inverse(gram, rank)
    for t in range(n):
        top = inbox[t, rank : rank + 1, rank : rank + 1]
        scaled = {key: value * top for key, value in inv.items()}
        for i, row in enumerate(solve_rows(scaled, inbox[t, 0:rank, 0:tok], rank)):
            if t == 0:
                z[i : i + 1, :] = row
            else:
                z[i : i + 1, :] += row
    for i, row in enumerate(solve_rows(inv, p_ref[...], rank)):
        ortho_ref[i : i + 1, :] = row
    terms = stack3(z[...], z3)
    for h in range(2):
        cols = slice(h * half, (h + 1) * half)
        fresh = sum3(dot(terms, g_ref[0, :, cols], (1, 0)), rank) * 1024.0
        for i, row in enumerate(solve_rows(inv, r_ref[:, cols], rank)):
            outbox[h, i : i + 1, :] = row + fresh[i : i + 1, :]
    keep_ref[...] = outbox[core]
    send_ref[...] = outbox[1 - core]


def add_kernel(*refs):
    refs[-1][...] = total_of(refs[:-1])


LEFT_TERMS = (0, 0, 1, 0, 2, 1)
RIGHT_TERMS = (0, 1, 0, 2, 0, 1)


def factor_kernel(scale, ortho_ref, mine_ref, other_ref, whole_ref, left_ref, right_ref, inbox, left, right):
    rank, half = mine_ref.shape
    core = lax.rem(lax.axis_index("dp"), 2)
    inbox[core] = mine_ref[...]
    inbox[1 - core] = other_ref[...]
    for h in range(2):
        whole_ref[:, h * half : (h + 1) * half] = inbox[h] * scale
    for terms, x, ref in (
        (LEFT_TERMS, ortho_ref[...], left),
        (RIGHT_TERMS, whole_ref[...], right),
    ):
        parts = split(x)
        for i, term in enumerate(terms):
            ref[i * rank : (i + 1) * rank, :] = parts[term]
    left_ref[...] = left[...].T.astype(BF16)
    right_ref[...] = right[...].astype(BF16)


def acts_kernel(n, a_ref, out_ref, acts):
    tok = a_ref.shape[1] // n
    me = lax.axis_index("tensor")
    for s in range(n):
        src = ring_source(me, s, n)
        here = a_ref[0, pl.ds(pl.multiple_of(src * tok, tok), tok), :]
        acts[s * tok : (s + 1) * tok, :] = here
    out_ref[...] = acts[...].T


def final_kernel(at, part, bases, acts_ref, left_ref, right_ref, e_ref, *refs):
    slots = refs[: len(bases)]
    rebuilt_hbm, error_hbm, rebuilt_v, error_v, sems = refs[-5:]
    rows = e_ref.shape[1]
    wide = 256
    high = rows // sems.shape[0]
    copies = []
    for r in range(sems.shape[0]):
        here = slice(r * high, (r + 1) * high)
        for c in range(part // wide):
            cols = slice(c * wide, (c + 1) * wide)
            there = slice(at + c * wide, at + (c + 1) * wide)
            grads = [
                slot[0, :, there.start - base : there.stop - base]
                for slot, base in zip(slots, bases)
            ]
            grad = dot(acts_ref[here, :], jnp.concatenate(grads, axis=0), (1, 0))
            matrix = grad + e_ref[0, here, there].astype(F32)
            rebuilt = dot(left_ref[here, :], right_ref[:, there], (1, 0))
            rebuilt_v[here, cols] = rebuilt.astype(BF16)
            error_v[here, cols] = (matrix - rebuilt).astype(BF16)
        strip = pl.ds(r * high, high)
        span = pl.ds(at, part)
        copies += [
            pltpu.make_async_copy(
                rebuilt_v.at[strip, :], rebuilt_hbm.at[strip, span], sems.at[r, 0]
            ),
            pltpu.make_async_copy(
                error_v.at[strip, :], error_hbm.at[0, strip, span], sems.at[r, 1]
            ),
        ]
        copies[-2].start()
        copies[-1].start()
    for copy in copies:
        copy.wait()


def per_device(activations, out_grads, error_buffer, warm_factor):
    m = lax.axis_size("dp")
    n = lax.axis_size("tensor")
    _, tokens, rows = activations.shape
    _, tok, width = out_grads.shape
    rank = warm_factor.shape[1]
    half = width // 2
    w = warm_factor.T
    sds = jax.ShapeDtypeStruct
    hbm = pl.BlockSpec(memory_space=pltpu.HBM)
    vmem = pl.BlockSpec(memory_space=pltpu.VMEM)
    dma = pltpu.SemaphoreType.DMA
    pin = lambda x: pltpu.with_memory_space_constraint(x, pltpu.HBM)

    def call(kernel, shapes, scratch, name, specs=None, flops=0):
        return pl.pallas_call(
            kernel,
            out_shape=shapes,
            **({"in_specs": specs} if specs else {}),
            scratch_shapes=scratch,
            compiler_params=params(16),
            cost_estimate=cost(flops),
            name=name,
        )

    def add(*terms):
        return call(add_kernel, sds(terms[0].shape, F32), [], "add")(*terms)

    def after(x, y):
        return lax.optimization_barrier((x, y))

    def cut(x, widths):
        shapes = [sds((1, tok, part), BF16) for part in widths]
        return call(cut_kernel, shapes, [dma((len(widths),))], "cut")(x)

    def step(x):
        return ring_step(x, "tensor", n)

    wide = width // 4
    narrow = width // 2 - wide
    ring = [out_grads, step(out_grads)]

    gw, w_terms = call(
        token_factor_kernel,
        [sds((8, 128), F32), sds((3 * rank, width), BF16)],
        [
            pltpu.VMEM((rank, width), F32),
            pltpu.VMEM((1, tok, width), BF16),
            pltpu.VMEM((3 * rank, width), F32),
            dma((2,)),
        ],
        "token_factor", [hbm, hbm],
    )(pin(w), pin(out_grads))
    ew, error_v = call(
        error_left_kernel,
        [sds((rank, rows), F32), sds((1, rows, width), BF16)],
        [dma((rows // 128,))],
        "error_left", [vmem, hbm], 4.6e9,
    )(w_terms, pin(error_buffer))

    gw, ew = after(gw, ew)
    gws = exchange([gw] * n, "tensor", n)
    ring[1], gws = after(ring[1], gws)
    x1, y1 = cut(ring[1], [2 * wide, 2 * narrow])
    xs, ys = [x1, step(x1)], [y1]
    left = call(
        left_kernel, sds((rank, rows), F32), [pltpu.VMEM((3 * rank, tok), F32)], "left"
    )(activations, ew, *gws)
    left = add(left, swap(left, "dp", m, 1))
    for group in groups(m // 2)[:-1]:
        left = add(*terms_of(left, "dp", m, [2 * bit for bit in group]))
    lefts = terms_of(left, "dp", m, [2 * bit for bit in groups(m // 2)[-1]])
    xs[1], lefts[1:] = after(xs[1], lefts[1:])
    mean, *msgs = call(
        functools.partial(mean_kernel, n, 1.0 / (SHRINK * m)),
        [sds((rank, rows), F32)] + [sds((8, 128), F32)] * n,
        [pltpu.VMEM((3 * rank, rows), F32), pltpu.VMEM((n, 8, 128), F32)],
        "mean",
    )(activations, *lefts)
    msgs = exchange(msgs, "tensor", n)

    right_raw = call(
        error_right_kernel,
        sds((rank, width), F32),
        [pltpu.VMEM((3 * rank, rows), F32)],
        "error_right", None, 1.2e9,
    )(mean, error_v)

    ortho, keep, send = call(
        functools.partial(right_kernel, n),
        [sds((rank, rows), F32), sds((rank, half), F32), sds((rank, half), F32)],
        [
            pltpu.VMEM((n, 8, 128), F32),
            pltpu.VMEM((rank, tok), F32),
            pltpu.VMEM((3 * rank, tok), F32),
            pltpu.VMEM((2, rank, half), F32),
        ],
        "right",
    )(mean, right_raw, out_grads, *msgs)
    total = add(keep, swap(send, "dp", m, 1))
    for _ in range(3, n):
        last, total = after(ys[-1], total)
        ys.append(step(last))
    for _ in range(4, n):
        last, total = after(xs[-1], total)
        xs.append(step(last))
    for group in groups(m // 2):
        total = add(*terms_of(total, "dp", m, [2 * bit for bit in group]))
    (xs[-1], ys[-1]), total = after((xs[-1], ys[-1]), total)
    for group in groups(n):
        total = add(*terms_of(total, "tensor", n, group))
    xa, xb = cut(xs[-1], [wide, wide])
    (xa, xb), total = after((xa, xb), total)
    xa, xb = step(xa), step(xb)

    terms = len(LEFT_TERMS) * rank
    whole, left_terms, right_terms = call(
        functools.partial(factor_kernel, 1.0 / m),
        [sds((rank, width), F32), sds((rows, terms), BF16), sds((terms, width), BF16)],
        [
            pltpu.VMEM((2, rank, half), F32),
            pltpu.VMEM((terms, rows), F32),
            pltpu.VMEM((terms, width), F32),
        ],
        "factor",
    )(ortho, total, swap(total, "dp", m, 1))

    acts = call(
        functools.partial(acts_kernel, n),
        sds((rows, tokens), BF16),
        [pltpu.VMEM((tokens, rows), BF16)],
        "acts",
    )(activations)
    last, right_terms = after(ys[-1], right_terms)
    ya, yb = cut(last, [narrow, narrow])
    pieces = []
    at = 0
    for part, base, held, newest in (
        (wide, 0, xs, xa),
        (wide, 0, xs, xb),
        (narrow, 2 * wide, ys, step(ya)),
        (narrow, 2 * wide, ys, step(yb)),
    ):
        slots = ring + held[1 : n - 2] + [newest]
        bases = [0, 0] + [base] * (n - 3) + [at]
        pieces.append((at, part, slots, bases))
        at += part

    outs = ()
    for at, part, slots, bases in pieces:
        outs = pl.pallas_call(
            functools.partial(final_kernel, at, part, bases),
            in_specs=[vmem] * (4 + n) + [pl.BlockSpec(memory_space=pl.ANY)] * len(outs),
            out_specs=[pl.BlockSpec(memory_space=pl.ANY)] * 2,
            out_shape=[sds((rows, width), BF16), sds((1, rows, width), BF16)],
            input_output_aliases={4 + n + j: j for j in range(len(outs))},
            scratch_shapes=[pltpu.VMEM((rows, part), BF16)] * 2 + [dma((3, 2))],
            compiler_params=params(16),
            cost_estimate=cost(0),
            name="rebuild",
        )(acts, left_terms, right_terms, error_v, *slots, *outs)
    rebuilt, error = outs
    return rebuilt, error, whole.T


def solution(mesh):
    return jax.shard_map(
        per_device,
        mesh=mesh,
        in_specs=(P("dp", None, "tensor"), P("dp", "tensor", None), P("dp", "tensor", None), P()),
        out_specs=(P("tensor", None), P("dp", "tensor", None), P()),
        check_vma=False,
    )
```

```python
import functools

import jax
import jax.numpy as jnp
from jax import lax
from jax.experimental import pallas as pl
from jax.experimental.pallas import tpu as pltpu
from jax.sharding import PartitionSpec as P

F32 = jnp.float32
BF16 = jnp.bfloat16
SHRINK = 2.0**-23
TINY = 1e-30
ROOM = 2.0**14
BLOCK = 512


def params(mib):
    return pltpu.CompilerParams(vmem_limit_bytes=mib * 2**20)


def cost(flops):
    return pl.CostEstimate(flops=int(flops) + 1, bytes_accessed=1, transcendentals=0)


def dot(a, b, contract):
    return lax.dot_general(a, b, ((contract[:1], contract[1:]), ((), ())), preferred_element_type=F32)


def split(x):
    hi = x.astype(BF16)
    rest = x - hi.astype(F32)
    mid = rest.astype(BF16)
    lo = (rest - mid.astype(F32)).astype(BF16)
    return hi.astype(F32), mid.astype(F32), lo.astype(F32)


def stack3(x, ref):
    rank = x.shape[0]
    for i, part in enumerate(split(x)):
        ref[i * rank : (i + 1) * rank, :] = part
    return ref[...].astype(BF16)


def sum3(y, rank):
    return (y[2 * rank :] + y[rank : 2 * rank]) + y[:rank]


def ring_of(n):
    return [2 * p if 2 * p < n else 2 * (n - p) - 1 for p in range(n)]


def ring_source(me, step, n):
    place = jnp.where(lax.rem(me, 2) == 0, me // 2, n - (me + 1) // 2)
    place = lax.rem(place - step + n, n)
    return jnp.where(2 * place < n, 2 * place, 2 * (n - place) - 1)


def ring_step(x, axis, n):
    ring = ring_of(n)
    return lax.ppermute(x, axis, [(ring[p], ring[(p + 1) % n]) for p in range(n)])


def exchange(pieces, axis, n):
    return [pieces[0]] + [
        lax.ppermute(pieces[k], axis, [(i, (i + k) % n) for i in range(n)]) for k in range(1, n)
    ]


def swap(x, axis, n, bit):
    return lax.ppermute(x, axis, [(i, i ^ bit) for i in range(n)])


def groups(n):
    assert n & (n - 1) == 0
    bits = [1 << i for i in range(n.bit_length() - 1)]
    return [bits[i : i + 2] for i in range(0, len(bits), 2)]


def terms_of(x, axis, n, group):
    others = group if len(group) == 1 else [group[0], group[1], group[0] | group[1]]
    return [x] + [swap(x, axis, n, bit) for bit in others]


def total_of(refs):
    total = refs[0][...] + refs[1][...]
    if len(refs) == 4:
        total = total + (refs[2][...] + refs[3][...])
    return total


def token_factor_kernel(w_hbm, g_hbm, gw_ref, terms_ref, w, g, w3, sems):
    rank = w.shape[0]
    copies = [
        pltpu.make_async_copy(w_hbm, w, sems.at[0]),
        pltpu.make_async_copy(g_hbm, g, sems.at[1]),
    ]
    for copy in copies:
        copy.start()
    copies[0].wait()
    terms = stack3(w[...] * SHRINK, w3)
    terms_ref[...] = terms
    copies[1].wait()
    gw_ref[...] = jnp.zeros_like(gw_ref)
    gw_ref[0:rank, 0 : g.shape[1]] = sum3(dot(terms, g[0], (1, 1)), rank)


def cut_kernel(x_ref, *refs):
    chunks, sems = refs[:-1], refs[-1]
    copies = []
    at = 0
    for c, chunk in enumerate(chunks):
        part = chunk.shape[2]
        copies.append(pltpu.make_async_copy(x_ref.at[:, :, pl.ds(at, part)], chunk, sems.at[c]))
        copies[-1].start()
        at += part
    for copy in copies:
        copy.wait()


def error_left_kernel(terms_ref, e_hbm, out_ref, e_ref, sems):
    rank = out_ref.shape[0]
    count = sems.shape[0]
    high = e_ref.shape[1] // count
    copies = []
    for c in range(count):
        rows = pl.ds(c * high, high)
        copies.append(pltpu.make_async_copy(e_hbm.at[:, rows, :], e_ref.at[:, rows, :], sems.at[c]))
        copies[-1].start()
    terms = terms_ref[...]
    for c in range(count):
        copies[c].wait()
        rows = slice(c * high, (c + 1) * high)
        out_ref[:, rows] = sum3(dot(terms, e_ref[0, rows, :], (1, 1)), rank)


def left_kernel(a_ref, e_ref, *refs):
    gws, out_ref, g3 = refs[:-2], refs[-2], refs[-1]
    n = len(gws)
    rank = e_ref.shape[0]
    tok = a_ref.shape[1] // n
    me = lax.axis_index("tensor")
    total = e_ref[...]
    for k in range(n):
        src = lax.rem(me - k + n, n)
        rows = a_ref[0, pl.ds(pl.multiple_of(src * tok, tok), tok), :]
        total += sum3(dot(stack3(gws[k][0:rank, 0:tok], g3), rows, (1, 0)), rank)
    out_ref[...] = total


def mean_kernel(n, scale, a_ref, *refs):
    terms = refs[:-7]
    p_ref, scaled_ref, extra_ref, held_ref, next_ref, p3, blocks = refs[-7:]
    rank = p_ref.shape[0]
    tok = a_ref.shape[1] // n
    me = lax.axis_index("tensor")
    mean = total_of(terms) * scale
    p_ref[...] = mean
    top = jnp.max(jnp.max(jnp.abs(mean), axis=1, keepdims=True), axis=0, keepdims=True)
    top = jnp.maximum(top, TINY)
    scaled = mean / (top * ROOM)
    scaled_ref[...] = scaled
    parts = stack3(scaled, p3)
    for t in range(n):
        blocks[t] = sum3(dot(parts, a_ref[0, t * tok : (t + 1) * tok, :], (1, 1)), rank)
    for s in range(n - 1):
        held_ref[:, s * tok : (s + 1) * tok] = blocks[ring_source(me, s, n)]
    next_ref[...] = jnp.zeros_like(next_ref)
    next_ref[0:rank, 0:tok] = blocks[ring_source(me, n - 1, n)]
    next_ref[rank : rank + 1, 0:1] = top
    extra_ref[...] = jnp.zeros_like(extra_ref)
    for i in range(rank):
        extra_ref[:, i : i + 1] = jnp.sum(mean * mean[i : i + 1, :], axis=1, keepdims=True)
    extra_ref[:, rank : rank + 1] = jnp.broadcast_to(top, (rank, 1))


def error_right_kernel(p_ref, e_ref, out_ref, p3):
    rank = p_ref.shape[0]
    parts = stack3(p_ref[...], p3)
    for c in range(e_ref.shape[2] // BLOCK):
        cols = slice(c * BLOCK, (c + 1) * BLOCK)
        out_ref[:, cols] = sum3(dot(parts, e_ref[0, :, cols], (1, 0)), rank)


def lower_inverse(gram, rank):
    at = lambda i, j: gram[i : i + 1, j : j + 1]
    low = {}
    for j in range(rank):
        d = at(j, j)
        for k in range(j):
            d = d - low[j, k] * low[j, k]
        low[j, j] = jnp.sqrt(d)
        for i in range(j + 1, rank):
            v = at(i, j)
            for k in range(j):
                v = v - low[i, k] * low[j, k]
            low[i, j] = v / low[j, j]
    inv = {}
    for j in range(rank):
        inv[j, j] = 1.0 / low[j, j]
        for i in range(j + 1, rank):
            v = low[i, j] * inv[j, j]
            for k in range(j + 1, i):
                v = v + low[i, k] * inv[k, j]
            inv[i, j] = -v / low[i, i]
    return inv


def solve_rows(inv, x, rank):
    rows = []
    for i in range(rank):
        row = inv[i, 0] * x[0:1, :]
        for j in range(1, i + 1):
            row = row + inv[i, j] * x[j : j + 1, :]
        rows.append(row)
    return rows


def right_kernel(r_ref, y_ref, got_ref, extra_ref, *refs):
    held, (keep_ref, send_ref, y3, outbox) = refs[:-4], refs[-4:]
    rank = r_ref.shape[0]
    tok = held[0].shape[1]
    half = r_ref.shape[1] // 2
    core = lax.rem(lax.axis_index("dp"), 2)
    mine = extra_ref[0:1, rank : rank + 1]
    theirs = got_ref[rank : rank + 1, 0:1]
    top = jnp.maximum(mine, theirs)
    products = y_ref[...] * (mine / top)
    joint = products[:, 0:tok] + got_ref[0:rank, 0:tok] * (theirs / top)
    terms = stack3(jnp.concatenate([joint, products[:, tok:]], axis=1), y3)
    for h in range(2):
        for c in range(half // BLOCK):
            at = h * half + c * BLOCK
            cols = slice(at, at + BLOCK)
            grads = jnp.concatenate([g[0, :, cols] for g in held], axis=0)
            fresh = sum3(dot(terms, grads, (1, 0)), rank)
            outbox[h, :, c * BLOCK : (c + 1) * BLOCK] = r_ref[:, cols] * (mine / top) + fresh
        outbox[h, :, half:] = extra_ref[...]
        outbox[h, :, half + rank : half + rank + 1] = jnp.broadcast_to(top, (rank, 1))
    keep_ref[...] = outbox[core]
    send_ref[...] = outbox[1 - core]


def join_kernel(rank, *refs):
    xs, out_ref = refs[:-1], refs[-1]
    half = out_ref.shape[1] - 128
    mark = slice(half + rank, half + rank + 1)
    tops = [x[0:1, mark] for x in xs]
    top = jnp.maximum(tops[0], tops[1])
    for other in tops[2:]:
        top = jnp.maximum(top, other)

    def total(terms):
        first = terms[0] + terms[1]
        return first + (terms[2] + terms[3]) if len(terms) == 4 else first

    out_ref[:, :half] = total([x[:, :half] * (t / top) for x, t in zip(xs, tops)])
    out_ref[:, half:] = total([x[:, half:] for x in xs])
    out_ref[:, mark] = jnp.broadcast_to(top, (rank, 1))


def add_kernel(*refs):
    refs[-1][...] = total_of(refs[:-1])


LEFT_TERMS = (0, 0, 1, 0, 2, 1)
RIGHT_TERMS = (0, 1, 0, 2, 0, 1)


def factor_kernel(m, p_ref, mine_ref, other_ref, whole_ref, left_ref, right_ref, inbox, ortho, left, right):
    rank = mine_ref.shape[0]
    half = mine_ref.shape[1] - 128
    core = lax.rem(lax.axis_index("dp"), 2)
    inbox[core] = mine_ref[...]
    inbox[1 - core] = other_ref[...]
    inv = lower_inverse(inbox[0, :, half : half + rank] * (1.0 / m), rank)
    top = inbox[0, 0:1, half + rank : half + rank + 1] * (ROOM / (m * m))
    scaled = {key: value * top for key, value in inv.items()}
    for i, row in enumerate(solve_rows(inv, p_ref[...], rank)):
        ortho[i : i + 1, :] = row
    for h in range(2):
        for i, row in enumerate(solve_rows(scaled, inbox[h, :, 0:half], rank)):
            whole_ref[i : i + 1, h * half : (h + 1) * half] = row
    for terms, x, ref in (
        (LEFT_TERMS, ortho[...], left),
        (RIGHT_TERMS, whole_ref[...], right),
    ):
        parts = split(x)
        for i, term in enumerate(terms):
            ref[i * rank : (i + 1) * rank, :] = parts[term]
    left_ref[...] = left[...].T.astype(BF16)
    right_ref[...] = right[...].astype(BF16)


def acts_kernel(n, a_ref, out_ref, acts):
    tok = a_ref.shape[1] // n
    me = lax.axis_index("tensor")
    for s in range(n):
        src = ring_source(me, s, n)
        here = a_ref[0, pl.ds(pl.multiple_of(src * tok, tok), tok), :]
        acts[s * tok : (s + 1) * tok, :] = here
    out_ref[...] = acts[...].T


def final_kernel(at, part, bases, acts_ref, left_ref, right_ref, e_ref, *refs):
    slots = refs[: len(bases)]
    rebuilt_hbm, error_hbm, rebuilt_v, error_v, sems = refs[-5:]
    rows = e_ref.shape[1]
    wide = 256
    high = rows // sems.shape[0]
    copies = []
    for r in range(sems.shape[0]):
        here = slice(r * high, (r + 1) * high)
        for c in range(part // wide):
            cols = slice(c * wide, (c + 1) * wide)
            there = slice(at + c * wide, at + (c + 1) * wide)
            grads = [
                slot[0, :, there.start - base : there.stop - base]
                for slot, base in zip(slots, bases)
            ]
            grad = dot(acts_ref[here, :], jnp.concatenate(grads, axis=0), (1, 0))
            matrix = grad + e_ref[0, here, there].astype(F32)
            rebuilt = dot(left_ref[here, :], right_ref[:, there], (1, 0))
            rebuilt_v[here, cols] = rebuilt.astype(BF16)
            error_v[here, cols] = (matrix - rebuilt).astype(BF16)
        strip = pl.ds(r * high, high)
        span = pl.ds(at, part)
        copies += [
            pltpu.make_async_copy(
                rebuilt_v.at[strip, :], rebuilt_hbm.at[strip, span], sems.at[r, 0]
            ),
            pltpu.make_async_copy(
                error_v.at[strip, :], error_hbm.at[0, strip, span], sems.at[r, 1]
            ),
        ]
        copies[-2].start()
        copies[-1].start()
    for copy in copies:
        copy.wait()


def per_device(activations, out_grads, error_buffer, warm_factor):
    m = lax.axis_size("dp")
    n = lax.axis_size("tensor")
    _, tokens, rows = activations.shape
    _, tok, width = out_grads.shape
    rank = warm_factor.shape[1]
    half = width // 2
    w = warm_factor.T
    sds = jax.ShapeDtypeStruct
    hbm = pl.BlockSpec(memory_space=pltpu.HBM)
    vmem = pl.BlockSpec(memory_space=pltpu.VMEM)
    dma = pltpu.SemaphoreType.DMA
    pin = lambda x: pltpu.with_memory_space_constraint(x, pltpu.HBM)

    def call(kernel, shapes, scratch, name, specs=None, flops=0):
        return pl.pallas_call(
            kernel,
            out_shape=shapes,
            **({"in_specs": specs} if specs else {}),
            scratch_shapes=scratch,
            compiler_params=params(16),
            cost_estimate=cost(flops),
            name=name,
        )

    def add(*terms):
        return call(add_kernel, sds(terms[0].shape, F32), [], "add")(*terms)

    def after(x, y):
        return lax.optimization_barrier((x, y))

    def cut(x, widths):
        shapes = [sds((1, tok, part), BF16) for part in widths]
        return call(cut_kernel, shapes, [dma((len(widths),))], "cut")(x)

    def step(x):
        return ring_step(x, "tensor", n)

    ring = [out_grads, step(out_grads)]

    gw, w_terms = call(
        token_factor_kernel,
        [sds((8, 128), F32), sds((3 * rank, width), BF16)],
        [
            pltpu.VMEM((rank, width), F32),
            pltpu.VMEM((1, tok, width), BF16),
            pltpu.VMEM((3 * rank, width), F32),
            dma((2,)),
        ],
        "token_factor", [hbm, hbm],
    )(pin(w), pin(out_grads))
    ew, error_v = call(
        error_left_kernel,
        [sds((rank, rows), F32), sds((1, rows, width), BF16)],
        [dma((rows // 128,))],
        "error_left", [vmem, hbm], 4.6e9,
    )(w_terms, pin(error_buffer))

    gw, ew = after(gw, ew)
    gws = exchange([gw] * n, "tensor", n)
    ring[1], gws = after(ring[1], gws)
    for _ in range(n - 2 - 1):
        ring.append(step(ring[-1]))
    left = call(
        left_kernel, sds((rank, rows), F32), [pltpu.VMEM((3 * rank, tok), F32)], "left"
    )(activations, ew, *gws)
    left = add(left, swap(left, "dp", m, 1))
    for group in groups(m // 2)[:-1]:
        left = add(*terms_of(left, "dp", m, [2 * bit for bit in group]))
    lefts = terms_of(left, "dp", m, [2 * bit for bit in groups(m // 2)[-1]])
    mean, scaled, extra, held, following = call(
        functools.partial(mean_kernel, n, 1.0 / (SHRINK * m)),
        [
            sds((rank, rows), F32),
            sds((rank, rows), F32),
            sds((rank, 128), F32),
            sds((rank, (n - 1) * tok), F32),
            sds((8, 128), F32),
        ],
        [pltpu.VMEM((3 * rank, rows), F32), pltpu.VMEM((n, rank, tok), F32)],
        "mean",
    )(activations, *lefts)
    got = step(following)

    right_raw = call(
        error_right_kernel,
        sds((rank, width), F32),
        [pltpu.VMEM((3 * rank, rows), F32)],
        "error_right", None, 1.2e9,
    )(scaled, error_v)

    keep, send = call(
        right_kernel,
        [sds((rank, half + 128), F32)] * 2,
        [
            pltpu.VMEM((3 * rank, (n - 1) * tok), F32),
            pltpu.VMEM((2, rank, half + 128), F32),
        ],
        "right",
    )(right_raw, held, got, extra, *ring)
    total = add(keep, swap(send, "dp", m, 1))

    widths = [half, half // 2, half // 2]
    last, total = after(ring[-1], total)
    newest = list(cut(last, widths))
    newest[0] = step(newest[0])
    for group in groups(m // 2):
        total = add(*terms_of(total, "dp", m, [2 * bit for bit in group]))
    newest[0], total = after(newest[0], total)
    for group in groups(n):
        parts = terms_of(total, "tensor", n, group)
        total = call(
            functools.partial(join_kernel, rank), sds(total.shape, F32), [], "join"
        )(*parts)
    for c in range(1, len(widths)):
        last, total = after(newest[c], total)
        newest[c] = step(last)

    terms = len(LEFT_TERMS) * rank
    whole, left_terms, right_terms = call(
        functools.partial(factor_kernel, m),
        [sds((rank, width), F32), sds((rows, terms), BF16), sds((terms, width), BF16)],
        [
            pltpu.VMEM((2, rank, half + 128), F32),
            pltpu.VMEM((rank, rows), F32),
            pltpu.VMEM((terms, rows), F32),
            pltpu.VMEM((terms, width), F32),
        ],
        "factor",
    )(mean, total, swap(total, "dp", m, 1))

    acts = call(
        functools.partial(acts_kernel, n),
        sds((rows, tokens), BF16),
        [pltpu.VMEM((tokens, rows), BF16)],
        "acts",
    )(activations)
    pieces = []
    at = 0
    for part, x in zip(widths, newest):
        pieces.append((at, part, ring + [x], [0] * (n - 1) + [at]))
        at += part

    outs = ()
    for at, part, slots, bases in pieces:
        outs = pl.pallas_call(
            functools.partial(final_kernel, at, part, bases),
            in_specs=[vmem] * (4 + n) + [pl.BlockSpec(memory_space=pl.ANY)] * len(outs),
            out_specs=[pl.BlockSpec(memory_space=pl.ANY)] * 2,
            out_shape=[sds((rows, width), BF16), sds((1, rows, width), BF16)],
            input_output_aliases={4 + n + j: j for j in range(len(outs))},
            scratch_shapes=[pltpu.VMEM((rows, part), BF16)] * 2 + [dma((3, 2))],
            compiler_params=params(16),
            cost_estimate=cost(0),
            name="rebuild",
        )(acts, left_terms, right_terms, error_v, *slots, *outs)
    rebuilt, error = outs
    return rebuilt, error, whole.T


def solution(mesh):
    return jax.shard_map(
        per_device,
        mesh=mesh,
        in_specs=(P("dp", None, "tensor"), P("dp", "tensor", None), P("dp", "tensor", None), P()),
        out_specs=(P("tensor", None), P("dp", "tensor", None), P()),
        check_vma=False,
    )
```

```python
import functools

import jax
import jax.numpy as jnp
from jax import lax
from jax.experimental import pallas as pl
from jax.experimental.pallas import tpu as pltpu
from jax.sharding import PartitionSpec as P

F32 = jnp.float32
BF16 = jnp.bfloat16
SHRINK = 2.0**-23
TINY = 1e-30
ROOM = 2.0**14
BLOCK = 512


def params(mib):
    return pltpu.CompilerParams(vmem_limit_bytes=mib * 2**20)


def cost(flops):
    return pl.CostEstimate(flops=int(flops) + 1, bytes_accessed=1, transcendentals=0)


def dot(a, b, contract):
    return lax.dot_general(a, b, ((contract[:1], contract[1:]), ((), ())), preferred_element_type=F32)


def split(x):
    hi = x.astype(BF16)
    rest = x - hi.astype(F32)
    mid = rest.astype(BF16)
    lo = (rest - mid.astype(F32)).astype(BF16)
    return hi.astype(F32), mid.astype(F32), lo.astype(F32)


def stack3(x, ref):
    rank = x.shape[0]
    for i, part in enumerate(split(x)):
        ref[i * rank : (i + 1) * rank, :] = part
    return ref[...].astype(BF16)


def sum3(y, rank):
    return (y[2 * rank :] + y[rank : 2 * rank]) + y[:rank]


def ring_of(n):
    return [2 * p if 2 * p < n else 2 * (n - p) - 1 for p in range(n)]


def ring_source(me, step, n):
    place = jnp.where(lax.rem(me, 2) == 0, me // 2, n - (me + 1) // 2)
    place = lax.rem(place - step + n, n)
    return jnp.where(2 * place < n, 2 * place, 2 * (n - place) - 1)


def ring_step(x, axis, n):
    ring = ring_of(n)
    return lax.ppermute(x, axis, [(ring[p], ring[(p + 1) % n]) for p in range(n)])


def exchange(pieces, axis, n):
    return [pieces[0]] + [
        lax.ppermute(pieces[k], axis, [(i, (i + k) % n) for i in range(n)]) for k in range(1, n)
    ]


def swap(x, axis, n, bit):
    return lax.ppermute(x, axis, [(i, i ^ bit) for i in range(n)])


def groups(n):
    assert n & (n - 1) == 0
    bits = [1 << i for i in range(n.bit_length() - 1)]
    return [bits[i : i + 2] for i in range(0, len(bits), 2)]


def terms_of(x, axis, n, group):
    others = group if len(group) == 1 else [group[0], group[1], group[0] | group[1]]
    return [x] + [swap(x, axis, n, bit) for bit in others]


def total_of(refs):
    total = refs[0][...] + refs[1][...]
    if len(refs) == 4:
        total = total + (refs[2][...] + refs[3][...])
    return total


def token_factor_kernel(w_hbm, g_hbm, gw_ref, terms_ref, w, g, w3, sems):
    rank = w.shape[0]
    copies = [
        pltpu.make_async_copy(w_hbm, w, sems.at[0]),
        pltpu.make_async_copy(g_hbm, g, sems.at[1]),
    ]
    for copy in copies:
        copy.start()
    copies[0].wait()
    terms = stack3(w[...] * SHRINK, w3)
    terms_ref[...] = terms
    copies[1].wait()
    gw_ref[...] = jnp.zeros_like(gw_ref)
    gw_ref[0:rank, 0 : g.shape[1]] = sum3(dot(terms, g[0], (1, 1)), rank)


def cut_kernel(x_ref, *refs):
    chunks, sems = refs[:-1], refs[-1]
    copies = []
    at = 0
    for c, chunk in enumerate(chunks):
        part = chunk.shape[2]
        copies.append(pltpu.make_async_copy(x_ref.at[:, :, pl.ds(at, part)], chunk, sems.at[c]))
        copies[-1].start()
        at += part
    for copy in copies:
        copy.wait()


def error_left_kernel(terms_ref, e_hbm, out_ref, e_ref, sems):
    rank = out_ref.shape[0]
    count = sems.shape[0]
    high = e_ref.shape[1] // count
    copies = []
    for c in range(count):
        rows = pl.ds(c * high, high)
        copies.append(pltpu.make_async_copy(e_hbm.at[:, rows, :], e_ref.at[:, rows, :], sems.at[c]))
        copies[-1].start()
    terms = terms_ref[...]
    for c in range(count):
        copies[c].wait()
        rows = slice(c * high, (c + 1) * high)
        out_ref[:, rows] = sum3(dot(terms, e_ref[0, rows, :], (1, 1)), rank)


def left_kernel(a_ref, e_ref, *refs):
    gws, out_ref, g3 = refs[:-2], refs[-2], refs[-1]
    n = len(gws)
    rank = e_ref.shape[0]
    tok = a_ref.shape[1] // n
    me = lax.axis_index("tensor")
    total = e_ref[...]
    for k in range(n):
        src = lax.rem(me - k + n, n)
        rows = a_ref[0, pl.ds(pl.multiple_of(src * tok, tok), tok), :]
        total += sum3(dot(stack3(gws[k][0:rank, 0:tok], g3), rows, (1, 0)), rank)
    out_ref[...] = total


def mean_kernel(n, scale, a_ref, *refs):
    terms = refs[:-7]
    p_ref, scaled_ref, extra_ref, held_ref, next_ref, p3, blocks = refs[-7:]
    rank = p_ref.shape[0]
    tok = a_ref.shape[1] // n
    me = lax.axis_index("tensor")
    mean = total_of(terms) * scale
    p_ref[...] = mean
    top = jnp.max(jnp.max(jnp.abs(mean), axis=1, keepdims=True), axis=0, keepdims=True)
    top = jnp.maximum(top, TINY)
    scaled = mean / (top * ROOM)
    scaled_ref[...] = scaled
    parts = stack3(scaled, p3)
    for t in range(n):
        blocks[t] = sum3(dot(parts, a_ref[0, t * tok : (t + 1) * tok, :], (1, 1)), rank)
    for s in range(n - 1):
        held_ref[:, s * tok : (s + 1) * tok] = blocks[ring_source(me, s, n)]
    next_ref[...] = jnp.zeros_like(next_ref)
    next_ref[0:rank, 0:tok] = blocks[ring_source(me, n - 1, n)]
    next_ref[rank : rank + 1, 0:1] = top
    extra_ref[...] = jnp.zeros_like(extra_ref)
    for i in range(rank):
        extra_ref[:, i : i + 1] = jnp.sum(mean * mean[i : i + 1, :], axis=1, keepdims=True)
    extra_ref[:, rank : rank + 1] = jnp.broadcast_to(top, (rank, 1))


def error_right_kernel(p_ref, e_ref, out_ref, p3):
    rank = p_ref.shape[0]
    parts = stack3(p_ref[...], p3)
    for c in range(e_ref.shape[2] // BLOCK):
        cols = slice(c * BLOCK, (c + 1) * BLOCK)
        out_ref[:, cols] = sum3(dot(parts, e_ref[0, :, cols], (1, 0)), rank)


def lower_inverse(gram, rank):
    at = lambda i, j: gram[i : i + 1, j : j + 1]
    low = {}
    for j in range(rank):
        d = at(j, j)
        for k in range(j):
            d = d - low[j, k] * low[j, k]
        low[j, j] = jnp.sqrt(d)
        for i in range(j + 1, rank):
            v = at(i, j)
            for k in range(j):
                v = v - low[i, k] * low[j, k]
            low[i, j] = v / low[j, j]
    inv = {}
    for j in range(rank):
        inv[j, j] = 1.0 / low[j, j]
        for i in range(j + 1, rank):
            v = low[i, j] * inv[j, j]
            for k in range(j + 1, i):
                v = v + low[i, k] * inv[k, j]
            inv[i, j] = -v / low[i, i]
    return inv


def solve(inv, x, rank):
    total = 0.0
    for j in range(rank):
        column = [inv.get((i, j), jnp.zeros((1, 1), F32)) for i in range(rank)]
        total = total + jnp.concatenate(column, axis=0) * x[j : j + 1, :]
    return total


def right_kernel(r_ref, y_ref, got_ref, extra_ref, *refs):
    held, (keep_ref, send_ref, y3, outbox) = refs[:-4], refs[-4:]
    rank = r_ref.shape[0]
    tok = held[0].shape[1]
    half = r_ref.shape[1] // 2
    core = lax.rem(lax.axis_index("dp"), 2)
    mine = extra_ref[0:1, rank : rank + 1]
    theirs = got_ref[rank : rank + 1, 0:1]
    top = jnp.maximum(mine, theirs)
    products = y_ref[...] * (mine / top)
    joint = products[:, 0:tok] + got_ref[0:rank, 0:tok] * (theirs / top)
    terms = stack3(jnp.concatenate([joint, products[:, tok:]], axis=1), y3)
    for h in range(2):
        for c in range(half // BLOCK):
            at = h * half + c * BLOCK
            cols = slice(at, at + BLOCK)
            grads = jnp.concatenate([g[0, :, cols] for g in held], axis=0)
            fresh = sum3(dot(terms, grads, (1, 0)), rank)
            outbox[h, :, c * BLOCK : (c + 1) * BLOCK] = r_ref[:, cols] * (mine / top) + fresh
        outbox[h, :, half:] = extra_ref[...]
        outbox[h, :, half + rank : half + rank + 1] = jnp.broadcast_to(top, (rank, 1))
    keep_ref[...] = outbox[core]
    send_ref[...] = outbox[1 - core]


def join_kernel(rank, *refs):
    xs, out_ref = refs[:-1], refs[-1]
    half = out_ref.shape[1] - 128
    mark = slice(half + rank, half + rank + 1)
    tops = [x[0:1, mark] for x in xs]
    top = jnp.maximum(tops[0], tops[1])
    for other in tops[2:]:
        top = jnp.maximum(top, other)

    def total(terms):
        first = terms[0] + terms[1]
        return first + (terms[2] + terms[3]) if len(terms) == 4 else first

    out_ref[:, :half] = total([x[:, :half] * (t / top) for x, t in zip(xs, tops)])
    out_ref[:, half:] = total([x[:, half:] for x in xs])
    out_ref[:, mark] = jnp.broadcast_to(top, (rank, 1))


def add_kernel(*refs):
    refs[-1][...] = total_of(refs[:-1])


LEFT_TERMS = (0, 0, 1, 0, 2, 1)
RIGHT_TERMS = (0, 1, 0, 2, 0, 1)


def factor_kernel(m, p_ref, mine_ref, other_ref, whole_ref, left_ref, right_ref, inbox, ortho, left, right):
    rank = mine_ref.shape[0]
    half = mine_ref.shape[1] - 128
    core = lax.rem(lax.axis_index("dp"), 2)
    inbox[core] = mine_ref[...]
    inbox[1 - core] = other_ref[...]
    inv = lower_inverse(inbox[0, :, half : half + rank] * (1.0 / m), rank)
    top = inbox[0, 0:1, half + rank : half + rank + 1] * (ROOM / (m * m))
    scaled = {key: value * top for key, value in inv.items()}
    ortho[...] = solve(inv, p_ref[...], rank)
    for h in range(2):
        whole_ref[:, h * half : (h + 1) * half] = solve(scaled, inbox[h, :, 0:half], rank)
    for terms, x, ref in (
        (LEFT_TERMS, ortho[...], left),
        (RIGHT_TERMS, whole_ref[...], right),
    ):
        parts = split(x)
        for i, term in enumerate(terms):
            ref[i * rank : (i + 1) * rank, :] = parts[term]
    left_ref[...] = left[...].T.astype(BF16)
    right_ref[...] = right[...].astype(BF16)


def acts_kernel(n, a_ref, out_ref, acts):
    tok = a_ref.shape[1] // n
    me = lax.axis_index("tensor")
    for s in range(n):
        src = ring_source(me, s, n)
        here = a_ref[0, pl.ds(pl.multiple_of(src * tok, tok), tok), :]
        acts[s * tok : (s + 1) * tok, :] = here
    out_ref[...] = acts[...].T


def final_kernel(at, part, bases, acts_ref, left_ref, right_ref, e_ref, *refs):
    slots = refs[: len(bases)]
    rebuilt_hbm, error_hbm, rebuilt_v, error_v, sems = refs[-5:]
    rows = e_ref.shape[1]
    wide = 256
    strips, sides, _ = sems.shape
    high = rows // strips
    side = part // sides
    copies = []
    for r in range(strips):
        here = slice(r * high, (r + 1) * high)
        for c in range(part // wide):
            cols = slice(c * wide, (c + 1) * wide)
            there = slice(at + c * wide, at + (c + 1) * wide)
            grads = [
                slot[0, :, there.start - base : there.stop - base]
                for slot, base in zip(slots, bases)
            ]
            grad = dot(acts_ref[here, :], jnp.concatenate(grads, axis=0), (1, 0))
            matrix = grad + e_ref[0, here, there].astype(F32)
            rebuilt = dot(left_ref[here, :], right_ref[:, there], (1, 0))
            rebuilt_v[here, cols] = rebuilt.astype(BF16)
            error_v[here, cols] = (matrix - rebuilt).astype(BF16)
            if (c + 1) * wide % side == 0:
                k = c * wide // side
                strip = pl.ds(r * high, high)
                near = rebuilt_v.at[strip, pl.ds(k * side, side)]
                far = rebuilt_hbm.at[strip, pl.ds(at + k * side, side)]
                copies.append(pltpu.make_async_copy(near, far, sems.at[r, k, 0]))
                near = error_v.at[strip, pl.ds(k * side, side)]
                far = error_hbm.at[0, strip, pl.ds(at + k * side, side)]
                copies.append(pltpu.make_async_copy(near, far, sems.at[r, k, 1]))
                copies[-2].start()
                copies[-1].start()
    for copy in copies:
        copy.wait()


def per_device(activations, out_grads, error_buffer, warm_factor):
    m = lax.axis_size("dp")
    n = lax.axis_size("tensor")
    _, tokens, rows = activations.shape
    _, tok, width = out_grads.shape
    rank = warm_factor.shape[1]
    half = width // 2
    w = warm_factor.T
    sds = jax.ShapeDtypeStruct
    hbm = pl.BlockSpec(memory_space=pltpu.HBM)
    vmem = pl.BlockSpec(memory_space=pltpu.VMEM)
    dma = pltpu.SemaphoreType.DMA
    pin = lambda x: pltpu.with_memory_space_constraint(x, pltpu.HBM)

    def call(kernel, shapes, scratch, name, specs=None, flops=0):
        return pl.pallas_call(
            kernel,
            out_shape=shapes,
            **({"in_specs": specs} if specs else {}),
            scratch_shapes=scratch,
            compiler_params=params(16),
            cost_estimate=cost(flops),
            name=name,
        )

    def add(*terms):
        return call(add_kernel, sds(terms[0].shape, F32), [], "add")(*terms)

    def after(x, y):
        return lax.optimization_barrier((x, y))

    def cut(x, widths):
        shapes = [sds((1, tok, part), BF16) for part in widths]
        return call(cut_kernel, shapes, [dma((len(widths),))], "cut")(x)

    def step(x):
        return ring_step(x, "tensor", n)

    ring = [out_grads, step(out_grads)]

    gw, w_terms = call(
        token_factor_kernel,
        [sds((8, 128), F32), sds((3 * rank, width), BF16)],
        [
            pltpu.VMEM((rank, width), F32),
            pltpu.VMEM((1, tok, width), BF16),
            pltpu.VMEM((3 * rank, width), F32),
            dma((2,)),
        ],
        "token_factor", [hbm, hbm],
    )(pin(w), pin(out_grads))
    ew, error_v = call(
        error_left_kernel,
        [sds((rank, rows), F32), sds((1, rows, width), BF16)],
        [dma((rows // 128,))],
        "error_left", [vmem, hbm], 4.6e9,
    )(w_terms, pin(error_buffer))

    gw, ew = after(gw, ew)
    gws = exchange([gw] * n, "tensor", n)
    ring[1], gws = after(ring[1], gws)
    for _ in range(n - 2 - 1):
        ring.append(step(ring[-1]))
    left = call(
        left_kernel, sds((rank, rows), F32), [pltpu.VMEM((3 * rank, tok), F32)], "left"
    )(activations, ew, *gws)
    left = add(left, swap(left, "dp", m, 1))
    for group in groups(m // 2)[:-1]:
        left = add(*terms_of(left, "dp", m, [2 * bit for bit in group]))
    lefts = terms_of(left, "dp", m, [2 * bit for bit in groups(m // 2)[-1]])
    mean, scaled, extra, held, following = call(
        functools.partial(mean_kernel, n, 1.0 / (SHRINK * m)),
        [
            sds((rank, rows), F32),
            sds((rank, rows), F32),
            sds((rank, 128), F32),
            sds((rank, (n - 1) * tok), F32),
            sds((8, 128), F32),
        ],
        [pltpu.VMEM((3 * rank, rows), F32), pltpu.VMEM((n, rank, tok), F32)],
        "mean",
    )(activations, *lefts)
    got = step(following)

    right_raw = call(
        error_right_kernel,
        sds((rank, width), F32),
        [pltpu.VMEM((3 * rank, rows), F32)],
        "error_right", None, 1.2e9,
    )(scaled, error_v)

    keep, send = call(
        right_kernel,
        [sds((rank, half + 128), F32)] * 2,
        [
            pltpu.VMEM((3 * rank, (n - 1) * tok), F32),
            pltpu.VMEM((2, rank, half + 128), F32),
        ],
        "right",
    )(right_raw, held, got, extra, *ring)
    total = add(keep, swap(send, "dp", m, 1))

    widths = [width * 3 // 5, width * 2 // 5]
    last, total = after(ring[-1], total)
    newest = list(cut(last, widths))
    newest[0] = step(newest[0])
    for group in groups(m // 2):
        total = add(*terms_of(total, "dp", m, [2 * bit for bit in group]))
    newest[0], total = after(newest[0], total)
    for group in groups(n):
        parts = terms_of(total, "tensor", n, group)
        total = call(
            functools.partial(join_kernel, rank), sds(total.shape, F32), [], "join"
        )(*parts)
    for c in range(1, len(widths)):
        last, total = after(newest[c], total)
        newest[c] = step(last)

    terms = len(LEFT_TERMS) * rank
    whole, left_terms, right_terms = call(
        functools.partial(factor_kernel, m),
        [sds((rank, width), F32), sds((rows, terms), BF16), sds((terms, width), BF16)],
        [
            pltpu.VMEM((2, rank, half + 128), F32),
            pltpu.VMEM((rank, rows), F32),
            pltpu.VMEM((terms, rows), F32),
            pltpu.VMEM((terms, width), F32),
        ],
        "factor",
    )(mean, total, swap(total, "dp", m, 1))

    acts = call(
        functools.partial(acts_kernel, n),
        sds((rows, tokens), BF16),
        [pltpu.VMEM((tokens, rows), BF16)],
        "acts",
    )(activations)
    pieces = []
    at = 0
    for part, x in zip(widths, newest):
        pieces.append((at, part, ring + [x], [0] * (n - 1) + [at]))
        at += part

    outs = ()
    for at, part, slots, bases in pieces:
        outs = pl.pallas_call(
            functools.partial(final_kernel, at, part, bases),
            in_specs=[vmem] * (4 + n) + [pl.BlockSpec(memory_space=pl.ANY)] * len(outs),
            out_specs=[pl.BlockSpec(memory_space=pl.ANY)] * 2,
            out_shape=[sds((rows, width), BF16), sds((1, rows, width), BF16)],
            input_output_aliases={4 + n + j: j for j in range(len(outs))},
            scratch_shapes=[pltpu.VMEM((rows, part), BF16)] * 2 + [dma((3, 2, 2))],
            compiler_params=params(16),
            cost_estimate=cost(0),
            name="rebuild",
        )(acts, left_terms, right_terms, error_v, *slots, *outs)
    rebuilt, error = outs
    return rebuilt, error, whole.T


def solution(mesh):
    return jax.shard_map(
        per_device,
        mesh=mesh,
        in_specs=(P("dp", None, "tensor"), P("dp", "tensor", None), P("dp", "tensor", None), P()),
        out_specs=(P("tensor", None), P("dp", "tensor", None), P()),
        check_vma=False,
    )
```

```python
import functools

import jax
import jax.numpy as jnp
from jax import lax
from jax.experimental import pallas as pl
from jax.experimental.pallas import tpu as pltpu
from jax.sharding import PartitionSpec as P

F32 = jnp.float32
BF16 = jnp.bfloat16
SHRINK = 2.0**-23
TINY = 1e-30
REBUILD = 4e9
ROOM = 2.0**14
BLOCK = 512


def params(mib):
    return pltpu.CompilerParams(vmem_limit_bytes=mib * 2**20)


def cost(flops):
    return pl.CostEstimate(flops=int(flops) + 1, bytes_accessed=1, transcendentals=0)


def dot(a, b, contract):
    return lax.dot_general(a, b, ((contract[:1], contract[1:]), ((), ())), preferred_element_type=F32)


def split(x):
    hi = x.astype(BF16)
    rest = x - hi.astype(F32)
    mid = rest.astype(BF16)
    lo = (rest - mid.astype(F32)).astype(BF16)
    return hi.astype(F32), mid.astype(F32), lo.astype(F32)


def stack3(x, ref):
    rank = x.shape[0]
    for i, part in enumerate(split(x)):
        ref[i * rank : (i + 1) * rank, :] = part
    return ref[...].astype(BF16)


def sum3(y, rank):
    return (y[2 * rank :] + y[rank : 2 * rank]) + y[:rank]


def ring_of(n):
    return [2 * p if 2 * p < n else 2 * (n - p) - 1 for p in range(n)]


def ring_source(me, step, n):
    place = jnp.where(lax.rem(me, 2) == 0, me // 2, n - (me + 1) // 2)
    place = lax.rem(place - step + n, n)
    return jnp.where(2 * place < n, 2 * place, 2 * (n - place) - 1)


def ring_step(x, axis, n):
    ring = ring_of(n)
    return lax.ppermute(x, axis, [(ring[p], ring[(p + 1) % n]) for p in range(n)])


def exchange(pieces, axis, n):
    return [pieces[0]] + [
        lax.ppermute(pieces[k], axis, [(i, (i + k) % n) for i in range(n)]) for k in range(1, n)
    ]


def swap(x, axis, n, bit):
    return lax.ppermute(x, axis, [(i, i ^ bit) for i in range(n)])


def groups(n):
    assert n & (n - 1) == 0
    bits = [1 << i for i in range(n.bit_length() - 1)]
    return [bits[i : i + 2] for i in range(0, len(bits), 2)]


def terms_of(x, axis, n, group):
    others = group if len(group) == 1 else [group[0], group[1], group[0] | group[1]]
    return [x] + [swap(x, axis, n, bit) for bit in others]


def total_of(refs):
    total = refs[0][...] + refs[1][...]
    if len(refs) == 4:
        total = total + (refs[2][...] + refs[3][...])
    return total


def token_factor_kernel(w_hbm, g_hbm, gw_ref, terms_ref, w, g, w3, sems):
    rank = w.shape[0]
    copies = [
        pltpu.make_async_copy(w_hbm, w, sems.at[0]),
        pltpu.make_async_copy(g_hbm, g, sems.at[1]),
    ]
    for copy in copies:
        copy.start()
    copies[0].wait()
    terms = stack3(w[...] * SHRINK, w3)
    terms_ref[...] = terms
    copies[1].wait()
    gw_ref[...] = jnp.zeros_like(gw_ref)
    gw_ref[0:rank, 0 : g.shape[1]] = sum3(dot(terms, g[0], (1, 1)), rank)


def cut_kernel(x_ref, *refs):
    chunks, sems = refs[:-1], refs[-1]
    copies = []
    at = 0
    for c, chunk in enumerate(chunks):
        part = chunk.shape[2]
        copies.append(pltpu.make_async_copy(x_ref.at[:, :, pl.ds(at, part)], chunk, sems.at[c]))
        copies[-1].start()
        at += part
    for copy in copies:
        copy.wait()


def error_left_kernel(terms_ref, e_hbm, out_ref, e_ref, sems):
    rank = out_ref.shape[0]
    count = sems.shape[0]
    high = e_ref.shape[1] // count
    copies = []
    for c in range(count):
        rows = pl.ds(c * high, high)
        copies.append(pltpu.make_async_copy(e_hbm.at[:, rows, :], e_ref.at[:, rows, :], sems.at[c]))
        copies[-1].start()
    terms = terms_ref[...]
    for c in range(count):
        copies[c].wait()
        rows = slice(c * high, (c + 1) * high)
        out_ref[:, rows] = sum3(dot(terms, e_ref[0, rows, :], (1, 1)), rank)


def left_kernel(a_ref, e_ref, *refs):
    gws, out_ref, g3 = refs[:-2], refs[-2], refs[-1]
    n = len(gws)
    rank = e_ref.shape[0]
    tok = a_ref.shape[1] // n
    me = lax.axis_index("tensor")
    total = e_ref[...]
    for k in range(n):
        src = lax.rem(me - k + n, n)
        rows = a_ref[0, pl.ds(pl.multiple_of(src * tok, tok), tok), :]
        total += sum3(dot(stack3(gws[k][0:rank, 0:tok], g3), rows, (1, 0)), rank)
    out_ref[...] = total


def mean_kernel(n, scale, a_ref, *refs):
    terms = refs[:-7]
    p_ref, scaled_ref, extra_ref, held_ref, next_ref, p3, blocks = refs[-7:]
    rank = p_ref.shape[0]
    tok = a_ref.shape[1] // n
    me = lax.axis_index("tensor")
    mean = total_of(terms) * scale
    p_ref[...] = mean
    top = jnp.max(jnp.max(jnp.abs(mean), axis=1, keepdims=True), axis=0, keepdims=True)
    top = jnp.maximum(top, TINY)
    scaled = mean / (top * ROOM)
    scaled_ref[...] = scaled
    parts = stack3(scaled, p3)
    for t in range(n):
        blocks[t] = sum3(dot(parts, a_ref[0, t * tok : (t + 1) * tok, :], (1, 1)), rank)
    for s in range(n - 1):
        held_ref[:, s * tok : (s + 1) * tok] = blocks[ring_source(me, s, n)]
    next_ref[...] = jnp.zeros_like(next_ref)
    next_ref[0:rank, 0:tok] = blocks[ring_source(me, n - 1, n)]
    next_ref[rank : rank + 1, 0:1] = top
    extra_ref[...] = jnp.zeros_like(extra_ref)
    for i in range(rank):
        extra_ref[:, i : i + 1] = jnp.sum(mean * mean[i : i + 1, :], axis=1, keepdims=True)
    extra_ref[:, rank : rank + 1] = jnp.broadcast_to(top, (rank, 1))


def error_right_kernel(p_ref, e_ref, out_ref, p3):
    rank = p_ref.shape[0]
    parts = stack3(p_ref[...], p3)
    for c in range(e_ref.shape[2] // BLOCK):
        cols = slice(c * BLOCK, (c + 1) * BLOCK)
        out_ref[:, cols] = sum3(dot(parts, e_ref[0, :, cols], (1, 0)), rank)


def lower_inverse(gram, rank):
    at = lambda i, j: gram[i : i + 1, j : j + 1]
    low, inv = {}, {}
    for j in range(rank):
        d = at(j, j)
        for k in range(j):
            d = d - low[j, k] * low[j, k]
        inv[j, j] = lax.rsqrt(d)
        for i in range(j + 1, rank):
            v = at(i, j)
            for k in range(j):
                v = v - low[i, k] * low[j, k]
            low[i, j] = v * inv[j, j]
    for j in range(rank):
        for i in range(j + 1, rank):
            v = low[i, j] * inv[j, j]
            for k in range(j + 1, i):
                v = v + low[i, k] * inv[k, j]
            inv[i, j] = -v * inv[i, i]
    return inv


def solve(inv, x, rank):
    total = 0.0
    for j in range(rank):
        column = [inv.get((i, j), jnp.zeros((1, 1), F32)) for i in range(rank)]
        total = total + jnp.concatenate(column, axis=0) * x[j : j + 1, :]
    return total


def right_kernel(r_ref, y_ref, got_ref, extra_ref, *refs):
    held, (keep_ref, send_ref, y3, outbox) = refs[:-4], refs[-4:]
    rank = r_ref.shape[0]
    tok = held[0].shape[1]
    half = r_ref.shape[1] // 2
    core = lax.rem(lax.axis_index("dp"), 2)
    mine = extra_ref[0:1, rank : rank + 1]
    theirs = got_ref[rank : rank + 1, 0:1]
    top = jnp.maximum(mine, theirs)
    products = y_ref[...] * (mine / top)
    joint = products[:, 0:tok] + got_ref[0:rank, 0:tok] * (theirs / top)
    terms = stack3(jnp.concatenate([joint, products[:, tok:]], axis=1), y3)
    for h in range(2):
        for c in range(half // BLOCK):
            at = h * half + c * BLOCK
            cols = slice(at, at + BLOCK)
            grads = jnp.concatenate([g[0, :, cols] for g in held], axis=0)
            fresh = sum3(dot(terms, grads, (1, 0)), rank)
            outbox[h, :, c * BLOCK : (c + 1) * BLOCK] = r_ref[:, cols] * (mine / top) + fresh
        outbox[h, :, half:] = extra_ref[...]
        outbox[h, :, half + rank : half + rank + 1] = jnp.broadcast_to(top, (rank, 1))
    keep_ref[...] = outbox[core]
    send_ref[...] = outbox[1 - core]


def join_kernel(rank, *refs):
    xs, out_ref = refs[:-1], refs[-1]
    half = out_ref.shape[1] - 128
    mark = slice(half + rank, half + rank + 1)
    tops = [x[0:1, mark] for x in xs]
    top = jnp.maximum(tops[0], tops[1])
    for other in tops[2:]:
        top = jnp.maximum(top, other)

    def total(terms):
        first = terms[0] + terms[1]
        return first + (terms[2] + terms[3]) if len(terms) == 4 else first

    out_ref[:, :half] = total([x[:, :half] * (t / top) for x, t in zip(xs, tops)])
    out_ref[:, half:] = total([x[:, half:] for x in xs])
    out_ref[:, mark] = jnp.broadcast_to(top, (rank, 1))


def add_kernel(*refs):
    refs[-1][...] = total_of(refs[:-1])


LEFT_TERMS = (0, 0, 1, 0, 2, 1)
RIGHT_TERMS = (0, 1, 0, 2, 0, 1)


def factor_kernel(m, p_ref, mine_ref, other_ref, whole_ref, left_ref, right_ref, inbox, ortho, left, right):
    rank = mine_ref.shape[0]
    half = mine_ref.shape[1] - 128
    core = lax.rem(lax.axis_index("dp"), 2)
    inbox[core] = mine_ref[...]
    inbox[1 - core] = other_ref[...]
    inv = lower_inverse(inbox[0, :, half : half + rank] * (1.0 / m), rank)
    top = inbox[0, 0:1, half + rank : half + rank + 1] * (ROOM / (m * m))
    scaled = {key: value * top for key, value in inv.items()}
    ortho[...] = solve(inv, p_ref[...], rank)
    for h in range(2):
        whole_ref[:, h * half : (h + 1) * half] = solve(scaled, inbox[h, :, 0:half], rank)
    for terms, x, ref in (
        (LEFT_TERMS, ortho[...], left),
        (RIGHT_TERMS, whole_ref[...], right),
    ):
        parts = split(x)
        for i, term in enumerate(terms):
            ref[i * rank : (i + 1) * rank, :] = parts[term]
    left_ref[...] = left[...].T.astype(BF16)
    right_ref[...] = right[...].astype(BF16)


def acts_kernel(n, a_ref, out_ref, acts):
    tok = a_ref.shape[1] // n
    me = lax.axis_index("tensor")
    for s in range(n):
        src = ring_source(me, s, n)
        here = a_ref[0, pl.ds(pl.multiple_of(src * tok, tok), tok), :]
        acts[s * tok : (s + 1) * tok, :] = here
    out_ref[...] = acts[...].T


def final_kernel(at, part, bases, acts_ref, left_ref, right_ref, e_ref, *refs):
    slots = refs[: len(bases)]
    rebuilt_hbm, error_hbm, rebuilt_v, error_v, sems = refs[-5:]
    rows = e_ref.shape[1]
    wide = 256
    strips, sides, _ = sems.shape
    high = rows // strips
    side = part // sides
    copies = []
    for r in range(strips):
        here = slice(r * high, (r + 1) * high)
        for c in range(part // wide):
            cols = slice(c * wide, (c + 1) * wide)
            there = slice(at + c * wide, at + (c + 1) * wide)
            grads = [
                slot[0, :, there.start - base : there.stop - base]
                for slot, base in zip(slots, bases)
            ]
            grad = dot(acts_ref[here, :], jnp.concatenate(grads, axis=0), (1, 0))
            matrix = grad + e_ref[0, here, there].astype(F32)
            rebuilt = dot(left_ref[here, :], right_ref[:, there], (1, 0))
            rebuilt_v[here, cols] = rebuilt.astype(BF16)
            error_v[here, cols] = (matrix - rebuilt).astype(BF16)
            if (c + 1) * wide % side == 0:
                k = c * wide // side
                strip = pl.ds(r * high, high)
                near = rebuilt_v.at[strip, pl.ds(k * side, side)]
                far = rebuilt_hbm.at[strip, pl.ds(at + k * side, side)]
                copies.append(pltpu.make_async_copy(near, far, sems.at[r, k, 0]))
                near = error_v.at[strip, pl.ds(k * side, side)]
                far = error_hbm.at[0, strip, pl.ds(at + k * side, side)]
                copies.append(pltpu.make_async_copy(near, far, sems.at[r, k, 1]))
                copies[-2].start()
                copies[-1].start()
    for copy in copies:
        copy.wait()


def per_device(activations, out_grads, error_buffer, warm_factor):
    m = lax.axis_size("dp")
    n = lax.axis_size("tensor")
    _, tokens, rows = activations.shape
    _, tok, width = out_grads.shape
    rank = warm_factor.shape[1]
    half = width // 2
    w = warm_factor.T
    sds = jax.ShapeDtypeStruct
    hbm = pl.BlockSpec(memory_space=pltpu.HBM)
    vmem = pl.BlockSpec(memory_space=pltpu.VMEM)
    dma = pltpu.SemaphoreType.DMA
    pin = lambda x: pltpu.with_memory_space_constraint(x, pltpu.HBM)

    def call(kernel, shapes, scratch, name, specs=None, flops=0):
        return pl.pallas_call(
            kernel,
            out_shape=shapes,
            **({"in_specs": specs} if specs else {}),
            scratch_shapes=scratch,
            compiler_params=params(16),
            cost_estimate=cost(flops),
            name=name,
        )

    def add(*terms):
        return call(add_kernel, sds(terms[0].shape, F32), [], "add")(*terms)

    def after(x, y):
        return lax.optimization_barrier((x, y))

    def cut(x, widths):
        shapes = [sds((1, tok, part), BF16) for part in widths]
        return call(cut_kernel, shapes, [dma((len(widths),))], "cut")(x)

    def step(x):
        return ring_step(x, "tensor", n)

    ring = [out_grads, step(out_grads)]

    gw, w_terms = call(
        token_factor_kernel,
        [sds((8, 128), F32), sds((3 * rank, width), BF16)],
        [
            pltpu.VMEM((rank, width), F32),
            pltpu.VMEM((1, tok, width), BF16),
            pltpu.VMEM((3 * rank, width), F32),
            dma((2,)),
        ],
        "token_factor", [hbm, hbm],
    )(pin(w), pin(out_grads))
    ew, error_v = call(
        error_left_kernel,
        [sds((rank, rows), F32), sds((1, rows, width), BF16)],
        [dma((rows // 128,))],
        "error_left", [vmem, hbm], 4.6e9,
    )(w_terms, pin(error_buffer))

    gw, ew = after(gw, ew)
    gws = exchange([gw] * n, "tensor", n)
    ring[1], gws = after(ring[1], gws)
    for _ in range(n - 2 - 1):
        ring.append(step(ring[-1]))
    left = call(
        left_kernel, sds((rank, rows), F32), [pltpu.VMEM((3 * rank, tok), F32)], "left"
    )(activations, ew, *gws)
    left = add(left, swap(left, "dp", m, 1))
    for group in groups(m // 2)[:-1]:
        left = add(*terms_of(left, "dp", m, [2 * bit for bit in group]))
    lefts = terms_of(left, "dp", m, [2 * bit for bit in groups(m // 2)[-1]])
    mean, scaled, extra, held, following = call(
        functools.partial(mean_kernel, n, 1.0 / (SHRINK * m)),
        [
            sds((rank, rows), F32),
            sds((rank, rows), F32),
            sds((rank, 128), F32),
            sds((rank, (n - 1) * tok), F32),
            sds((8, 128), F32),
        ],
        [pltpu.VMEM((3 * rank, rows), F32), pltpu.VMEM((n, rank, tok), F32)],
        "mean",
    )(activations, *lefts)
    got = step(following)

    right_raw = call(
        error_right_kernel,
        sds((rank, width), F32),
        [pltpu.VMEM((3 * rank, rows), F32)],
        "error_right", None, 1.2e9,
    )(scaled, error_v)

    widths = [width * 3 // 5, width * 2 // 5]
    last, (got, right_raw) = after(ring[-1], (got, right_raw))
    newest = list(cut(last, widths))
    newest[0] = step(newest[0])

    keep, send = call(
        right_kernel,
        [sds((rank, half + 128), F32)] * 2,
        [
            pltpu.VMEM((3 * rank, (n - 1) * tok), F32),
            pltpu.VMEM((2, rank, half + 128), F32),
        ],
        "right",
    )(right_raw, held, got, extra, *ring)
    total = add(keep, swap(send, "dp", m, 1))

    for group in groups(m // 2):
        total = add(*terms_of(total, "dp", m, [2 * bit for bit in group]))
    newest[0], total = after(newest[0], total)
    for group in groups(n):
        parts = terms_of(total, "tensor", n, group)
        total = call(
            functools.partial(join_kernel, rank), sds(total.shape, F32), [], "join"
        )(*parts)
    for c in range(1, len(widths)):
        last, total = after(newest[c], total)
        newest[c] = step(last)

    terms = len(LEFT_TERMS) * rank
    whole, left_terms, right_terms = call(
        functools.partial(factor_kernel, m),
        [sds((rank, width), F32), sds((rows, terms), BF16), sds((terms, width), BF16)],
        [
            pltpu.VMEM((2, rank, half + 128), F32),
            pltpu.VMEM((rank, rows), F32),
            pltpu.VMEM((terms, rows), F32),
            pltpu.VMEM((terms, width), F32),
        ],
        "factor",
    )(mean, total, swap(total, "dp", m, 1))

    acts = call(
        functools.partial(acts_kernel, n),
        sds((rows, tokens), BF16),
        [pltpu.VMEM((tokens, rows), BF16)],
        "acts",
    )(activations)
    pieces = []
    at = 0
    for part, x in zip(widths, newest):
        pieces.append((at, part, ring + [x], [0] * (n - 1) + [at]))
        at += part

    outs = ()
    for at, part, slots, bases in pieces:
        outs = pl.pallas_call(
            functools.partial(final_kernel, at, part, bases),
            in_specs=[vmem] * (4 + n) + [pl.BlockSpec(memory_space=pl.ANY)] * len(outs),
            out_specs=[pl.BlockSpec(memory_space=pl.ANY)] * 2,
            out_shape=[sds((rows, width), BF16), sds((1, rows, width), BF16)],
            input_output_aliases={4 + n + j: j for j in range(len(outs))},
            scratch_shapes=[pltpu.VMEM((rows, part), BF16)] * 2 + [dma((3, 2, 2))],
            compiler_params=params(16),
            cost_estimate=cost(REBUILD),
            name="rebuild",
        )(acts, left_terms, right_terms, error_v, *slots, *outs)
    rebuilt, error = outs
    return rebuilt, error, whole.T


def solution(mesh):
    return jax.shard_map(
        per_device,
        mesh=mesh,
        in_specs=(P("dp", None, "tensor"), P("dp", "tensor", None), P("dp", "tensor", None), P()),
        out_specs=(P("tensor", None), P("dp", "tensor", None), P()),
        check_vma=False,
    )
```

```python
import functools

import jax
import jax.numpy as jnp
from jax import lax
from jax.experimental import pallas as pl
from jax.experimental.pallas import tpu as pltpu
from jax.sharding import PartitionSpec as P

F32 = jnp.float32
BF16 = jnp.bfloat16
SHRINK = 2.0**-23
TINY = 1e-30
REBUILD = 4e9
ROOM = 2.0**14
BLOCK = 512


def params(mib):
    return pltpu.CompilerParams(vmem_limit_bytes=mib * 2**20)


def cost(flops):
    return pl.CostEstimate(flops=int(flops) + 1, bytes_accessed=1, transcendentals=0)


def dot(a, b, contract):
    return lax.dot_general(a, b, ((contract[:1], contract[1:]), ((), ())), preferred_element_type=F32)


def split(x):
    hi = x.astype(BF16)
    rest = x - hi.astype(F32)
    mid = rest.astype(BF16)
    lo = (rest - mid.astype(F32)).astype(BF16)
    return hi.astype(F32), mid.astype(F32), lo.astype(F32)


def stack3(x, ref):
    rank = x.shape[0]
    for i, part in enumerate(split(x)):
        ref[i * rank : (i + 1) * rank, :] = part
    return ref[...].astype(BF16)


def sum3(y, rank):
    return (y[2 * rank :] + y[rank : 2 * rank]) + y[:rank]


def ring_of(n):
    return [2 * p if 2 * p < n else 2 * (n - p) - 1 for p in range(n)]


def ring_source(me, step, n):
    place = jnp.where(lax.rem(me, 2) == 0, me // 2, n - (me + 1) // 2)
    place = lax.rem(place - step + n, n)
    return jnp.where(2 * place < n, 2 * place, 2 * (n - place) - 1)


def ring_step(x, axis, n):
    ring = ring_of(n)
    return lax.ppermute(x, axis, [(ring[p], ring[(p + 1) % n]) for p in range(n)])


def exchange(pieces, axis, n):
    return [pieces[0]] + [
        lax.ppermute(pieces[k], axis, [(i, (i + k) % n) for i in range(n)]) for k in range(1, n)
    ]


def swap(x, axis, n, bit):
    return lax.ppermute(x, axis, [(i, i ^ bit) for i in range(n)])


def groups(n):
    assert n & (n - 1) == 0
    bits = [1 << i for i in range(n.bit_length() - 1)]
    return [bits[i : i + 2] for i in range(0, len(bits), 2)]


def terms_of(x, axis, n, group):
    others = group if len(group) == 1 else [group[0], group[1], group[0] | group[1]]
    return [x] + [swap(x, axis, n, bit) for bit in others]


def total_of(refs):
    total = refs[0][...] + refs[1][...]
    if len(refs) == 4:
        total = total + (refs[2][...] + refs[3][...])
    return total


def token_factor_kernel(w_hbm, g_hbm, gw_ref, terms_ref, w, g, w3, sems):
    rank = w.shape[0]
    copies = [
        pltpu.make_async_copy(w_hbm, w, sems.at[0]),
        pltpu.make_async_copy(g_hbm, g, sems.at[1]),
    ]
    for copy in copies:
        copy.start()
    copies[0].wait()
    terms = stack3(w[...] * SHRINK, w3)
    terms_ref[...] = terms
    copies[1].wait()
    gw_ref[...] = jnp.zeros_like(gw_ref)
    gw_ref[0:rank, 0 : g.shape[1]] = sum3(dot(terms, g[0], (1, 1)), rank)


def cut_kernel(x_ref, *refs):
    chunks, sems = refs[:-1], refs[-1]
    copies = []
    at = 0
    for c, chunk in enumerate(chunks):
        part = chunk.shape[2]
        copies.append(pltpu.make_async_copy(x_ref.at[:, :, pl.ds(at, part)], chunk, sems.at[c]))
        copies[-1].start()
        at += part
    for copy in copies:
        copy.wait()


def error_left_kernel(terms_ref, e_hbm, out_ref, e_ref, sems):
    rank = out_ref.shape[0]
    count = sems.shape[0]
    high = e_ref.shape[1] // count
    copies = []
    for c in range(count):
        rows = pl.ds(c * high, high)
        copies.append(pltpu.make_async_copy(e_hbm.at[:, rows, :], e_ref.at[:, rows, :], sems.at[c]))
        copies[-1].start()
    terms = terms_ref[...]
    for c in range(count):
        copies[c].wait()
        rows = slice(c * high, (c + 1) * high)
        out_ref[:, rows] = sum3(dot(terms, e_ref[0, rows, :], (1, 1)), rank)


def left_kernel(a_ref, e_ref, *refs):
    gws, out_ref, g3 = refs[:-2], refs[-2], refs[-1]
    n = len(gws)
    rank = e_ref.shape[0]
    tok = a_ref.shape[1] // n
    me = lax.axis_index("tensor")
    total = e_ref[...]
    for k in range(n):
        src = lax.rem(me - k + n, n)
        rows = a_ref[0, pl.ds(pl.multiple_of(src * tok, tok), tok), :]
        total += sum3(dot(stack3(gws[k][0:rank, 0:tok], g3), rows, (1, 0)), rank)
    out_ref[...] = total


def mean_kernel(n, scale, a_ref, *refs):
    terms = refs[:-7]
    p_ref, scaled_ref, extra_ref, held_ref, next_ref, p3, blocks = refs[-7:]
    rank = p_ref.shape[0]
    tok = a_ref.shape[1] // n
    me = lax.axis_index("tensor")
    mean = total_of(terms) * scale
    p_ref[...] = mean
    top = jnp.max(jnp.max(jnp.abs(mean), axis=1, keepdims=True), axis=0, keepdims=True)
    top = jnp.maximum(top, TINY)
    scaled = mean / (top * ROOM)
    scaled_ref[...] = scaled
    parts = stack3(scaled, p3)
    for t in range(n):
        blocks[t] = sum3(dot(parts, a_ref[0, t * tok : (t + 1) * tok, :], (1, 1)), rank)
    for s in range(n - 1):
        held_ref[:, s * tok : (s + 1) * tok] = blocks[ring_source(me, s, n)]
    next_ref[...] = jnp.zeros_like(next_ref)
    next_ref[0:rank, 0:tok] = blocks[ring_source(me, n - 1, n)]
    next_ref[rank : rank + 1, 0:1] = top
    extra_ref[...] = jnp.zeros_like(extra_ref)
    for i in range(rank):
        extra_ref[:, i : i + 1] = jnp.sum(mean * mean[i : i + 1, :], axis=1, keepdims=True)
    extra_ref[:, rank : rank + 1] = jnp.broadcast_to(top, (rank, 1))


def error_right_kernel(p_ref, e_ref, out_ref, p3):
    rank = p_ref.shape[0]
    parts = stack3(p_ref[...], p3)
    for c in range(e_ref.shape[2] // BLOCK):
        cols = slice(c * BLOCK, (c + 1) * BLOCK)
        out_ref[:, cols] = sum3(dot(parts, e_ref[0, :, cols], (1, 0)), rank)


def lower_inverse(gram, rank):
    at = lambda i, j: gram[i : i + 1, j : j + 1]
    low, inv = {}, {}
    for j in range(rank):
        d = at(j, j)
        for k in range(j):
            d = d - low[j, k] * low[j, k]
        inv[j, j] = lax.rsqrt(d)
        for i in range(j + 1, rank):
            v = at(i, j)
            for k in range(j):
                v = v - low[i, k] * low[j, k]
            low[i, j] = v * inv[j, j]
    for j in range(rank):
        for i in range(j + 1, rank):
            v = low[i, j] * inv[j, j]
            for k in range(j + 1, i):
                v = v + low[i, k] * inv[k, j]
            inv[i, j] = -v * inv[i, i]
    return inv


def solve(inv, x, rank):
    total = 0.0
    for j in range(rank):
        column = [inv.get((i, j), jnp.zeros((1, 1), F32)) for i in range(rank)]
        total = total + jnp.concatenate(column, axis=0) * x[j : j + 1, :]
    return total


def right_kernel(r_ref, y_ref, got_ref, extra_ref, *refs):
    held, (keep_ref, send_ref, y3, outbox) = refs[:-4], refs[-4:]
    rank = r_ref.shape[0]
    tok = held[0].shape[1]
    half = r_ref.shape[1] // 2
    core = lax.rem(lax.axis_index("dp"), 2)
    mine = extra_ref[0:1, rank : rank + 1]
    theirs = got_ref[rank : rank + 1, 0:1]
    top = jnp.maximum(mine, theirs)
    products = y_ref[...] * (mine / top)
    joint = products[:, 0:tok] + got_ref[0:rank, 0:tok] * (theirs / top)
    terms = stack3(jnp.concatenate([joint, products[:, tok:]], axis=1), y3)
    for h in range(2):
        for c in range(half // BLOCK):
            at = h * half + c * BLOCK
            cols = slice(at, at + BLOCK)
            grads = jnp.concatenate([g[0, :, cols] for g in held], axis=0)
            fresh = sum3(dot(terms, grads, (1, 0)), rank)
            outbox[h, :, c * BLOCK : (c + 1) * BLOCK] = r_ref[:, cols] * (mine / top) + fresh
        outbox[h, :, half:] = extra_ref[...]
        outbox[h, :, half + rank : half + rank + 1] = jnp.broadcast_to(top, (rank, 1))
    keep_ref[...] = outbox[core]
    send_ref[...] = outbox[1 - core]


def join_kernel(rank, *refs):
    xs, out_ref = refs[:-1], refs[-1]
    half = out_ref.shape[1] - 128
    mark = slice(half + rank, half + rank + 1)
    tops = [x[0:1, mark] for x in xs]
    top = jnp.maximum(tops[0], tops[1])
    for other in tops[2:]:
        top = jnp.maximum(top, other)

    def total(terms):
        first = terms[0] + terms[1]
        return first + (terms[2] + terms[3]) if len(terms) == 4 else first

    out_ref[:, :half] = total([x[:, :half] * (t / top) for x, t in zip(xs, tops)])
    out_ref[:, half:] = total([x[:, half:] for x in xs])
    out_ref[:, mark] = jnp.broadcast_to(top, (rank, 1))


def add_kernel(*refs):
    refs[-1][...] = total_of(refs[:-1])


LEFT_TERMS = (0, 0, 1, 0, 2, 1)
RIGHT_TERMS = (0, 1, 0, 2, 0, 1)


def stack_terms(terms, x, ref):
    parts = split(x)
    rank = x.shape[0]
    for i, term in enumerate(terms):
        ref[i * rank : (i + 1) * rank, :] = parts[term]
    return ref[...]


def factor_solve(m, total_ref):
    rank = total_ref.shape[0]
    half = total_ref.shape[1] - 128
    inv = lower_inverse(total_ref[:, half : half + rank] * (1.0 / m), rank)
    top = total_ref[0:1, half + rank : half + rank + 1] * (ROOM / (m * m))
    scaled = {key: value * top for key, value in inv.items()}
    return inv, solve(scaled, total_ref[:, 0:half], rank)


def half_kernel(m, p_ref, mine_ref, left_ref, whole_ref, right_ref, left, right):
    inv, half = factor_solve(m, mine_ref)
    whole_ref[...] = half
    right_ref[...] = stack_terms(RIGHT_TERMS, half, right).astype(BF16)
    ortho = solve(inv, p_ref[...], p_ref.shape[0])
    left_ref[...] = stack_terms(LEFT_TERMS, ortho, left).T.astype(BF16)


def factor_kernel(m, other_ref, mine_ref, mine_terms_ref, whole_ref, right_ref, right):
    half = mine_ref.shape[1]
    core = lax.rem(lax.axis_index("dp"), 2)
    _, other = factor_solve(m, other_ref)
    terms = stack_terms(RIGHT_TERMS, other, right).astype(BF16)
    for c in range(2):

        @pl.when(core == c)
        def _():
            here = slice(c * half, (c + 1) * half)
            there = slice((1 - c) * half, (2 - c) * half)
            whole_ref[:, here] = mine_ref[...]
            whole_ref[:, there] = other
            right_ref[:, here] = mine_terms_ref[...]
            right_ref[:, there] = terms


def acts_kernel(n, a_ref, out_ref, acts):
    tok = a_ref.shape[1] // n
    me = lax.axis_index("tensor")
    for s in range(n):
        src = ring_source(me, s, n)
        here = a_ref[0, pl.ds(pl.multiple_of(src * tok, tok), tok), :]
        acts[s * tok : (s + 1) * tok, :] = here
    out_ref[...] = acts[...].T


def final_kernel(at, part, bases, acts_ref, left_ref, right_ref, e_ref, *refs):
    slots = refs[: len(bases)]
    rebuilt_hbm, error_hbm, rebuilt_v, error_v, sems = refs[-5:]
    rows = e_ref.shape[1]
    wide = 256
    strips, sides, _ = sems.shape
    high = rows // strips
    side = part // sides
    copies = []
    for r in range(strips):
        here = slice(r * high, (r + 1) * high)
        for c in range(part // wide):
            cols = slice(c * wide, (c + 1) * wide)
            there = slice(at + c * wide, at + (c + 1) * wide)
            grads = [
                slot[0, :, there.start - base : there.stop - base]
                for slot, base in zip(slots, bases)
            ]
            grad = dot(acts_ref[here, :], jnp.concatenate(grads, axis=0), (1, 0))
            matrix = grad + e_ref[0, here, there].astype(F32)
            rebuilt = dot(left_ref[here, :], right_ref[:, there], (1, 0))
            rebuilt_v[here, cols] = rebuilt.astype(BF16)
            error_v[here, cols] = (matrix - rebuilt).astype(BF16)
            if (c + 1) * wide % side == 0:
                k = c * wide // side
                strip = pl.ds(r * high, high)
                near = rebuilt_v.at[strip, pl.ds(k * side, side)]
                far = rebuilt_hbm.at[strip, pl.ds(at + k * side, side)]
                copies.append(pltpu.make_async_copy(near, far, sems.at[r, k, 0]))
                near = error_v.at[strip, pl.ds(k * side, side)]
                far = error_hbm.at[0, strip, pl.ds(at + k * side, side)]
                copies.append(pltpu.make_async_copy(near, far, sems.at[r, k, 1]))
                copies[-2].start()
                copies[-1].start()
    for copy in copies:
        copy.wait()


def per_device(activations, out_grads, error_buffer, warm_factor):
    m = lax.axis_size("dp")
    n = lax.axis_size("tensor")
    _, tokens, rows = activations.shape
    _, tok, width = out_grads.shape
    rank = warm_factor.shape[1]
    half = width // 2
    w = warm_factor.T
    sds = jax.ShapeDtypeStruct
    hbm = pl.BlockSpec(memory_space=pltpu.HBM)
    vmem = pl.BlockSpec(memory_space=pltpu.VMEM)
    dma = pltpu.SemaphoreType.DMA
    pin = lambda x: pltpu.with_memory_space_constraint(x, pltpu.HBM)

    def call(kernel, shapes, scratch, name, specs=None, flops=0):
        return pl.pallas_call(
            kernel,
            out_shape=shapes,
            **({"in_specs": specs} if specs else {}),
            scratch_shapes=scratch,
            compiler_params=params(16),
            cost_estimate=cost(flops),
            name=name,
        )

    def add(*terms):
        return call(add_kernel, sds(terms[0].shape, F32), [], "add")(*terms)

    def after(x, y):
        return lax.optimization_barrier((x, y))

    def cut(x, widths):
        shapes = [sds((1, tok, part), BF16) for part in widths]
        return call(cut_kernel, shapes, [dma((len(widths),))], "cut")(x)

    def step(x):
        return ring_step(x, "tensor", n)

    ring = [out_grads, step(out_grads)]

    gw, w_terms = call(
        token_factor_kernel,
        [sds((8, 128), F32), sds((3 * rank, width), BF16)],
        [
            pltpu.VMEM((rank, width), F32),
            pltpu.VMEM((1, tok, width), BF16),
            pltpu.VMEM((3 * rank, width), F32),
            dma((2,)),
        ],
        "token_factor", [hbm, hbm],
    )(pin(w), pin(out_grads))
    ew, error_v = call(
        error_left_kernel,
        [sds((rank, rows), F32), sds((1, rows, width), BF16)],
        [dma((rows // 128,))],
        "error_left", [vmem, hbm], 4.6e9,
    )(w_terms, pin(error_buffer))

    gw, ew = after(gw, ew)
    gws = exchange([gw] * n, "tensor", n)
    ring[1], gws = after(ring[1], gws)
    for _ in range(n - 2 - 1):
        ring.append(step(ring[-1]))
    left = call(
        left_kernel, sds((rank, rows), F32), [pltpu.VMEM((3 * rank, tok), F32)], "left"
    )(activations, ew, *gws)
    left = add(left, swap(left, "dp", m, 1))
    for group in groups(m // 2)[:-1]:
        left = add(*terms_of(left, "dp", m, [2 * bit for bit in group]))
    lefts = terms_of(left, "dp", m, [2 * bit for bit in groups(m // 2)[-1]])
    mean, scaled, extra, held, following = call(
        functools.partial(mean_kernel, n, 1.0 / (SHRINK * m)),
        [
            sds((rank, rows), F32),
            sds((rank, rows), F32),
            sds((rank, 128), F32),
            sds((rank, (n - 1) * tok), F32),
            sds((8, 128), F32),
        ],
        [pltpu.VMEM((3 * rank, rows), F32), pltpu.VMEM((n, rank, tok), F32)],
        "mean",
    )(activations, *lefts)
    got = step(following)

    right_raw = call(
        error_right_kernel,
        sds((rank, width), F32),
        [pltpu.VMEM((3 * rank, rows), F32)],
        "error_right", None, 1.2e9,
    )(scaled, error_v)

    widths = [width * 7 // 10, width * 3 // 10]
    last, (got, right_raw) = after(ring[-1], (got, right_raw))
    newest = list(cut(last, widths))
    newest[0] = step(newest[0])

    keep, send = call(
        right_kernel,
        [sds((rank, half + 128), F32)] * 2,
        [
            pltpu.VMEM((3 * rank, (n - 1) * tok), F32),
            pltpu.VMEM((2, rank, half + 128), F32),
        ],
        "right",
    )(right_raw, held, got, extra, *ring)
    total = add(keep, swap(send, "dp", m, 1))

    for group in groups(m // 2):
        total = add(*terms_of(total, "dp", m, [2 * bit for bit in group]))
    newest[0], total = after(newest[0], total)
    for group in groups(n):
        parts = terms_of(total, "tensor", n, group)
        total = call(
            functools.partial(join_kernel, rank), sds(total.shape, F32), [], "join"
        )(*parts)
    for c in range(1, len(widths)):
        last, total = after(newest[c], total)
        newest[c] = step(last)

    terms = len(LEFT_TERMS) * rank
    other = swap(total, "dp", m, 1)
    left_terms, mine, mine_terms = call(
        functools.partial(half_kernel, m),
        [sds((rows, terms), BF16), sds((rank, half), F32), sds((terms, half), BF16)],
        [pltpu.VMEM((terms, rows), F32), pltpu.VMEM((terms, half), F32)],
        "half", None, 1e9,
    )(mean, total)
    whole, right_terms = call(
        functools.partial(factor_kernel, m),
        [sds((rank, width), F32), sds((terms, width), BF16)],
        [pltpu.VMEM((terms, half), F32)],
        "factor",
    )(other, mine, mine_terms)

    acts = call(
        functools.partial(acts_kernel, n),
        sds((rows, tokens), BF16),
        [pltpu.VMEM((tokens, rows), BF16)],
        "acts",
    )(activations)
    pieces = []
    at = 0
    for part, x in zip(widths, newest):
        pieces.append((at, part, ring + [x], [0] * (n - 1) + [at]))
        at += part

    outs = ()
    for at, part, slots, bases in pieces:
        outs = pl.pallas_call(
            functools.partial(final_kernel, at, part, bases),
            in_specs=[vmem] * (4 + n) + [pl.BlockSpec(memory_space=pl.ANY)] * len(outs),
            out_specs=[pl.BlockSpec(memory_space=pl.ANY)] * 2,
            out_shape=[sds((rows, width), BF16), sds((1, rows, width), BF16)],
            input_output_aliases={4 + n + j: j for j in range(len(outs))},
            scratch_shapes=[pltpu.VMEM((rows, part), BF16)] * 2 + [dma((3, 2, 2))],
            compiler_params=params(16),
            cost_estimate=cost(REBUILD),
            name="rebuild",
        )(acts, left_terms, right_terms, error_v, *slots, *outs)
    rebuilt, error = outs
    return rebuilt, error, whole.T


def solution(mesh):
    return jax.shard_map(
        per_device,
        mesh=mesh,
        in_specs=(P("dp", None, "tensor"), P("dp", "tensor", None), P("dp", "tensor", None), P()),
        out_specs=(P("tensor", None), P("dp", "tensor", None), P()),
        check_vma=False,
    )
```

```python
import functools

import jax
import jax.numpy as jnp
from jax import lax
from jax.experimental import pallas as pl
from jax.experimental.pallas import tpu as pltpu
from jax.sharding import PartitionSpec as P

F32 = jnp.float32
BF16 = jnp.bfloat16
SHRINK = 2.0**-23
TINY = 1e-30
REBUILD = 4e9
ROOM = 2.0**14
BLOCK = 512


def params(mib):
    return pltpu.CompilerParams(vmem_limit_bytes=mib * 2**20)


def cost(flops):
    return pl.CostEstimate(flops=int(flops) + 1, bytes_accessed=1, transcendentals=0)


def dot(a, b, contract):
    return lax.dot_general(a, b, ((contract[:1], contract[1:]), ((), ())), preferred_element_type=F32)


def split(x):
    hi = x.astype(BF16)
    rest = x - hi.astype(F32)
    mid = rest.astype(BF16)
    lo = (rest - mid.astype(F32)).astype(BF16)
    return hi.astype(F32), mid.astype(F32), lo.astype(F32)


def stack3(x, ref):
    rank = x.shape[0]
    for i, part in enumerate(split(x)):
        ref[i * rank : (i + 1) * rank, :] = part
    return ref[...].astype(BF16)


def sum3(y, rank):
    return (y[2 * rank :] + y[rank : 2 * rank]) + y[:rank]


def ring_of(n):
    return [2 * p if 2 * p < n else 2 * (n - p) - 1 for p in range(n)]


def ring_source(me, step, n):
    place = jnp.where(lax.rem(me, 2) == 0, me // 2, n - (me + 1) // 2)
    place = lax.rem(place - step + n, n)
    return jnp.where(2 * place < n, 2 * place, 2 * (n - place) - 1)


def ring_step(x, axis, n):
    ring = ring_of(n)
    return lax.ppermute(x, axis, [(ring[p], ring[(p + 1) % n]) for p in range(n)])


def swap(x, axis, n, bit):
    return lax.ppermute(x, axis, [(i, i ^ bit) for i in range(n)])


def groups(n):
    assert n & (n - 1) == 0
    bits = [1 << i for i in range(n.bit_length() - 1)]
    return [bits[i : i + 2] for i in range(0, len(bits), 2)]


def terms_of(x, axis, n, group):
    others = group if len(group) == 1 else [group[0], group[1], group[0] | group[1]]
    return [x] + [swap(x, axis, n, bit) for bit in others]


def total_of(refs):
    total = refs[0][...] + refs[1][...]
    if len(refs) == 4:
        total = total + (refs[2][...] + refs[3][...])
    return total


def token_factor_kernel(w_hbm, g_hbm, gw_ref, terms_ref, w, g, w3, sems):
    rank = w.shape[0]
    copies = [
        pltpu.make_async_copy(w_hbm, w, sems.at[0]),
        pltpu.make_async_copy(g_hbm, g, sems.at[1]),
    ]
    for copy in copies:
        copy.start()
    copies[0].wait()
    terms = stack3(w[...] * SHRINK, w3)
    terms_ref[...] = terms
    copies[1].wait()
    gw_ref[...] = jnp.zeros_like(gw_ref)
    gw_ref[0:rank, 0 : g.shape[1]] = sum3(dot(terms, g[0], (1, 1)), rank)


def cut_kernel(x_ref, *refs):
    chunks, sems = refs[:-1], refs[-1]
    copies = []
    at = 0
    for c, chunk in enumerate(chunks):
        part = chunk.shape[2]
        copies.append(pltpu.make_async_copy(x_ref.at[:, :, pl.ds(at, part)], chunk, sems.at[c]))
        copies[-1].start()
        at += part
    for copy in copies:
        copy.wait()


def error_left_kernel(terms_ref, e_hbm, out_ref, e_ref, sems):
    rank = out_ref.shape[0]
    count = sems.shape[0]
    high = e_ref.shape[1] // count
    copies = []
    for c in range(count):
        rows = pl.ds(c * high, high)
        copies.append(pltpu.make_async_copy(e_hbm.at[:, rows, :], e_ref.at[:, rows, :], sems.at[c]))
        copies[-1].start()
    terms = terms_ref[...]
    for c in range(count):
        copies[c].wait()
        rows = slice(c * high, (c + 1) * high)
        out_ref[:, rows] = sum3(dot(terms, e_ref[0, rows, :], (1, 1)), rank)


def left_kernel(a_ref, e_ref, *refs):
    gws, out_ref, g3 = refs[:-2], refs[-2], refs[-1]
    n = len(gws)
    rank = e_ref.shape[0]
    tok = a_ref.shape[1] // n
    me = lax.axis_index("tensor")
    total = e_ref[...]
    for k in range(n):
        src = me ^ k
        rows = a_ref[0, pl.ds(pl.multiple_of(src * tok, tok), tok), :]
        total += sum3(dot(stack3(gws[k][0:rank, 0:tok], g3), rows, (1, 0)), rank)
    out_ref[...] = total


def mean_kernel(n, scale, a_ref, *refs):
    terms = refs[:-7]
    p_ref, scaled_ref, extra_ref, held_ref, next_ref, p3, blocks = refs[-7:]
    rank = p_ref.shape[0]
    tok = a_ref.shape[1] // n
    me = lax.axis_index("tensor")
    mean = total_of(terms) * scale
    p_ref[...] = mean
    top = jnp.max(jnp.max(jnp.abs(mean), axis=1, keepdims=True), axis=0, keepdims=True)
    top = jnp.maximum(top, TINY)
    scaled = mean / (top * ROOM)
    scaled_ref[...] = scaled
    parts = stack3(scaled, p3)
    for t in range(n):
        blocks[t] = sum3(dot(parts, a_ref[0, t * tok : (t + 1) * tok, :], (1, 1)), rank)
    for s in range(n - 1):
        held_ref[:, s * tok : (s + 1) * tok] = blocks[ring_source(me, s, n)]
    next_ref[...] = jnp.zeros_like(next_ref)
    next_ref[0:rank, 0:tok] = blocks[ring_source(me, n - 1, n)]
    next_ref[rank : rank + 1, 0:1] = top
    extra_ref[...] = jnp.zeros_like(extra_ref)
    for i in range(rank):
        extra_ref[:, i : i + 1] = jnp.sum(mean * mean[i : i + 1, :], axis=1, keepdims=True)
    extra_ref[:, rank : rank + 1] = jnp.broadcast_to(top, (rank, 1))


def error_right_kernel(p_ref, e_ref, out_ref, p3):
    rank = p_ref.shape[0]
    parts = stack3(p_ref[...], p3)
    for c in range(e_ref.shape[2] // BLOCK):
        cols = slice(c * BLOCK, (c + 1) * BLOCK)
        out_ref[:, cols] = sum3(dot(parts, e_ref[0, :, cols], (1, 0)), rank)


def lower_inverse(gram, rank):
    at = lambda i, j: gram[i : i + 1, j : j + 1]
    low, inv = {}, {}
    for j in range(rank):
        d = at(j, j)
        for k in range(j):
            d = d - low[j, k] * low[j, k]
        inv[j, j] = lax.rsqrt(d)
        for i in range(j + 1, rank):
            v = at(i, j)
            for k in range(j):
                v = v - low[i, k] * low[j, k]
            low[i, j] = v * inv[j, j]
    for j in range(rank):
        for i in range(j + 1, rank):
            v = low[i, j] * inv[j, j]
            for k in range(j + 1, i):
                v = v + low[i, k] * inv[k, j]
            inv[i, j] = -v * inv[i, i]
    return inv


def solve(inv, x, rank):
    total = 0.0
    for j in range(rank):
        column = [inv.get((i, j), jnp.zeros((1, 1), F32)) for i in range(rank)]
        total = total + jnp.concatenate(column, axis=0) * x[j : j + 1, :]
    return total


def right_kernel(r_ref, y_ref, got_ref, extra_ref, *refs):
    held, (keep_ref, send_ref, y3, outbox) = refs[:-4], refs[-4:]
    rank = r_ref.shape[0]
    tok = held[0].shape[1]
    half = r_ref.shape[1] // 2
    core = lax.rem(lax.axis_index("dp"), 2)
    mine = extra_ref[0:1, rank : rank + 1]
    theirs = got_ref[rank : rank + 1, 0:1]
    top = jnp.maximum(mine, theirs)
    products = y_ref[...] * (mine / top)
    joint = products[:, 0:tok] + got_ref[0:rank, 0:tok] * (theirs / top)
    terms = stack3(jnp.concatenate([joint, products[:, tok:]], axis=1), y3)
    for h in range(2):
        for c in range(half // BLOCK):
            at = h * half + c * BLOCK
            cols = slice(at, at + BLOCK)
            grads = jnp.concatenate([g[0, :, cols] for g in held], axis=0)
            fresh = sum3(dot(terms, grads, (1, 0)), rank)
            outbox[h, :, c * BLOCK : (c + 1) * BLOCK] = r_ref[:, cols] * (mine / top) + fresh
        outbox[h, :, half:] = extra_ref[...]
        outbox[h, :, half + rank : half + rank + 1] = jnp.broadcast_to(top, (rank, 1))
    keep_ref[...] = outbox[core]
    send_ref[...] = outbox[1 - core]


def join_kernel(rank, *refs):
    xs, out_ref = refs[:-1], refs[-1]
    half = out_ref.shape[1] - 128
    mark = slice(half + rank, half + rank + 1)
    tops = [x[0:1, mark] for x in xs]
    top = jnp.maximum(tops[0], tops[1])
    for other in tops[2:]:
        top = jnp.maximum(top, other)

    def total(terms):
        first = terms[0] + terms[1]
        return first + (terms[2] + terms[3]) if len(terms) == 4 else first

    out_ref[:, :half] = total([x[:, :half] * (t / top) for x, t in zip(xs, tops)])
    out_ref[:, half:] = total([x[:, half:] for x in xs])
    out_ref[:, mark] = jnp.broadcast_to(top, (rank, 1))


def add_kernel(*refs):
    refs[-1][...] = total_of(refs[:-1])


LEFT_TERMS = (0, 0, 1, 0, 2, 1)
RIGHT_TERMS = (0, 1, 0, 2, 0, 1)


def stack_terms(terms, x, ref):
    parts = split(x)
    rank = x.shape[0]
    for i, term in enumerate(terms):
        ref[i * rank : (i + 1) * rank, :] = parts[term]
    return ref[...]


def factor_solve(m, total_ref):
    rank = total_ref.shape[0]
    half = total_ref.shape[1] - 128
    inv = lower_inverse(total_ref[:, half : half + rank] * (1.0 / m), rank)
    top = total_ref[0:1, half + rank : half + rank + 1] * (ROOM / (m * m))
    scaled = {key: value * top for key, value in inv.items()}
    return inv, solve(scaled, total_ref[:, 0:half], rank)


def half_kernel(m, p_ref, mine_ref, left_ref, whole_ref, right_ref, left, right):
    inv, half = factor_solve(m, mine_ref)
    whole_ref[...] = half
    right_ref[...] = stack_terms(RIGHT_TERMS, half, right).astype(BF16)
    ortho = solve(inv, p_ref[...], p_ref.shape[0])
    left_ref[...] = stack_terms(LEFT_TERMS, ortho, left).T.astype(BF16)


def factor_kernel(m, other_ref, mine_ref, mine_terms_ref, whole_ref, right_ref, right):
    half = mine_ref.shape[1]
    core = lax.rem(lax.axis_index("dp"), 2)
    _, other = factor_solve(m, other_ref)
    terms = stack_terms(RIGHT_TERMS, other, right).astype(BF16)
    for c in range(2):

        @pl.when(core == c)
        def _():
            here = slice(c * half, (c + 1) * half)
            there = slice((1 - c) * half, (2 - c) * half)
            whole_ref[:, here] = mine_ref[...]
            whole_ref[:, there] = other
            right_ref[:, here] = mine_terms_ref[...]
            right_ref[:, there] = terms


def acts_kernel(n, a_ref, out_ref, acts):
    tok = a_ref.shape[1] // n
    me = lax.axis_index("tensor")
    for s in range(n):
        src = ring_source(me, s, n)
        here = a_ref[0, pl.ds(pl.multiple_of(src * tok, tok), tok), :]
        acts[s * tok : (s + 1) * tok, :] = here
    out_ref[...] = acts[...].T


def final_kernel(at, part, bases, last, acts_ref, left_ref, right_ref, e_ref, *refs):
    slots = refs[: len(bases)]
    outs, (rebuilt_v, error_v, sems) = refs[-5 - last : -3], refs[-3:]
    rebuilt_hbm, error_hbm = outs[:2]
    rows = e_ref.shape[1]
    wide = 256
    strips, sides, _ = sems.shape
    strips -= 1
    high = rows // strips
    side = part // sides
    copies = []
    if last:
        copies.append(pltpu.make_async_copy(refs[len(bases)], outs[2], sems.at[strips, 0, 0]))
        copies[-1].start()
    for r in range(strips):
        here = slice(r * high, (r + 1) * high)
        for c in range(part // wide):
            cols = slice(c * wide, (c + 1) * wide)
            there = slice(at + c * wide, at + (c + 1) * wide)
            grads = [
                slot[0, :, there.start - base : there.stop - base]
                for slot, base in zip(slots, bases)
            ]
            grad = dot(acts_ref[here, :], jnp.concatenate(grads, axis=0), (1, 0))
            matrix = grad + e_ref[0, here, there].astype(F32)
            rebuilt = dot(left_ref[here, :], right_ref[:, there], (1, 0))
            rebuilt_v[here, cols] = rebuilt.astype(BF16)
            error_v[here, cols] = (matrix - rebuilt).astype(BF16)
            if (c + 1) * wide % side == 0:
                k = c * wide // side
                strip = pl.ds(r * high, high)
                near = rebuilt_v.at[strip, pl.ds(k * side, side)]
                far = rebuilt_hbm.at[strip, pl.ds(at + k * side, side)]
                copies.append(pltpu.make_async_copy(near, far, sems.at[r, k, 0]))
                near = error_v.at[strip, pl.ds(k * side, side)]
                far = error_hbm.at[0, strip, pl.ds(at + k * side, side)]
                copies.append(pltpu.make_async_copy(near, far, sems.at[r, k, 1]))
                copies[-2].start()
                copies[-1].start()
    for copy in copies:
        copy.wait()


def per_device(activations, out_grads, error_buffer, warm_factor):
    m = lax.axis_size("dp")
    n = lax.axis_size("tensor")
    _, tokens, rows = activations.shape
    _, tok, width = out_grads.shape
    rank = warm_factor.shape[1]
    half = width // 2
    w = warm_factor.T
    sds = jax.ShapeDtypeStruct
    hbm = pl.BlockSpec(memory_space=pltpu.HBM)
    vmem = pl.BlockSpec(memory_space=pltpu.VMEM)
    dma = pltpu.SemaphoreType.DMA
    pin = lambda x: pltpu.with_memory_space_constraint(x, pltpu.HBM)

    def call(kernel, shapes, scratch, name, specs=None, flops=0):
        return pl.pallas_call(
            kernel,
            out_shape=shapes,
            **({"in_specs": specs} if specs else {}),
            scratch_shapes=scratch,
            compiler_params=params(16),
            cost_estimate=cost(flops),
            name=name,
        )

    def add(*terms):
        return call(add_kernel, sds(terms[0].shape, F32), [], "add")(*terms)

    def after(x, y):
        return lax.optimization_barrier((x, y))

    def cut(x, widths):
        shapes = [sds((1, tok, part), BF16) for part in widths]
        return call(cut_kernel, shapes, [dma((len(widths),))], "cut")(x)

    def step(x):
        return ring_step(x, "tensor", n)

    ring = [out_grads, step(out_grads)]

    gw, w_terms = call(
        token_factor_kernel,
        [sds((8, 128), F32), sds((3 * rank, width), BF16)],
        [
            pltpu.VMEM((rank, width), F32),
            pltpu.VMEM((1, tok, width), BF16),
            pltpu.VMEM((3 * rank, width), F32),
            dma((2,)),
        ],
        "token_factor", [hbm, hbm],
    )(pin(w), pin(out_grads))
    ew, error_v = call(
        error_left_kernel,
        [sds((rank, rows), F32), sds((1, rows, width), BF16)],
        [dma((rows // 128,))],
        "error_left", [vmem, hbm], 4.6e9,
    )(w_terms, pin(error_buffer))

    gw, ew = after(gw, ew)
    gws = [gw] + [swap(gw, "tensor", n, k) for k in range(1, n)]
    ring[1], gws = after(ring[1], gws)
    for _ in range(n - 2 - 1):
        ring.append(step(ring[-1]))
    left = call(
        left_kernel, sds((rank, rows), F32), [pltpu.VMEM((3 * rank, tok), F32)], "left"
    )(activations, ew, *gws)
    left = add(left, swap(left, "dp", m, 1))
    for group in groups(m // 2)[:-1]:
        left = add(*terms_of(left, "dp", m, [2 * bit for bit in group]))
    lefts = terms_of(left, "dp", m, [2 * bit for bit in groups(m // 2)[-1]])
    mean, scaled, extra, held, following = call(
        functools.partial(mean_kernel, n, 1.0 / (SHRINK * m)),
        [
            sds((rank, rows), F32),
            sds((rank, rows), F32),
            sds((rank, 128), F32),
            sds((rank, (n - 1) * tok), F32),
            sds((8, 128), F32),
        ],
        [pltpu.VMEM((3 * rank, rows), F32), pltpu.VMEM((n, rank, tok), F32)],
        "mean",
    )(activations, *lefts)
    got = step(following)

    right_raw = call(
        error_right_kernel,
        sds((rank, width), F32),
        [pltpu.VMEM((3 * rank, rows), F32)],
        "error_right", None, 1.2e9,
    )(scaled, error_v)

    widths = [width * 7 // 10, width * 3 // 10]
    last, (got, right_raw) = after(ring[-1], (got, right_raw))
    newest = list(cut(last, widths))
    newest[0] = step(newest[0])

    keep, send = call(
        right_kernel,
        [sds((rank, half + 128), F32)] * 2,
        [
            pltpu.VMEM((3 * rank, (n - 1) * tok), F32),
            pltpu.VMEM((2, rank, half + 128), F32),
        ],
        "right",
    )(right_raw, held, got, extra, *ring)
    total = add(keep, swap(send, "dp", m, 1))

    for group in groups(m // 2):
        total = add(*terms_of(total, "dp", m, [2 * bit for bit in group]))
    newest[0], total = after(newest[0], total)
    for group in groups(n):
        parts = terms_of(total, "tensor", n, group)
        total = call(
            functools.partial(join_kernel, rank), sds(total.shape, F32), [], "join"
        )(*parts)
    for c in range(1, len(widths)):
        last, total = after(newest[c], total)
        newest[c] = step(last)

    terms = len(LEFT_TERMS) * rank
    other = swap(total, "dp", m, 1)
    left_terms, mine, mine_terms = call(
        functools.partial(half_kernel, m),
        [sds((rows, terms), BF16), sds((rank, half), F32), sds((terms, half), BF16)],
        [pltpu.VMEM((terms, rows), F32), pltpu.VMEM((terms, half), F32)],
        "half", None, 1e9,
    )(mean, total)
    whole, right_terms = call(
        functools.partial(factor_kernel, m),
        [sds((rank, width), F32), sds((terms, width), BF16)],
        [pltpu.VMEM((terms, half), F32)],
        "factor",
    )(other, mine, mine_terms)

    acts = call(
        functools.partial(acts_kernel, n),
        sds((rows, tokens), BF16),
        [pltpu.VMEM((tokens, rows), BF16)],
        "acts",
    )(activations)
    pieces = []
    at = 0
    for part, x in zip(widths, newest):
        pieces.append((at, part, ring + [x], [0] * (n - 1) + [at]))
        at += part

    outs = ()
    for at, part, slots, bases in pieces:
        last = at + part == width
        inputs = [acts, left_terms, right_terms, error_v, *slots] + [whole] * last
        outs = pl.pallas_call(
            functools.partial(final_kernel, at, part, bases, last),
            in_specs=[vmem] * len(inputs) + [pl.BlockSpec(memory_space=pl.ANY)] * len(outs),
            out_specs=[pl.BlockSpec(memory_space=pl.ANY)] * (2 + last),
            out_shape=[sds((rows, width), BF16), sds((1, rows, width), BF16)]
            + [sds((rank, width), F32)] * last,
            input_output_aliases={len(inputs) + k: k for k in range(len(outs))},
            scratch_shapes=[pltpu.VMEM((rows, part), BF16)] * 2 + [dma((4, 2, 2))],
            compiler_params=params(16),
            cost_estimate=cost(REBUILD),
            name="rebuild",
        )(*inputs, *outs)
    rebuilt, error, factor = outs
    return rebuilt, error, factor.T


def solution(mesh):
    return jax.shard_map(
        per_device,
        mesh=mesh,
        in_specs=(P("dp", None, "tensor"), P("dp", "tensor", None), P("dp", "tensor", None), P()),
        out_specs=(P("tensor", None), P("dp", "tensor", None), P()),
        check_vma=False,
    )
```

```python
import functools

import jax
import jax.numpy as jnp
from jax import lax
from jax.experimental import pallas as pl
from jax.experimental.pallas import tpu as pltpu
from jax.sharding import PartitionSpec as P

F32 = jnp.float32
BF16 = jnp.bfloat16
SHRINK = 2.0**-23
TINY = 1e-30
REBUILD = 4e9
ROOM = 2.0**14
BLOCK = 512


def params(mib):
    return pltpu.CompilerParams(vmem_limit_bytes=mib * 2**20)


def cost(flops):
    return pl.CostEstimate(flops=int(flops) + 1, bytes_accessed=1, transcendentals=0)


def dot(a, b, contract):
    return lax.dot_general(a, b, ((contract[:1], contract[1:]), ((), ())), preferred_element_type=F32)


def split(x):
    hi = x.astype(BF16)
    rest = x - hi.astype(F32)
    mid = rest.astype(BF16)
    lo = (rest - mid.astype(F32)).astype(BF16)
    return hi.astype(F32), mid.astype(F32), lo.astype(F32)


def stack3(x, ref):
    rank = x.shape[0]
    for i, part in enumerate(split(x)):
        ref[i * rank : (i + 1) * rank, :] = part
    return ref[...].astype(BF16)


def sum3(y, rank):
    return (y[2 * rank :] + y[rank : 2 * rank]) + y[:rank]


def ring_of(n):
    return [2 * p if 2 * p < n else 2 * (n - p) - 1 for p in range(n)]


def ring_source(me, step, n):
    place = jnp.where(lax.rem(me, 2) == 0, me // 2, n - (me + 1) // 2)
    place = lax.rem(place - step + n, n)
    return jnp.where(2 * place < n, 2 * place, 2 * (n - place) - 1)


def ring_step(x, axis, n):
    ring = ring_of(n)
    return lax.ppermute(x, axis, [(ring[p], ring[(p + 1) % n]) for p in range(n)])


def exchange(pieces, axis, n):
    return [pieces[0]] + [
        lax.ppermute(pieces[k], axis, [(i, (i + k) % n) for i in range(n)]) for k in range(1, n)
    ]


def swap(x, axis, n, bit):
    return lax.ppermute(x, axis, [(i, i ^ bit) for i in range(n)])


def groups(n):
    assert n & (n - 1) == 0
    bits = [1 << i for i in range(n.bit_length() - 1)]
    return [bits[i : i + 2] for i in range(0, len(bits), 2)]


def terms_of(x, axis, n, group):
    others = group if len(group) == 1 else [group[0], group[1], group[0] | group[1]]
    return [x] + [swap(x, axis, n, bit) for bit in others]


def total_of(refs):
    total = refs[0][...] + refs[1][...]
    if len(refs) == 4:
        total = total + (refs[2][...] + refs[3][...])
    return total


def token_factor_kernel(w_hbm, g_hbm, gw_ref, terms_ref, w, g, w3, sems):
    rank = w.shape[0]
    copies = [
        pltpu.make_async_copy(w_hbm, w, sems.at[0]),
        pltpu.make_async_copy(g_hbm, g, sems.at[1]),
    ]
    for copy in copies:
        copy.start()
    copies[0].wait()
    terms = stack3(w[...] * SHRINK, w3)
    terms_ref[...] = terms
    copies[1].wait()
    gw_ref[...] = jnp.zeros_like(gw_ref)
    gw_ref[0:rank, 0 : g.shape[1]] = sum3(dot(terms, g[0], (1, 1)), rank)


def cut_kernel(x_ref, *refs):
    chunks, sems = refs[:-1], refs[-1]
    copies = []
    at = 0
    for c, chunk in enumerate(chunks):
        part = chunk.shape[2]
        copies.append(pltpu.make_async_copy(x_ref.at[:, :, pl.ds(at, part)], chunk, sems.at[c]))
        copies[-1].start()
        at += part
    for copy in copies:
        copy.wait()


def error_left_kernel(terms_ref, e_hbm, out_ref, e_ref, sems):
    rank = out_ref.shape[0]
    count = sems.shape[0]
    high = e_ref.shape[1] // count
    copies = []
    for c in range(count):
        rows = pl.ds(c * high, high)
        copies.append(pltpu.make_async_copy(e_hbm.at[:, rows, :], e_ref.at[:, rows, :], sems.at[c]))
        copies[-1].start()
    terms = terms_ref[...]
    for c in range(count):
        copies[c].wait()
        rows = slice(c * high, (c + 1) * high)
        out_ref[:, rows] = sum3(dot(terms, e_ref[0, rows, :], (1, 1)), rank)


def left_kernel(a_ref, e_ref, *refs):
    gws, out_ref, g3 = refs[:-2], refs[-2], refs[-1]
    n = len(gws)
    rank = e_ref.shape[0]
    tok = a_ref.shape[1] // n
    me = lax.axis_index("tensor")
    total = e_ref[...]
    for k in range(n):
        src = lax.rem(me - k + n, n)
        rows = a_ref[0, pl.ds(pl.multiple_of(src * tok, tok), tok), :]
        total += sum3(dot(stack3(gws[k][0:rank, 0:tok], g3), rows, (1, 0)), rank)
    out_ref[...] = total


def mean_kernel(n, scale, a_ref, *refs):
    terms = refs[:-7]
    p_ref, scaled_ref, extra_ref, held_ref, next_ref, p3, blocks = refs[-7:]
    rank = p_ref.shape[0]
    tok = a_ref.shape[1] // n
    me = lax.axis_index("tensor")
    mean = total_of(terms) * scale
    p_ref[...] = mean
    top = jnp.max(jnp.max(jnp.abs(mean), axis=1, keepdims=True), axis=0, keepdims=True)
    top = jnp.maximum(top, TINY)
    scaled = mean / (top * ROOM)
    scaled_ref[...] = scaled
    parts = stack3(scaled, p3)
    for t in range(n):
        blocks[t] = sum3(dot(parts, a_ref[0, t * tok : (t + 1) * tok, :], (1, 1)), rank)
    for s in range(n - 1):
        held_ref[:, s * tok : (s + 1) * tok] = blocks[ring_source(me, s, n)]
    next_ref[...] = jnp.zeros_like(next_ref)
    next_ref[0:rank, 0:tok] = blocks[ring_source(me, n - 1, n)]
    next_ref[rank : rank + 1, 0:1] = top
    extra_ref[...] = jnp.zeros_like(extra_ref)
    for i in range(rank):
        extra_ref[:, i : i + 1] = jnp.sum(mean * mean[i : i + 1, :], axis=1, keepdims=True)
    extra_ref[:, rank : rank + 1] = jnp.broadcast_to(top, (rank, 1))


def error_right_kernel(p_ref, e_ref, out_ref, p3):
    rank = p_ref.shape[0]
    parts = stack3(p_ref[...], p3)
    for c in range(e_ref.shape[2] // BLOCK):
        cols = slice(c * BLOCK, (c + 1) * BLOCK)
        out_ref[:, cols] = sum3(dot(parts, e_ref[0, :, cols], (1, 0)), rank)


def lower_inverse(gram, rank):
    at = lambda i, j: gram[i : i + 1, j : j + 1]
    low, inv = {}, {}
    for j in range(rank):
        d = at(j, j)
        for k in range(j):
            d = d - low[j, k] * low[j, k]
        inv[j, j] = lax.rsqrt(d)
        for i in range(j + 1, rank):
            v = at(i, j)
            for k in range(j):
                v = v - low[i, k] * low[j, k]
            low[i, j] = v * inv[j, j]
    for j in range(rank):
        for i in range(j + 1, rank):
            v = low[i, j] * inv[j, j]
            for k in range(j + 1, i):
                v = v + low[i, k] * inv[k, j]
            inv[i, j] = -v * inv[i, i]
    return inv


def solve(inv, x, rank):
    total = 0.0
    for j in range(rank):
        column = [inv.get((i, j), jnp.zeros((1, 1), F32)) for i in range(rank)]
        total = total + jnp.concatenate(column, axis=0) * x[j : j + 1, :]
    return total


def right_kernel(r_ref, y_ref, got_ref, extra_ref, *refs):
    held, (keep_ref, send_ref, y3, outbox) = refs[:-4], refs[-4:]
    rank = r_ref.shape[0]
    tok = held[0].shape[1]
    half = r_ref.shape[1] // 2
    core = lax.rem(lax.axis_index("dp"), 2)
    mine = extra_ref[0:1, rank : rank + 1]
    theirs = got_ref[rank : rank + 1, 0:1]
    top = jnp.maximum(mine, theirs)
    products = y_ref[...] * (mine / top)
    joint = products[:, 0:tok] + got_ref[0:rank, 0:tok] * (theirs / top)
    terms = stack3(jnp.concatenate([joint, products[:, tok:]], axis=1), y3)
    for h in range(2):
        for c in range(half // BLOCK):
            at = h * half + c * BLOCK
            cols = slice(at, at + BLOCK)
            grads = jnp.concatenate([g[0, :, cols] for g in held], axis=0)
            fresh = sum3(dot(terms, grads, (1, 0)), rank)
            outbox[h, :, c * BLOCK : (c + 1) * BLOCK] = r_ref[:, cols] * (mine / top) + fresh
        outbox[h, :, half:] = extra_ref[...]
        outbox[h, :, half + rank : half + rank + 1] = jnp.broadcast_to(top, (rank, 1))
    keep_ref[...] = outbox[core]
    send_ref[...] = outbox[1 - core]


def join_kernel(rank, *refs):
    xs, out_ref = refs[:-1], refs[-1]
    half = out_ref.shape[1] - 128
    mark = slice(half + rank, half + rank + 1)
    tops = [x[0:1, mark] for x in xs]
    top = jnp.maximum(tops[0], tops[1])
    for other in tops[2:]:
        top = jnp.maximum(top, other)

    def total(terms):
        first = terms[0] + terms[1]
        return first + (terms[2] + terms[3]) if len(terms) == 4 else first

    out_ref[:, :half] = total([x[:, :half] * (t / top) for x, t in zip(xs, tops)])
    out_ref[:, half:] = total([x[:, half:] for x in xs])
    out_ref[:, mark] = jnp.broadcast_to(top, (rank, 1))


def add_kernel(*refs):
    refs[-1][...] = total_of(refs[:-1])


LEFT_TERMS = (0, 0, 1, 0, 2, 1)
RIGHT_TERMS = (0, 1, 0, 2, 0, 1)


def stack_terms(terms, x, ref):
    parts = split(x)
    rank = x.shape[0]
    for i, term in enumerate(terms):
        ref[i * rank : (i + 1) * rank, :] = parts[term]
    return ref[...]


def factor_solve(m, total_ref):
    rank = total_ref.shape[0]
    half = total_ref.shape[1] - 128
    inv = lower_inverse(total_ref[:, half : half + rank] * (1.0 / m), rank)
    top = total_ref[0:1, half + rank : half + rank + 1] * (ROOM / (m * m))
    scaled = {key: value * top for key, value in inv.items()}
    return inv, solve(scaled, total_ref[:, 0:half], rank)


def half_kernel(m, p_ref, mine_ref, left_ref, whole_ref, right_ref, left, right):
    inv, half = factor_solve(m, mine_ref)
    whole_ref[...] = half
    right_ref[...] = stack_terms(RIGHT_TERMS, half, right).astype(BF16)
    ortho = solve(inv, p_ref[...], p_ref.shape[0])
    left_ref[...] = stack_terms(LEFT_TERMS, ortho, left).T.astype(BF16)


def factor_kernel(m, other_ref, mine_ref, mine_terms_ref, whole_ref, right_ref, right):
    half = mine_ref.shape[1]
    core = lax.rem(lax.axis_index("dp"), 2)
    _, other = factor_solve(m, other_ref)
    terms = stack_terms(RIGHT_TERMS, other, right).astype(BF16)
    for c in range(2):

        @pl.when(core == c)
        def _():
            here = slice(c * half, (c + 1) * half)
            there = slice((1 - c) * half, (2 - c) * half)
            whole_ref[:, here] = mine_ref[...]
            whole_ref[:, there] = other
            right_ref[:, here] = mine_terms_ref[...]
            right_ref[:, there] = terms


def acts_kernel(n, a_ref, out_ref, acts):
    tok = a_ref.shape[1] // n
    me = lax.axis_index("tensor")
    for s in range(n):
        src = ring_source(me, s, n)
        here = a_ref[0, pl.ds(pl.multiple_of(src * tok, tok), tok), :]
        acts[s * tok : (s + 1) * tok, :] = here
    out_ref[...] = acts[...].T


def final_kernel(at, part, bases, last, acts_ref, left_ref, right_ref, e_ref, *refs):
    slots = refs[: len(bases)]
    outs, (rebuilt_v, error_v, sems) = refs[-5 - last : -3], refs[-3:]
    rebuilt_hbm, error_hbm = outs[:2]
    rows = e_ref.shape[1]
    wide = 256
    strips, sides, _ = sems.shape
    strips -= 1
    high = rows // strips
    side = part // sides
    copies = []
    if last:
        copies.append(pltpu.make_async_copy(refs[len(bases)], outs[2], sems.at[strips, 0, 0]))
        copies[-1].start()
    for r in range(strips):
        here = slice(r * high, (r + 1) * high)
        for c in range(part // wide):
            cols = slice(c * wide, (c + 1) * wide)
            there = slice(at + c * wide, at + (c + 1) * wide)
            grads = [
                slot[0, :, there.start - base : there.stop - base]
                for slot, base in zip(slots, bases)
            ]
            grad = dot(acts_ref[here, :], jnp.concatenate(grads, axis=0), (1, 0))
            matrix = grad + e_ref[0, here, there].astype(F32)
            rebuilt = dot(left_ref[here, :], right_ref[:, there], (1, 0))
            rebuilt_v[here, cols] = rebuilt.astype(BF16)
            error_v[here, cols] = (matrix - rebuilt).astype(BF16)
            if (c + 1) * wide % side == 0:
                k = c * wide // side
                strip = pl.ds(r * high, high)
                near = rebuilt_v.at[strip, pl.ds(k * side, side)]
                far = rebuilt_hbm.at[strip, pl.ds(at + k * side, side)]
                copies.append(pltpu.make_async_copy(near, far, sems.at[r, k, 0]))
                near = error_v.at[strip, pl.ds(k * side, side)]
                far = error_hbm.at[0, strip, pl.ds(at + k * side, side)]
                copies.append(pltpu.make_async_copy(near, far, sems.at[r, k, 1]))
                copies[-2].start()
                copies[-1].start()
    for copy in copies:
        copy.wait()


def per_device(activations, out_grads, error_buffer, warm_factor):
    m = lax.axis_size("dp")
    n = lax.axis_size("tensor")
    _, tokens, rows = activations.shape
    _, tok, width = out_grads.shape
    rank = warm_factor.shape[1]
    half = width // 2
    w = warm_factor.T
    sds = jax.ShapeDtypeStruct
    hbm = pl.BlockSpec(memory_space=pltpu.HBM)
    vmem = pl.BlockSpec(memory_space=pltpu.VMEM)
    dma = pltpu.SemaphoreType.DMA
    pin = lambda x: pltpu.with_memory_space_constraint(x, pltpu.HBM)

    def call(kernel, shapes, scratch, name, specs=None, flops=0):
        return pl.pallas_call(
            kernel,
            out_shape=shapes,
            **({"in_specs": specs} if specs else {}),
            scratch_shapes=scratch,
            compiler_params=params(16),
            cost_estimate=cost(flops),
            name=name,
        )

    def add(*terms):
        return call(add_kernel, sds(terms[0].shape, F32), [], "add")(*terms)

    def after(x, y):
        return lax.optimization_barrier((x, y))

    def cut(x, widths):
        shapes = [sds((1, tok, part), BF16) for part in widths]
        return call(cut_kernel, shapes, [dma((len(widths),))], "cut")(x)

    def step(x):
        return ring_step(x, "tensor", n)

    ring = [out_grads, step(out_grads)]

    gw, w_terms = call(
        token_factor_kernel,
        [sds((8, 128), F32), sds((3 * rank, width), BF16)],
        [
            pltpu.VMEM((rank, width), F32),
            pltpu.VMEM((1, tok, width), BF16),
            pltpu.VMEM((3 * rank, width), F32),
            dma((2,)),
        ],
        "token_factor", [hbm, hbm],
    )(pin(w), pin(out_grads))
    ew, error_v = call(
        error_left_kernel,
        [sds((rank, rows), F32), sds((1, rows, width), BF16)],
        [dma((rows // 128,))],
        "error_left", [vmem, hbm], 4.6e9,
    )(w_terms, pin(error_buffer))

    gw, ew = after(gw, ew)
    gws = exchange([gw] * n, "tensor", n)
    ring[1], gws = after(ring[1], gws)
    for _ in range(n - 2 - 1):
        ring.append(step(ring[-1]))
    left = call(
        left_kernel, sds((rank, rows), F32), [pltpu.VMEM((3 * rank, tok), F32)], "left"
    )(activations, ew, *gws)
    left = add(left, swap(left, "dp", m, 1))
    for group in groups(m // 2)[:-1]:
        left = add(*terms_of(left, "dp", m, [2 * bit for bit in group]))
    lefts = terms_of(left, "dp", m, [2 * bit for bit in groups(m // 2)[-1]])
    mean, scaled, extra, held, following = call(
        functools.partial(mean_kernel, n, 1.0 / (SHRINK * m)),
        [
            sds((rank, rows), F32),
            sds((rank, rows), F32),
            sds((rank, 128), F32),
            sds((rank, (n - 1) * tok), F32),
            sds((8, 128), F32),
        ],
        [pltpu.VMEM((3 * rank, rows), F32), pltpu.VMEM((n, rank, tok), F32)],
        "mean",
    )(activations, *lefts)
    got = step(following)

    right_raw = call(
        error_right_kernel,
        sds((rank, width), F32),
        [pltpu.VMEM((3 * rank, rows), F32)],
        "error_right", None, 1.2e9,
    )(scaled, error_v)

    widths = [width * 7 // 10, width * 3 // 10]
    last, (got, right_raw) = after(ring[-1], (got, right_raw))
    newest = list(cut(last, widths))
    newest[0] = step(newest[0])

    keep, send = call(
        right_kernel,
        [sds((rank, half + 128), F32)] * 2,
        [
            pltpu.VMEM((3 * rank, (n - 1) * tok), F32),
            pltpu.VMEM((2, rank, half + 128), F32),
        ],
        "right",
    )(right_raw, held, got, extra, *ring)
    total = add(keep, swap(send, "dp", m, 1))

    for group in groups(m // 2):
        total = add(*terms_of(total, "dp", m, [2 * bit for bit in group]))
    newest[0], total = after(newest[0], total)
    for group in groups(n):
        parts = terms_of(total, "tensor", n, group)
        total = call(
            functools.partial(join_kernel, rank), sds(total.shape, F32), [], "join"
        )(*parts)
    for c in range(1, len(widths)):
        last, total = after(newest[c], total)
        newest[c] = step(last)

    terms = len(LEFT_TERMS) * rank
    other = swap(total, "dp", m, 1)
    left_terms, mine, mine_terms = call(
        functools.partial(half_kernel, m),
        [sds((rows, terms), BF16), sds((rank, half), F32), sds((terms, half), BF16)],
        [pltpu.VMEM((terms, rows), F32), pltpu.VMEM((terms, half), F32)],
        "half", None, 1e9,
    )(mean, total)
    whole, right_terms = call(
        functools.partial(factor_kernel, m),
        [sds((rank, width), F32), sds((terms, width), BF16)],
        [pltpu.VMEM((terms, half), F32)],
        "factor",
    )(other, mine, mine_terms)

    acts = call(
        functools.partial(acts_kernel, n),
        sds((rows, tokens), BF16),
        [pltpu.VMEM((tokens, rows), BF16)],
        "acts",
    )(activations)
    pieces = []
    at = 0
    for part, x in zip(widths, newest):
        pieces.append((at, part, ring + [x], [0] * (n - 1) + [at]))
        at += part

    outs = ()
    for at, part, slots, bases in pieces:
        last = at + part == width
        inputs = [acts, left_terms, right_terms, error_v, *slots] + [whole] * last
        outs = pl.pallas_call(
            functools.partial(final_kernel, at, part, bases, last),
            in_specs=[vmem] * len(inputs) + [pl.BlockSpec(memory_space=pl.ANY)] * len(outs),
            out_specs=[pl.BlockSpec(memory_space=pl.ANY)] * (2 + last),
            out_shape=[sds((rows, width), BF16), sds((1, rows, width), BF16)]
            + [sds((rank, width), F32)] * last,
            input_output_aliases={len(inputs) + k: k for k in range(len(outs))},
            scratch_shapes=[pltpu.VMEM((rows, part), BF16)] * 2 + [dma((4, 2, 2))],
            compiler_params=params(16),
            cost_estimate=cost(REBUILD),
            name="rebuild",
        )(*inputs, *outs)
    rebuilt, error, factor = outs
    return rebuilt, error, factor.T


def solution(mesh):
    return jax.shard_map(
        per_device,
        mesh=mesh,
        in_specs=(P("dp", None, "tensor"), P("dp", "tensor", None), P("dp", "tensor", None), P()),
        out_specs=(P("tensor", None), P("dp", "tensor", None), P()),
        check_vma=False,
    )
```

```python
import functools

import jax
import jax.numpy as jnp
from jax import lax
from jax.experimental import pallas as pl
from jax.experimental.pallas import tpu as pltpu
from jax.sharding import PartitionSpec as P

F32 = jnp.float32
BF16 = jnp.bfloat16
SHRINK = 2.0**-23
TINY = 1e-30
REBUILD = 4e9
ROOM = 2.0**14
BLOCK = 512


def params(mib):
    return pltpu.CompilerParams(vmem_limit_bytes=mib * 2**20)


def cost(flops):
    return pl.CostEstimate(flops=int(flops) + 1, bytes_accessed=1, transcendentals=0)


def dot(a, b, contract):
    return lax.dot_general(a, b, ((contract[:1], contract[1:]), ((), ())), preferred_element_type=F32)


def split(x):
    hi = x.astype(BF16)
    rest = x - hi.astype(F32)
    mid = rest.astype(BF16)
    lo = (rest - mid.astype(F32)).astype(BF16)
    return hi.astype(F32), mid.astype(F32), lo.astype(F32)


def stack3(x, ref):
    rank = x.shape[0]
    for i, part in enumerate(split(x)):
        ref[i * rank : (i + 1) * rank, :] = part
    return ref[...].astype(BF16)


def sum3(y, rank):
    return (y[2 * rank :] + y[rank : 2 * rank]) + y[:rank]


def ring_of(n):
    return [2 * p if 2 * p < n else 2 * (n - p) - 1 for p in range(n)]


def ring_source(me, step, n):
    place = jnp.where(lax.rem(me, 2) == 0, me // 2, n - (me + 1) // 2)
    place = lax.rem(place - step + n, n)
    return jnp.where(2 * place < n, 2 * place, 2 * (n - place) - 1)


def ring_step(x, axis, n):
    ring = ring_of(n)
    return lax.ppermute(x, axis, [(ring[p], ring[(p + 1) % n]) for p in range(n)])


def exchange(pieces, axis, n):
    return [pieces[0]] + [
        lax.ppermute(pieces[k], axis, [(i, (i + k) % n) for i in range(n)]) for k in range(1, n)
    ]


def swap(x, axis, n, bit):
    return lax.ppermute(x, axis, [(i, i ^ bit) for i in range(n)])


def groups(n):
    assert n & (n - 1) == 0
    bits = [1 << i for i in range(n.bit_length() - 1)]
    return [bits[i : i + 2] for i in range(0, len(bits), 2)]


def terms_of(x, axis, n, group):
    others = group if len(group) == 1 else [group[0], group[1], group[0] | group[1]]
    return [x] + [swap(x, axis, n, bit) for bit in others]


def total_of(refs):
    total = refs[0][...] + refs[1][...]
    if len(refs) == 4:
        total = total + (refs[2][...] + refs[3][...])
    return total


def token_factor_kernel(w_hbm, g_hbm, gw_ref, terms_ref, w, g, w3, sems):
    rank = w.shape[0]
    copies = [
        pltpu.make_async_copy(w_hbm, w, sems.at[0]),
        pltpu.make_async_copy(g_hbm, g, sems.at[1]),
    ]
    for copy in copies:
        copy.start()
    copies[0].wait()
    terms = stack3(w[...] * SHRINK, w3)
    terms_ref[...] = terms
    copies[1].wait()
    gw_ref[...] = jnp.zeros_like(gw_ref)
    gw_ref[0:rank, 0 : g.shape[1]] = sum3(dot(terms, g[0], (1, 1)), rank)


def cut_kernel(x_ref, *refs):
    chunks, sems = refs[:-1], refs[-1]
    copies = []
    at = 0
    for c, chunk in enumerate(chunks):
        part = chunk.shape[2]
        copies.append(pltpu.make_async_copy(x_ref.at[:, :, pl.ds(at, part)], chunk, sems.at[c]))
        copies[-1].start()
        at += part
    for copy in copies:
        copy.wait()


def error_left_kernel(terms_ref, e_hbm, out_ref, e_ref, sems):
    rank = out_ref.shape[0]
    count = sems.shape[0]
    high = e_ref.shape[1] // count
    copies = []
    for c in range(count):
        rows = pl.ds(c * high, high)
        copies.append(pltpu.make_async_copy(e_hbm.at[:, rows, :], e_ref.at[:, rows, :], sems.at[c]))
        copies[-1].start()
    terms = terms_ref[...]
    for c in range(count):
        copies[c].wait()
        rows = slice(c * high, (c + 1) * high)
        out_ref[:, rows] = sum3(dot(terms, e_ref[0, rows, :], (1, 1)), rank)


def left_kernel(a_ref, e_ref, *refs):
    gws, out_ref, g3 = refs[:-2], refs[-2], refs[-1]
    n = len(gws)
    rank = e_ref.shape[0]
    tok = a_ref.shape[1] // n
    me = lax.axis_index("tensor")
    total = e_ref[...]
    for k in range(n):
        src = lax.rem(me - k + n, n)
        rows = a_ref[0, pl.ds(pl.multiple_of(src * tok, tok), tok), :]
        total += sum3(dot(stack3(gws[k][0:rank, 0:tok], g3), rows, (1, 0)), rank)
    out_ref[...] = total


def mean_kernel(n, scale, a_ref, *refs):
    terms = refs[:-7]
    p_ref, scaled_ref, extra_ref, held_ref, next_ref, p3, blocks = refs[-7:]
    rank = p_ref.shape[0]
    tok = a_ref.shape[1] // n
    me = lax.axis_index("tensor")
    mean = total_of(terms) * scale
    p_ref[...] = mean
    top = jnp.max(jnp.max(jnp.abs(mean), axis=1, keepdims=True), axis=0, keepdims=True)
    top = jnp.maximum(top, TINY)
    scaled = mean / (top * ROOM)
    scaled_ref[...] = scaled
    parts = stack3(scaled, p3)
    for t in range(n):
        blocks[t] = sum3(dot(parts, a_ref[0, t * tok : (t + 1) * tok, :], (1, 1)), rank)
    for s in range(n - 1):
        held_ref[:, s * tok : (s + 1) * tok] = blocks[ring_source(me, s, n)]
    next_ref[...] = jnp.zeros_like(next_ref)
    next_ref[0:rank, 0:tok] = blocks[ring_source(me, n - 1, n)]
    next_ref[rank : rank + 1, 0:1] = top
    extra_ref[...] = jnp.zeros_like(extra_ref)
    for i in range(rank):
        extra_ref[:, i : i + 1] = jnp.sum(mean * mean[i : i + 1, :], axis=1, keepdims=True)
    extra_ref[:, rank : rank + 1] = jnp.broadcast_to(top, (rank, 1))


def error_right_kernel(p_ref, e_ref, out_ref, p3):
    rank = p_ref.shape[0]
    parts = stack3(p_ref[...], p3)
    for c in range(e_ref.shape[2] // BLOCK):
        cols = slice(c * BLOCK, (c + 1) * BLOCK)
        out_ref[:, cols] = sum3(dot(parts, e_ref[0, :, cols], (1, 0)), rank)


def lower_inverse(gram, rank):
    at = lambda i, j: gram[i : i + 1, j : j + 1]
    low, inv = {}, {}
    for j in range(rank):
        d = at(j, j)
        for k in range(j):
            d = d - low[j, k] * low[j, k]
        inv[j, j] = lax.rsqrt(d)
        for i in range(j + 1, rank):
            v = at(i, j)
            for k in range(j):
                v = v - low[i, k] * low[j, k]
            low[i, j] = v * inv[j, j]
    for j in range(rank):
        for i in range(j + 1, rank):
            v = low[i, j] * inv[j, j]
            for k in range(j + 1, i):
                v = v + low[i, k] * inv[k, j]
            inv[i, j] = -v * inv[i, i]
    return inv


def solve(inv, x, rank):
    total = 0.0
    for j in range(rank):
        column = [inv.get((i, j), jnp.zeros((1, 1), F32)) for i in range(rank)]
        total = total + jnp.concatenate(column, axis=0) * x[j : j + 1, :]
    return total


def right_kernel(r_ref, y_ref, got_ref, extra_ref, *refs):
    held, (keep_ref, send_ref, y3, outbox) = refs[:-4], refs[-4:]
    rank = r_ref.shape[0]
    tok = held[0].shape[1]
    half = r_ref.shape[1] // 2
    core = lax.rem(lax.axis_index("dp"), 2)
    mine = extra_ref[0:1, rank : rank + 1]
    theirs = got_ref[rank : rank + 1, 0:1]
    top = jnp.maximum(mine, theirs)
    products = y_ref[...] * (mine / top)
    joint = products[:, 0:tok] + got_ref[0:rank, 0:tok] * (theirs / top)
    terms = stack3(jnp.concatenate([joint, products[:, tok:]], axis=1), y3)
    for h in range(2):
        for c in range(half // BLOCK):
            at = h * half + c * BLOCK
            cols = slice(at, at + BLOCK)
            grads = jnp.concatenate([g[0, :, cols] for g in held], axis=0)
            fresh = sum3(dot(terms, grads, (1, 0)), rank)
            outbox[h, :, c * BLOCK : (c + 1) * BLOCK] = r_ref[:, cols] * (mine / top) + fresh
        outbox[h, :, half:] = extra_ref[...]
        outbox[h, :, half + rank : half + rank + 1] = jnp.broadcast_to(top, (rank, 1))
    keep_ref[...] = outbox[core]
    send_ref[...] = outbox[1 - core]


def join_kernel(rank, *refs):
    xs, out_ref = refs[:-1], refs[-1]
    half = out_ref.shape[1] - 128
    mark = slice(half + rank, half + rank + 1)
    tops = [x[0:1, mark] for x in xs]
    top = jnp.maximum(tops[0], tops[1])
    for other in tops[2:]:
        top = jnp.maximum(top, other)

    def total(terms):
        first = terms[0] + terms[1]
        return first + (terms[2] + terms[3]) if len(terms) == 4 else first

    out_ref[:, :half] = total([x[:, :half] * (t / top) for x, t in zip(xs, tops)])
    out_ref[:, half:] = total([x[:, half:] for x in xs])
    out_ref[:, mark] = jnp.broadcast_to(top, (rank, 1))


def add_kernel(*refs):
    refs[-1][...] = total_of(refs[:-1])


LEFT_TERMS = (0, 0, 1, 0, 2, 1)
RIGHT_TERMS = (0, 1, 0, 2, 0, 1)


def stack_terms(terms, x, ref):
    parts = split(x)
    rank = x.shape[0]
    for i, term in enumerate(terms):
        ref[i * rank : (i + 1) * rank, :] = parts[term]
    return ref[...]


def factor_solve(m, total_ref):
    rank = total_ref.shape[0]
    half = total_ref.shape[1] - 128
    inv = lower_inverse(total_ref[:, half : half + rank] * (1.0 / m), rank)
    top = total_ref[0:1, half + rank : half + rank + 1] * (ROOM / (m * m))
    scaled = {key: value * top for key, value in inv.items()}
    return inv, solve(scaled, total_ref[:, 0:half], rank)


def half_kernel(m, p_ref, mine_ref, left_ref, whole_ref, right_ref, left, right):
    inv, half = factor_solve(m, mine_ref)
    whole_ref[...] = half
    right_ref[...] = stack_terms(RIGHT_TERMS, half, right).astype(BF16)
    ortho = solve(inv, p_ref[...], p_ref.shape[0])
    left_ref[...] = stack_terms(LEFT_TERMS, ortho, left).T.astype(BF16)


def factor_kernel(m, other_ref, mine_ref, mine_terms_ref, whole_ref, right_ref, right):
    half = mine_ref.shape[1]
    core = lax.rem(lax.axis_index("dp"), 2)
    _, other = factor_solve(m, other_ref)
    terms = stack_terms(RIGHT_TERMS, other, right).astype(BF16)
    for c in range(2):

        @pl.when(core == c)
        def _():
            here = slice(c * half, (c + 1) * half)
            there = slice((1 - c) * half, (2 - c) * half)
            whole_ref[:, here] = mine_ref[...]
            whole_ref[:, there] = other
            right_ref[:, here] = mine_terms_ref[...]
            right_ref[:, there] = terms


def acts_kernel(n, a_ref, out_ref, acts):
    tok = a_ref.shape[1] // n
    me = lax.axis_index("tensor")
    for s in range(n):
        src = ring_source(me, s, n)
        here = a_ref[0, pl.ds(pl.multiple_of(src * tok, tok), tok), :]
        acts[s * tok : (s + 1) * tok, :] = here
    out_ref[...] = acts[...].T


def final_kernel(at, part, bases, last, acts_ref, left_ref, right_ref, e_ref, *refs):
    slots = refs[: len(bases)]
    outs, (rebuilt_v, error_v, sems) = refs[-5 - last : -3], refs[-3:]
    rebuilt_hbm, error_hbm = outs[:2]
    rows = e_ref.shape[1]
    wide = 256
    strips = sems.shape[0] - 1
    high = rows // strips
    tiles = part // wide
    group = -(-tiles // sems.shape[1])
    copies = []
    if last:
        copies.append(pltpu.make_async_copy(refs[len(bases)], outs[2], sems.at[strips, 0, 0]))
        copies[-1].start()
    for r in range(strips):
        here = slice(r * high, (r + 1) * high)
        for c in range(part // wide):
            cols = slice(c * wide, (c + 1) * wide)
            there = slice(at + c * wide, at + (c + 1) * wide)
            grads = [
                slot[0, :, there.start - base : there.stop - base]
                for slot, base in zip(slots, bases)
            ]
            grad = dot(acts_ref[here, :], jnp.concatenate(grads, axis=0), (1, 0))
            matrix = grad + e_ref[0, here, there].astype(F32)
            rebuilt = dot(left_ref[here, :], right_ref[:, there], (1, 0))
            rebuilt_v[here, cols] = rebuilt.astype(BF16)
            error_v[here, cols] = (matrix - rebuilt).astype(BF16)
            if (c + 1) % group == 0 or c + 1 == tiles:
                k = c // group
                size = (c + 1 - k * group) * wide
                strip, span = pl.ds(r * high, high), pl.ds(k * group * wide, size)
                far = pl.ds(at + k * group * wide, size)
                copies += [
                    pltpu.make_async_copy(
                        rebuilt_v.at[strip, span], rebuilt_hbm.at[strip, far], sems.at[r, k, 0]
                    ),
                    pltpu.make_async_copy(
                        error_v.at[strip, span], error_hbm.at[0, strip, far], sems.at[r, k, 1]
                    ),
                ]
                copies[-2].start()
                copies[-1].start()
    for copy in copies:
        copy.wait()


def per_device(activations, out_grads, error_buffer, warm_factor):
    m = lax.axis_size("dp")
    n = lax.axis_size("tensor")
    _, tokens, rows = activations.shape
    _, tok, width = out_grads.shape
    rank = warm_factor.shape[1]
    half = width // 2
    w = warm_factor.T
    sds = jax.ShapeDtypeStruct
    hbm = pl.BlockSpec(memory_space=pltpu.HBM)
    vmem = pl.BlockSpec(memory_space=pltpu.VMEM)
    dma = pltpu.SemaphoreType.DMA
    pin = lambda x: pltpu.with_memory_space_constraint(x, pltpu.HBM)

    def call(kernel, shapes, scratch, name, specs=None, flops=0):
        return pl.pallas_call(
            kernel,
            out_shape=shapes,
            **({"in_specs": specs} if specs else {}),
            scratch_shapes=scratch,
            compiler_params=params(16),
            cost_estimate=cost(flops),
            name=name,
        )

    def add(*terms):
        return call(add_kernel, sds(terms[0].shape, F32), [], "add")(*terms)

    def after(x, y):
        return lax.optimization_barrier((x, y))

    def cut(x, widths):
        shapes = [sds((1, tok, part), BF16) for part in widths]
        return call(cut_kernel, shapes, [dma((len(widths),))], "cut")(x)

    def step(x):
        return ring_step(x, "tensor", n)

    ring = [out_grads, step(out_grads)]

    gw, w_terms = call(
        token_factor_kernel,
        [sds((8, 128), F32), sds((3 * rank, width), BF16)],
        [
            pltpu.VMEM((rank, width), F32),
            pltpu.VMEM((1, tok, width), BF16),
            pltpu.VMEM((3 * rank, width), F32),
            dma((2,)),
        ],
        "token_factor", [hbm, hbm],
    )(pin(w), pin(out_grads))
    ew, error_v = call(
        error_left_kernel,
        [sds((rank, rows), F32), sds((1, rows, width), BF16)],
        [dma((rows // 128,))],
        "error_left", [vmem, hbm], 4.6e9,
    )(w_terms, pin(error_buffer))

    gw, ew = after(gw, ew)
    gws = exchange([gw] * n, "tensor", n)
    ring[1], gws = after(ring[1], gws)
    for _ in range(n - 2 - 1):
        ring.append(step(ring[-1]))
    left = call(
        left_kernel, sds((rank, rows), F32), [pltpu.VMEM((3 * rank, tok), F32)], "left"
    )(activations, ew, *gws)
    left = add(left, swap(left, "dp", m, 1))
    for group in groups(m // 2)[:-1]:
        left = add(*terms_of(left, "dp", m, [2 * bit for bit in group]))
    lefts = terms_of(left, "dp", m, [2 * bit for bit in groups(m // 2)[-1]])
    mean, scaled, extra, held, following = call(
        functools.partial(mean_kernel, n, 1.0 / (SHRINK * m)),
        [
            sds((rank, rows), F32),
            sds((rank, rows), F32),
            sds((rank, 128), F32),
            sds((rank, (n - 1) * tok), F32),
            sds((8, 128), F32),
        ],
        [pltpu.VMEM((3 * rank, rows), F32), pltpu.VMEM((n, rank, tok), F32)],
        "mean",
    )(activations, *lefts)
    got = step(following)

    right_raw = call(
        error_right_kernel,
        sds((rank, width), F32),
        [pltpu.VMEM((3 * rank, rows), F32)],
        "error_right", None, 1.2e9,
    )(scaled, error_v)

    widths = [width * 7 // 10, width * 3 // 10]
    last, (got, right_raw) = after(ring[-1], (got, right_raw))
    newest = list(cut(last, widths))
    newest[0] = step(newest[0])

    keep, send = call(
        right_kernel,
        [sds((rank, half + 128), F32)] * 2,
        [
            pltpu.VMEM((3 * rank, (n - 1) * tok), F32),
            pltpu.VMEM((2, rank, half + 128), F32),
        ],
        "right",
    )(right_raw, held, got, extra, *ring)
    total = add(keep, swap(send, "dp", m, 1))

    for group in groups(m // 2):
        total = add(*terms_of(total, "dp", m, [2 * bit for bit in group]))
    for group in groups(n):
        parts = terms_of(total, "tensor", n, group)
        if group == groups(n)[-1]:
            newest[0], parts[1:] = after(newest[0], parts[1:])
        total = call(
            functools.partial(join_kernel, rank), sds(total.shape, F32), [], "join"
        )(*parts)
    for c in range(1, len(widths)):
        last, total = after(newest[c], total)
        newest[c] = step(last)

    terms = len(LEFT_TERMS) * rank
    other = swap(total, "dp", m, 1)
    left_terms, mine, mine_terms = call(
        functools.partial(half_kernel, m),
        [sds((rows, terms), BF16), sds((rank, half), F32), sds((terms, half), BF16)],
        [pltpu.VMEM((terms, rows), F32), pltpu.VMEM((terms, half), F32)],
        "half", None, 1e9,
    )(mean, total)
    whole, right_terms = call(
        functools.partial(factor_kernel, m),
        [sds((rank, width), F32), sds((terms, width), BF16)],
        [pltpu.VMEM((terms, half), F32)],
        "factor",
    )(other, mine, mine_terms)

    acts = call(
        functools.partial(acts_kernel, n),
        sds((rows, tokens), BF16),
        [pltpu.VMEM((tokens, rows), BF16)],
        "acts",
    )(activations)
    pieces = []
    at = 0
    for part, x in zip(widths, newest):
        pieces.append((at, part, ring + [x], [0] * (n - 1) + [at]))
        at += part

    outs = ()
    for at, part, slots, bases in pieces:
        last = at + part == width
        inputs = [acts, left_terms, right_terms, error_v, *slots] + [whole] * last
        outs = pl.pallas_call(
            functools.partial(final_kernel, at, part, bases, last),
            in_specs=[vmem] * len(inputs) + [pl.BlockSpec(memory_space=pl.ANY)] * len(outs),
            out_specs=[pl.BlockSpec(memory_space=pl.ANY)] * (2 + last),
            out_shape=[sds((rows, width), BF16), sds((1, rows, width), BF16)]
            + [sds((rank, width), F32)] * last,
            input_output_aliases={len(inputs) + k: k for k in range(len(outs))},
            scratch_shapes=[pltpu.VMEM((rows, part), BF16)] * 2 + [dma((4, 4 if part > half else 3, 2))],
            compiler_params=params(16),
            cost_estimate=cost(REBUILD),
            name="rebuild",
        )(*inputs, *outs)
    rebuilt, error, factor = outs
    return rebuilt, error, factor.T


def solution(mesh):
    return jax.shard_map(
        per_device,
        mesh=mesh,
        in_specs=(P("dp", None, "tensor"), P("dp", "tensor", None), P("dp", "tensor", None), P()),
        out_specs=(P("tensor", None), P("dp", "tensor", None), P()),
        check_vma=False,
    )
```

```python
import functools

import jax
import jax.numpy as jnp
from jax import lax
from jax.experimental import pallas as pl
from jax.experimental.pallas import tpu as pltpu
from jax.sharding import PartitionSpec as P

F32 = jnp.float32
BF16 = jnp.bfloat16
SHRINK = 2.0**-23
TINY = 1e-30
REBUILD = 4e9
RIGHT = 8e9
ROOM = 2.0**14
BLOCK = 512


def params(mib):
    return pltpu.CompilerParams(vmem_limit_bytes=mib * 2**20)


def cost(flops):
    return pl.CostEstimate(flops=int(flops) + 1, bytes_accessed=1, transcendentals=0)


def dot(a, b, contract):
    return lax.dot_general(a, b, ((contract[:1], contract[1:]), ((), ())), preferred_element_type=F32)


def split(x):
    hi = x.astype(BF16)
    rest = x - hi.astype(F32)
    mid = rest.astype(BF16)
    lo = (rest - mid.astype(F32)).astype(BF16)
    return hi.astype(F32), mid.astype(F32), lo.astype(F32)


def stack3(x, ref):
    rank = x.shape[0]
    for i, part in enumerate(split(x)):
        ref[i * rank : (i + 1) * rank, :] = part
    return ref[...].astype(BF16)


def sum3(y, rank):
    return (y[2 * rank :] + y[rank : 2 * rank]) + y[:rank]


def ring_of(n):
    return [2 * p if 2 * p < n else 2 * (n - p) - 1 for p in range(n)]


def ring_source(me, step, n):
    place = jnp.where(lax.rem(me, 2) == 0, me // 2, n - (me + 1) // 2)
    place = lax.rem(place - step + n, n)
    return jnp.where(2 * place < n, 2 * place, 2 * (n - place) - 1)


def ring_step(x, axis, n, by=1):
    ring = ring_of(n)
    return lax.ppermute(x, axis, [(ring[p], ring[(p + by) % n]) for p in range(n)])


def exchange(pieces, axis, n):
    return [pieces[0]] + [
        lax.ppermute(pieces[k], axis, [(i, (i + k) % n) for i in range(n)]) for k in range(1, n)
    ]


def swap(x, axis, n, bit):
    return lax.ppermute(x, axis, [(i, i ^ bit) for i in range(n)])


def groups(n):
    assert n & (n - 1) == 0
    bits = [1 << i for i in range(n.bit_length() - 1)]
    return [bits[i : i + 2] for i in range(0, len(bits), 2)]


def terms_of(x, axis, n, group):
    others = group if len(group) == 1 else [group[0], group[1], group[0] | group[1]]
    return [x] + [swap(x, axis, n, bit) for bit in others]


def total_of(refs):
    total = refs[0][...] + refs[1][...]
    if len(refs) == 4:
        total = total + (refs[2][...] + refs[3][...])
    return total


def token_factor_kernel(w_hbm, g_hbm, gw_ref, terms_ref, w, g, w3, sems):
    rank = w.shape[0]
    copies = [
        pltpu.make_async_copy(w_hbm, w, sems.at[0]),
        pltpu.make_async_copy(g_hbm, g, sems.at[1]),
    ]
    for copy in copies:
        copy.start()
    copies[0].wait()
    terms = stack3(w[...] * SHRINK, w3)
    terms_ref[...] = terms
    copies[1].wait()
    gw_ref[...] = jnp.zeros_like(gw_ref)
    gw_ref[0:rank, 0 : g.shape[1]] = sum3(dot(terms, g[0], (1, 1)), rank)


def cut_kernel(x_ref, *refs):
    chunks, sems = refs[:-1], refs[-1]
    copies = []
    at = 0
    for c, chunk in enumerate(chunks):
        part = chunk.shape[2]
        copies.append(pltpu.make_async_copy(x_ref.at[:, :, pl.ds(at, part)], chunk, sems.at[c]))
        copies[-1].start()
        at += part
    for copy in copies:
        copy.wait()


def error_left_kernel(terms_ref, e_hbm, out_ref, e_ref, sems):
    rank = out_ref.shape[0]
    count = sems.shape[0]
    high = e_ref.shape[1] // count
    copies = []
    for c in range(count):
        rows = pl.ds(c * high, high)
        copies.append(pltpu.make_async_copy(e_hbm.at[:, rows, :], e_ref.at[:, rows, :], sems.at[c]))
        copies[-1].start()
    terms = terms_ref[...]
    for c in range(count):
        copies[c].wait()
        rows = slice(c * high, (c + 1) * high)
        out_ref[:, rows] = sum3(dot(terms, e_ref[0, rows, :], (1, 1)), rank)


def left_kernel(a_ref, e_ref, *refs):
    gws, out_ref, g3 = refs[:-2], refs[-2], refs[-1]
    n = len(gws)
    rank = e_ref.shape[0]
    tok = a_ref.shape[1] // n
    me = lax.axis_index("tensor")
    total = e_ref[...]
    for k in range(n):
        src = lax.rem(me - k + n, n)
        rows = a_ref[0, pl.ds(pl.multiple_of(src * tok, tok), tok), :]
        total += sum3(dot(stack3(gws[k][0:rank, 0:tok], g3), rows, (1, 0)), rank)
    out_ref[...] = total


def mean_kernel(n, scale, a_ref, *refs):
    terms = refs[:-7]
    p_ref, scaled_ref, extra_ref, held_ref, next_ref, p3, blocks = refs[-7:]
    rank = p_ref.shape[0]
    tok = a_ref.shape[1] // n
    me = lax.axis_index("tensor")
    mean = total_of(terms) * scale
    p_ref[...] = mean
    top = jnp.max(jnp.max(jnp.abs(mean), axis=1, keepdims=True), axis=0, keepdims=True)
    top = jnp.maximum(top, TINY)
    scaled = mean / (top * ROOM)
    scaled_ref[...] = scaled
    parts = stack3(scaled, p3)
    for t in range(n):
        blocks[t] = sum3(dot(parts, a_ref[0, t * tok : (t + 1) * tok, :], (1, 1)), rank)
    for s in range(n - 1):
        held_ref[:, s * tok : (s + 1) * tok] = blocks[ring_source(me, s, n)]
    next_ref[...] = jnp.zeros_like(next_ref)
    next_ref[0:rank, 0:tok] = blocks[ring_source(me, n - 1, n)]
    next_ref[rank : rank + 1, 0:1] = top
    extra_ref[...] = jnp.zeros_like(extra_ref)
    for i in range(rank):
        extra_ref[:, i : i + 1] = jnp.sum(mean * mean[i : i + 1, :], axis=1, keepdims=True)
    extra_ref[:, rank : rank + 1] = jnp.broadcast_to(top, (rank, 1))


def error_right_kernel(p_ref, e_ref, out_ref, p3):
    rank = p_ref.shape[0]
    parts = stack3(p_ref[...], p3)
    for c in range(e_ref.shape[2] // BLOCK):
        cols = slice(c * BLOCK, (c + 1) * BLOCK)
        out_ref[:, cols] = sum3(dot(parts, e_ref[0, :, cols], (1, 0)), rank)


def lower_inverse(gram, rank):
    at = lambda i, j: gram[i : i + 1, j : j + 1]
    low, inv = {}, {}
    for j in range(rank):
        d = at(j, j)
        for k in range(j):
            d = d - low[j, k] * low[j, k]
        inv[j, j] = lax.rsqrt(d)
        for i in range(j + 1, rank):
            v = at(i, j)
            for k in range(j):
                v = v - low[i, k] * low[j, k]
            low[i, j] = v * inv[j, j]
    for j in range(rank):
        for i in range(j + 1, rank):
            v = low[i, j] * inv[j, j]
            for k in range(j + 1, i):
                v = v + low[i, k] * inv[k, j]
            inv[i, j] = -v * inv[i, i]
    return inv


def solve(inv, x, rank):
    total = 0.0
    for j in range(rank):
        column = [inv.get((i, j), jnp.zeros((1, 1), F32)) for i in range(rank)]
        total = total + jnp.concatenate(column, axis=0) * x[j : j + 1, :]
    return total


def right_kernel(r_ref, y_ref, got_ref, extra_ref, *refs):
    held, (keep_ref, send_ref, y3, outbox) = refs[:-4], refs[-4:]
    rank = r_ref.shape[0]
    tok = held[0].shape[1]
    half = r_ref.shape[1] // 2
    core = lax.rem(lax.axis_index("dp"), 2)
    mine = extra_ref[0:1, rank : rank + 1]
    theirs = got_ref[rank : rank + 1, 0:1]
    top = jnp.maximum(mine, theirs)
    products = y_ref[...] * (mine / top)
    joint = products[:, 0:tok] + got_ref[0:rank, 0:tok] * (theirs / top)
    terms = stack3(jnp.concatenate([joint, products[:, tok:]], axis=1), y3)
    for h in range(2):
        for c in range(half // BLOCK):
            at = h * half + c * BLOCK
            cols = slice(at, at + BLOCK)
            grads = jnp.concatenate([g[0, :, cols] for g in held], axis=0)
            fresh = sum3(dot(terms, grads, (1, 0)), rank)
            outbox[h, :, c * BLOCK : (c + 1) * BLOCK] = r_ref[:, cols] * (mine / top) + fresh
        outbox[h, :, half:] = extra_ref[...]
        outbox[h, :, half + rank : half + rank + 1] = jnp.broadcast_to(top, (rank, 1))
    keep_ref[...] = outbox[core]
    send_ref[...] = outbox[1 - core]


def join_kernel(rank, *refs):
    xs, out_ref = refs[:-1], refs[-1]
    half = out_ref.shape[1] - 128
    mark = slice(half + rank, half + rank + 1)
    tops = [x[0:1, mark] for x in xs]
    top = jnp.maximum(tops[0], tops[1])
    for other in tops[2:]:
        top = jnp.maximum(top, other)

    def total(terms):
        first = terms[0] + terms[1]
        return first + (terms[2] + terms[3]) if len(terms) == 4 else first

    out_ref[:, :half] = total([x[:, :half] * (t / top) for x, t in zip(xs, tops)])
    out_ref[:, half:] = total([x[:, half:] for x in xs])
    out_ref[:, mark] = jnp.broadcast_to(top, (rank, 1))


def add_kernel(*refs):
    refs[-1][...] = total_of(refs[:-1])


LEFT_TERMS = (0, 0, 1, 0, 2, 1)
RIGHT_TERMS = (0, 1, 0, 2, 0, 1)


def stack_terms(terms, x, ref):
    parts = split(x)
    rank = x.shape[0]
    for i, term in enumerate(terms):
        ref[i * rank : (i + 1) * rank, :] = parts[term]
    return ref[...]


def factor_solve(m, total_ref):
    rank = total_ref.shape[0]
    half = total_ref.shape[1] - 128
    inv = lower_inverse(total_ref[:, half : half + rank] * (1.0 / m), rank)
    top = total_ref[0:1, half + rank : half + rank + 1] * (ROOM / (m * m))
    scaled = {key: value * top for key, value in inv.items()}
    return inv, solve(scaled, total_ref[:, 0:half], rank)


def half_kernel(m, p_ref, mine_ref, left_ref, whole_ref, right_ref, left, right):
    inv, half = factor_solve(m, mine_ref)
    whole_ref[...] = half
    right_ref[...] = stack_terms(RIGHT_TERMS, half, right).astype(BF16)
    ortho = solve(inv, p_ref[...], p_ref.shape[0])
    left_ref[...] = stack_terms(LEFT_TERMS, ortho, left).T.astype(BF16)


def factor_kernel(m, other_ref, mine_ref, mine_terms_ref, whole_ref, right_ref, right):
    half = mine_ref.shape[1]
    core = lax.rem(lax.axis_index("dp"), 2)
    _, other = factor_solve(m, other_ref)
    terms = stack_terms(RIGHT_TERMS, other, right).astype(BF16)
    for c in range(2):

        @pl.when(core == c)
        def _():
            here = slice(c * half, (c + 1) * half)
            there = slice((1 - c) * half, (2 - c) * half)
            whole_ref[:, here] = mine_ref[...]
            whole_ref[:, there] = other
            right_ref[:, here] = mine_terms_ref[...]
            right_ref[:, there] = terms


def acts_kernel(n, a_ref, out_ref, acts):
    tok = a_ref.shape[1] // n
    me = lax.axis_index("tensor")
    for s in range(n):
        src = ring_source(me, s, n)
        here = a_ref[0, pl.ds(pl.multiple_of(src * tok, tok), tok), :]
        acts[s * tok : (s + 1) * tok, :] = here
    out_ref[...] = acts[...].T


def final_kernel(at, part, bases, last, acts_ref, left_ref, right_ref, e_ref, *refs):
    slots = refs[: len(bases)]
    outs, (rebuilt_v, error_v, sems) = refs[-5 - last : -3], refs[-3:]
    rebuilt_hbm, error_hbm = outs[:2]
    rows = e_ref.shape[1]
    wide = 256
    strips = sems.shape[0] - 1
    high = rows // strips
    tiles = part // wide
    group = -(-tiles // sems.shape[1])
    copies = []
    if last:
        copies.append(pltpu.make_async_copy(refs[len(bases)], outs[2], sems.at[strips, 0, 0]))
        copies[-1].start()
    for r in range(strips):
        here = slice(r * high, (r + 1) * high)
        for c in range(part // wide):
            cols = slice(c * wide, (c + 1) * wide)
            there = slice(at + c * wide, at + (c + 1) * wide)
            grads = [
                slot[0, :, there.start - base : there.stop - base]
                for slot, base in zip(slots, bases)
            ]
            grad = dot(acts_ref[here, :], jnp.concatenate(grads, axis=0), (1, 0))
            matrix = grad + e_ref[0, here, there].astype(F32)
            rebuilt = dot(left_ref[here, :], right_ref[:, there], (1, 0))
            rebuilt_v[here, cols] = rebuilt.astype(BF16)
            error_v[here, cols] = (matrix - rebuilt).astype(BF16)
            if (c + 1) % group == 0 or c + 1 == tiles:
                k = c // group
                size = (c + 1 - k * group) * wide
                strip, span = pl.ds(r * high, high), pl.ds(k * group * wide, size)
                far = pl.ds(at + k * group * wide, size)
                copies += [
                    pltpu.make_async_copy(
                        rebuilt_v.at[strip, span], rebuilt_hbm.at[strip, far], sems.at[r, k, 0]
                    ),
                    pltpu.make_async_copy(
                        error_v.at[strip, span], error_hbm.at[0, strip, far], sems.at[r, k, 1]
                    ),
                ]
                copies[-2].start()
                copies[-1].start()
    for copy in copies:
        copy.wait()


def per_device(activations, out_grads, error_buffer, warm_factor):
    m = lax.axis_size("dp")
    n = lax.axis_size("tensor")
    _, tokens, rows = activations.shape
    _, tok, width = out_grads.shape
    rank = warm_factor.shape[1]
    half = width // 2
    w = warm_factor.T
    sds = jax.ShapeDtypeStruct
    hbm = pl.BlockSpec(memory_space=pltpu.HBM)
    vmem = pl.BlockSpec(memory_space=pltpu.VMEM)
    dma = pltpu.SemaphoreType.DMA
    pin = lambda x: pltpu.with_memory_space_constraint(x, pltpu.HBM)

    def call(kernel, shapes, scratch, name, specs=None, flops=0):
        return pl.pallas_call(
            kernel,
            out_shape=shapes,
            **({"in_specs": specs} if specs else {}),
            scratch_shapes=scratch,
            compiler_params=params(16),
            cost_estimate=cost(flops),
            name=name,
        )

    def add(*terms):
        return call(add_kernel, sds(terms[0].shape, F32), [], "add")(*terms)

    def after(x, y):
        return lax.optimization_barrier((x, y))

    def cut(x, widths):
        shapes = [sds((1, tok, part), BF16) for part in widths]
        return call(cut_kernel, shapes, [dma((len(widths),))], "cut")(x)

    def step(x):
        return ring_step(x, "tensor", n)

    ring = [out_grads, step(out_grads)]

    gw, w_terms = call(
        token_factor_kernel,
        [sds((8, 128), F32), sds((3 * rank, width), BF16)],
        [
            pltpu.VMEM((rank, width), F32),
            pltpu.VMEM((1, tok, width), BF16),
            pltpu.VMEM((3 * rank, width), F32),
            dma((2,)),
        ],
        "token_factor", [hbm, hbm],
    )(pin(w), pin(out_grads))
    ew, error_v = call(
        error_left_kernel,
        [sds((rank, rows), F32), sds((1, rows, width), BF16)],
        [dma((rows // 128,))],
        "error_left", [vmem, hbm], 4.6e9,
    )(w_terms, pin(error_buffer))

    gw, ew = after(gw, ew)
    gws = exchange([gw] * n, "tensor", n)
    ring[1], gws = after(ring[1], gws)
    for _ in range(n - 2 - 1):
        ring.append(step(ring[-1]))
    left = call(
        left_kernel, sds((rank, rows), F32), [pltpu.VMEM((3 * rank, tok), F32)], "left"
    )(activations, ew, *gws)
    left = add(left, swap(left, "dp", m, 1))
    for group in groups(m // 2)[:-1]:
        left = add(*terms_of(left, "dp", m, [2 * bit for bit in group]))
    lefts = terms_of(left, "dp", m, [2 * bit for bit in groups(m // 2)[-1]])
    mean, scaled, extra, held, following = call(
        functools.partial(mean_kernel, n, 1.0 / (SHRINK * m)),
        [
            sds((rank, rows), F32),
            sds((rank, rows), F32),
            sds((rank, 128), F32),
            sds((rank, (n - 1) * tok), F32),
            sds((8, 128), F32),
        ],
        [pltpu.VMEM((3 * rank, rows), F32), pltpu.VMEM((n, rank, tok), F32)],
        "mean",
    )(activations, *lefts)
    got = step(following)

    right_raw = call(
        error_right_kernel,
        sds((rank, width), F32),
        [pltpu.VMEM((3 * rank, rows), F32)],
        "error_right", None, 1.2e9,
    )(scaled, error_v)

    widths = [width * 7 // 10, width * 3 // 10]
    newest = list(cut(out_grads, widths))
    newest[0], right_raw = after(newest[0], right_raw)
    newest[0] = ring_step(newest[0], "tensor", n, -1)

    keep, send = call(
        right_kernel,
        [sds((rank, half + 128), F32)] * 2,
        [
            pltpu.VMEM((3 * rank, (n - 1) * tok), F32),
            pltpu.VMEM((2, rank, half + 128), F32),
        ],
        "right", None, RIGHT,
    )(right_raw, held, got, extra, *ring)
    total = add(keep, swap(send, "dp", m, 1))

    for group in groups(m // 2):
        total = add(*terms_of(total, "dp", m, [2 * bit for bit in group]))
    for group in groups(n):
        parts = terms_of(total, "tensor", n, group)
        if group == groups(n)[-1]:
            newest[0], parts[1:] = after(newest[0], parts[1:])
        total = call(
            functools.partial(join_kernel, rank), sds(total.shape, F32), [], "join"
        )(*parts)
    for c in range(1, len(widths)):
        last, total = after(newest[c], total)
        newest[c] = ring_step(last, "tensor", n, -1)

    terms = len(LEFT_TERMS) * rank
    other = swap(total, "dp", m, 1)
    left_terms, mine, mine_terms = call(
        functools.partial(half_kernel, m),
        [sds((rows, terms), BF16), sds((rank, half), F32), sds((terms, half), BF16)],
        [pltpu.VMEM((terms, rows), F32), pltpu.VMEM((terms, half), F32)],
        "half", None, 1e9,
    )(mean, total)
    whole, right_terms = call(
        functools.partial(factor_kernel, m),
        [sds((rank, width), F32), sds((terms, width), BF16)],
        [pltpu.VMEM((terms, half), F32)],
        "factor",
    )(other, mine, mine_terms)

    acts = call(
        functools.partial(acts_kernel, n),
        sds((rows, tokens), BF16),
        [pltpu.VMEM((tokens, rows), BF16)],
        "acts",
    )(activations)
    pieces = []
    at = 0
    for part, x in zip(widths, newest):
        pieces.append((at, part, ring + [x], [0] * (n - 1) + [at]))
        at += part

    outs = ()
    for at, part, slots, bases in pieces:
        last = at + part == width
        inputs = [acts, left_terms, right_terms, error_v, *slots] + [whole] * last
        outs = pl.pallas_call(
            functools.partial(final_kernel, at, part, bases, last),
            in_specs=[vmem] * len(inputs) + [pl.BlockSpec(memory_space=pl.ANY)] * len(outs),
            out_specs=[pl.BlockSpec(memory_space=pl.ANY)] * (2 + last),
            out_shape=[sds((rows, width), BF16), sds((1, rows, width), BF16)]
            + [sds((rank, width), F32)] * last,
            input_output_aliases={len(inputs) + k: k for k in range(len(outs))},
            scratch_shapes=[pltpu.VMEM((rows, part), BF16)] * 2 + [dma((4, 4 if part > half else 3, 2))],
            compiler_params=params(16),
            cost_estimate=cost(REBUILD),
            name="rebuild",
        )(*inputs, *outs)
    rebuilt, error, factor = outs
    return rebuilt, error, factor.T


def solution(mesh):
    return jax.shard_map(
        per_device,
        mesh=mesh,
        in_specs=(P("dp", None, "tensor"), P("dp", "tensor", None), P("dp", "tensor", None), P()),
        out_specs=(P("tensor", None), P("dp", "tensor", None), P()),
        check_vma=False,
    )
```

```python
import functools

import jax
import jax.numpy as jnp
from jax import lax
from jax.experimental import pallas as pl
from jax.experimental.pallas import tpu as pltpu
from jax.sharding import PartitionSpec as P

F32 = jnp.float32
BF16 = jnp.bfloat16
SHRINK = 2.0**-23
TINY = 1e-30
REBUILD = 4e9
ROOM = 2.0**14
BLOCK = 512


def params(mib):
    return pltpu.CompilerParams(vmem_limit_bytes=mib * 2**20)


def cost(flops):
    return pl.CostEstimate(flops=int(flops) + 1, bytes_accessed=1, transcendentals=0)


def dot(a, b, contract):
    return lax.dot_general(a, b, ((contract[:1], contract[1:]), ((), ())), preferred_element_type=F32)


def split(x):
    hi = x.astype(BF16)
    rest = x - hi.astype(F32)
    mid = rest.astype(BF16)
    lo = (rest - mid.astype(F32)).astype(BF16)
    return hi.astype(F32), mid.astype(F32), lo.astype(F32)


def stack3(x, ref):
    rank = x.shape[0]
    for i, part in enumerate(split(x)):
        ref[i * rank : (i + 1) * rank, :] = part
    return ref[...].astype(BF16)


def sum3(y, rank):
    return (y[2 * rank :] + y[rank : 2 * rank]) + y[:rank]


def ring_of(n):
    return [2 * p if 2 * p < n else 2 * (n - p) - 1 for p in range(n)]


def ring_source(me, step, n):
    place = jnp.where(lax.rem(me, 2) == 0, me // 2, n - (me + 1) // 2)
    place = lax.rem(place - step + n, n)
    return jnp.where(2 * place < n, 2 * place, 2 * (n - place) - 1)


def ring_step(x, axis, n):
    ring = ring_of(n)
    return lax.ppermute(x, axis, [(ring[p], ring[(p + 1) % n]) for p in range(n)])


def exchange(pieces, axis, n):
    return [pieces[0]] + [
        lax.ppermute(pieces[k], axis, [(i, (i + k) % n) for i in range(n)]) for k in range(1, n)
    ]


def swap(x, axis, n, bit):
    return lax.ppermute(x, axis, [(i, i ^ bit) for i in range(n)])


def groups(n):
    assert n & (n - 1) == 0
    bits = [1 << i for i in range(n.bit_length() - 1)]
    return [bits[i : i + 2] for i in range(0, len(bits), 2)]


def terms_of(x, axis, n, group):
    others = group if len(group) == 1 else [group[0], group[1], group[0] | group[1]]
    return [x] + [swap(x, axis, n, bit) for bit in others]


def total_of(refs):
    total = refs[0][...] + refs[1][...]
    if len(refs) == 4:
        total = total + (refs[2][...] + refs[3][...])
    return total


def token_factor_kernel(w_hbm, g_hbm, gw_ref, terms_ref, w, g, w3, sems):
    rank = w.shape[0]
    copies = [
        pltpu.make_async_copy(w_hbm, w, sems.at[0]),
        pltpu.make_async_copy(g_hbm, g, sems.at[1]),
    ]
    for copy in copies:
        copy.start()
    copies[0].wait()
    terms = stack3(w[...] * SHRINK, w3)
    terms_ref[...] = terms
    copies[1].wait()
    gw_ref[...] = jnp.zeros_like(gw_ref)
    gw_ref[0:rank, 0 : g.shape[1]] = sum3(dot(terms, g[0], (1, 1)), rank)


def cut_kernel(x_ref, *refs):
    chunks, sems = refs[:-1], refs[-1]
    copies = []
    at = 0
    for c, chunk in enumerate(chunks):
        part = chunk.shape[2]
        copies.append(pltpu.make_async_copy(x_ref.at[:, :, pl.ds(at, part)], chunk, sems.at[c]))
        copies[-1].start()
        at += part
    for copy in copies:
        copy.wait()


def error_left_kernel(terms_ref, e_hbm, out_ref, e_ref, sems):
    rank = out_ref.shape[0]
    count = sems.shape[0]
    high = e_ref.shape[1] // count
    copies = []
    for c in range(count):
        rows = pl.ds(c * high, high)
        copies.append(pltpu.make_async_copy(e_hbm.at[:, rows, :], e_ref.at[:, rows, :], sems.at[c]))
        copies[-1].start()
    terms = terms_ref[...]
    for c in range(count):
        copies[c].wait()
        rows = slice(c * high, (c + 1) * high)
        out_ref[:, rows] = sum3(dot(terms, e_ref[0, rows, :], (1, 1)), rank)


def left_kernel(a_ref, e_ref, *refs):
    gws, out_ref, g3 = refs[:-2], refs[-2], refs[-1]
    n = len(gws)
    rank = e_ref.shape[0]
    tok = a_ref.shape[1] // n
    me = lax.axis_index("tensor")
    total = e_ref[...]
    for k in range(n):
        src = lax.rem(me - k + n, n)
        rows = a_ref[0, pl.ds(pl.multiple_of(src * tok, tok), tok), :]
        total += sum3(dot(stack3(gws[k][0:rank, 0:tok], g3), rows, (1, 0)), rank)
    out_ref[...] = total


def mean_kernel(n, scale, a_ref, *refs):
    terms = refs[:-7]
    p_ref, scaled_ref, extra_ref, held_ref, next_ref, p3, blocks = refs[-7:]
    rank = p_ref.shape[0]
    tok = a_ref.shape[1] // n
    me = lax.axis_index("tensor")
    mean = total_of(terms) * scale
    p_ref[...] = mean
    top = jnp.max(jnp.max(jnp.abs(mean), axis=1, keepdims=True), axis=0, keepdims=True)
    top = jnp.maximum(top, TINY)
    scaled = mean / (top * ROOM)
    scaled_ref[...] = scaled
    parts = stack3(scaled, p3)
    for t in range(n):
        blocks[t] = sum3(dot(parts, a_ref[0, t * tok : (t + 1) * tok, :], (1, 1)), rank)
    for s in range(n - 1):
        held_ref[:, s * tok : (s + 1) * tok] = blocks[ring_source(me, s, n)]
    next_ref[...] = jnp.zeros_like(next_ref)
    next_ref[0:rank, 0:tok] = blocks[ring_source(me, n - 1, n)]
    next_ref[rank : rank + 1, 0:1] = top
    extra_ref[...] = jnp.zeros_like(extra_ref)
    for i in range(rank):
        extra_ref[:, i : i + 1] = jnp.sum(mean * mean[i : i + 1, :], axis=1, keepdims=True)
    extra_ref[:, rank : rank + 1] = jnp.broadcast_to(top, (rank, 1))


def error_right_kernel(p_ref, e_ref, out_ref, p3):
    rank = p_ref.shape[0]
    parts = stack3(p_ref[...], p3)
    for c in range(e_ref.shape[2] // BLOCK):
        cols = slice(c * BLOCK, (c + 1) * BLOCK)
        out_ref[:, cols] = sum3(dot(parts, e_ref[0, :, cols], (1, 0)), rank)


def lower_inverse(gram, rank):
    at = lambda i, j: gram[i : i + 1, j : j + 1]
    low, inv = {}, {}
    for j in range(rank):
        d = at(j, j)
        for k in range(j):
            d = d - low[j, k] * low[j, k]
        inv[j, j] = lax.rsqrt(d)
        for i in range(j + 1, rank):
            v = at(i, j)
            for k in range(j):
                v = v - low[i, k] * low[j, k]
            low[i, j] = v * inv[j, j]
    for j in range(rank):
        for i in range(j + 1, rank):
            v = low[i, j] * inv[j, j]
            for k in range(j + 1, i):
                v = v + low[i, k] * inv[k, j]
            inv[i, j] = -v * inv[i, i]
    return inv


def solve(inv, x, rank):
    total = 0.0
    for j in range(rank):
        column = [inv.get((i, j), jnp.zeros((1, 1), F32)) for i in range(rank)]
        total = total + jnp.concatenate(column, axis=0) * x[j : j + 1, :]
    return total


def right_kernel(r_ref, y_ref, got_ref, extra_ref, *refs):
    held, (keep_ref, send_ref, y3, outbox) = refs[:-4], refs[-4:]
    rank = r_ref.shape[0]
    tok = held[0].shape[1]
    half = r_ref.shape[1] // 2
    core = lax.rem(lax.axis_index("dp"), 2)
    mine = extra_ref[0:1, rank : rank + 1]
    theirs = got_ref[rank : rank + 1, 0:1]
    top = jnp.maximum(mine, theirs)
    products = y_ref[...] * (mine / top)
    joint = products[:, 0:tok] + got_ref[0:rank, 0:tok] * (theirs / top)
    terms = stack3(jnp.concatenate([joint, products[:, tok:]], axis=1), y3)
    for h in range(2):
        for c in range(half // BLOCK):
            at = h * half + c * BLOCK
            cols = slice(at, at + BLOCK)
            grads = jnp.concatenate([g[0, :, cols] for g in held], axis=0)
            fresh = sum3(dot(terms, grads, (1, 0)), rank)
            outbox[h, :, c * BLOCK : (c + 1) * BLOCK] = r_ref[:, cols] * (mine / top) + fresh
        outbox[h, :, half:] = extra_ref[...]
        outbox[h, :, half + rank : half + rank + 1] = jnp.broadcast_to(top, (rank, 1))
    keep_ref[...] = outbox[core]
    send_ref[...] = outbox[1 - core]


def join_kernel(rank, *refs):
    xs, out_ref = refs[:-1], refs[-1]
    half = out_ref.shape[1] - 128
    mark = slice(half + rank, half + rank + 1)
    tops = [x[0:1, mark] for x in xs]
    top = jnp.maximum(tops[0], tops[1])
    for other in tops[2:]:
        top = jnp.maximum(top, other)

    def total(terms):
        first = terms[0] + terms[1]
        return first + (terms[2] + terms[3]) if len(terms) == 4 else first

    out_ref[:, :half] = total([x[:, :half] * (t / top) for x, t in zip(xs, tops)])
    out_ref[:, half:] = total([x[:, half:] for x in xs])
    out_ref[:, mark] = jnp.broadcast_to(top, (rank, 1))


def add_kernel(*refs):
    refs[-1][...] = total_of(refs[:-1])


LEFT_TERMS = (0, 0, 1, 0, 2, 1)
RIGHT_TERMS = (0, 1, 0, 2, 0, 1)


def stack_terms(terms, x, ref):
    parts = split(x)
    rank = x.shape[0]
    for i, term in enumerate(terms):
        ref[i * rank : (i + 1) * rank, :] = parts[term]
    return ref[...]


def factor_solve(m, total_ref):
    rank = total_ref.shape[0]
    half = total_ref.shape[1] - 128
    inv = lower_inverse(total_ref[:, half : half + rank] * (1.0 / m), rank)
    top = total_ref[0:1, half + rank : half + rank + 1] * (ROOM / (m * m))
    scaled = {key: value * top for key, value in inv.items()}
    return inv, solve(scaled, total_ref[:, 0:half], rank)


def half_kernel(m, p_ref, mine_ref, left_ref, whole_ref, right_ref, left, right):
    inv, half = factor_solve(m, mine_ref)
    whole_ref[...] = half
    right_ref[...] = stack_terms(RIGHT_TERMS, half, right).astype(BF16)
    ortho = solve(inv, p_ref[...], p_ref.shape[0])
    left_ref[...] = stack_terms(LEFT_TERMS, ortho, left).T.astype(BF16)


def factor_kernel(m, other_ref, mine_ref, mine_terms_ref, whole_ref, right_ref, right):
    half = mine_ref.shape[1]
    core = lax.rem(lax.axis_index("dp"), 2)
    _, other = factor_solve(m, other_ref)
    terms = stack_terms(RIGHT_TERMS, other, right).astype(BF16)
    for c in range(2):

        @pl.when(core == c)
        def _():
            here = slice(c * half, (c + 1) * half)
            there = slice((1 - c) * half, (2 - c) * half)
            whole_ref[:, here] = mine_ref[...]
            whole_ref[:, there] = other
            right_ref[:, here] = mine_terms_ref[...]
            right_ref[:, there] = terms


def acts_kernel(n, a_ref, out_ref, acts):
    tok = a_ref.shape[1] // n
    me = lax.axis_index("tensor")
    for s in range(n):
        src = ring_source(me, s, n)
        here = a_ref[0, pl.ds(pl.multiple_of(src * tok, tok), tok), :]
        acts[s * tok : (s + 1) * tok, :] = here
    out_ref[...] = acts[...].T


def final_kernel(at, part, bases, last, acts_ref, left_ref, right_ref, e_ref, *refs):
    slots = refs[: len(bases)]
    outs, (rebuilt_v, error_v, sems) = refs[-5 - last : -3], refs[-3:]
    rebuilt_hbm, error_hbm = outs[:2]
    rows = e_ref.shape[1]
    wide = 256
    strips = sems.shape[0] - 1
    high = rows // strips
    tiles = part // wide
    group = -(-tiles // sems.shape[1])
    copies = []
    if last:
        copies.append(pltpu.make_async_copy(refs[len(bases)], outs[2], sems.at[strips, 0, 0]))
        copies[-1].start()
    for r in range(strips):
        here = slice(r * high, (r + 1) * high)
        for c in range(part // wide):
            cols = slice(c * wide, (c + 1) * wide)
            there = slice(at + c * wide, at + (c + 1) * wide)
            grads = [
                slot[0, :, there.start - base : there.stop - base]
                for slot, base in zip(slots, bases)
            ]
            grad = dot(acts_ref[here, :], jnp.concatenate(grads, axis=0), (1, 0))
            matrix = grad + e_ref[0, here, there].astype(F32)
            rebuilt = dot(left_ref[here, :], right_ref[:, there], (1, 0))
            rebuilt_v[here, cols] = rebuilt.astype(BF16)
            error_v[here, cols] = (matrix - rebuilt).astype(BF16)
            if (c + 1) % group == 0 or c + 1 == tiles:
                k = c // group
                size = (c + 1 - k * group) * wide
                strip, span = pl.ds(r * high, high), pl.ds(k * group * wide, size)
                far = pl.ds(at + k * group * wide, size)
                copies += [
                    pltpu.make_async_copy(
                        rebuilt_v.at[strip, span], rebuilt_hbm.at[strip, far], sems.at[r, k, 0]
                    ),
                    pltpu.make_async_copy(
                        error_v.at[strip, span], error_hbm.at[0, strip, far], sems.at[r, k, 1]
                    ),
                ]
                copies[-2].start()
                copies[-1].start()
    for copy in copies:
        copy.wait()


def per_device(activations, out_grads, error_buffer, warm_factor):
    m = lax.axis_size("dp")
    n = lax.axis_size("tensor")
    _, tokens, rows = activations.shape
    _, tok, width = out_grads.shape
    rank = warm_factor.shape[1]
    half = width // 2
    w = warm_factor.T
    sds = jax.ShapeDtypeStruct
    hbm = pl.BlockSpec(memory_space=pltpu.HBM)
    vmem = pl.BlockSpec(memory_space=pltpu.VMEM)
    dma = pltpu.SemaphoreType.DMA
    pin = lambda x: pltpu.with_memory_space_constraint(x, pltpu.HBM)

    def call(kernel, shapes, scratch, name, specs=None, flops=0):
        return pl.pallas_call(
            kernel,
            out_shape=shapes,
            **({"in_specs": specs} if specs else {}),
            scratch_shapes=scratch,
            compiler_params=params(16),
            cost_estimate=cost(flops),
            name=name,
        )

    def add(*terms):
        return call(add_kernel, sds(terms[0].shape, F32), [], "add")(*terms)

    def after(x, y):
        return lax.optimization_barrier((x, y))

    def cut(x, widths):
        shapes = [sds((1, tok, part), BF16) for part in widths]
        return call(cut_kernel, shapes, [dma((len(widths),))], "cut")(x)

    def step(x):
        return ring_step(x, "tensor", n)

    ring = [out_grads, step(out_grads)]

    gw, w_terms = call(
        token_factor_kernel,
        [sds((8, 128), F32), sds((3 * rank, width), BF16)],
        [
            pltpu.VMEM((rank, width), F32),
            pltpu.VMEM((1, tok, width), BF16),
            pltpu.VMEM((3 * rank, width), F32),
            dma((2,)),
        ],
        "token_factor", [hbm, hbm],
    )(pin(w), pin(out_grads))
    ew, error_v = call(
        error_left_kernel,
        [sds((rank, rows), F32), sds((1, rows, width), BF16)],
        [dma((rows // 128,))],
        "error_left", [vmem, hbm], 4.6e9,
    )(w_terms, pin(error_buffer))

    gw, ew = after(gw, ew)
    gws = exchange([gw] * n, "tensor", n)
    ring[1], gws = after(ring[1], gws)
    for _ in range(n - 2 - 1):
        ring.append(step(ring[-1]))
    left = call(
        left_kernel, sds((rank, rows), F32), [pltpu.VMEM((3 * rank, tok), F32)], "left"
    )(activations, ew, *gws)
    left = add(left, swap(left, "dp", m, 1))
    for group in groups(m // 2)[:-1]:
        left = add(*terms_of(left, "dp", m, [2 * bit for bit in group]))
    lefts = terms_of(left, "dp", m, [2 * bit for bit in groups(m // 2)[-1]])
    mean, scaled, extra, held, following = call(
        functools.partial(mean_kernel, n, 1.0 / (SHRINK * m)),
        [
            sds((rank, rows), F32),
            sds((rank, rows), F32),
            sds((rank, 128), F32),
            sds((rank, (n - 1) * tok), F32),
            sds((8, 128), F32),
        ],
        [pltpu.VMEM((3 * rank, rows), F32), pltpu.VMEM((n, rank, tok), F32)],
        "mean",
    )(activations, *lefts)
    got = step(following)

    right_raw = call(
        error_right_kernel,
        sds((rank, width), F32),
        [pltpu.VMEM((3 * rank, rows), F32)],
        "error_right", None, 1.2e9,
    )(scaled, error_v)

    widths = [width * 7 // 10, width * 3 // 10]
    last, (got, right_raw) = after(ring[-1], (got, right_raw))
    newest = list(cut(last, widths))
    newest[0] = step(newest[0])

    keep, send = call(
        right_kernel,
        [sds((rank, half + 128), F32)] * 2,
        [
            pltpu.VMEM((3 * rank, (n - 1) * tok), F32),
            pltpu.VMEM((2, rank, half + 128), F32),
        ],
        "right",
    )(right_raw, held, got, extra, *ring)
    total = add(keep, swap(send, "dp", m, 1))

    for group in groups(m // 2):
        total = add(*terms_of(total, "dp", m, [2 * bit for bit in group]))
    for group in groups(n):
        parts = terms_of(total, "tensor", n, group)
        if group == groups(n)[-1]:
            newest[0], parts[1:] = after(newest[0], parts[1:])
        total = call(
            functools.partial(join_kernel, rank), sds(total.shape, F32), [], "join"
        )(*parts)
    for c in range(1, len(widths)):
        last, total = after(newest[c], total)
        newest[c] = step(last)

    terms = len(LEFT_TERMS) * rank
    other = swap(total, "dp", m, 1)
    left_terms, mine, mine_terms = call(
        functools.partial(half_kernel, m),
        [sds((rows, terms), BF16), sds((rank, half), F32), sds((terms, half), BF16)],
        [pltpu.VMEM((terms, rows), F32), pltpu.VMEM((terms, half), F32)],
        "half", None, 1e9,
    )(mean, total)
    whole, right_terms = call(
        functools.partial(factor_kernel, m),
        [sds((rank, width), F32), sds((terms, width), BF16)],
        [pltpu.VMEM((terms, half), F32)],
        "factor",
    )(other, mine, mine_terms)

    acts = call(
        functools.partial(acts_kernel, n),
        sds((rows, tokens), BF16),
        [pltpu.VMEM((tokens, rows), BF16)],
        "acts",
    )(activations)
    pieces = []
    at = 0
    for part, x in zip(widths, newest):
        pieces.append((at, part, ring + [x], [0] * (n - 1) + [at]))
        at += part

    outs = ()
    for at, part, slots, bases in pieces:
        last = at + part == width
        inputs = [acts, left_terms, right_terms, error_v, *slots] + [whole] * last
        outs = pl.pallas_call(
            functools.partial(final_kernel, at, part, bases, last),
            in_specs=[vmem] * len(inputs) + [pl.BlockSpec(memory_space=pl.ANY)] * len(outs),
            out_specs=[pl.BlockSpec(memory_space=pl.ANY)] * (2 + last),
            out_shape=[sds((rows, width), BF16), sds((1, rows, width), BF16)]
            + [sds((rank, width), F32)] * last,
            input_output_aliases={len(inputs) + k: k for k in range(len(outs))},
            scratch_shapes=[pltpu.VMEM((rows, part), BF16)] * 2 + [dma((3, 4 if part > half else 3, 2))],
            compiler_params=params(16),
            cost_estimate=cost(REBUILD),
            name="rebuild",
        )(*inputs, *outs)
    rebuilt, error, factor = outs
    return rebuilt, error, factor.T


def solution(mesh):
    return jax.shard_map(
        per_device,
        mesh=mesh,
        in_specs=(P("dp", None, "tensor"), P("dp", "tensor", None), P("dp", "tensor", None), P()),
        out_specs=(P("tensor", None), P("dp", "tensor", None), P()),
        check_vma=False,
    )
```

```python
import functools

import jax
import jax.numpy as jnp
from jax import lax
from jax.experimental import pallas as pl
from jax.experimental.pallas import tpu as pltpu
from jax.sharding import PartitionSpec as P

F32 = jnp.float32
BF16 = jnp.bfloat16
SHRINK = 2.0**-23
TINY = 1e-30
REBUILD = 4e9
ROOM = 2.0**14
BLOCK = 512


def params(mib):
    return pltpu.CompilerParams(vmem_limit_bytes=mib * 2**20)


def cost(flops):
    return pl.CostEstimate(flops=int(flops) + 1, bytes_accessed=1, transcendentals=0)


def dot(a, b, contract):
    return lax.dot_general(a, b, ((contract[:1], contract[1:]), ((), ())), preferred_element_type=F32)


def split(x):
    hi = x.astype(BF16)
    rest = x - hi.astype(F32)
    mid = rest.astype(BF16)
    lo = (rest - mid.astype(F32)).astype(BF16)
    return hi.astype(F32), mid.astype(F32), lo.astype(F32)


def stack3(x, ref):
    rank = x.shape[0]
    for i, part in enumerate(split(x)):
        ref[i * rank : (i + 1) * rank, :] = part
    return ref[...].astype(BF16)


def sum3(y, rank):
    return (y[2 * rank :] + y[rank : 2 * rank]) + y[:rank]


def ring_of(n):
    return [2 * p if 2 * p < n else 2 * (n - p) - 1 for p in range(n)]


def ring_source(me, step, n):
    place = jnp.where(lax.rem(me, 2) == 0, me // 2, n - (me + 1) // 2)
    place = lax.rem(place - step + n, n)
    return jnp.where(2 * place < n, 2 * place, 2 * (n - place) - 1)


def ring_step(x, axis, n):
    ring = ring_of(n)
    return lax.ppermute(x, axis, [(ring[p], ring[(p + 1) % n]) for p in range(n)])


def exchange(pieces, axis, n):
    return [pieces[0]] + [
        lax.ppermute(pieces[k], axis, [(i, (i + k) % n) for i in range(n)]) for k in range(1, n)
    ]


def swap(x, axis, n, bit):
    return lax.ppermute(x, axis, [(i, i ^ bit) for i in range(n)])


def groups(n):
    assert n & (n - 1) == 0
    bits = [1 << i for i in range(n.bit_length() - 1)]
    return [bits[i : i + 2] for i in range(0, len(bits), 2)]


def terms_of(x, axis, n, group):
    others = group if len(group) == 1 else [group[0], group[1], group[0] | group[1]]
    return [x] + [swap(x, axis, n, bit) for bit in others]


def total_of(refs):
    total = refs[0][...] + refs[1][...]
    if len(refs) == 4:
        total = total + (refs[2][...] + refs[3][...])
    return total


def token_factor_kernel(w_hbm, g_hbm, gw_ref, terms_ref, w, g, w3, sems):
    rank = w.shape[0]
    copies = [
        pltpu.make_async_copy(w_hbm, w, sems.at[0]),
        pltpu.make_async_copy(g_hbm, g, sems.at[1]),
    ]
    for copy in copies:
        copy.start()
    copies[0].wait()
    terms = stack3(w[...] * SHRINK, w3)
    terms_ref[...] = terms
    copies[1].wait()
    gw_ref[...] = jnp.zeros_like(gw_ref)
    gw_ref[0:rank, 0 : g.shape[1]] = sum3(dot(terms, g[0], (1, 1)), rank)


def cut_kernel(x_ref, *refs):
    chunks, sems = refs[:-1], refs[-1]
    copies = []
    at = 0
    for c, chunk in enumerate(chunks):
        part = chunk.shape[2]
        copies.append(pltpu.make_async_copy(x_ref.at[:, :, pl.ds(at, part)], chunk, sems.at[c]))
        copies[-1].start()
        at += part
    for copy in copies:
        copy.wait()


def error_left_kernel(terms_ref, e_hbm, out_ref, e_ref, sems):
    rank = out_ref.shape[0]
    count = sems.shape[0]
    high = e_ref.shape[1] // count
    copies = []
    for c in range(count):
        rows = pl.ds(c * high, high)
        copies.append(pltpu.make_async_copy(e_hbm.at[:, rows, :], e_ref.at[:, rows, :], sems.at[c]))
        copies[-1].start()
    terms = terms_ref[...]
    for c in range(count):
        copies[c].wait()
        rows = slice(c * high, (c + 1) * high)
        out_ref[:, rows] = sum3(dot(terms, e_ref[0, rows, :], (1, 1)), rank)


def left_kernel(a_ref, e_ref, *refs):
    gws, out_ref, g3 = refs[:-2], refs[-2], refs[-1]
    n = len(gws)
    rank = e_ref.shape[0]
    tok = a_ref.shape[1] // n
    me = lax.axis_index("tensor")
    total = e_ref[...]
    for k in range(n):
        src = lax.rem(me - k + n, n)
        rows = a_ref[0, pl.ds(pl.multiple_of(src * tok, tok), tok), :]
        total += sum3(dot(stack3(gws[k][0:rank, 0:tok], g3), rows, (1, 0)), rank)
    out_ref[...] = total


def mean_kernel(n, scale, a_ref, *refs):
    terms = refs[:-7]
    p_ref, scaled_ref, extra_ref, held_ref, next_ref, p3, blocks = refs[-7:]
    rank = p_ref.shape[0]
    tok = a_ref.shape[1] // n
    me = lax.axis_index("tensor")
    mean = total_of(terms) * scale
    p_ref[...] = mean
    top = jnp.max(jnp.max(jnp.abs(mean), axis=1, keepdims=True), axis=0, keepdims=True)
    top = jnp.maximum(top, TINY)
    scaled = mean / (top * ROOM)
    scaled_ref[...] = scaled
    parts = stack3(scaled, p3)
    for t in range(n):
        blocks[t] = sum3(dot(parts, a_ref[0, t * tok : (t + 1) * tok, :], (1, 1)), rank)
    for s in range(n - 1):
        held_ref[:, s * tok : (s + 1) * tok] = blocks[ring_source(me, s, n)]
    next_ref[...] = jnp.zeros_like(next_ref)
    next_ref[0:rank, 0:tok] = blocks[ring_source(me, n - 1, n)]
    next_ref[rank : rank + 1, 0:1] = top
    extra_ref[...] = jnp.zeros_like(extra_ref)
    for i in range(rank):
        extra_ref[:, i : i + 1] = jnp.sum(mean * mean[i : i + 1, :], axis=1, keepdims=True)
    extra_ref[:, rank : rank + 1] = jnp.broadcast_to(top, (rank, 1))


def error_right_kernel(p_ref, e_ref, out_ref, p3):
    rank = p_ref.shape[0]
    parts = stack3(p_ref[...], p3)
    for c in range(e_ref.shape[2] // BLOCK):
        cols = slice(c * BLOCK, (c + 1) * BLOCK)
        out_ref[:, cols] = sum3(dot(parts, e_ref[0, :, cols], (1, 0)), rank)


def lower_inverse(gram, rank):
    at = lambda i, j: gram[i : i + 1, j : j + 1]
    low, inv = {}, {}
    for j in range(rank):
        d = at(j, j)
        for k in range(j):
            d = d - low[j, k] * low[j, k]
        inv[j, j] = lax.rsqrt(d)
        for i in range(j + 1, rank):
            v = at(i, j)
            for k in range(j):
                v = v - low[i, k] * low[j, k]
            low[i, j] = v * inv[j, j]
    for j in range(rank):
        for i in range(j + 1, rank):
            v = low[i, j] * inv[j, j]
            for k in range(j + 1, i):
                v = v + low[i, k] * inv[k, j]
            inv[i, j] = -v * inv[i, i]
    return inv


def solve(inv, x, rank):
    total = 0.0
    for j in range(rank):
        column = [inv.get((i, j), jnp.zeros((1, 1), F32)) for i in range(rank)]
        total = total + jnp.concatenate(column, axis=0) * x[j : j + 1, :]
    return total


def right_kernel(r_ref, y_ref, got_ref, extra_ref, *refs):
    held, (keep_ref, send_ref, y3, outbox) = refs[:-4], refs[-4:]
    rank = r_ref.shape[0]
    tok = held[0].shape[1]
    half = r_ref.shape[1] // 2
    core = lax.rem(lax.axis_index("dp"), 2)
    mine = extra_ref[0:1, rank : rank + 1]
    theirs = got_ref[rank : rank + 1, 0:1]
    top = jnp.maximum(mine, theirs)
    products = y_ref[...] * (mine / top)
    joint = products[:, 0:tok] + got_ref[0:rank, 0:tok] * (theirs / top)
    terms = stack3(jnp.concatenate([joint, products[:, tok:]], axis=1), y3)
    for h in range(2):
        for c in range(half // BLOCK):
            at = h * half + c * BLOCK
            cols = slice(at, at + BLOCK)
            grads = jnp.concatenate([g[0, :, cols] for g in held], axis=0)
            fresh = sum3(dot(terms, grads, (1, 0)), rank)
            outbox[h, :, c * BLOCK : (c + 1) * BLOCK] = r_ref[:, cols] * (mine / top) + fresh
        outbox[h, :, half:] = extra_ref[...]
        outbox[h, :, half + rank : half + rank + 1] = jnp.broadcast_to(top, (rank, 1))
    keep_ref[...] = outbox[core]
    send_ref[...] = outbox[1 - core]


def join_kernel(rank, *refs):
    xs, out_ref = refs[:-1], refs[-1]
    half = out_ref.shape[1] - 128
    mark = slice(half + rank, half + rank + 1)
    tops = [x[0:1, mark] for x in xs]
    top = jnp.maximum(tops[0], tops[1])
    for other in tops[2:]:
        top = jnp.maximum(top, other)

    def total(terms):
        first = terms[0] + terms[1]
        return first + (terms[2] + terms[3]) if len(terms) == 4 else first

    out_ref[:, :half] = total([x[:, :half] * (t / top) for x, t in zip(xs, tops)])
    out_ref[:, half:] = total([x[:, half:] for x in xs])
    out_ref[:, mark] = jnp.broadcast_to(top, (rank, 1))


def add_kernel(*refs):
    refs[-1][...] = total_of(refs[:-1])


LEFT_TERMS = (0, 0, 1, 0, 2, 1)
RIGHT_TERMS = (0, 1, 0, 2, 0, 1)


def stack_terms(terms, x, ref):
    parts = split(x)
    rank = x.shape[0]
    for i, term in enumerate(terms):
        ref[i * rank : (i + 1) * rank, :] = parts[term]
    return ref[...]


def factor_solve(m, total_ref):
    rank = total_ref.shape[0]
    half = total_ref.shape[1] - 128
    inv = lower_inverse(total_ref[:, half : half + rank] * (1.0 / m), rank)
    top = total_ref[0:1, half + rank : half + rank + 1] * (ROOM / (m * m))
    scaled = {key: value * top for key, value in inv.items()}
    return inv, solve(scaled, total_ref[:, 0:half], rank)


def half_kernel(m, p_ref, mine_ref, left_ref, whole_ref, right_ref, left, right):
    inv, half = factor_solve(m, mine_ref)
    whole_ref[...] = half
    right_ref[...] = stack_terms(RIGHT_TERMS, half, right).astype(BF16)
    ortho = solve(inv, p_ref[...], p_ref.shape[0])
    left_ref[...] = stack_terms(LEFT_TERMS, ortho, left).T.astype(BF16)


def factor_kernel(m, other_ref, mine_ref, mine_terms_ref, whole_ref, right_ref, right):
    half = mine_ref.shape[1]
    core = lax.rem(lax.axis_index("dp"), 2)
    _, other = factor_solve(m, other_ref)
    terms = stack_terms(RIGHT_TERMS, other, right).astype(BF16)
    for c in range(2):

        @pl.when(core == c)
        def _():
            here = slice(c * half, (c + 1) * half)
            there = slice((1 - c) * half, (2 - c) * half)
            whole_ref[:, here] = mine_ref[...]
            whole_ref[:, there] = other
            right_ref[:, here] = mine_terms_ref[...]
            right_ref[:, there] = terms


def acts_kernel(n, a_ref, out_ref, acts):
    tok = a_ref.shape[1] // n
    me = lax.axis_index("tensor")
    for s in range(n):
        src = ring_source(me, s, n)
        here = a_ref[0, pl.ds(pl.multiple_of(src * tok, tok), tok), :]
        acts[s * tok : (s + 1) * tok, :] = here
    out_ref[...] = acts[...].T


def final_kernel(at, part, bases, last, acts_ref, left_ref, right_ref, e_ref, *refs):
    slots = refs[: len(bases)]
    outs, (rebuilt_v, error_v, sems) = refs[-5 - last : -3], refs[-3:]
    rebuilt_hbm, error_hbm = outs[:2]
    rows = e_ref.shape[1]
    wide = 256
    strips = sems.shape[0] - 1
    high = rows // strips
    tiles = part // wide
    group = -(-tiles // sems.shape[1])
    copies = []
    if last:
        copies.append(pltpu.make_async_copy(refs[len(bases)], outs[2], sems.at[strips, 0, 0]))
        copies[-1].start()
    for r in range(strips):
        here = slice(r * high, (r + 1) * high)
        for c in range(part // wide):
            cols = slice(c * wide, (c + 1) * wide)
            there = slice(at + c * wide, at + (c + 1) * wide)
            grads = [
                slot[0, :, there.start - base : there.stop - base]
                for slot, base in zip(slots, bases)
            ]
            grad = dot(acts_ref[here, :], jnp.concatenate(grads, axis=0), (1, 0))
            matrix = grad + e_ref[0, here, there].astype(F32)
            rebuilt = dot(left_ref[here, :], right_ref[:, there], (1, 0))
            rebuilt_v[here, cols] = rebuilt.astype(BF16)
            error_v[here, cols] = (matrix - rebuilt).astype(BF16)
            if (c + 1) % group == 0 or c + 1 == tiles:
                k = c // group
                size = (c + 1 - k * group) * wide
                strip, span = pl.ds(r * high, high), pl.ds(k * group * wide, size)
                far = pl.ds(at + k * group * wide, size)
                copies += [
                    pltpu.make_async_copy(
                        rebuilt_v.at[strip, span], rebuilt_hbm.at[strip, far], sems.at[r, k, 0]
                    ),
                    pltpu.make_async_copy(
                        error_v.at[strip, span], error_hbm.at[0, strip, far], sems.at[r, k, 1]
                    ),
                ]
                copies[-2].start()
                copies[-1].start()
    for copy in copies:
        copy.wait()


def per_device(activations, out_grads, error_buffer, warm_factor):
    m = lax.axis_size("dp")
    n = lax.axis_size("tensor")
    _, tokens, rows = activations.shape
    _, tok, width = out_grads.shape
    rank = warm_factor.shape[1]
    half = width // 2
    w = warm_factor.T
    sds = jax.ShapeDtypeStruct
    hbm = pl.BlockSpec(memory_space=pltpu.HBM)
    vmem = pl.BlockSpec(memory_space=pltpu.VMEM)
    dma = pltpu.SemaphoreType.DMA
    pin = lambda x: pltpu.with_memory_space_constraint(x, pltpu.HBM)

    def call(kernel, shapes, scratch, name, specs=None, flops=0):
        return pl.pallas_call(
            kernel,
            out_shape=shapes,
            **({"in_specs": specs} if specs else {}),
            scratch_shapes=scratch,
            compiler_params=params(16),
            cost_estimate=cost(flops),
            name=name,
        )

    def add(*terms):
        return call(add_kernel, sds(terms[0].shape, F32), [], "add")(*terms)

    def after(x, y):
        return lax.optimization_barrier((x, y))

    def cut(x, widths):
        shapes = [sds((1, tok, part), BF16) for part in widths]
        return call(cut_kernel, shapes, [dma((len(widths),))], "cut")(x)

    def step(x):
        return ring_step(x, "tensor", n)

    ring = [out_grads, step(out_grads)]

    gw, w_terms = call(
        token_factor_kernel,
        [sds((8, 128), F32), sds((3 * rank, width), BF16)],
        [
            pltpu.VMEM((rank, width), F32),
            pltpu.VMEM((1, tok, width), BF16),
            pltpu.VMEM((3 * rank, width), F32),
            dma((2,)),
        ],
        "token_factor", [hbm, hbm],
    )(pin(w), pin(out_grads))
    ew, error_v = call(
        error_left_kernel,
        [sds((rank, rows), F32), sds((1, rows, width), BF16)],
        [dma((rows // 128,))],
        "error_left", [vmem, hbm], 4.6e9,
    )(w_terms, pin(error_buffer))

    gw, ew = after(gw, ew)
    gws = exchange([gw] * n, "tensor", n)
    ring[1], gws = after(ring[1], gws)
    for _ in range(n - 2 - 1):
        ring.append(step(ring[-1]))
    left = call(
        left_kernel, sds((rank, rows), F32), [pltpu.VMEM((3 * rank, tok), F32)], "left"
    )(activations, ew, *gws)
    left = add(left, swap(left, "dp", m, 1))
    for group in groups(m // 2)[:-1]:
        left = add(*terms_of(left, "dp", m, [2 * bit for bit in group]))
    lefts = terms_of(left, "dp", m, [2 * bit for bit in groups(m // 2)[-1]])
    mean, scaled, extra, held, following = call(
        functools.partial(mean_kernel, n, 1.0 / (SHRINK * m)),
        [
            sds((rank, rows), F32),
            sds((rank, rows), F32),
            sds((rank, 128), F32),
            sds((rank, (n - 1) * tok), F32),
            sds((8, 128), F32),
        ],
        [pltpu.VMEM((3 * rank, rows), F32), pltpu.VMEM((n, rank, tok), F32)],
        "mean",
    )(activations, *lefts)
    got = step(following)

    right_raw = call(
        error_right_kernel,
        sds((rank, width), F32),
        [pltpu.VMEM((3 * rank, rows), F32)],
        "error_right", None, 1.2e9,
    )(scaled, error_v)

    widths = [width * 7 // 10, width * 3 // 10]
    last, (got, right_raw) = after(ring[-1], (got, right_raw))
    newest = list(cut(last, widths))
    newest[0] = step(newest[0])

    keep, send = call(
        right_kernel,
        [sds((rank, half + 128), F32)] * 2,
        [
            pltpu.VMEM((3 * rank, (n - 1) * tok), F32),
            pltpu.VMEM((2, rank, half + 128), F32),
        ],
        "right",
    )(right_raw, held, got, extra, *ring)
    total = add(keep, swap(send, "dp", m, 1))

    for group in groups(m // 2):
        total = add(*terms_of(total, "dp", m, [2 * bit for bit in group]))
    for group in groups(n):
        parts = terms_of(total, "tensor", n, group)
        if group == groups(n)[-1]:
            newest[0], parts[1:] = after(newest[0], parts[1:])
        total = call(
            functools.partial(join_kernel, rank), sds(total.shape, F32), [], "join"
        )(*parts)
    for c in range(1, len(widths)):
        last, total = after(newest[c], total)
        newest[c] = step(last)

    terms = len(LEFT_TERMS) * rank
    other = swap(total, "dp", m, 1)
    left_terms, mine, mine_terms = call(
        functools.partial(half_kernel, m),
        [sds((rows, terms), BF16), sds((rank, half), F32), sds((terms, half), BF16)],
        [pltpu.VMEM((terms, rows), F32), pltpu.VMEM((terms, half), F32)],
        "half", None, 1e9,
    )(mean, total)
    whole, right_terms = call(
        functools.partial(factor_kernel, m),
        [sds((rank, width), F32), sds((terms, width), BF16)],
        [pltpu.VMEM((terms, half), F32)],
        "factor",
    )(other, mine, mine_terms)

    acts = call(
        functools.partial(acts_kernel, n),
        sds((rows, tokens), BF16),
        [pltpu.VMEM((tokens, rows), BF16)],
        "acts",
    )(activations)
    pieces = []
    at = 0
    for part, x in zip(widths, newest):
        pieces.append((at, part, ring + [x], [0] * (n - 1) + [at]))
        at += part

    outs = ()
    for at, part, slots, bases in pieces:
        last = at + part == width
        inputs = [acts, left_terms, right_terms, error_v, *slots] + [whole] * last
        outs = pl.pallas_call(
            functools.partial(final_kernel, at, part, bases, last),
            in_specs=[vmem] * len(inputs) + [pl.BlockSpec(memory_space=pl.ANY)] * len(outs),
            out_specs=[pl.BlockSpec(memory_space=pl.ANY)] * (2 + last),
            out_shape=[sds((rows, width), BF16), sds((1, rows, width), BF16)]
            + [sds((rank, width), F32)] * last,
            input_output_aliases={len(inputs) + k: k for k in range(len(outs))},
            scratch_shapes=[pltpu.VMEM((rows, part), BF16)] * 2 + [dma((7, 4 if part > half else 3, 2))],
            compiler_params=params(16),
            cost_estimate=cost(REBUILD),
            name="rebuild",
        )(*inputs, *outs)
    rebuilt, error, factor = outs
    return rebuilt, error, factor.T


def solution(mesh):
    return jax.shard_map(
        per_device,
        mesh=mesh,
        in_specs=(P("dp", None, "tensor"), P("dp", "tensor", None), P("dp", "tensor", None), P()),
        out_specs=(P("tensor", None), P("dp", "tensor", None), P()),
        check_vma=False,
    )
```

```python
import functools

import jax
import jax.numpy as jnp
from jax import lax
from jax.experimental import pallas as pl
from jax.experimental.pallas import tpu as pltpu
from jax.sharding import PartitionSpec as P

F32 = jnp.float32
BF16 = jnp.bfloat16
SHRINK = 2.0**-23
TINY = 1e-30
REBUILD = 4e9
ROOM = 2.0**14
BLOCK = 512


def params(mib):
    return pltpu.CompilerParams(vmem_limit_bytes=mib * 2**20)


def cost(flops):
    return pl.CostEstimate(flops=int(flops) + 1, bytes_accessed=1, transcendentals=0)


def dot(a, b, contract):
    return lax.dot_general(a, b, ((contract[:1], contract[1:]), ((), ())), preferred_element_type=F32)


def split(x):
    hi = x.astype(BF16)
    rest = x - hi.astype(F32)
    mid = rest.astype(BF16)
    lo = (rest - mid.astype(F32)).astype(BF16)
    return hi.astype(F32), mid.astype(F32), lo.astype(F32)


def stack3(x, ref):
    rank = x.shape[0]
    for i, part in enumerate(split(x)):
        ref[i * rank : (i + 1) * rank, :] = part
    return ref[...].astype(BF16)


def sum3(y, rank):
    return (y[2 * rank :] + y[rank : 2 * rank]) + y[:rank]


def ring_of(n):
    return [2 * p if 2 * p < n else 2 * (n - p) - 1 for p in range(n)]


def ring_source(me, step, n):
    place = jnp.where(lax.rem(me, 2) == 0, me // 2, n - (me + 1) // 2)
    place = lax.rem(place - step + n, n)
    return jnp.where(2 * place < n, 2 * place, 2 * (n - place) - 1)


def ring_step(x, axis, n):
    ring = ring_of(n)
    return lax.ppermute(x, axis, [(ring[p], ring[(p + 1) % n]) for p in range(n)])


def exchange(pieces, axis, n):
    return [pieces[0]] + [
        lax.ppermute(pieces[k], axis, [(i, (i + k) % n) for i in range(n)]) for k in range(1, n)
    ]


def swap(x, axis, n, bit):
    return lax.ppermute(x, axis, [(i, i ^ bit) for i in range(n)])


def groups(n):
    assert n & (n - 1) == 0
    bits = [1 << i for i in range(n.bit_length() - 1)]
    return [bits[i : i + 2] for i in range(0, len(bits), 2)]


def terms_of(x, axis, n, group):
    others = group if len(group) == 1 else [group[0], group[1], group[0] | group[1]]
    return [x] + [swap(x, axis, n, bit) for bit in others]


def total_of(refs):
    total = refs[0][...] + refs[1][...]
    if len(refs) == 4:
        total = total + (refs[2][...] + refs[3][...])
    return total


def token_factor_kernel(w_hbm, g_hbm, gw_ref, terms_ref, w, g, w3, sems):
    rank = w.shape[0]
    copies = [
        pltpu.make_async_copy(w_hbm, w, sems.at[0]),
        pltpu.make_async_copy(g_hbm, g, sems.at[1]),
    ]
    for copy in copies:
        copy.start()
    copies[0].wait()
    terms = stack3(w[...] * SHRINK, w3)
    terms_ref[...] = terms
    copies[1].wait()
    gw_ref[...] = jnp.zeros_like(gw_ref)
    gw_ref[0:rank, 0 : g.shape[1]] = sum3(dot(terms, g[0], (1, 1)), rank)


def cut_kernel(x_ref, *refs):
    chunks, sems = refs[:-1], refs[-1]
    copies = []
    at = 0
    for c, chunk in enumerate(chunks):
        part = chunk.shape[2]
        copies.append(pltpu.make_async_copy(x_ref.at[:, :, pl.ds(at, part)], chunk, sems.at[c]))
        copies[-1].start()
        at += part
    for copy in copies:
        copy.wait()


def error_left_kernel(terms_ref, e_hbm, out_ref, e_ref, sems):
    rank = out_ref.shape[0]
    count = sems.shape[0]
    high = e_ref.shape[1] // count
    copies = []
    for c in range(count):
        rows = pl.ds(c * high, high)
        copies.append(pltpu.make_async_copy(e_hbm.at[:, rows, :], e_ref.at[:, rows, :], sems.at[c]))
        copies[-1].start()
    terms = terms_ref[...]
    for c in range(count):
        copies[c].wait()
        rows = slice(c * high, (c + 1) * high)
        out_ref[:, rows] = sum3(dot(terms, e_ref[0, rows, :], (1, 1)), rank)


def left_kernel(a_ref, e_ref, *refs):
    gws, out_ref, g3 = refs[:-2], refs[-2], refs[-1]
    n = len(gws)
    rank = e_ref.shape[0]
    tok = a_ref.shape[1] // n
    me = lax.axis_index("tensor")
    total = e_ref[...]
    for k in range(n):
        src = lax.rem(me - k + n, n)
        rows = a_ref[0, pl.ds(pl.multiple_of(src * tok, tok), tok), :]
        total += sum3(dot(stack3(gws[k][0:rank, 0:tok], g3), rows, (1, 0)), rank)
    out_ref[...] = total


def mean_kernel(n, scale, a_ref, *refs):
    terms = refs[:-7]
    p_ref, scaled_ref, extra_ref, held_ref, next_ref, p3, blocks = refs[-7:]
    rank = p_ref.shape[0]
    tok = a_ref.shape[1] // n
    me = lax.axis_index("tensor")
    mean = total_of(terms) * scale
    p_ref[...] = mean
    top = jnp.max(jnp.max(jnp.abs(mean), axis=1, keepdims=True), axis=0, keepdims=True)
    top = jnp.maximum(top, TINY)
    scaled = mean / (top * ROOM)
    scaled_ref[...] = scaled
    parts = stack3(scaled, p3)
    for t in range(n):
        blocks[t] = sum3(dot(parts, a_ref[0, t * tok : (t + 1) * tok, :], (1, 1)), rank)
    for s in range(n - 1):
        held_ref[:, s * tok : (s + 1) * tok] = blocks[ring_source(me, s, n)]
    next_ref[...] = jnp.zeros_like(next_ref)
    next_ref[0:rank, 0:tok] = blocks[ring_source(me, n - 1, n)]
    next_ref[rank : rank + 1, 0:1] = top
    extra_ref[...] = jnp.zeros_like(extra_ref)
    for i in range(rank):
        extra_ref[:, i : i + 1] = jnp.sum(mean * mean[i : i + 1, :], axis=1, keepdims=True)
    extra_ref[:, rank : rank + 1] = jnp.broadcast_to(top, (rank, 1))


def error_right_kernel(p_ref, e_ref, out_ref, p3):
    rank = p_ref.shape[0]
    parts = stack3(p_ref[...], p3)
    for c in range(e_ref.shape[2] // BLOCK):
        cols = slice(c * BLOCK, (c + 1) * BLOCK)
        out_ref[:, cols] = sum3(dot(parts, e_ref[0, :, cols], (1, 0)), rank)


def lower_inverse(gram, rank):
    at = lambda i, j: gram[i : i + 1, j : j + 1]
    low, inv = {}, {}
    for j in range(rank):
        d = at(j, j)
        for k in range(j):
            d = d - low[j, k] * low[j, k]
        inv[j, j] = lax.rsqrt(d)
        for i in range(j + 1, rank):
            v = at(i, j)
            for k in range(j):
                v = v - low[i, k] * low[j, k]
            low[i, j] = v * inv[j, j]
    for j in range(rank):
        for i in range(j + 1, rank):
            v = low[i, j] * inv[j, j]
            for k in range(j + 1, i):
                v = v + low[i, k] * inv[k, j]
            inv[i, j] = -v * inv[i, i]
    return inv


def solve(inv, x, rank):
    total = 0.0
    for j in range(rank):
        column = [inv.get((i, j), jnp.zeros((1, 1), F32)) for i in range(rank)]
        total = total + jnp.concatenate(column, axis=0) * x[j : j + 1, :]
    return total


def right_kernel(r_ref, y_ref, got_ref, extra_ref, *refs):
    held, (keep_ref, send_ref, y3, outbox) = refs[:-4], refs[-4:]
    rank = r_ref.shape[0]
    tok = held[0].shape[1]
    half = r_ref.shape[1] // 2
    core = lax.rem(lax.axis_index("dp"), 2)
    mine = extra_ref[0:1, rank : rank + 1]
    theirs = got_ref[rank : rank + 1, 0:1]
    top = jnp.maximum(mine, theirs)
    products = y_ref[...] * (mine / top)
    joint = products[:, 0:tok] + got_ref[0:rank, 0:tok] * (theirs / top)
    terms = stack3(jnp.concatenate([joint, products[:, tok:]], axis=1), y3)
    for h in range(2):
        for c in range(half // BLOCK):
            at = h * half + c * BLOCK
            cols = slice(at, at + BLOCK)
            grads = jnp.concatenate([g[0, :, cols] for g in held], axis=0)
            fresh = sum3(dot(terms, grads, (1, 0)), rank)
            outbox[h, :, c * BLOCK : (c + 1) * BLOCK] = r_ref[:, cols] * (mine / top) + fresh
        outbox[h, :, half:] = extra_ref[...]
        outbox[h, :, half + rank : half + rank + 1] = jnp.broadcast_to(top, (rank, 1))
    keep_ref[...] = outbox[core]
    send_ref[...] = outbox[1 - core]


def join_kernel(rank, *refs):
    xs, out_ref = refs[:-1], refs[-1]
    half = out_ref.shape[1] - 128
    mark = slice(half + rank, half + rank + 1)
    tops = [x[0:1, mark] for x in xs]
    top = jnp.maximum(tops[0], tops[1])
    for other in tops[2:]:
        top = jnp.maximum(top, other)

    def total(terms):
        first = terms[0] + terms[1]
        return first + (terms[2] + terms[3]) if len(terms) == 4 else first

    out_ref[:, :half] = total([x[:, :half] * (t / top) for x, t in zip(xs, tops)])
    out_ref[:, half:] = total([x[:, half:] for x in xs])
    out_ref[:, mark] = jnp.broadcast_to(top, (rank, 1))


def add_kernel(*refs):
    refs[-1][...] = total_of(refs[:-1])


LEFT_TERMS = (0, 0, 1, 0, 2, 1)
RIGHT_TERMS = (0, 1, 0, 2, 0, 1)


def stack_terms(terms, x, ref):
    parts = split(x)
    rank = x.shape[0]
    for i, term in enumerate(terms):
        ref[i * rank : (i + 1) * rank, :] = parts[term]
    return ref[...]


def factor_solve(m, total_ref):
    rank = total_ref.shape[0]
    half = total_ref.shape[1] - 128
    inv = lower_inverse(total_ref[:, half : half + rank] * (1.0 / m), rank)
    top = total_ref[0:1, half + rank : half + rank + 1] * (ROOM / (m * m))
    scaled = {key: value * top for key, value in inv.items()}
    return inv, scaled, solve(scaled, total_ref[:, 0:half], rank)


def half_kernel(m, p_ref, mine_ref, left_ref, whole_ref, right_ref, inv_ref, left, right):
    inv, scaled, half = factor_solve(m, mine_ref)
    inv_ref[...] = jnp.zeros_like(inv_ref)
    for (i, j), value in scaled.items():
        inv_ref[i : i + 1, j : j + 1] = value
    whole_ref[...] = half
    right_ref[...] = stack_terms(RIGHT_TERMS, half, right).astype(BF16)
    ortho = solve(inv, p_ref[...], p_ref.shape[0])
    left_ref[...] = stack_terms(LEFT_TERMS, ortho, left).T.astype(BF16)


def factor_kernel(other_ref, mine_ref, mine_terms_ref, inv_ref, whole_ref, right_ref, right):
    rank, half = mine_ref.shape
    core = lax.rem(lax.axis_index("dp"), 2)
    other = 0.0
    for j in range(rank):
        other = other + inv_ref[0:rank, j : j + 1] * other_ref[j : j + 1, 0:half]
    terms = stack_terms(RIGHT_TERMS, other, right).astype(BF16)
    for c in range(2):

        @pl.when(core == c)
        def _():
            here = slice(c * half, (c + 1) * half)
            there = slice((1 - c) * half, (2 - c) * half)
            whole_ref[:, here] = mine_ref[...]
            whole_ref[:, there] = other
            right_ref[:, here] = mine_terms_ref[...]
            right_ref[:, there] = terms


def acts_kernel(n, a_ref, out_ref, acts):
    tok = a_ref.shape[1] // n
    me = lax.axis_index("tensor")
    for s in range(n):
        src = ring_source(me, s, n)
        here = a_ref[0, pl.ds(pl.multiple_of(src * tok, tok), tok), :]
        acts[s * tok : (s + 1) * tok, :] = here
    out_ref[...] = acts[...].T


def final_kernel(at, part, bases, last, acts_ref, left_ref, right_ref, e_ref, *refs):
    slots = refs[: len(bases)]
    outs, (rebuilt_v, error_v, sems) = refs[-5 - last : -3], refs[-3:]
    rebuilt_hbm, error_hbm = outs[:2]
    rows = e_ref.shape[1]
    wide = 256
    strips = sems.shape[0] - 1
    high = rows // strips
    tiles = part // wide
    group = -(-tiles // sems.shape[1])
    copies = []
    if last:
        copies.append(pltpu.make_async_copy(refs[len(bases)], outs[2], sems.at[strips, 0, 0]))
        copies[-1].start()
    for r in range(strips):
        here = slice(r * high, (r + 1) * high)
        for c in range(part // wide):
            cols = slice(c * wide, (c + 1) * wide)
            there = slice(at + c * wide, at + (c + 1) * wide)
            grads = [
                slot[0, :, there.start - base : there.stop - base]
                for slot, base in zip(slots, bases)
            ]
            grad = dot(acts_ref[here, :], jnp.concatenate(grads, axis=0), (1, 0))
            matrix = grad + e_ref[0, here, there].astype(F32)
            rebuilt = dot(left_ref[here, :], right_ref[:, there], (1, 0))
            rebuilt_v[here, cols] = rebuilt.astype(BF16)
            error_v[here, cols] = (matrix - rebuilt).astype(BF16)
            if (c + 1) % group == 0 or c + 1 == tiles:
                k = c // group
                size = (c + 1 - k * group) * wide
                strip, span = pl.ds(r * high, high), pl.ds(k * group * wide, size)
                far = pl.ds(at + k * group * wide, size)
                copies += [
                    pltpu.make_async_copy(
                        rebuilt_v.at[strip, span], rebuilt_hbm.at[strip, far], sems.at[r, k, 0]
                    ),
                    pltpu.make_async_copy(
                        error_v.at[strip, span], error_hbm.at[0, strip, far], sems.at[r, k, 1]
                    ),
                ]
                copies[-2].start()
                copies[-1].start()
    for copy in copies:
        copy.wait()


def per_device(activations, out_grads, error_buffer, warm_factor):
    m = lax.axis_size("dp")
    n = lax.axis_size("tensor")
    _, tokens, rows = activations.shape
    _, tok, width = out_grads.shape
    rank = warm_factor.shape[1]
    half = width // 2
    w = warm_factor.T
    sds = jax.ShapeDtypeStruct
    hbm = pl.BlockSpec(memory_space=pltpu.HBM)
    vmem = pl.BlockSpec(memory_space=pltpu.VMEM)
    dma = pltpu.SemaphoreType.DMA
    pin = lambda x: pltpu.with_memory_space_constraint(x, pltpu.HBM)

    def call(kernel, shapes, scratch, name, specs=None, flops=0):
        return pl.pallas_call(
            kernel,
            out_shape=shapes,
            **({"in_specs": specs} if specs else {}),
            scratch_shapes=scratch,
            compiler_params=params(16),
            cost_estimate=cost(flops),
            name=name,
        )

    def add(*terms):
        return call(add_kernel, sds(terms[0].shape, F32), [], "add")(*terms)

    def after(x, y):
        return lax.optimization_barrier((x, y))

    def cut(x, widths):
        shapes = [sds((1, tok, part), BF16) for part in widths]
        return call(cut_kernel, shapes, [dma((len(widths),))], "cut")(x)

    def step(x):
        return ring_step(x, "tensor", n)

    ring = [out_grads, step(out_grads)]

    gw, w_terms = call(
        token_factor_kernel,
        [sds((8, 128), F32), sds((3 * rank, width), BF16)],
        [
            pltpu.VMEM((rank, width), F32),
            pltpu.VMEM((1, tok, width), BF16),
            pltpu.VMEM((3 * rank, width), F32),
            dma((2,)),
        ],
        "token_factor", [hbm, hbm],
    )(pin(w), pin(out_grads))
    ew, error_v = call(
        error_left_kernel,
        [sds((rank, rows), F32), sds((1, rows, width), BF16)],
        [dma((rows // 128,))],
        "error_left", [vmem, hbm], 4.6e9,
    )(w_terms, pin(error_buffer))

    gw, ew = after(gw, ew)
    gws = exchange([gw] * n, "tensor", n)
    ring[1], gws = after(ring[1], gws)
    for _ in range(n - 2 - 1):
        ring.append(step(ring[-1]))
    left = call(
        left_kernel, sds((rank, rows), F32), [pltpu.VMEM((3 * rank, tok), F32)], "left"
    )(activations, ew, *gws)
    left = add(left, swap(left, "dp", m, 1))
    for group in groups(m // 2)[:-1]:
        left = add(*terms_of(left, "dp", m, [2 * bit for bit in group]))
    lefts = terms_of(left, "dp", m, [2 * bit for bit in groups(m // 2)[-1]])
    mean, scaled, extra, held, following = call(
        functools.partial(mean_kernel, n, 1.0 / (SHRINK * m)),
        [
            sds((rank, rows), F32),
            sds((rank, rows), F32),
            sds((rank, 128), F32),
            sds((rank, (n - 1) * tok), F32),
            sds((8, 128), F32),
        ],
        [pltpu.VMEM((3 * rank, rows), F32), pltpu.VMEM((n, rank, tok), F32)],
        "mean",
    )(activations, *lefts)
    got = step(following)

    right_raw = call(
        error_right_kernel,
        sds((rank, width), F32),
        [pltpu.VMEM((3 * rank, rows), F32)],
        "error_right", None, 1.2e9,
    )(scaled, error_v)

    widths = [width * 3 // 4, width // 4]
    last, (got, right_raw) = after(ring[-1], (got, right_raw))
    newest = list(cut(last, widths))
    newest[0] = step(newest[0])

    keep, send = call(
        right_kernel,
        [sds((rank, half + 128), F32)] * 2,
        [
            pltpu.VMEM((3 * rank, (n - 1) * tok), F32),
            pltpu.VMEM((2, rank, half + 128), F32),
        ],
        "right",
    )(right_raw, held, got, extra, *ring)
    total = add(keep, swap(send, "dp", m, 1))

    for group in groups(m // 2):
        total = add(*terms_of(total, "dp", m, [2 * bit for bit in group]))
    for group in groups(n):
        parts = terms_of(total, "tensor", n, group)
        if group == groups(n)[-1]:
            newest[0], parts[1:] = after(newest[0], parts[1:])
        total = call(
            functools.partial(join_kernel, rank), sds(total.shape, F32), [], "join"
        )(*parts)
    for c in range(1, len(widths)):
        last, total = after(newest[c], total)
        newest[c] = step(last)

    terms = len(LEFT_TERMS) * rank
    other = swap(total, "dp", m, 1)
    left_terms, mine, mine_terms, inverse = call(
        functools.partial(half_kernel, m),
        [
            sds((rows, terms), BF16),
            sds((rank, half), F32),
            sds((terms, half), BF16),
            sds((8, 128), F32),
        ],
        [pltpu.VMEM((terms, rows), F32), pltpu.VMEM((terms, half), F32)],
        "half", None, 1e9,
    )(mean, total)
    whole, right_terms = call(
        factor_kernel,
        [sds((rank, width), F32), sds((terms, width), BF16)],
        [pltpu.VMEM((terms, half), F32)],
        "factor",
    )(other, mine, mine_terms, inverse)

    acts = call(
        functools.partial(acts_kernel, n),
        sds((rows, tokens), BF16),
        [pltpu.VMEM((tokens, rows), BF16)],
        "acts",
    )(activations)
    pieces = []
    at = 0
    for part, x in zip(widths, newest):
        pieces.append((at, part, ring + [x], [0] * (n - 1) + [at]))
        at += part

    outs = ()
    for at, part, slots, bases in pieces:
        last = at + part == width
        inputs = [acts, left_terms, right_terms, error_v, *slots] + [whole] * last
        outs = pl.pallas_call(
            functools.partial(final_kernel, at, part, bases, last),
            in_specs=[vmem] * len(inputs) + [pl.BlockSpec(memory_space=pl.ANY)] * len(outs),
            out_specs=[pl.BlockSpec(memory_space=pl.ANY)] * (2 + last),
            out_shape=[sds((rows, width), BF16), sds((1, rows, width), BF16)]
            + [sds((rank, width), F32)] * last,
            input_output_aliases={len(inputs) + k: k for k in range(len(outs))},
            scratch_shapes=[pltpu.VMEM((rows, part), BF16)] * 2 + [dma((4, 4 if part > half else 3, 2))],
            compiler_params=params(16),
            cost_estimate=cost(REBUILD),
            name="rebuild",
        )(*inputs, *outs)
    rebuilt, error, factor = outs
    return rebuilt, error, factor.T


def solution(mesh):
    return jax.shard_map(
        per_device,
        mesh=mesh,
        in_specs=(P("dp", None, "tensor"), P("dp", "tensor", None), P("dp", "tensor", None), P()),
        out_specs=(P("tensor", None), P("dp", "tensor", None), P()),
        check_vma=False,
    )
```
